32 devices in a mesh: group: 2 (over y), expert: 8 (over z, x), dp: 2 (over core).
Axes of the slice: x: 2, y: 2, z: 4, core: 2. Of those that a mesh axis runs over, the one named last changes fastest.
Arguments:
- tokens: bfloat16 [4096, 2048], P(('group', 'expert', 'dp')), parts along dimension 0, may hold values from -6 to 6
- routes: int32 [4096, 8], P(('group', 'expert', 'dp')), parts along dimension 0, may hold values from 0 to 15, as said below
- gate_levels: int32 [4096, 8], P(('group', 'expert', 'dp')), parts along dimension 0, may hold values from 1 to 1024
- latent_grad: bfloat16 [4096, 512], P(('group', 'expert', 'dp')), parts along dimension 0, may hold values from -6 to 6
- down_weight: bfloat16 [2048, 512], P(('expert', 'dp')), may hold values from -0.125 to 0.125
- expert_in: bfloat16 [16, 512, 512], P(('expert', 'dp')), may hold values from -0.25 to 0.25
- expert_out: bfloat16 [16, 512, 512], P(('expert', 'dp')), may hold values from -0.25 to 0.25
Outputs:
- latent_out: bfloat16 [4096, 512], P(('group', 'expert', 'dp')), parts along dimension 0
- grad_tokens: bfloat16 [4096, 2048], P(('group', 'expert', 'dp')), parts along dimension 0
- grad_down: float32 [4096, 512], P(('group', 'expert', 'dp')), parts along dimension 0
- grad_in: bfloat16 [32, 512, 512], P(('group', 'expert', 'dp')), parts along dimension 0
- grad_out: bfloat16 [32, 512, 512], P(('group', 'expert', 'dp')), parts along dimension 0
The draws below stay inside these ranges and needn't reach their ends.
There are 2 independent parts, one for each index of `group`. The reference program is written for one: setup_inputs(seed, part) draws one part's arguments, and reference() takes and returns one part's arrays. A program takes and returns all parts, laid end to end along the dimension named above; an argument that names none is the same for every part. Nothing has to cross between parts.
Inputs may be any that keep to these rules, and one draw needn't show every extreme that they name: `routes`: each row names 8 different experts. Among the 128 rows of one device no expert is named more than 96 times, and some expert is named exactly 96 times by the rows of every device.
All inputs are finite; a program needn't handle non-finite values.
Results may differ from the reference program's by a relative error of at most 0.0076.
Values may be sent and summed in bfloat16 or wider, within the bound.
No kernel may reach another device: no remote copies, remote signals or barrier semaphores. Data moves between devices by JAX's collectives and lax.ppermute only.
A program may use at most 128 MiB of HBM per device.

```python
import jax
import jax.numpy as jnp
from jax import lax

D = 2048
L = 512
H = 512
TOP = 8
TOK_DEV = 128
EXPERTS = 16
TOKENS = 2048
CAP = 96


def draw_routes(key, part):
    key = jax.random.fold_in(key, 11)
    blocks = TOKENS // TOK_DEV
    copies = EXPERTS * CAP
    keep_count = TOK_DEV * TOP
    level_key, block_key, pick_key = jax.random.split(key, 3)
    base_level = jax.random.randint(level_key, (EXPERTS,), 0, 3)
    forced = jax.random.randint(pick_key, (), 0, EXPERTS)
    owner = jnp.repeat(jnp.arange(EXPERTS, dtype=jnp.int32), CAP)

    def one_block(block_seed):
        first_key, second_key, third_key = jax.random.split(block_seed, 3)
        block_level = jax.random.randint(first_key, (EXPERTS,), 0, 3)
        level = base_level + block_level + jnp.where(jnp.arange(EXPERTS) == forced, 8, 0)
        level = jnp.repeat(level, CAP)
        noise = jax.random.randint(second_key, (copies,), 0, 4096)
        score = (level * 4096 + noise) * copies + jnp.arange(copies, dtype=jnp.int32)
        threshold = lax.top_k(score, keep_count)[0][keep_count - 1]
        chosen = (score >= threshold).astype(jnp.int32)
        position = jnp.cumsum(chosen) - 1
        target = jnp.where(chosen == 1, position, keep_count)
        slots = jnp.zeros((keep_count,), jnp.int32).at[target].set(owner, mode='drop')
        table = slots.reshape(TOP, TOK_DEV).T
        order = jax.random.permutation(third_key, TOK_DEV)
        return table[order]
    seeds = jax.random.split(block_key, blocks)
    return jax.vmap(one_block)(seeds).reshape(TOKENS, TOP).astype(jnp.int32)


def touch_ends(values, stream_key, least, largest):
    longest = values.shape.index(max(values.shape))
    spots = []
    for shift in (0, 1):
        where = [jax.random.randint(jax.random.fold_in(stream_key, axis), (), 0, length) for axis, length in enumerate(values.shape)]
        where[longest] = (where[longest] + shift) % values.shape[longest]
        spots.append(tuple(where))
    return values.at[spots[0]].set(least).at[spots[1]].set(largest)


def with_spikes(values, key, source, target, parts, factor):
    owner, partner = [(jnp.arange(values.shape[dim]) // (values.shape[dim] // parts)).reshape([-1 if axis == dim else 1 for axis in range(values.ndim)]) for dim in (source, target)]
    chosen = jax.random.permutation(key, parts)[partner]
    strong = (owner == chosen) | (owner == (partner + parts // 2) % parts)
    return jnp.where(strong, factor * values, values)


def level_of(own_key, extent, pieces, low, high):
    level = 1.0
    for dim, shards_of in pieces:
        steps = jax.random.uniform(jax.random.fold_in(jax.random.fold_in(own_key, 6), dim), (shards_of,), jnp.float32, low / len(pieces), high / len(pieces))
        level = level * jnp.repeat(jnp.exp(steps), extent[dim] // shards_of).reshape((-1,) + (1,) * (len(extent) - 1 - dim))
    return level


def normal_values(key, dims, scale, limit, shards=(), held_as=jnp.bfloat16):
    values = scale * jax.random.normal(key, dims, jnp.float32)
    if shards:
        values = values * level_of(key, dims, shards, -0.22, 0.18)
    return jnp.clip(values, -limit, limit).astype(held_as)


def noise_with(rng, shape, deviation, most, cuts, heavy, held_as=jnp.bfloat16):
    array = deviation * jax.random.normal(rng, shape, jnp.float32)
    if cuts:
        array = array * level_of(rng, shape, cuts, -0.22, 0.18)
    return jnp.clip(with_spikes(array, jax.random.fold_in(rng, 3), *heavy), -most, most).astype(held_as)


def setup_inputs(seed: int = 0, part: int = 0) -> dict:
    arg_keys = jax.random.split(jax.random.key(seed), 8)
    own_keys = jax.random.split(jax.random.fold_in(arg_keys[7], part), 8)
    tokens = noise_with(own_keys[0], (TOKENS, D), 1.0, 6.0, ((0, 16),), (0, 1, 16, 2.0))
    routes = draw_routes(jax.random.fold_in(jax.random.fold_in(arg_keys[7], part), 71), part)
    gate_levels = touch_ends(jax.random.randint(own_keys[2], (TOKENS, TOP), 1, 1025), jax.random.fold_in(own_keys[2], 1), 1, 1024).astype(jnp.int32)
    latent_grad = normal_values(own_keys[3], (TOKENS, L), 1.0, 6.0, ((0, 16),))
    down_weight = normal_values(arg_keys[4], (D, L), D ** -0.5, 0.125, ((0, 16),))
    expert_in = normal_values(arg_keys[5], (EXPERTS, L, H), L ** -0.5, 0.25, ((0, 16),))
    expert_out = normal_values(arg_keys[6], (EXPERTS, H, L), H ** -0.5, 0.25, ((0, 16),))
    return {"tokens": tokens, "routes": routes, "gate_levels": gate_levels, "latent_grad": latent_grad, "down_weight": down_weight, "expert_in": expert_in, "expert_out": expert_out}


gate_unit = 1.0 / 1024.0


def block_rank(block):
    count = block.shape[0]
    order = jnp.arange(count, dtype=jnp.int32)
    same = (block[:, None] == block[None, :]) & (order[None, :] < order[:, None])
    return jnp.sum(jnp.where(same, 1, 0), axis=1).astype(jnp.int32)


def reference(tokens, routes, gate_levels, latent_grad, down_weight, expert_in, expert_out):
    total = tokens.shape[0]
    blocks = total // TOK_DEV
    entries = total * TOP
    latent = jnp.dot(tokens, down_weight, preferred_element_type=jnp.float32).astype(jnp.bfloat16)
    gates = gate_levels.astype(jnp.float32) * gate_unit
    scaled = (gates[:, :, None] * latent_grad.astype(jnp.float32)[:, None, :]).astype(jnp.bfloat16)
    scaled = scaled.reshape(entries, L)
    flat_blocks = routes.reshape(blocks, TOK_DEV * TOP).astype(jnp.int32)
    ranks = lax.map(block_rank, flat_blocks)
    block_ids = jnp.arange(blocks, dtype=jnp.int32)[:, None]
    dest = flat_blocks * (blocks * CAP) + block_ids * CAP + ranks
    table = jnp.full((EXPERTS * blocks * CAP,), entries, jnp.int32)
    table = table.at[dest.reshape(-1)].set(jnp.arange(entries, dtype=jnp.int32))
    table = table.reshape(EXPERTS, blocks * CAP)
    latent_pad = jnp.concatenate([latent, jnp.zeros((1, L), jnp.bfloat16)], axis=0)
    scaled_pad = jnp.concatenate([scaled, jnp.zeros((1, L), jnp.bfloat16)], axis=0)
    gates_pad = jnp.concatenate([gates.reshape(-1), jnp.zeros((1,), jnp.float32)], axis=0)

    def expert_step(carry, inputs):
        combined, delta = carry
        source, w_in, w_out = inputs
        token_of = jnp.where(source < entries, source // TOP, total).astype(jnp.int32)
        rows = latent_pad[token_of]
        grads = scaled_pad[source]
        before = jnp.dot(rows, w_in, preferred_element_type=jnp.float32)
        active = jnp.maximum(before, 0.0)
        hidden = (active * active).astype(jnp.bfloat16)
        result = jnp.dot(hidden, w_out, preferred_element_type=jnp.float32).astype(jnp.bfloat16)
        back_hidden = jnp.dot(grads, w_out.T, preferred_element_type=jnp.float32)
        back_pre = (back_hidden * 2.0 * active).astype(jnp.bfloat16)
        dw_out = jnp.dot(hidden.T, grads, preferred_element_type=jnp.float32).astype(jnp.bfloat16)
        dw_in = jnp.dot(rows.T, back_pre, preferred_element_type=jnp.float32).astype(jnp.bfloat16)
        back_rows = jnp.dot(back_pre, w_in.T, preferred_element_type=jnp.float32).astype(jnp.bfloat16)
        weights = gates_pad[source]
        combined = combined.at[token_of].add(weights[:, None] * result.astype(jnp.float32))
        delta = delta.at[token_of].add(back_rows.astype(jnp.float32))
        return (combined, delta), (dw_in, dw_out)

    start = (jnp.zeros((total + 1, L), jnp.float32), jnp.zeros((total + 1, L), jnp.float32))
    (combined, delta), (grad_in, grad_out) = lax.scan(expert_step, start, (table, expert_in, expert_out))
    latent_out = combined[:total].astype(jnp.bfloat16)
    latent_delta = delta[:total].astype(jnp.bfloat16)
    grad_tokens = jnp.dot(latent_delta, down_weight.T, preferred_element_type=jnp.float32).astype(jnp.bfloat16)
    grad_down = jnp.dot(tokens.T, latent_delta, preferred_element_type=jnp.float32)
    return (latent_out, grad_tokens, grad_down, grad_in, grad_out)
```

```python
import jax
import jax.numpy as jnp
from jax import lax
from jax.sharding import PartitionSpec as P

gate_unit = 1.0 / 1024.0
contract_last = (((1,), (1,)), ((), ()))
contract_first = (((0,), (0,)), ((), ()))
plane = ("expert", "dp")


def device_pairs(n_line, move):
    pairs = []
    for z in range(n_line):
        for x in range(2):
            for c in range(2):
                to_z, to_x, to_c = move(z, x, c)
                pairs.append(((z * 2 + x) * 2 + c, (to_z * 2 + to_x) * 2 + to_c))
    return pairs


def turn(value, n_line, by):
    return lax.ppermute(value, plane, device_pairs(n_line, lambda z, x, c: ((z + by) % n_line, x, c)))


def swap_x(value, n_line):
    return lax.ppermute(value, plane, device_pairs(n_line, lambda z, x, c: (z, 1 - x, c)))


def swap_core(value, n_line):
    return lax.ppermute(value, plane, device_pairs(n_line, lambda z, x, c: (z, x, 1 - c)))


def spread(rows, n_line):
    line = jnp.stack([rows] + [turn(rows, n_line, by) for by in range(1, n_line)])
    sheet = jnp.stack([line, swap_x(line, n_line)])
    return jnp.stack([sheet, swap_core(sheet, n_line)])


def add_up(parts, n_line):
    wide = jnp.float32
    half = parts[0].astype(wide) + swap_core(parts[1], n_line).astype(wide)
    half = half.astype(jnp.bfloat16)
    line = half[0].astype(wide) + swap_x(half[1], n_line).astype(wide)
    line = line.astype(jnp.bfloat16)
    return add_line(line, n_line)


def add_line(line, n_line):
    total = line[0].astype(jnp.float32)
    for back in range(1, n_line):
        total = total + turn(line[back], n_line, n_line - back).astype(jnp.float32)
    return total


def all_rows(tokens, routes, gate_levels, latent_grad, down_weight, expert_in, expert_out):
    tok_rows = tokens.shape[0]
    width = tokens.shape[1]
    latent_width = down_weight.shape[1]
    n_major = lax.axis_size("expert")
    n_line = n_major // 2
    n_experts = n_major * 2
    block = width // n_experts
    place = lax.axis_index("expert")
    my_z, my_x, my_c = place // 2, place % 2, lax.axis_index("dp")
    core, side, back = jnp.meshgrid(jnp.arange(2), jnp.arange(2), jnp.arange(n_line), indexing="ij")
    order = ((my_z - back) % n_line * 2 + (my_x + side) % 2) * 2 + (my_c + core) % 2
    order = order.reshape(-1).astype(jnp.int32)

    experts = jnp.arange(n_experts, dtype=jnp.int32)
    levels = jnp.sum(
        jnp.where(routes[:, :, None] == experts, gate_levels[:, :, None], 0), axis=1
    )
    gates = levels.astype(jnp.float32) * gate_unit
    all_gates = lax.all_gather(gates.T, plane, axis=0, tiled=False)
    my_expert = place * 2 + my_c
    my_gates = lax.dynamic_index_in_dim(all_gates, my_expert, 1, keepdims=False)[order].reshape(-1, 1)

    full_down = spread(down_weight, n_line).reshape(width, latent_width)
    token_blocks = tokens.reshape(tok_rows, n_experts, block)
    turned_tokens = jnp.take(token_blocks, order, axis=1).reshape(tok_rows, width)
    latent = jnp.dot(turned_tokens, full_down, preferred_element_type=jnp.float32)
    latent = latent.astype(jnp.bfloat16)
    rows = spread(latent, n_line).reshape(-1, latent_width)
    cotangent = spread(latent_grad, n_line).reshape(-1, latent_width)
    scaled = (my_gates * cotangent.astype(jnp.float32)).astype(jnp.bfloat16)

    weight_in = expert_in[0]
    weight_out = expert_out[0]
    before = jnp.dot(rows, weight_in, preferred_element_type=jnp.float32)
    active = jnp.maximum(before, 0.0)
    hidden = (active * active).astype(jnp.bfloat16)
    result = jnp.dot(hidden, weight_out, preferred_element_type=jnp.float32).astype(jnp.bfloat16)
    back_hidden = lax.dot_general(
        scaled, weight_out, contract_last, preferred_element_type=jnp.float32
    )
    back_pre = (back_hidden * 2.0 * active).astype(jnp.bfloat16)
    grad_out = lax.dot_general(
        hidden, scaled, contract_first, preferred_element_type=jnp.float32
    ).astype(jnp.bfloat16)
    grad_in = lax.dot_general(
        rows, back_pre, contract_first, preferred_element_type=jnp.float32
    ).astype(jnp.bfloat16)
    back_rows = lax.dot_general(
        back_pre, weight_in, contract_last, preferred_element_type=jnp.float32
    ).astype(jnp.bfloat16)
    parts = (2, 2, n_line, tok_rows, latent_width)
    latent_delta = add_up(back_rows.reshape(parts), n_line).astype(jnp.bfloat16)
    weighted = (my_gates * result.astype(jnp.float32)).astype(jnp.bfloat16)
    latent_out = add_up(weighted.reshape(parts), n_line).astype(jnp.bfloat16)

    turned_grad = lax.dot_general(
        latent_delta, full_down, contract_last, preferred_element_type=jnp.float32
    ).astype(jnp.bfloat16)
    undo = jnp.zeros((n_experts,), jnp.int32).at[order].set(experts)
    grad_tokens = jnp.take(turned_grad.reshape(tok_rows, n_experts, block), undo, axis=1)
    grad_tokens = grad_tokens.reshape(tok_rows, width)

    kept = turned_tokens.reshape(tok_rows, 2, 2, n_line * block).transpose(1, 2, 0, 3)
    by_x = jnp.stack([kept[:, 0], swap_x(kept[:, 1], n_line)])
    by_core = jnp.stack([by_x[:, 0], swap_core(by_x[:, 1], n_line)])
    near_tokens = by_core.reshape(4 * tok_rows, n_line * block)
    near_delta = jnp.stack([latent_delta, swap_x(latent_delta, n_line)])
    near_delta = jnp.stack([near_delta, swap_core(near_delta, n_line)])
    near_delta = near_delta.reshape(4 * tok_rows, latent_width)
    partial = lax.dot_general(
        near_tokens, near_delta, contract_first, preferred_element_type=jnp.float32
    )
    grad_down = add_line(partial.astype(jnp.bfloat16).reshape(n_line, block, latent_width), n_line)
    return (latent_out, grad_tokens, grad_down, grad_in[None], grad_out[None])


def slot_table(routes, capacity):
    flat = routes.reshape(-1)
    count = flat.shape[0]
    order = jnp.arange(count, dtype=jnp.int32)
    same = (flat[:, None] == flat[None, :]) & (order[None, :] < order[:, None])
    placed = jnp.sum(jnp.where(same, 1, 0), axis=1).astype(jnp.int32)
    return flat * capacity + placed


def routed_rows(tokens, routes, gate_levels, latent_grad, down_weight, expert_in, expert_out):
    tok_rows = tokens.shape[0]
    top = routes.shape[1]
    latent_width = down_weight.shape[1]
    n_major = lax.axis_size("expert")
    n_minor = lax.axis_size("dp")
    n_experts = n_major * n_minor
    capacity = 3 * tok_rows * top // (2 * n_experts)
    entries = tok_rows * top
    contract_last = (((1,), (1,)), ((), ()))
    contract_first = (((0,), (0,)), ((), ()))
    full_down = lax.all_gather(down_weight, ("expert", "dp"), axis=0, tiled=True)
    latent = jnp.dot(tokens, full_down, preferred_element_type=jnp.float32)
    latent = latent.astype(jnp.bfloat16)
    dest = slot_table(routes, capacity)
    source = (
        jnp.full((n_experts * capacity,), entries, jnp.int32)
        .at[dest]
        .set(jnp.arange(entries, dtype=jnp.int32))
    )
    token_of = jnp.where(source < entries, source // top, tok_rows)
    gates = gate_levels.astype(jnp.float32) * gate_unit
    zero_row = jnp.zeros((1, latent_width), jnp.bfloat16)
    latent_pad = jnp.concatenate([latent, zero_row], axis=0)
    send_latent = latent_pad[token_of].reshape(n_major, n_minor, capacity, latent_width)
    scaled = (gates[:, :, None] * latent_grad.astype(jnp.float32)[:, None, :]).astype(jnp.bfloat16)
    scaled_pad = jnp.concatenate([scaled.reshape(entries, latent_width), zero_row], axis=0)
    send_grad = scaled_pad[source].reshape(n_major, n_minor, capacity, latent_width)
    arrived = lax.all_to_all(
        lax.all_to_all(send_latent, "expert", split_axis=0, concat_axis=0, tiled=True),
        "dp",
        split_axis=1,
        concat_axis=1,
        tiled=True,
    )
    rows = arrived.reshape(-1, latent_width)
    weight_in = expert_in[0]
    weight_out = expert_out[0]
    before = jnp.dot(rows, weight_in, preferred_element_type=jnp.float32)
    active = jnp.maximum(before, 0.0)
    hidden = (active * active).astype(jnp.bfloat16)
    result = jnp.dot(hidden, weight_out, preferred_element_type=jnp.float32).astype(jnp.bfloat16)
    returned = lax.all_to_all(
        lax.all_to_all(
            result.reshape(n_major, n_minor, capacity, latent_width),
            "expert",
            split_axis=0,
            concat_axis=0,
            tiled=True,
        ),
        "dp",
        split_axis=1,
        concat_axis=1,
        tiled=True,
    )
    picked = returned.reshape(n_experts * capacity, latent_width)[dest].astype(jnp.float32)
    picked = picked.reshape(tok_rows, top, latent_width)
    latent_out = jnp.sum(gates[:, :, None] * picked, axis=1).astype(jnp.bfloat16)
    arrived_grad = lax.all_to_all(
        lax.all_to_all(send_grad, "expert", split_axis=0, concat_axis=0, tiled=True),
        "dp",
        split_axis=1,
        concat_axis=1,
        tiled=True,
    )
    grad_rows = arrived_grad.reshape(-1, latent_width)
    back_hidden = lax.dot_general(
        grad_rows, weight_out, contract_last, preferred_element_type=jnp.float32
    )
    back_pre = (back_hidden * 2.0 * active).astype(jnp.bfloat16)
    grad_out = lax.dot_general(
        hidden, grad_rows, contract_first, preferred_element_type=jnp.float32
    ).astype(jnp.bfloat16)
    grad_in = lax.dot_general(
        rows, back_pre, contract_first, preferred_element_type=jnp.float32
    ).astype(jnp.bfloat16)
    back_rows = lax.dot_general(
        back_pre, weight_in, contract_last, preferred_element_type=jnp.float32
    ).astype(jnp.bfloat16)
    came_back = lax.all_to_all(
        lax.all_to_all(
            back_rows.reshape(n_major, n_minor, capacity, latent_width),
            "expert",
            split_axis=0,
            concat_axis=0,
            tiled=True,
        ),
        "dp",
        split_axis=1,
        concat_axis=1,
        tiled=True,
    )
    gathered_back = came_back.reshape(n_experts * capacity, latent_width)[dest].astype(jnp.float32)
    latent_delta = jnp.sum(gathered_back.reshape(tok_rows, top, latent_width), axis=1).astype(
        jnp.bfloat16
    )
    grad_tokens = lax.dot_general(
        latent_delta, full_down, contract_last, preferred_element_type=jnp.float32
    )
    grad_tokens = grad_tokens.astype(jnp.bfloat16)
    grad_down = lax.psum_scatter(
        lax.dot_general(tokens, latent_delta, contract_first, preferred_element_type=jnp.float32),
        ("expert", "dp"),
        scatter_dimension=0,
        tiled=True,
    )
    return (latent_out, grad_tokens, grad_down, grad_in[None], grad_out[None])


def on_device(tokens, routes, *others):
    n_major = lax.axis_size("expert")
    n_experts = n_major * lax.axis_size("dp")
    few = n_experts <= 2 * routes.shape[1] and n_major % 2 == 0 and lax.axis_size("dp") == 2
    return (all_rows if few else routed_rows)(tokens, routes, *others)


def solution(mesh):
    in_specs = (
        P(("group", "expert", "dp"), None),
        P(("group", "expert", "dp"), None),
        P(("group", "expert", "dp"), None),
        P(("group", "expert", "dp"), None),
        P(("expert", "dp"), None),
        P(("expert", "dp"), None, None),
        P(("expert", "dp"), None, None),
    )
    out_specs = (
        P(("group", "expert", "dp"), None),
        P(("group", "expert", "dp"), None),
        P(("group", "expert", "dp"), None),
        P(("group", "expert", "dp"), None, None),
        P(("group", "expert", "dp"), None, None),
    )
    return jax.shard_map(
        on_device, mesh=mesh, in_specs=in_specs, out_specs=out_specs, check_vma=False
    )
```

```python
import functools

import jax
import jax.numpy as jnp
from jax import lax
from jax.experimental import pallas as pl
from jax.experimental.pallas import tpu as pltpu
from jax.sharding import PartitionSpec as P

gate_unit = 1.0 / 1024.0
contract_last = (((1,), (1,)), ((), ()))
contract_first = (((0,), (0,)), ((), ()))
plane = ("expert", "dp")
wide = jnp.float32
narrow = jnp.bfloat16


def device_pairs(n_line, move):
    pairs = []
    for z in range(n_line):
        for x in range(2):
            for c in range(2):
                to_z, to_x, to_c = move(z, x, c)
                pairs.append(((z * 2 + x) * 2 + c, (to_z * 2 + to_x) * 2 + to_c))
    return pairs


def turn(value, n_line, by):
    return lax.ppermute(value, plane, device_pairs(n_line, lambda z, x, c: ((z + by) % n_line, x, c)))


def swap(value, n_line, core, side):
    return lax.ppermute(value, plane, device_pairs(n_line, lambda z, x, c: (z, x ^ side, c ^ core)))


def after(value, *earlier):
    return lax.optimization_barrier((value,) + earlier)[0]


def call(body, outs, name, scratch=(), flops=0, nbytes=0):
    vmem = pl.BlockSpec(memory_space=pltpu.VMEM)

    def run(place, *operands):
        return pl.pallas_call(
            body,
            out_shape=outs,
            in_specs=[pl.BlockSpec(memory_space=pltpu.SMEM)] + [vmem] * len(operands),
            out_specs=[vmem] * len(outs),
            scratch_shapes=list(scratch),
            compiler_params=pltpu.CompilerParams(vmem_limit_bytes=40 * 1024 * 1024),
            cost_estimate=pl.CostEstimate(flops=flops, bytes_accessed=nbytes, transcendentals=0),
            name=name,
        )(place, *operands)

    return run


def prepare_body(n_line, block, place, tokens, routes, levels, cotangent, *outs):
    pieces, payload = outs[:4], outs[4]
    for core in range(2):
        for side in range(2):
            owner = (place[1] ^ side) * 2 + (place[2] ^ core)
            for z in range(n_line):
                start = pl.multiple_of((z * 4 + owner) * block, block)
                pieces[core * 2 + side][:, z * block : (z + 1) * block] = tokens[:, pl.ds(start, block)]
    tok_rows = cotangent.shape[0]
    gate_rows = payload.shape[0] - tok_rows
    payload[:tok_rows, :] = cotangent[...]
    expert = lax.broadcasted_iota(jnp.int32, (gate_rows, tok_rows), 0)
    total = jnp.zeros((gate_rows, tok_rows), jnp.int32)
    for k in range(routes.shape[0]):
        total = total + jnp.where(expert == routes[k : k + 1, :], levels[k : k + 1, :], 0)
    low = total & 31
    payload[tok_rows:, :tok_rows] = (total - low).astype(wide).astype(narrow)
    payload[tok_rows:, tok_rows : 2 * tok_rows] = low.astype(wide).astype(narrow)
    rest = payload.shape[1] - 2 * tok_rows
    payload[tok_rows:, 2 * tok_rows :] = jnp.zeros((gate_rows, rest), narrow)


def project_body(n_line, place, *refs):
    pieces, downs = refs[:4], refs[4 : 4 + n_line]
    keep, send, down = refs[4 + n_line :]
    block = downs[0].shape[0]
    for back in range(n_line):
        z = lax.rem(place[0] + n_line - back, n_line)
        down[pl.ds(pl.multiple_of(z * block, block), block), :] = downs[back][...]
    for core, out in ((1, send), (0, keep)):
        for side in range(2):
            out[side] = jnp.dot(pieces[core * 2 + side][...], down[...], preferred_element_type=wide)


def gate_tile(payload, tok_rows, expert):
    packed = payload[tok_rows:, :]
    rows = lax.broadcasted_iota(jnp.int32, (packed.shape[0], 128), 0)
    pick = jnp.where(rows == expert, 1.0, 0.0).astype(narrow)
    dot = functools.partial(lax.dot_general, dimension_numbers=contract_first, preferred_element_type=wide)
    total = dot(packed[:, :tok_rows], pick) + dot(packed[:, tok_rows : 2 * tok_rows], pick)
    return total * gate_unit


def expert_body(count, place, *refs):
    rows_in, payloads = refs[:count], refs[count : 2 * count]
    weights = refs[2 * count : 2 * count + 4]
    outs = refs[2 * count + 4 :]
    combined, deltas = outs[:count], outs[count : 2 * count]
    hiddens, scaleds, back_pres = outs[2 * count :]
    tok_rows, width = rows_in[0].shape
    for first in range(0, count, 2):
        pair = (first, first + 1)
        span = slice(first * tok_rows, (first + 2) * tok_rows)
        rows = jnp.concatenate([rows_in[i][...] for i in pair], axis=0)
        cotangent = jnp.concatenate([payloads[i][:tok_rows, :] for i in pair], axis=0).astype(wide)
        out_sum = jnp.zeros((2 * tok_rows, width), wide)
        delta_sum = jnp.zeros((2 * tok_rows, width), wide)
        for e in range(2):
            weight_in, weight_out = weights[2 * e], weights[2 * e + 1]
            expert = place[3 + e]
            gate = jnp.concatenate([gate_tile(payloads[i], tok_rows, expert) for i in pair], axis=0)
            gate = jnp.concatenate([gate] * (width // 128), axis=1)
            active = jnp.maximum(jnp.dot(rows, weight_in[...], preferred_element_type=wide), 0.0)
            hidden = (active * active).astype(narrow)
            hiddens[e, span, :] = hidden
            scaled = (gate * cotangent).astype(narrow)
            scaleds[e, span, :] = scaled
            back_hidden = lax.dot_general(scaled, weight_out[...], contract_last, preferred_element_type=wide)
            back_pre = (back_hidden * 2.0 * active).astype(narrow)
            back_pres[e, span, :] = back_pre
            result = jnp.dot(hidden, weight_out[...], preferred_element_type=wide).astype(narrow)
            out_sum = out_sum + gate * result.astype(wide)
            back_rows = lax.dot_general(back_pre, weight_in[...], contract_last, preferred_element_type=wide)
            delta_sum = delta_sum + back_rows.astype(narrow).astype(wide)
        for i in pair:
            part = slice((i - first) * tok_rows, (i - first + 1) * tok_rows)
            combined[i][...] = out_sum[part].astype(combined[i].dtype)
            deltas[i][...] = delta_sum[part].astype(deltas[i].dtype)


def weight_grad_body(n_rows, n_sets, place, *refs):
    rows_in = refs[:n_rows]
    sets = [refs[n_rows + 3 * i : n_rows + 3 * i + 3] for i in range(n_sets)]
    keep_in, keep_out, send_in, send_out = refs[n_rows + 3 * n_sets :]
    dot = functools.partial(lax.dot_general, dimension_numbers=contract_first, preferred_element_type=wide)
    rows = jnp.concatenate([r[...] for r in rows_in], axis=0)
    for e, out_in, out_out in ((1, send_in, send_out), (0, keep_in, keep_out)):
        hidden = jnp.concatenate([s[0][e] for s in sets], axis=0)
        scaled = jnp.concatenate([s[1][e] for s in sets], axis=0)
        back_pre = jnp.concatenate([s[2][e] for s in sets], axis=0)
        out_out[...] = dot(hidden, scaled).astype(out_out.dtype)
        out_in[...] = dot(rows, back_pre).astype(out_in.dtype)


def tail_body(n_line, place, *refs):
    pieces, deltas, down = refs[:4], refs[4:8], refs[8]
    blocks, grads = refs[9 : 9 + n_line], refs[9 + n_line :]
    tokens = jnp.concatenate([p[...] for p in pieces], axis=0)
    delta = jnp.concatenate([d[...] for d in deltas], axis=0)
    part = lax.dot_general(tokens, delta, contract_first, preferred_element_type=wide)
    block = blocks[0].shape[0]
    for z in range(n_line):
        for back in range(n_line):

            @pl.when(lax.rem(place[0] + n_line - back, n_line) == z)
            def _(z=z, back=back):
                blocks[back][...] = part[z * block : (z + 1) * block].astype(blocks[back].dtype)

    for i in range(4):
        grads[i][...] = lax.dot_general(
            deltas[i][...], down[...], contract_last, preferred_element_type=wide
        ).astype(narrow)


def arrange_body(n_line, block, place, *refs):
    pieces, out = refs[:4], refs[4]
    for core in range(2):
        for side in range(2):
            owner = (place[1] ^ side) * 2 + (place[2] ^ core)
            for z in range(n_line):
                start = pl.multiple_of((z * 4 + owner) * block, block)
                out[:, pl.ds(start, block)] = pieces[core * 2 + side][:, z * block : (z + 1) * block]


def all_rows(tokens, routes, gate_levels, latent_grad, down_weight, expert_in, expert_out):
    tok_rows, width = tokens.shape
    latent_width = down_weight.shape[1]
    hidden_width = expert_in.shape[2]
    n_major = lax.axis_size("expert")
    n_line = n_major // 2
    n_experts = n_major * 2
    block = width // n_experts
    major = lax.axis_index("expert")
    my_core = lax.axis_index("dp")
    place = jnp.stack(
        [major // 2, major % 2, my_core, major * 2 + my_core, major * 2 + 1 - my_core]
    ).astype(jnp.int32)
    shape = jax.ShapeDtypeStruct
    rows_of = lambda kind: shape((tok_rows, latent_width), kind)

    downs = [down_weight] + [turn(down_weight, n_line, back) for back in range(1, n_line)]

    gate_rows = -(-n_experts // 16) * 16
    prepare = call(
        functools.partial(prepare_body, n_line, block),
        [shape((tok_rows, n_line * block), narrow)] * 4 + [shape((tok_rows + gate_rows, latent_width), narrow)],
        "prepare",
        nbytes=3 * tok_rows * width * 2,
    )
    *columns, payload = prepare(place, tokens, routes.T, gate_levels.T, latent_grad)
    near_tokens = [
        columns[core * 2 + side] if core + side == 0 else swap(columns[core * 2 + side], n_line, core, side)
        for core in range(2)
        for side in range(2)
    ]
    own = (expert_in[0], expert_out[0])
    weights = own + tuple(swap(w, n_line, 1, 0) for w in own)

    project = call(
        functools.partial(project_body, n_line),
        [shape((2, tok_rows, latent_width), wide)] * 2 + [shape((n_line * block, latent_width), narrow)],
        "project",
        flops=2 * 4 * tok_rows * n_line * block * latent_width,
    )
    keep, send, down = project(place, *near_tokens, *downs)
    half = keep + swap(send, n_line, 1, 0)
    latent = (half[0] + swap(half[1], n_line, 0, 1)).astype(narrow)

    payload = after(payload, downs[-1])
    payloads = [payload] + [turn(payload, n_line, back) for back in range(1, n_line)]
    far_payloads = [swap(p, n_line, 0, 1) for p in payloads]
    rows = [latent] + [turn(latent, n_line, back) for back in range(1, n_line)]
    far_rows = [swap(r, n_line, 0, 1) for r in rows]

    def experts(count, kind, name):
        saved = shape((2, count * tok_rows, hidden_width), narrow)
        return call(
            functools.partial(expert_body, count),
            [rows_of(kind)] * (2 * count) + [saved] * 3,
            name,
            flops=2 * 2 * 4 * count * tok_rows * latent_width * hidden_width,
            nbytes=4 * latent_width * hidden_width * 2,
        )

    outs = experts(n_line, wide, "near_experts")(place, *rows, *payloads, *weights)
    near_out, near_delta, near_saved = outs[:n_line], outs[n_line : 2 * n_line], outs[2 * n_line :]
    outs = experts(n_line, narrow, "far_experts")(place, *far_rows, *far_payloads, *weights)
    far_out, far_delta, far_saved = outs[:n_line], outs[n_line : 2 * n_line], outs[2 * n_line :]

    def return_sums(near, far):
        total = None
        for back in [*range(1, n_line), 0]:
            line = near[back] + swap(far[back], n_line, 0, 1).astype(wide)
            if back:
                line = turn(line.astype(narrow), n_line, n_line - back).astype(wide)
            total = line if total is None else total + line
        return total.astype(narrow)

    delta = return_sums(near_delta, far_delta)
    latent_out = return_sums(near_out, far_out)

    weight_grad = call(
        functools.partial(weight_grad_body, 2 * n_line, 2),
        [shape((latent_width, hidden_width), wide), shape((hidden_width, latent_width), wide)]
        + [shape((latent_width, hidden_width), narrow), shape((hidden_width, latent_width), narrow)],
        "weight_grads",
        flops=2 * 2 * 2 * 2 * n_line * tok_rows * latent_width * hidden_width,
    )
    keep_in, keep_out, send_in, send_out = weight_grad(place, *rows, *far_rows, *near_saved, *far_saved)
    grad_in = (keep_in + swap(send_in, n_line, 1, 0).astype(wide)).astype(narrow)
    grad_out = (keep_out + swap(send_out, n_line, 1, 0).astype(wide)).astype(narrow)

    side_delta = swap(delta, n_line, 0, 1)
    deltas = [delta, side_delta, swap(delta, n_line, 1, 0), swap(side_delta, n_line, 1, 0)]
    tail = call(
        functools.partial(tail_body, n_line),
        [shape((block, latent_width), wide)]
        + [shape((block, latent_width), narrow)] * (n_line - 1)
        + [shape((tok_rows, n_line * block), narrow)] * 4,
        "tail",
        flops=2 * 2 * 4 * tok_rows * n_line * block * latent_width,
    )
    outs = tail(place, *near_tokens, *deltas, down)
    blocks, grads = outs[:n_line], outs[n_line:]
    grad_down = blocks[0]
    for back in range(1, n_line):
        grad_down = grad_down + turn(blocks[back], n_line, n_line - back).astype(wide)
    grads = [
        grads[core * 2 + side] if core + side == 0 else swap(grads[core * 2 + side], n_line, core, side)
        for core in range(2)
        for side in range(2)
    ]
    arrange = call(
        functools.partial(arrange_body, n_line, block),
        [shape((tok_rows, width), narrow)],
        "arrange",
        nbytes=2 * tok_rows * width * 2,
    )
    (grad_tokens,) = arrange(place, *grads)
    return (latent_out, grad_tokens, grad_down, grad_in[None], grad_out[None])


def slot_table(routes, capacity):
    flat = routes.reshape(-1)
    count = flat.shape[0]
    order = jnp.arange(count, dtype=jnp.int32)
    same = (flat[:, None] == flat[None, :]) & (order[None, :] < order[:, None])
    placed = jnp.sum(jnp.where(same, 1, 0), axis=1).astype(jnp.int32)
    return flat * capacity + placed


def routed_rows(tokens, routes, gate_levels, latent_grad, down_weight, expert_in, expert_out):
    tok_rows = tokens.shape[0]
    top = routes.shape[1]
    latent_width = down_weight.shape[1]
    n_major = lax.axis_size("expert")
    n_minor = lax.axis_size("dp")
    n_experts = n_major * n_minor
    capacity = 3 * tok_rows * top // (2 * n_experts)
    entries = tok_rows * top
    contract_last = (((1,), (1,)), ((), ()))
    contract_first = (((0,), (0,)), ((), ()))
    full_down = lax.all_gather(down_weight, ("expert", "dp"), axis=0, tiled=True)
    latent = jnp.dot(tokens, full_down, preferred_element_type=jnp.float32)
    latent = latent.astype(jnp.bfloat16)
    dest = slot_table(routes, capacity)
    source = (
        jnp.full((n_experts * capacity,), entries, jnp.int32)
        .at[dest]
        .set(jnp.arange(entries, dtype=jnp.int32))
    )
    token_of = jnp.where(source < entries, source // top, tok_rows)
    gates = gate_levels.astype(jnp.float32) * gate_unit
    zero_row = jnp.zeros((1, latent_width), jnp.bfloat16)
    latent_pad = jnp.concatenate([latent, zero_row], axis=0)
    send_latent = latent_pad[token_of].reshape(n_major, n_minor, capacity, latent_width)
    scaled = (gates[:, :, None] * latent_grad.astype(jnp.float32)[:, None, :]).astype(jnp.bfloat16)
    scaled_pad = jnp.concatenate([scaled.reshape(entries, latent_width), zero_row], axis=0)
    send_grad = scaled_pad[source].reshape(n_major, n_minor, capacity, latent_width)
    arrived = lax.all_to_all(
        lax.all_to_all(send_latent, "expert", split_axis=0, concat_axis=0, tiled=True),
        "dp",
        split_axis=1,
        concat_axis=1,
        tiled=True,
    )
    rows = arrived.reshape(-1, latent_width)
    weight_in = expert_in[0]
    weight_out = expert_out[0]
    before = jnp.dot(rows, weight_in, preferred_element_type=jnp.float32)
    active = jnp.maximum(before, 0.0)
    hidden = (active * active).astype(jnp.bfloat16)
    result = jnp.dot(hidden, weight_out, preferred_element_type=jnp.float32).astype(jnp.bfloat16)
    returned = lax.all_to_all(
        lax.all_to_all(
            result.reshape(n_major, n_minor, capacity, latent_width),
            "expert",
            split_axis=0,
            concat_axis=0,
            tiled=True,
        ),
        "dp",
        split_axis=1,
        concat_axis=1,
        tiled=True,
    )
    picked = returned.reshape(n_experts * capacity, latent_width)[dest].astype(jnp.float32)
    picked = picked.reshape(tok_rows, top, latent_width)
    latent_out = jnp.sum(gates[:, :, None] * picked, axis=1).astype(jnp.bfloat16)
    arrived_grad = lax.all_to_all(
        lax.all_to_all(send_grad, "expert", split_axis=0, concat_axis=0, tiled=True),
        "dp",
        split_axis=1,
        concat_axis=1,
        tiled=True,
    )
    grad_rows = arrived_grad.reshape(-1, latent_width)
    back_hidden = lax.dot_general(
        grad_rows, weight_out, contract_last, preferred_element_type=jnp.float32
    )
    back_pre = (back_hidden * 2.0 * active).astype(jnp.bfloat16)
    grad_out = lax.dot_general(
        hidden, grad_rows, contract_first, preferred_element_type=jnp.float32
    ).astype(jnp.bfloat16)
    grad_in = lax.dot_general(
        rows, back_pre, contract_first, preferred_element_type=jnp.float32
    ).astype(jnp.bfloat16)
    back_rows = lax.dot_general(
        back_pre, weight_in, contract_last, preferred_element_type=jnp.float32
    ).astype(jnp.bfloat16)
    came_back = lax.all_to_all(
        lax.all_to_all(
            back_rows.reshape(n_major, n_minor, capacity, latent_width),
            "expert",
            split_axis=0,
            concat_axis=0,
            tiled=True,
        ),
        "dp",
        split_axis=1,
        concat_axis=1,
        tiled=True,
    )
    gathered_back = came_back.reshape(n_experts * capacity, latent_width)[dest].astype(jnp.float32)
    latent_delta = jnp.sum(gathered_back.reshape(tok_rows, top, latent_width), axis=1).astype(
        jnp.bfloat16
    )
    grad_tokens = lax.dot_general(
        latent_delta, full_down, contract_last, preferred_element_type=jnp.float32
    )
    grad_tokens = grad_tokens.astype(jnp.bfloat16)
    grad_down = lax.psum_scatter(
        lax.dot_general(tokens, latent_delta, contract_first, preferred_element_type=jnp.float32),
        ("expert", "dp"),
        scatter_dimension=0,
        tiled=True,
    )
    return (latent_out, grad_tokens, grad_down, grad_in[None], grad_out[None])


def on_device(tokens, routes, *others):
    n_major = lax.axis_size("expert")
    n_experts = n_major * lax.axis_size("dp")
    few = n_experts <= 2 * routes.shape[1] and n_major % 4 == 0 and lax.axis_size("dp") == 2
    return (all_rows if few else routed_rows)(tokens, routes, *others)


def solution(mesh):
    in_specs = (
        P(("group", "expert", "dp"), None),
        P(("group", "expert", "dp"), None),
        P(("group", "expert", "dp"), None),
        P(("group", "expert", "dp"), None),
        P(("expert", "dp"), None),
        P(("expert", "dp"), None, None),
        P(("expert", "dp"), None, None),
    )
    out_specs = (
        P(("group", "expert", "dp"), None),
        P(("group", "expert", "dp"), None),
        P(("group", "expert", "dp"), None),
        P(("group", "expert", "dp"), None, None),
        P(("group", "expert", "dp"), None, None),
    )
    return jax.shard_map(
        on_device, mesh=mesh, in_specs=in_specs, out_specs=out_specs, check_vma=False
    )
```

```python
import functools

import jax
import jax.numpy as jnp
from jax import lax
from jax.experimental import pallas as pl
from jax.experimental.pallas import tpu as pltpu
from jax.sharding import PartitionSpec as P

gate_unit = 1.0 / 1024.0
contract_last = (((1,), (1,)), ((), ()))
contract_first = (((0,), (0,)), ((), ()))
plane = ("expert", "dp")
wide = jnp.float32
narrow = jnp.bfloat16


def device_pairs(n_line, move):
    pairs = []
    for z in range(n_line):
        for x in range(2):
            for c in range(2):
                to_z, to_x, to_c = move(z, x, c)
                pairs.append(((z * 2 + x) * 2 + c, (to_z * 2 + to_x) * 2 + to_c))
    return pairs


def turn(value, n_line, by):
    return lax.ppermute(value, plane, device_pairs(n_line, lambda z, x, c: ((z + by) % n_line, x, c)))


def swap(value, n_line, core, side):
    return lax.ppermute(value, plane, device_pairs(n_line, lambda z, x, c: (z, x ^ side, c ^ core)))


def after(value, *earlier):
    return lax.optimization_barrier((value,) + earlier)[0]


def call(body, outs, name, scratch=(), flops=0, nbytes=0):
    vmem = pl.BlockSpec(memory_space=pltpu.VMEM)

    def run(place, *operands):
        return pl.pallas_call(
            body,
            out_shape=outs,
            in_specs=[pl.BlockSpec(memory_space=pltpu.SMEM)] + [vmem] * len(operands),
            out_specs=[vmem] * len(outs),
            scratch_shapes=list(scratch),
            compiler_params=pltpu.CompilerParams(vmem_limit_bytes=40 * 1024 * 1024),
            cost_estimate=pl.CostEstimate(flops=flops, bytes_accessed=nbytes, transcendentals=0),
            name=name,
        )(place, *operands)

    return run


def prepare_body(n_line, block, place, tokens, routes, levels, cotangent, *outs):
    pieces, payload = outs[:4], outs[4]
    for core in range(2):
        for side in range(2):
            owner = (place[1] ^ side) * 2 + (place[2] ^ core)
            for z in range(n_line):
                start = pl.multiple_of((z * 4 + owner) * block, block)
                pieces[core * 2 + side][:, z * block : (z + 1) * block] = tokens[:, pl.ds(start, block)]
    tok_rows = cotangent.shape[0]
    gate_rows = payload.shape[0] - tok_rows
    payload[:tok_rows, :] = cotangent[...]
    expert = lax.broadcasted_iota(jnp.int32, (gate_rows, tok_rows), 0)
    total = jnp.zeros((gate_rows, tok_rows), jnp.int32)
    for k in range(routes.shape[0]):
        total = total + jnp.where(expert == routes[k : k + 1, :], levels[k : k + 1, :], 0)
    low = total & 31
    payload[tok_rows:, :tok_rows] = (total - low).astype(wide).astype(narrow)
    payload[tok_rows:, tok_rows : 2 * tok_rows] = low.astype(wide).astype(narrow)
    rest = payload.shape[1] - 2 * tok_rows
    payload[tok_rows:, 2 * tok_rows :] = jnp.zeros((gate_rows, rest), narrow)


def project_body(n_line, place, *refs):
    pieces, downs = refs[:4], refs[4 : 4 + n_line]
    keep, send, down = refs[4 + n_line :]
    block = downs[0].shape[0]
    for back in range(n_line):
        z = lax.rem(place[0] + n_line - back, n_line)
        down[pl.ds(pl.multiple_of(z * block, block), block), :] = downs[back][...]
    for core, out in ((1, send), (0, keep)):
        for side in range(2):
            out[side] = jnp.dot(pieces[core * 2 + side][...], down[...], preferred_element_type=wide)


def gate_tile(payload, tok_rows, expert):
    packed = payload[tok_rows:, :]
    rows = lax.broadcasted_iota(jnp.int32, (packed.shape[0], 128), 0)
    pick = jnp.where(rows == expert, 1.0, 0.0).astype(narrow)
    dot = functools.partial(lax.dot_general, dimension_numbers=contract_first, preferred_element_type=wide)
    total = dot(packed[:, :tok_rows], pick) + dot(packed[:, tok_rows : 2 * tok_rows], pick)
    return total * gate_unit


def expert_body(count, place, *refs):
    rows_in, payloads = refs[:count], refs[count : 2 * count]
    weights = refs[2 * count : 2 * count + 4]
    outs = refs[2 * count + 4 :]
    combined, deltas = outs[:count], outs[count : 2 * count]
    hiddens, scaleds, back_pres = outs[2 * count :]
    tok_rows, width = rows_in[0].shape
    for first in range(0, count, 2):
        pair = (first, first + 1)
        span = slice(first * tok_rows, (first + 2) * tok_rows)
        rows = jnp.concatenate([rows_in[i][...] for i in pair], axis=0)
        cotangent = jnp.concatenate([payloads[i][:tok_rows, :] for i in pair], axis=0).astype(wide)
        out_sum = jnp.zeros((2 * tok_rows, width), wide)
        delta_sum = jnp.zeros((2 * tok_rows, width), wide)
        for e in range(2):
            weight_in, weight_out = weights[2 * e], weights[2 * e + 1]
            expert = place[3 + e]
            gate = jnp.concatenate([gate_tile(payloads[i], tok_rows, expert) for i in pair], axis=0)
            gate = jnp.concatenate([gate] * (width // 128), axis=1)
            active = jnp.maximum(jnp.dot(rows, weight_in[...], preferred_element_type=wide), 0.0)
            hidden = (active * active).astype(narrow)
            hiddens[e, span, :] = hidden
            scaled = (gate * cotangent).astype(narrow)
            scaleds[e, span, :] = scaled
            back_hidden = lax.dot_general(scaled, weight_out[...], contract_last, preferred_element_type=wide)
            back_pre = (back_hidden * 2.0 * active).astype(narrow)
            back_pres[e, span, :] = back_pre
            result = jnp.dot(hidden, weight_out[...], preferred_element_type=wide).astype(narrow)
            out_sum = out_sum + gate * result.astype(wide)
            back_rows = lax.dot_general(back_pre, weight_in[...], contract_last, preferred_element_type=wide)
            delta_sum = delta_sum + back_rows.astype(narrow).astype(wide)
        for i in pair:
            part = slice((i - first) * tok_rows, (i - first + 1) * tok_rows)
            combined[i][...] = out_sum[part].astype(combined[i].dtype)
            deltas[i][...] = delta_sum[part].astype(deltas[i].dtype)


def weight_grad_body(n_rows, n_sets, place, *refs):
    rows_in = refs[:n_rows]
    sets = [refs[n_rows + 3 * i : n_rows + 3 * i + 3] for i in range(n_sets)]
    keep_in, keep_out, send_in, send_out = refs[n_rows + 3 * n_sets :]
    dot = functools.partial(lax.dot_general, dimension_numbers=contract_first, preferred_element_type=wide)
    rows = jnp.concatenate([r[...] for r in rows_in], axis=0)
    for e, out_in, out_out in ((1, send_in, send_out), (0, keep_in, keep_out)):
        hidden = jnp.concatenate([s[0][e] for s in sets], axis=0)
        scaled = jnp.concatenate([s[1][e] for s in sets], axis=0)
        back_pre = jnp.concatenate([s[2][e] for s in sets], axis=0)
        out_out[...] = dot(hidden, scaled).astype(out_out.dtype)
        out_in[...] = dot(rows, back_pre).astype(out_in.dtype)


def down_grad_body(n_line, place, *refs):
    pieces, deltas, blocks = refs[:4], refs[4:8], refs[8:]
    tokens = jnp.concatenate([p[...] for p in pieces], axis=0)
    delta = jnp.concatenate([d[...] for d in deltas], axis=0)
    part = lax.dot_general(tokens, delta, contract_first, preferred_element_type=wide)
    block = blocks[0].shape[0]
    for z in range(n_line):
        for back in range(n_line):

            @pl.when(lax.rem(place[0] + n_line - back, n_line) == z)
            def _(z=z, back=back):
                blocks[back][...] = part[z * block : (z + 1) * block].astype(blocks[back].dtype)


def token_grad_body(place, *refs):
    deltas, down, grads = refs[:4], refs[4], refs[5:]
    for delta, grad in zip(deltas, grads):
        grad[...] = lax.dot_general(
            delta[...], down[...], contract_last, preferred_element_type=wide
        ).astype(narrow)


def arrange_body(n_line, block, place, *refs):
    pieces, out = refs[:4], refs[4]
    for core in range(2):
        for side in range(2):
            owner = (place[1] ^ side) * 2 + (place[2] ^ core)
            for z in range(n_line):
                start = pl.multiple_of((z * 4 + owner) * block, block)
                out[:, pl.ds(start, block)] = pieces[core * 2 + side][:, z * block : (z + 1) * block]


def all_rows(tokens, routes, gate_levels, latent_grad, down_weight, expert_in, expert_out):
    tok_rows, width = tokens.shape
    latent_width = down_weight.shape[1]
    hidden_width = expert_in.shape[2]
    n_major = lax.axis_size("expert")
    n_line = n_major // 2
    n_experts = n_major * 2
    block = width // n_experts
    major = lax.axis_index("expert")
    my_core = lax.axis_index("dp")
    place = jnp.stack(
        [major // 2, major % 2, my_core, major * 2 + my_core, major * 2 + 1 - my_core]
    ).astype(jnp.int32)
    shape = jax.ShapeDtypeStruct
    rows_of = lambda kind: shape((tok_rows, latent_width), kind)

    downs = [down_weight] + [turn(down_weight, n_line, back) for back in range(1, n_line)]

    gate_rows = -(-n_experts // 16) * 16
    prepare = call(
        functools.partial(prepare_body, n_line, block),
        [shape((tok_rows, n_line * block), narrow)] * 4 + [shape((tok_rows + gate_rows, latent_width), narrow)],
        "prepare",
        nbytes=3 * tok_rows * width * 2,
    )
    *columns, payload = prepare(place, tokens, routes.T, gate_levels.T, latent_grad)
    near_tokens = columns[:1] + [
        swap(after(columns[core * 2 + side], downs[1]), n_line, core, side)
        for core, side in ((0, 1), (1, 0), (1, 1))
    ]
    own = (expert_in[0], expert_out[0])
    weights = own + tuple(swap(w, n_line, 1, 0) for w in own)

    project = call(
        functools.partial(project_body, n_line),
        [shape((2, tok_rows, latent_width), wide)] * 2 + [shape((n_line * block, latent_width), narrow)],
        "project",
        flops=2 * 4 * tok_rows * n_line * block * latent_width,
    )
    keep, send, down = project(place, *near_tokens, *downs)
    half = keep + swap(send, n_line, 1, 0)
    latent = (half[0] + swap(half[1], n_line, 0, 1)).astype(narrow)

    later_payload = after(payload, half)
    payloads = [payload] + [turn(later_payload, n_line, back) for back in range(1, n_line)]
    rows = [latent] + [turn(latent, n_line, back) for back in range(1, n_line)]
    far_rows = [swap(r, n_line, 0, 1) for r in rows]
    far_payloads = [swap(after(payload, near_tokens[1]), n_line, 0, 1)] + [
        swap(after(p, latent), n_line, 0, 1) for p in payloads[1:]
    ]

    def experts(count, kind, name):
        saved = shape((2, count * tok_rows, hidden_width), narrow)
        return call(
            functools.partial(expert_body, count),
            [rows_of(kind)] * (2 * count) + [saved] * 3,
            name,
            flops=2 * 2 * 4 * count * tok_rows * latent_width * hidden_width,
            nbytes=4 * latent_width * hidden_width * 2,
        )

    outs = experts(n_line, wide, "near_experts")(place, *rows, *payloads, *weights)
    near_out, near_delta, saved = outs[:n_line], outs[n_line : 2 * n_line], [outs[2 * n_line :]]
    far_out, far_delta = [], []
    part = n_line // 2
    for first in range(0, n_line, part):
        span = slice(first, first + part)
        outs = experts(part, narrow, "far_experts")(place, *far_rows[span], *far_payloads[span], *weights)
        far_out += outs[:part]
        far_delta += outs[part : 2 * part]
        saved.append(outs[2 * part :])

    def return_lines(near, far):
        lines = []
        for back in range(n_line):
            line = near[back] + far[back].astype(wide)
            if back:
                line = turn(line.astype(narrow), n_line, n_line - back)
            lines.append(line)
        return lines

    far_delta = [swap(d, n_line, 0, 1) for d in far_delta]
    delta = sum(line.astype(wide) for line in return_lines(near_delta, far_delta)).astype(narrow)
    far_out = [swap(after(o, far_delta[-1]), n_line, 0, 1) for o in far_out]
    out_lines = return_lines(near_out, far_out)

    weight_grad = call(
        functools.partial(weight_grad_body, 2 * n_line, len(saved)),
        [shape((latent_width, hidden_width), wide), shape((hidden_width, latent_width), wide)]
        + [shape((latent_width, hidden_width), narrow), shape((hidden_width, latent_width), narrow)],
        "weight_grads",
        flops=2 * 2 * 2 * 2 * n_line * tok_rows * latent_width * hidden_width,
    )
    keep_in, keep_out, send_in, send_out = weight_grad(
        place, *rows, *far_rows, *(value for values in saved for value in values)
    )
    grad_in = (keep_in + swap(send_in, n_line, 1, 0).astype(wide)).astype(narrow)
    grad_out = (keep_out + swap(send_out, n_line, 1, 0).astype(wide)).astype(narrow)

    side_delta = swap(delta, n_line, 0, 1)
    deltas = [delta, side_delta, swap(delta, n_line, 1, 0), swap(side_delta, n_line, 1, 0)]
    narrow_columns = shape((tok_rows, n_line * block), narrow)
    down_grad = call(
        functools.partial(down_grad_body, n_line),
        [shape((block, latent_width), wide)] + [shape((block, latent_width), narrow)] * (n_line - 1),
        "down_grad",
        flops=2 * 4 * tok_rows * n_line * block * latent_width,
    )
    blocks = down_grad(place, *near_tokens, *deltas)
    token_grad = call(
        token_grad_body,
        [narrow_columns] * 4,
        "token_grad",
        flops=2 * 4 * tok_rows * n_line * block * latent_width,
    )
    grads = token_grad(place, *deltas, down)
    blocks = [blocks[0]] + [turn(blocks[back], n_line, n_line - back) for back in range(1, n_line)]
    grad_down = sum(value.astype(wide) for value in blocks)
    out_lines = [after(line, blocks[1]) for line in out_lines]
    latent_out = sum(line.astype(wide) for line in out_lines).astype(narrow)
    grads = [
        grads[core * 2 + side] if core + side == 0 else swap(grads[core * 2 + side], n_line, core, side)
        for core in range(2)
        for side in range(2)
    ]
    arrange = call(
        functools.partial(arrange_body, n_line, block),
        [shape((tok_rows, width), narrow)],
        "arrange",
        nbytes=2 * tok_rows * width * 2,
    )
    (grad_tokens,) = arrange(place, *grads)
    return (latent_out, grad_tokens, grad_down, grad_in[None], grad_out[None])


def slot_table(routes, capacity):
    flat = routes.reshape(-1)
    count = flat.shape[0]
    order = jnp.arange(count, dtype=jnp.int32)
    same = (flat[:, None] == flat[None, :]) & (order[None, :] < order[:, None])
    placed = jnp.sum(jnp.where(same, 1, 0), axis=1).astype(jnp.int32)
    return flat * capacity + placed


def routed_rows(tokens, routes, gate_levels, latent_grad, down_weight, expert_in, expert_out):
    tok_rows = tokens.shape[0]
    top = routes.shape[1]
    latent_width = down_weight.shape[1]
    n_major = lax.axis_size("expert")
    n_minor = lax.axis_size("dp")
    n_experts = n_major * n_minor
    capacity = 3 * tok_rows * top // (2 * n_experts)
    entries = tok_rows * top
    contract_last = (((1,), (1,)), ((), ()))
    contract_first = (((0,), (0,)), ((), ()))
    full_down = lax.all_gather(down_weight, ("expert", "dp"), axis=0, tiled=True)
    latent = jnp.dot(tokens, full_down, preferred_element_type=jnp.float32)
    latent = latent.astype(jnp.bfloat16)
    dest = slot_table(routes, capacity)
    source = (
        jnp.full((n_experts * capacity,), entries, jnp.int32)
        .at[dest]
        .set(jnp.arange(entries, dtype=jnp.int32))
    )
    token_of = jnp.where(source < entries, source // top, tok_rows)
    gates = gate_levels.astype(jnp.float32) * gate_unit
    zero_row = jnp.zeros((1, latent_width), jnp.bfloat16)
    latent_pad = jnp.concatenate([latent, zero_row], axis=0)
    send_latent = latent_pad[token_of].reshape(n_major, n_minor, capacity, latent_width)
    scaled = (gates[:, :, None] * latent_grad.astype(jnp.float32)[:, None, :]).astype(jnp.bfloat16)
    scaled_pad = jnp.concatenate([scaled.reshape(entries, latent_width), zero_row], axis=0)
    send_grad = scaled_pad[source].reshape(n_major, n_minor, capacity, latent_width)
    arrived = lax.all_to_all(
        lax.all_to_all(send_latent, "expert", split_axis=0, concat_axis=0, tiled=True),
        "dp",
        split_axis=1,
        concat_axis=1,
        tiled=True,
    )
    rows = arrived.reshape(-1, latent_width)
    weight_in = expert_in[0]
    weight_out = expert_out[0]
    before = jnp.dot(rows, weight_in, preferred_element_type=jnp.float32)
    active = jnp.maximum(before, 0.0)
    hidden = (active * active).astype(jnp.bfloat16)
    result = jnp.dot(hidden, weight_out, preferred_element_type=jnp.float32).astype(jnp.bfloat16)
    returned = lax.all_to_all(
        lax.all_to_all(
            result.reshape(n_major, n_minor, capacity, latent_width),
            "expert",
            split_axis=0,
            concat_axis=0,
            tiled=True,
        ),
        "dp",
        split_axis=1,
        concat_axis=1,
        tiled=True,
    )
    picked = returned.reshape(n_experts * capacity, latent_width)[dest].astype(jnp.float32)
    picked = picked.reshape(tok_rows, top, latent_width)
    latent_out = jnp.sum(gates[:, :, None] * picked, axis=1).astype(jnp.bfloat16)
    arrived_grad = lax.all_to_all(
        lax.all_to_all(send_grad, "expert", split_axis=0, concat_axis=0, tiled=True),
        "dp",
        split_axis=1,
        concat_axis=1,
        tiled=True,
    )
    grad_rows = arrived_grad.reshape(-1, latent_width)
    back_hidden = lax.dot_general(
        grad_rows, weight_out, contract_last, preferred_element_type=jnp.float32
    )
    back_pre = (back_hidden * 2.0 * active).astype(jnp.bfloat16)
    grad_out = lax.dot_general(
        hidden, grad_rows, contract_first, preferred_element_type=jnp.float32
    ).astype(jnp.bfloat16)
    grad_in = lax.dot_general(
        rows, back_pre, contract_first, preferred_element_type=jnp.float32
    ).astype(jnp.bfloat16)
    back_rows = lax.dot_general(
        back_pre, weight_in, contract_last, preferred_element_type=jnp.float32
    ).astype(jnp.bfloat16)
    came_back = lax.all_to_all(
        lax.all_to_all(
            back_rows.reshape(n_major, n_minor, capacity, latent_width),
            "expert",
            split_axis=0,
            concat_axis=0,
            tiled=True,
        ),
        "dp",
        split_axis=1,
        concat_axis=1,
        tiled=True,
    )
    gathered_back = came_back.reshape(n_experts * capacity, latent_width)[dest].astype(jnp.float32)
    latent_delta = jnp.sum(gathered_back.reshape(tok_rows, top, latent_width), axis=1).astype(
        jnp.bfloat16
    )
    grad_tokens = lax.dot_general(
        latent_delta, full_down, contract_last, preferred_element_type=jnp.float32
    )
    grad_tokens = grad_tokens.astype(jnp.bfloat16)
    grad_down = lax.psum_scatter(
        lax.dot_general(tokens, latent_delta, contract_first, preferred_element_type=jnp.float32),
        ("expert", "dp"),
        scatter_dimension=0,
        tiled=True,
    )
    return (latent_out, grad_tokens, grad_down, grad_in[None], grad_out[None])


def on_device(tokens, routes, *others):
    n_major = lax.axis_size("expert")
    n_experts = n_major * lax.axis_size("dp")
    few = n_experts <= 2 * routes.shape[1] and n_major % 4 == 0 and lax.axis_size("dp") == 2
    return (all_rows if few else routed_rows)(tokens, routes, *others)


def solution(mesh):
    in_specs = (
        P(("group", "expert", "dp"), None),
        P(("group", "expert", "dp"), None),
        P(("group", "expert", "dp"), None),
        P(("group", "expert", "dp"), None),
        P(("expert", "dp"), None),
        P(("expert", "dp"), None, None),
        P(("expert", "dp"), None, None),
    )
    out_specs = (
        P(("group", "expert", "dp"), None),
        P(("group", "expert", "dp"), None),
        P(("group", "expert", "dp"), None),
        P(("group", "expert", "dp"), None, None),
        P(("group", "expert", "dp"), None, None),
    )
    return jax.shard_map(
        on_device, mesh=mesh, in_specs=in_specs, out_specs=out_specs, check_vma=False
    )
```

```python
import functools

import jax
import jax.numpy as jnp
from jax import lax
from jax.experimental import pallas as pl
from jax.experimental.pallas import tpu as pltpu
from jax.sharding import PartitionSpec as P

gate_unit = 1.0 / 1024.0
contract_last = (((1,), (1,)), ((), ()))
contract_first = (((0,), (0,)), ((), ()))
plane = ("expert", "dp")
wide = jnp.float32
narrow = jnp.bfloat16


def device_pairs(n_line, move):
    pairs = []
    for z in range(n_line):
        for x in range(2):
            for c in range(2):
                to_z, to_x, to_c = move(z, x, c)
                pairs.append(((z * 2 + x) * 2 + c, (to_z * 2 + to_x) * 2 + to_c))
    return pairs


def turn(value, n_line, by):
    return lax.ppermute(value, plane, device_pairs(n_line, lambda z, x, c: ((z + by) % n_line, x, c)))


def swap(value, n_line, core, side):
    return lax.ppermute(value, plane, device_pairs(n_line, lambda z, x, c: (z, x ^ side, c ^ core)))


def after(value, *earlier):
    return lax.optimization_barrier((value,) + earlier)[0]


def call(body, outs, name, scratch=(), flops=0, nbytes=0):
    vmem = pl.BlockSpec(memory_space=pltpu.VMEM)

    def run(place, *operands):
        return pl.pallas_call(
            body,
            out_shape=outs,
            in_specs=[pl.BlockSpec(memory_space=pltpu.SMEM)] + [vmem] * len(operands),
            out_specs=[vmem] * len(outs),
            scratch_shapes=list(scratch),
            compiler_params=pltpu.CompilerParams(vmem_limit_bytes=40 * 1024 * 1024),
            cost_estimate=pl.CostEstimate(flops=flops, bytes_accessed=nbytes, transcendentals=0),
            name=name,
        )(place, *operands)

    return run


def prepare_body(n_line, block, place, tokens, routes, levels, cotangent, *outs):
    pieces, payload = outs[:4], outs[4]
    for core in range(2):
        for side in range(2):
            owner = (place[1] ^ side) * 2 + (place[2] ^ core)
            for z in range(n_line):
                start = pl.multiple_of((z * 4 + owner) * block, block)
                pieces[core * 2 + side][:, z * block : (z + 1) * block] = tokens[:, pl.ds(start, block)]
    tok_rows = cotangent.shape[0]
    gate_rows = payload.shape[0] - tok_rows
    payload[:tok_rows, :] = cotangent[...]
    expert = lax.broadcasted_iota(jnp.int32, (gate_rows, tok_rows), 0)
    total = jnp.zeros((gate_rows, tok_rows), jnp.int32)
    for k in range(routes.shape[0]):
        total = total + jnp.where(expert == routes[k : k + 1, :], levels[k : k + 1, :], 0)
    low = total & 31
    payload[tok_rows:, :tok_rows] = (total - low).astype(wide).astype(narrow)
    payload[tok_rows:, tok_rows : 2 * tok_rows] = low.astype(wide).astype(narrow)
    rest = payload.shape[1] - 2 * tok_rows
    payload[tok_rows:, 2 * tok_rows :] = jnp.zeros((gate_rows, rest), narrow)


def project_body(n_line, place, *refs):
    pieces, downs = refs[:4], refs[4 : 4 + n_line]
    keep, send, down = refs[4 + n_line :]
    block = downs[0].shape[0]
    for back in range(n_line):
        z = lax.rem(place[0] + n_line - back, n_line)
        down[pl.ds(pl.multiple_of(z * block, block), block), :] = downs[back][...]
    for core, out in ((1, send), (0, keep)):
        for side in range(2):
            out[side] = jnp.dot(pieces[core * 2 + side][...], down[...], preferred_element_type=wide)


def gate_tile(payload, tok_rows, expert):
    packed = payload[tok_rows:, :]
    rows = lax.broadcasted_iota(jnp.int32, (packed.shape[0], 128), 0)
    pick = jnp.where(rows == expert, 1.0, 0.0).astype(narrow)
    dot = functools.partial(lax.dot_general, dimension_numbers=contract_first, preferred_element_type=wide)
    total = dot(packed[:, :tok_rows], pick) + dot(packed[:, tok_rows : 2 * tok_rows], pick)
    return total * gate_unit


def expert_body(count, place, *refs):
    rows_in, payloads = refs[:count], refs[count : 2 * count]
    weights = refs[2 * count : 2 * count + 8]
    outs = refs[2 * count + 8 :]
    combined, deltas = outs[:count], outs[count : 2 * count]
    hiddens, scaleds, back_pres = outs[2 * count :]
    tok_rows, width = rows_in[0].shape
    for first in range(0, count, 2):
        group = range(first, min(first + 2, count))
        span = slice(first * tok_rows, (first + len(group)) * tok_rows)
        stack = lambda values: jnp.concatenate(list(values), axis=0)
        rows = stack(rows_in[i][...] for i in group)
        cotangent = stack(payloads[i][:tok_rows, :] for i in group).astype(wide)
        out_sum = jnp.zeros(rows.shape, wide)
        delta_sum = jnp.zeros(rows.shape, wide)
        for e in range(4):
            weight_in, weight_out = weights[2 * e], weights[2 * e + 1]
            gate = stack(gate_tile(payloads[i], tok_rows, place[3 + e]) for i in group)
            gate = jnp.concatenate([gate] * (width // 128), axis=1)
            active = jnp.maximum(jnp.dot(rows, weight_in[...], preferred_element_type=wide), 0.0)
            hidden = (active * active).astype(narrow)
            hiddens[e, span, :] = hidden
            scaled = (gate * cotangent).astype(narrow)
            scaleds[e, span, :] = scaled
            back_hidden = lax.dot_general(scaled, weight_out[...], contract_last, preferred_element_type=wide)
            back_pre = (back_hidden * 2.0 * active).astype(narrow)
            back_pres[e, span, :] = back_pre
            result = jnp.dot(hidden, weight_out[...], preferred_element_type=wide).astype(narrow)
            out_sum = out_sum + gate * result.astype(wide)
            back_rows = lax.dot_general(back_pre, weight_in[...], contract_last, preferred_element_type=wide)
            delta_sum = delta_sum + back_rows.astype(narrow).astype(wide)
        for i in group:
            part = slice((i - first) * tok_rows, (i - first + 1) * tok_rows)
            combined[i][...] = out_sum[part].astype(combined[i].dtype)
            deltas[i][...] = delta_sum[part].astype(deltas[i].dtype)


def weight_grad_body(side, n_rows, n_sets, place, *refs):
    rows_in = refs[:n_rows]
    sets = [refs[n_rows + 3 * i : n_rows + 3 * i + 3] for i in range(n_sets)]
    outs = refs[n_rows + 3 * n_sets :]
    dot = functools.partial(lax.dot_general, dimension_numbers=contract_first, preferred_element_type=wide)
    rows = jnp.concatenate([r[...] for r in rows_in], axis=0)
    for core in (1, 0):
        hidden, scaled, back_pre = (
            jnp.concatenate([values[i][core * 2 + side] for values in sets], axis=0) for i in range(3)
        )
        outs[2 * core][...] = dot(rows, back_pre).astype(outs[2 * core].dtype)
        outs[2 * core + 1][...] = dot(hidden, scaled).astype(outs[2 * core + 1].dtype)


def down_grad_body(n_line, place, *refs):
    pieces, deltas, blocks = refs[:4], refs[4:8], refs[8:]
    tokens = jnp.concatenate([p[...] for p in pieces], axis=0)
    delta = jnp.concatenate([d[...] for d in deltas], axis=0)
    part = lax.dot_general(tokens, delta, contract_first, preferred_element_type=wide)
    block = blocks[0].shape[0]
    for z in range(n_line):
        for back in range(n_line):

            @pl.when(lax.rem(place[0] + n_line - back, n_line) == z)
            def _(z=z, back=back):
                blocks[back][...] = part[z * block : (z + 1) * block].astype(blocks[back].dtype)


def token_grad_body(n_line, block, place, delta, *refs):
    downs, out = refs[:4], refs[4]
    for core in range(2):
        for side in range(2):
            owner = (place[1] ^ side) * 2 + (place[2] ^ core)
            part = lax.dot_general(
                delta[...], downs[core * 2 + side][...], contract_last, preferred_element_type=wide
            ).astype(narrow)
            for z in range(n_line):
                start = pl.multiple_of((z * 4 + owner) * block, block)
                out[:, pl.ds(start, block)] = part[:, z * block : (z + 1) * block]


def all_rows(tokens, routes, gate_levels, latent_grad, down_weight, expert_in, expert_out):
    tok_rows, width = tokens.shape
    latent_width = down_weight.shape[1]
    hidden_width = expert_in.shape[2]
    n_major = lax.axis_size("expert")
    n_line = n_major // 2
    n_experts = n_major * 2
    block = width // n_experts
    major = lax.axis_index("expert")
    my_core = lax.axis_index("dp")
    place = jnp.stack(
        [major // 2, major % 2, my_core]
        + [(major ^ side) * 2 + (my_core ^ core) for core in range(2) for side in range(2)]
    ).astype(jnp.int32)
    shape = jax.ShapeDtypeStruct
    rows_of = lambda kind: shape((tok_rows, latent_width), kind)

    downs = [down_weight] + [turn(down_weight, n_line, back) for back in range(1, n_line)]

    gate_rows = -(-n_experts // 16) * 16
    prepare = call(
        functools.partial(prepare_body, n_line, block),
        [shape((tok_rows, n_line * block), narrow)] * 4 + [shape((tok_rows + gate_rows, latent_width), narrow)],
        "prepare",
        nbytes=3 * tok_rows * width * 2,
    )
    *columns, payload = prepare(place, tokens, routes.T, gate_levels.T, latent_grad)
    own = [expert_in[0], expert_out[0]]
    side_in = swap(own[0], n_line, 0, 1)
    near_tokens = columns[:1] + [
        swap(after(columns[core * 2 + side], side_in), n_line, core, side)
        for core, side in ((0, 1), (1, 0), (1, 1))
    ]
    payloads = [payload] + [None] * (n_line - 1)
    payloads[1] = turn(after(payload, *downs[1:]), n_line, 1)
    near_tokens[0] = after(near_tokens[0], payloads[1])

    project = call(
        functools.partial(project_body, n_line),
        [shape((2, tok_rows, latent_width), wide)] * 2 + [shape((n_line * block, latent_width), narrow)],
        "project",
        flops=2 * 4 * tok_rows * n_line * block * latent_width,
    )
    keep, send, down = project(place, *near_tokens, *downs)
    half = keep + swap(send, n_line, 1, 0)
    for back in range(2, n_line):
        payloads[back] = turn(after(payload, half), n_line, back)
    latent = (half[0] + after(swap(half[1], n_line, 0, 1), *payloads[2:])).astype(narrow)
    ends = [1, n_line - 1]
    middle = list(range(2, n_line - 1))
    groups = [ends, [0], middle]
    rows = [latent] + [None] * (n_line - 1)
    for back in ends:
        rows[back] = turn(latent, n_line, back)
    end_rows = [rows[back] for back in ends]
    for back in middle:
        rows[back] = turn(after(latent, *end_rows), n_line, back)

    side_out = after(swap(after(own[1], latent), n_line, 0, 1), *end_rows)
    side_down = swap(after(down, side_out), n_line, 0, 1)
    near = own + [side_in, side_out]
    all_down = [down, side_down] + [swap(d, n_line, 1, 0) for d in (down, side_down)]
    weights = near + [swap(w, n_line, 1, 0) for w in near]

    outs_of, deltas_of, saved = [None] * n_line, [None] * n_line, []
    for group in groups:
        count = len(group)
        kind = narrow if group[0] else wide
        values = call(
            functools.partial(expert_body, count),
            [rows_of(kind)] * (2 * count) + [shape((4, count * tok_rows, hidden_width), narrow)] * 3,
            "experts",
            flops=4 * 2 * 4 * count * tok_rows * latent_width * hidden_width,
            nbytes=8 * latent_width * hidden_width * 2,
        )(place, *(rows[i] for i in group), *(payloads[i] for i in group), *weights)
        for i, back in enumerate(group):
            outs_of[back], deltas_of[back] = values[i], values[count + i]
        saved.append(list(values[2 * count :]))

    def home(value, back):
        return turn(value, n_line, n_line - back) if back else value

    delta_lines = [home(value, back) for back, value in enumerate(deltas_of)]

    def weight_grads(side, *earlier):
        sizes = [(latent_width, hidden_width), (hidden_width, latent_width)]
        values = call(
            functools.partial(weight_grad_body, side, n_line, len(groups)),
            [shape(size, kind) for kind in (wide, narrow) for size in sizes],
            "weight_grads",
            flops=2 * 2 * 2 * n_line * tok_rows * latent_width * hidden_width,
        )(
            after(place, *earlier),
            *(rows[i] for group in groups for i in group),
            *(value for values in saved for value in values),
        )
        return [mine + swap(other, n_line, 1, 0).astype(wide) for mine, other in zip(values[:2], values[2:])]

    far_in, far_out = (
        value.astype(narrow) for value in weight_grads(1, *(delta_lines[back] for back in ends))
    )
    delta_lines = [after(line, far_in, *all_down) for line in delta_lines]
    delta = sum(line.astype(wide) for line in delta_lines).astype(narrow)
    side_delta = swap(delta, n_line, 0, 1)
    out_lines = [outs_of[0]] + [None] * (n_line - 1)
    for back in ends:
        out_lines[back] = home(after(outs_of[back], delta), back)
    near_in, near_out = weight_grads(0, *(out_lines[back] for back in ends))
    far_out = swap(far_out, n_line, 0, 1)
    grad_out = near_out + far_out.astype(wide)
    far_in = swap(after(far_in, side_delta), n_line, 0, 1)
    grad_in = near_in + far_in.astype(wide)
    deltas = [delta, side_delta, swap(delta, n_line, 1, 0), swap(side_delta, n_line, 1, 0)]
    blocks = call(
        functools.partial(down_grad_body, n_line),
        [shape((block, latent_width), wide)] + [shape((block, latent_width), narrow)] * (n_line - 1),
        "down_grad",
        flops=2 * 4 * tok_rows * n_line * block * latent_width,
    )(place, *near_tokens, *deltas)
    sent = [after(value, far_out, *(out_lines[back] for back in ends)) for value in blocks]
    (grad_tokens,) = call(
        functools.partial(token_grad_body, n_line, block),
        [shape((tok_rows, width), narrow)],
        "token_grad",
        flops=2 * 4 * tok_rows * n_line * block * latent_width,
    )(place, after(delta, blocks[1]), *all_down)
    blocks = [blocks[0]] + [home(sent[back], back) for back in range(1, n_line)]
    for back in middle:
        out_lines[back] = home(after(outs_of[back], *(out_lines[end] for end in ends)), back)
    grad_down = sum(after(value, far_in).astype(wide) for value in blocks)
    latent_out = sum(line.astype(wide) for line in out_lines).astype(narrow)
    return (latent_out, grad_tokens, grad_down, grad_in.astype(narrow)[None], grad_out.astype(narrow)[None])


def slot_table(routes, capacity):
    flat = routes.reshape(-1)
    count = flat.shape[0]
    order = jnp.arange(count, dtype=jnp.int32)
    same = (flat[:, None] == flat[None, :]) & (order[None, :] < order[:, None])
    placed = jnp.sum(jnp.where(same, 1, 0), axis=1).astype(jnp.int32)
    return flat * capacity + placed


def routed_rows(tokens, routes, gate_levels, latent_grad, down_weight, expert_in, expert_out):
    tok_rows = tokens.shape[0]
    top = routes.shape[1]
    latent_width = down_weight.shape[1]
    n_major = lax.axis_size("expert")
    n_minor = lax.axis_size("dp")
    n_experts = n_major * n_minor
    capacity = 3 * tok_rows * top // (2 * n_experts)
    entries = tok_rows * top
    contract_last = (((1,), (1,)), ((), ()))
    contract_first = (((0,), (0,)), ((), ()))
    full_down = lax.all_gather(down_weight, ("expert", "dp"), axis=0, tiled=True)
    latent = jnp.dot(tokens, full_down, preferred_element_type=jnp.float32)
    latent = latent.astype(jnp.bfloat16)
    dest = slot_table(routes, capacity)
    source = (
        jnp.full((n_experts * capacity,), entries, jnp.int32)
        .at[dest]
        .set(jnp.arange(entries, dtype=jnp.int32))
    )
    token_of = jnp.where(source < entries, source // top, tok_rows)
    gates = gate_levels.astype(jnp.float32) * gate_unit
    zero_row = jnp.zeros((1, latent_width), jnp.bfloat16)
    latent_pad = jnp.concatenate([latent, zero_row], axis=0)
    send_latent = latent_pad[token_of].reshape(n_major, n_minor, capacity, latent_width)
    scaled = (gates[:, :, None] * latent_grad.astype(jnp.float32)[:, None, :]).astype(jnp.bfloat16)
    scaled_pad = jnp.concatenate([scaled.reshape(entries, latent_width), zero_row], axis=0)
    send_grad = scaled_pad[source].reshape(n_major, n_minor, capacity, latent_width)
    arrived = lax.all_to_all(
        lax.all_to_all(send_latent, "expert", split_axis=0, concat_axis=0, tiled=True),
        "dp",
        split_axis=1,
        concat_axis=1,
        tiled=True,
    )
    rows = arrived.reshape(-1, latent_width)
    weight_in = expert_in[0]
    weight_out = expert_out[0]
    before = jnp.dot(rows, weight_in, preferred_element_type=jnp.float32)
    active = jnp.maximum(before, 0.0)
    hidden = (active * active).astype(jnp.bfloat16)
    result = jnp.dot(hidden, weight_out, preferred_element_type=jnp.float32).astype(jnp.bfloat16)
    returned = lax.all_to_all(
        lax.all_to_all(
            result.reshape(n_major, n_minor, capacity, latent_width),
            "expert",
            split_axis=0,
            concat_axis=0,
            tiled=True,
        ),
        "dp",
        split_axis=1,
        concat_axis=1,
        tiled=True,
    )
    picked = returned.reshape(n_experts * capacity, latent_width)[dest].astype(jnp.float32)
    picked = picked.reshape(tok_rows, top, latent_width)
    latent_out = jnp.sum(gates[:, :, None] * picked, axis=1).astype(jnp.bfloat16)
    arrived_grad = lax.all_to_all(
        lax.all_to_all(send_grad, "expert", split_axis=0, concat_axis=0, tiled=True),
        "dp",
        split_axis=1,
        concat_axis=1,
        tiled=True,
    )
    grad_rows = arrived_grad.reshape(-1, latent_width)
    back_hidden = lax.dot_general(
        grad_rows, weight_out, contract_last, preferred_element_type=jnp.float32
    )
    back_pre = (back_hidden * 2.0 * active).astype(jnp.bfloat16)
    grad_out = lax.dot_general(
        hidden, grad_rows, contract_first, preferred_element_type=jnp.float32
    ).astype(jnp.bfloat16)
    grad_in = lax.dot_general(
        rows, back_pre, contract_first, preferred_element_type=jnp.float32
    ).astype(jnp.bfloat16)
    back_rows = lax.dot_general(
        back_pre, weight_in, contract_last, preferred_element_type=jnp.float32
    ).astype(jnp.bfloat16)
    came_back = lax.all_to_all(
        lax.all_to_all(
            back_rows.reshape(n_major, n_minor, capacity, latent_width),
            "expert",
            split_axis=0,
            concat_axis=0,
            tiled=True,
        ),
        "dp",
        split_axis=1,
        concat_axis=1,
        tiled=True,
    )
    gathered_back = came_back.reshape(n_experts * capacity, latent_width)[dest].astype(jnp.float32)
    latent_delta = jnp.sum(gathered_back.reshape(tok_rows, top, latent_width), axis=1).astype(
        jnp.bfloat16
    )
    grad_tokens = lax.dot_general(
        latent_delta, full_down, contract_last, preferred_element_type=jnp.float32
    )
    grad_tokens = grad_tokens.astype(jnp.bfloat16)
    grad_down = lax.psum_scatter(
        lax.dot_general(tokens, latent_delta, contract_first, preferred_element_type=jnp.float32),
        ("expert", "dp"),
        scatter_dimension=0,
        tiled=True,
    )
    return (latent_out, grad_tokens, grad_down, grad_in[None], grad_out[None])


def on_device(tokens, routes, *others):
    n_major = lax.axis_size("expert")
    n_experts = n_major * lax.axis_size("dp")
    few = n_experts <= 2 * routes.shape[1] and n_major % 2 == 0 and n_major >= 6 and lax.axis_size("dp") == 2
    return (all_rows if few else routed_rows)(tokens, routes, *others)


def solution(mesh):
    in_specs = (
        P(("group", "expert", "dp"), None),
        P(("group", "expert", "dp"), None),
        P(("group", "expert", "dp"), None),
        P(("group", "expert", "dp"), None),
        P(("expert", "dp"), None),
        P(("expert", "dp"), None, None),
        P(("expert", "dp"), None, None),
    )
    out_specs = (
        P(("group", "expert", "dp"), None),
        P(("group", "expert", "dp"), None),
        P(("group", "expert", "dp"), None),
        P(("group", "expert", "dp"), None, None),
        P(("group", "expert", "dp"), None, None),
    )
    return jax.shard_map(
        on_device, mesh=mesh, in_specs=in_specs, out_specs=out_specs, check_vma=False
    )
```

```python
import functools

import jax
import jax.numpy as jnp
from jax import lax
from jax.experimental import pallas as pl
from jax.experimental.pallas import tpu as pltpu
from jax.sharding import PartitionSpec as P

gate_unit = 1.0 / 1024.0
contract_last = (((1,), (1,)), ((), ()))
contract_first = (((0,), (0,)), ((), ()))
plane = ("expert", "dp")
wide = jnp.float32
narrow = jnp.bfloat16


def device_pairs(n_line, move):
    pairs = []
    for z in range(n_line):
        for x in range(2):
            for c in range(2):
                to_z, to_x, to_c = move(z, x, c)
                pairs.append(((z * 2 + x) * 2 + c, (to_z * 2 + to_x) * 2 + to_c))
    return pairs


def turn(value, n_line, by):
    return lax.ppermute(value, plane, device_pairs(n_line, lambda z, x, c: ((z + by) % n_line, x, c)))


def swap(value, n_line, core, side):
    return lax.ppermute(value, plane, device_pairs(n_line, lambda z, x, c: (z, x ^ side, c ^ core)))


def after(value, *earlier):
    return lax.optimization_barrier((value,) + earlier)[0]


def call(body, outs, name, scratch=(), outside=0):
    vmem = pl.BlockSpec(memory_space=pltpu.VMEM)
    anywhere = pl.BlockSpec(memory_space=pl.ANY)

    def run(place, *operands):
        return pl.pallas_call(
            body,
            out_shape=outs,
            in_specs=[pl.BlockSpec(memory_space=pltpu.SMEM)]
            + [anywhere] * outside
            + [vmem] * (len(operands) - outside),
            out_specs=[vmem] * len(outs),
            scratch_shapes=list(scratch),
            compiler_params=pltpu.CompilerParams(vmem_limit_bytes=40 * 1024 * 1024),
            cost_estimate=pl.CostEstimate(flops=0, bytes_accessed=0, transcendentals=0),
            name=name,
        )(place, *operands)

    return run


def columns_body(n_line, block, place, tokens, *refs):
    own, other, across, sems = refs
    pieces = (own, across.at[0], other, across.at[1])
    copies = []
    for core in range(2):
        for side in range(2):
            owner = (place[1] ^ side) * 2 + (place[2] ^ core)
            for z in range(n_line):
                start = pl.multiple_of((z * 4 + owner) * block, block)
                piece = pieces[core * 2 + side].at[:, pl.ds(z * block, block)]
                copies.append(
                    pltpu.make_async_copy(tokens.at[:, pl.ds(start, block)], piece, sems.at[len(copies)])
                )
    for copy in copies:
        copy.start()
    for copy in copies:
        copy.wait()


def payload_body(place, routes, levels, cotangent, payload):
    tok_rows = cotangent.shape[0]
    gate_rows = payload.shape[0] - tok_rows
    payload[:tok_rows, :] = cotangent[...]
    expert = lax.broadcasted_iota(jnp.int32, (gate_rows, tok_rows), 0)
    total = jnp.zeros((gate_rows, tok_rows), jnp.int32)
    for k in range(routes.shape[0]):
        total = total + jnp.where(expert == routes[k : k + 1, :], levels[k : k + 1, :], 0)
    low = total & 31
    payload[tok_rows:, :tok_rows] = (total - low).astype(wide).astype(narrow)
    payload[tok_rows:, tok_rows : 2 * tok_rows] = low.astype(wide).astype(narrow)
    rest = payload.shape[1] - 2 * tok_rows
    payload[tok_rows:, 2 * tok_rows :] = jnp.zeros((gate_rows, rest), narrow)


def project_body(n_line, place, *refs):
    pieces, downs = refs[:4], refs[4 : 4 + n_line]
    keep, send, down = refs[4 + n_line :]
    block = downs[0].shape[0]
    for back in range(n_line):
        z = lax.rem(place[0] + n_line - back, n_line)
        down[pl.ds(pl.multiple_of(z * block, block), block), :] = downs[back][...]
    for core, out in ((1, send), (0, keep)):
        for side in range(2):
            out[side] = jnp.dot(pieces[core * 2 + side][...], down[...], preferred_element_type=wide)


def gate_tile(payload, tok_rows, expert):
    packed = payload[tok_rows:, :]
    rows = lax.broadcasted_iota(jnp.int32, (packed.shape[0], 128), 0)
    pick = jnp.where(rows == expert, 1.0, 0.0).astype(narrow)
    dot = functools.partial(lax.dot_general, dimension_numbers=contract_first, preferred_element_type=wide)
    total = dot(packed[:, :tok_rows], pick) + dot(packed[:, tok_rows : 2 * tok_rows], pick)
    return total * gate_unit


def expert_body(count, place, *refs):
    rows_in, payloads = refs[:count], refs[count : 2 * count]
    weights = refs[2 * count : 2 * count + 8]
    outs = refs[2 * count + 8 :]
    combined, deltas = outs[:count], outs[count : 2 * count]
    hiddens, scaleds, back_pres = outs[2 * count :]
    tok_rows, width = rows_in[0].shape
    for first in range(0, count, 2):
        group = range(first, min(first + 2, count))
        span = slice(first * tok_rows, (first + len(group)) * tok_rows)
        stack = lambda values: jnp.concatenate(list(values), axis=0)
        rows = stack(rows_in[i][...] for i in group)
        cotangent = stack(payloads[i][:tok_rows, :] for i in group).astype(wide)
        out_sum = jnp.zeros(rows.shape, wide)
        delta_sum = jnp.zeros(rows.shape, wide)
        for e in range(4):
            weight_in, weight_out = weights[2 * e], weights[2 * e + 1]
            gate = stack(gate_tile(payloads[i], tok_rows, place[3 + e]) for i in group)
            gate = jnp.concatenate([gate] * (width // 128), axis=1)
            active = jnp.maximum(jnp.dot(rows, weight_in[...], preferred_element_type=wide), 0.0)
            hidden = (active * active).astype(narrow)
            hiddens[e, span, :] = hidden
            scaled = (gate * cotangent).astype(narrow)
            scaleds[e, span, :] = scaled
            back_hidden = lax.dot_general(scaled, weight_out[...], contract_last, preferred_element_type=wide)
            back_pre = (back_hidden * 2.0 * active).astype(narrow)
            back_pres[e, span, :] = back_pre
            result = jnp.dot(hidden, weight_out[...], preferred_element_type=wide).astype(narrow)
            out_sum = out_sum + gate * result.astype(wide)
            back_rows = lax.dot_general(back_pre, weight_in[...], contract_last, preferred_element_type=wide)
            delta_sum = delta_sum + back_rows.astype(narrow).astype(wide)
        for i in group:
            part = slice((i - first) * tok_rows, (i - first + 1) * tok_rows)
            combined[i][...] = out_sum[part].astype(combined[i].dtype)
            deltas[i][...] = delta_sum[part].astype(deltas[i].dtype)


def weight_grad_body(side, n_rows, n_sets, place, *refs):
    rows_in = refs[:n_rows]
    sets = [refs[n_rows + 3 * i : n_rows + 3 * i + 3] for i in range(n_sets)]
    outs = refs[n_rows + 3 * n_sets :]
    dot = functools.partial(lax.dot_general, dimension_numbers=contract_first, preferred_element_type=wide)
    rows = jnp.concatenate([r[...] for r in rows_in], axis=0)
    for core in (1, 0):
        hidden, scaled, back_pre = (
            jnp.concatenate([values[i][core * 2 + side] for values in sets], axis=0) for i in range(3)
        )
        outs[core][0] = dot(rows, back_pre).astype(outs[core].dtype)
        outs[core][1] = dot(hidden, scaled).astype(outs[core].dtype)


def order_body(n_line, place, *refs):
    pieces, out = refs[:n_line], refs[n_line]
    tok_rows = pieces[0].shape[0]
    for back in range(n_line):
        z = lax.rem(place[0] + n_line - back, n_line)
        out[pl.ds(pl.multiple_of(z * tok_rows, tok_rows), tok_rows), :] = pieces[back][...].astype(out.dtype)


def down_grad_body(n_line, place, *refs):
    pieces, deltas, blocks = refs[:4], refs[4:8], refs[8:]
    tokens = jnp.concatenate([p[...] for p in pieces], axis=0)
    delta = jnp.concatenate([d[...] for d in deltas], axis=0)
    part = lax.dot_general(tokens, delta, contract_first, preferred_element_type=wide)
    block = blocks[0].shape[0]
    for z in range(n_line):
        for back in range(n_line):

            @pl.when(lax.rem(place[0] + n_line - back, n_line) == z)
            def _(z=z, back=back):
                blocks[back][...] = part[z * block : (z + 1) * block].astype(blocks[back].dtype)


def token_grad_body(n_line, block, place, delta, *refs):
    downs, out = refs[:4], refs[4]
    for core in range(2):
        for side in range(2):
            owner = (place[1] ^ side) * 2 + (place[2] ^ core)
            part = lax.dot_general(
                delta[...], downs[core * 2 + side][...], contract_last, preferred_element_type=wide
            ).astype(narrow)
            for z in range(n_line):
                start = pl.multiple_of((z * 4 + owner) * block, block)
                out[:, pl.ds(start, block)] = part[:, z * block : (z + 1) * block]


def all_rows(tokens, routes, gate_levels, latent_grad, down_weight, expert_in, expert_out):
    tok_rows, width = tokens.shape
    latent_width = down_weight.shape[1]
    hidden_width = expert_in.shape[2]
    n_major = lax.axis_size("expert")
    n_line = n_major // 2
    n_experts = n_major * 2
    block = width // n_experts
    major = lax.axis_index("expert")
    my_core = lax.axis_index("dp")
    place = jnp.stack(
        [major // 2, major % 2, my_core]
        + [(major ^ side) * 2 + (my_core ^ core) for core in range(2) for side in range(2)]
    ).astype(jnp.int32)
    shape = jax.ShapeDtypeStruct
    rows_of = lambda kind: shape((tok_rows, latent_width), kind)

    downs = [down_weight] + [turn(down_weight, n_line, back) for back in range(1, n_line)]

    gate_rows = -(-n_experts // 16) * 16
    columns = call(
        functools.partial(columns_body, n_line, block),
        [shape((tok_rows, n_line * block), narrow)] * 2 + [shape((2, tok_rows, n_line * block), narrow)],
        "columns",
        scratch=[pltpu.SemaphoreType.DMA((4 * n_line,))],
        outside=1,
    )(place, tokens)
    (payload,) = call(payload_body, [shape((tok_rows + gate_rows, latent_width), narrow)], "payload")(
        place, routes.T, gate_levels.T, latent_grad
    )
    own = [expert_in[0], expert_out[0]]
    side_in = swap(own[0], n_line, 0, 1)
    across = swap(columns[2], n_line, 0, 1)
    near_tokens = [columns[0], across[0], swap(after(columns[1], across), n_line, 1, 0), swap(across[1], n_line, 1, 0)]
    payloads = [payload, turn(after(payload, *downs[1:]), n_line, 1)]

    project = call(
        functools.partial(project_body, n_line),
        [shape((2, tok_rows, latent_width), wide)] * 2 + [shape((n_line * block, latent_width), narrow)],
        "project",
    )
    keep, send, down = project(after(place, side_in), *near_tokens, *downs)
    half = keep + after(swap(send, n_line, 1, 0), payloads[1])
    payloads += [turn(after(payload, half), n_line, back) for back in range(2, n_line)]
    core_in = [swap(after(w, half), n_line, 1, 0) for w in (own[0], side_in)]
    latent = (half[0] + after(swap(half[1], n_line, 0, 1), *core_in, *payloads[2:])).astype(narrow)
    ends = [1, n_line - 1]
    middle = list(range(2, n_line - 1))
    groups = [ends, [0], middle]
    rows = [latent] + [None] * (n_line - 1)
    for back in ends:
        rows[back] = turn(latent, n_line, back)
    end_rows = [rows[back] for back in ends]
    for back in middle:
        rows[back] = turn(after(latent, *end_rows), n_line, back)

    side_out = swap(after(own[1], latent), n_line, 0, 1)
    core_out = [swap(after(own[1], latent), n_line, 1, 0), swap(after(side_out, *end_rows), n_line, 1, 0)]
    weights = [own[0], own[1], side_in, side_out, core_in[0], core_out[0], core_in[1], core_out[1]]
    side_down = swap(after(down, side_out), n_line, 0, 1)
    all_down = [down, side_down] + [swap(d, n_line, 1, 0) for d in (down, side_down)]

    outs_of, deltas_of, saved = [None] * n_line, [None] * n_line, []
    for group in groups:
        count = len(group)
        kind = narrow if group[0] else wide
        if group == middle:
            rows[group[0]] = after(rows[group[0]], deltas_of[0])
        if not group[0]:
            rows[0] = after(latent, deltas_of[1])
        values = call(
            functools.partial(expert_body, count),
            [rows_of(kind)] * (2 * count) + [shape((4, count * tok_rows, hidden_width), narrow)] * 3,
            "experts",
        )(place, *(rows[i] for i in group), *(payloads[i] for i in group), *weights)
        for i, back in enumerate(group):
            outs_of[back], deltas_of[back] = values[i], values[count + i]
        saved.append(list(values[2 * count :]))

    def home(value, back):
        return turn(value, n_line, n_line - back) if back else value

    delta_lines = [home(value, back) for back, value in enumerate(deltas_of)]

    def weight_grads(side, *earlier):
        mine, other = call(
            functools.partial(weight_grad_body, side, n_line, len(groups)),
            [shape((2, latent_width, hidden_width), kind) for kind in (wide, narrow)],
            "weight_grads",
        )(
            after(place, *earlier),
            *(rows[i] for group in groups for i in group),
            *(value for values in saved for value in values),
        )
        return mine, swap(other, n_line, 1, 0)

    (sums,) = call(
        functools.partial(order_body, n_line),
        [shape((n_line * tok_rows, latent_width), narrow)],
        "order",
    )(place, *outs_of)
    first_lines = [delta_lines[back] for back in ends]
    mine, other = weight_grads(1, side_down, sums, *first_lines)
    near_mine, near_other = weight_grads(0, mine)
    far_sums = [(mine[i] + other[i].astype(wide)).astype(narrow) for i in range(2)]
    delta_lines = [after(line, near_mine, *far_sums) for line in delta_lines]
    delta = sum(line.astype(wide) for line in delta_lines).astype(narrow)
    side_delta = swap(delta, n_line, 0, 1)
    latent_out = lax.psum_scatter(
        sums,
        plane,
        scatter_dimension=0,
        axis_index_groups=[[z * 4 + i for z in range(n_line)] for i in range(4)],
        tiled=True,
    )
    far_in = swap(after(far_sums[0], delta), n_line, 0, 1)
    deltas = [delta, side_delta, swap(delta, n_line, 1, 0), swap(side_delta, n_line, 1, 0)]
    blocks = call(
        functools.partial(down_grad_body, n_line),
        [shape((block, latent_width), wide)] + [shape((block, latent_width), narrow)] * (n_line - 1),
        "down_grad",
    )(after(place, near_other, *all_down[2:]), *near_tokens, *deltas)
    far_out = swap(after(far_sums[1], far_in, blocks[1]), n_line, 0, 1)
    grad_in, grad_out = (
        (near_mine[i] + near_other[i].astype(wide) + far.astype(wide)).astype(narrow)
        for i, far in enumerate((far_in, far_out))
    )
    (grad_tokens,) = call(
        functools.partial(token_grad_body, n_line, block),
        [shape((tok_rows, width), narrow)],
        "token_grad",
    )(place, after(delta, blocks[1], far_in, latent_out), *all_down)
    blocks = [blocks[0]] + [home(blocks[back], back) for back in range(1, n_line)]
    grad_down = sum(after(value, grad_tokens).astype(wide) for value in blocks)
    return (latent_out, grad_tokens, grad_down, grad_in[None], grad_out[None])


def slot_table(routes, capacity):
    flat = routes.reshape(-1)
    count = flat.shape[0]
    order = jnp.arange(count, dtype=jnp.int32)
    same = (flat[:, None] == flat[None, :]) & (order[None, :] < order[:, None])
    placed = jnp.sum(jnp.where(same, 1, 0), axis=1).astype(jnp.int32)
    return flat * capacity + placed


def routed_rows(tokens, routes, gate_levels, latent_grad, down_weight, expert_in, expert_out):
    tok_rows = tokens.shape[0]
    top = routes.shape[1]
    latent_width = down_weight.shape[1]
    n_major = lax.axis_size("expert")
    n_minor = lax.axis_size("dp")
    n_experts = n_major * n_minor
    capacity = 3 * tok_rows * top // (2 * n_experts)
    entries = tok_rows * top
    contract_last = (((1,), (1,)), ((), ()))
    contract_first = (((0,), (0,)), ((), ()))
    full_down = lax.all_gather(down_weight, ("expert", "dp"), axis=0, tiled=True)
    latent = jnp.dot(tokens, full_down, preferred_element_type=jnp.float32)
    latent = latent.astype(jnp.bfloat16)
    dest = slot_table(routes, capacity)
    source = (
        jnp.full((n_experts * capacity,), entries, jnp.int32)
        .at[dest]
        .set(jnp.arange(entries, dtype=jnp.int32))
    )
    token_of = jnp.where(source < entries, source // top, tok_rows)
    gates = gate_levels.astype(jnp.float32) * gate_unit
    zero_row = jnp.zeros((1, latent_width), jnp.bfloat16)
    latent_pad = jnp.concatenate([latent, zero_row], axis=0)
    send_latent = latent_pad[token_of].reshape(n_major, n_minor, capacity, latent_width)
    scaled = (gates[:, :, None] * latent_grad.astype(jnp.float32)[:, None, :]).astype(jnp.bfloat16)
    scaled_pad = jnp.concatenate([scaled.reshape(entries, latent_width), zero_row], axis=0)
    send_grad = scaled_pad[source].reshape(n_major, n_minor, capacity, latent_width)
    arrived = lax.all_to_all(
        lax.all_to_all(send_latent, "expert", split_axis=0, concat_axis=0, tiled=True),
        "dp",
        split_axis=1,
        concat_axis=1,
        tiled=True,
    )
    rows = arrived.reshape(-1, latent_width)
    weight_in = expert_in[0]
    weight_out = expert_out[0]
    before = jnp.dot(rows, weight_in, preferred_element_type=jnp.float32)
    active = jnp.maximum(before, 0.0)
    hidden = (active * active).astype(jnp.bfloat16)
    result = jnp.dot(hidden, weight_out, preferred_element_type=jnp.float32).astype(jnp.bfloat16)
    returned = lax.all_to_all(
        lax.all_to_all(
            result.reshape(n_major, n_minor, capacity, latent_width),
            "expert",
            split_axis=0,
            concat_axis=0,
            tiled=True,
        ),
        "dp",
        split_axis=1,
        concat_axis=1,
        tiled=True,
    )
    picked = returned.reshape(n_experts * capacity, latent_width)[dest].astype(jnp.float32)
    picked = picked.reshape(tok_rows, top, latent_width)
    latent_out = jnp.sum(gates[:, :, None] * picked, axis=1).astype(jnp.bfloat16)
    arrived_grad = lax.all_to_all(
        lax.all_to_all(send_grad, "expert", split_axis=0, concat_axis=0, tiled=True),
        "dp",
        split_axis=1,
        concat_axis=1,
        tiled=True,
    )
    grad_rows = arrived_grad.reshape(-1, latent_width)
    back_hidden = lax.dot_general(
        grad_rows, weight_out, contract_last, preferred_element_type=jnp.float32
    )
    back_pre = (back_hidden * 2.0 * active).astype(jnp.bfloat16)
    grad_out = lax.dot_general(
        hidden, grad_rows, contract_first, preferred_element_type=jnp.float32
    ).astype(jnp.bfloat16)
    grad_in = lax.dot_general(
        rows, back_pre, contract_first, preferred_element_type=jnp.float32
    ).astype(jnp.bfloat16)
    back_rows = lax.dot_general(
        back_pre, weight_in, contract_last, preferred_element_type=jnp.float32
    ).astype(jnp.bfloat16)
    came_back = lax.all_to_all(
        lax.all_to_all(
            back_rows.reshape(n_major, n_minor, capacity, latent_width),
            "expert",
            split_axis=0,
            concat_axis=0,
            tiled=True,
        ),
        "dp",
        split_axis=1,
        concat_axis=1,
        tiled=True,
    )
    gathered_back = came_back.reshape(n_experts * capacity, latent_width)[dest].astype(jnp.float32)
    latent_delta = jnp.sum(gathered_back.reshape(tok_rows, top, latent_width), axis=1).astype(
        jnp.bfloat16
    )
    grad_tokens = lax.dot_general(
        latent_delta, full_down, contract_last, preferred_element_type=jnp.float32
    )
    grad_tokens = grad_tokens.astype(jnp.bfloat16)
    grad_down = lax.psum_scatter(
        lax.dot_general(tokens, latent_delta, contract_first, preferred_element_type=jnp.float32),
        ("expert", "dp"),
        scatter_dimension=0,
        tiled=True,
    )
    return (latent_out, grad_tokens, grad_down, grad_in[None], grad_out[None])


def on_device(tokens, routes, *others):
    n_major = lax.axis_size("expert")
    n_experts = n_major * lax.axis_size("dp")
    few = n_experts <= 2 * routes.shape[1] and n_major % 2 == 0 and n_major >= 6 and lax.axis_size("dp") == 2
    return (all_rows if few else routed_rows)(tokens, routes, *others)


def solution(mesh):
    in_specs = (
        P(("group", "expert", "dp"), None),
        P(("group", "expert", "dp"), None),
        P(("group", "expert", "dp"), None),
        P(("group", "expert", "dp"), None),
        P(("expert", "dp"), None),
        P(("expert", "dp"), None, None),
        P(("expert", "dp"), None, None),
    )
    out_specs = (
        P(("group", "expert", "dp"), None),
        P(("group", "expert", "dp"), None),
        P(("group", "expert", "dp"), None),
        P(("group", "expert", "dp"), None, None),
        P(("group", "expert", "dp"), None, None),
    )
    return jax.shard_map(
        on_device, mesh=mesh, in_specs=in_specs, out_specs=out_specs, check_vma=False
    )
```

```python
import functools

import jax
import jax.numpy as jnp
from jax import lax
from jax.experimental import pallas as pl
from jax.experimental.pallas import tpu as pltpu
from jax.sharding import PartitionSpec as P

gate_unit = 1.0 / 1024.0
contract_last = (((1,), (1,)), ((), ()))
contract_first = (((0,), (0,)), ((), ()))
plane = ("expert", "dp")
wide = jnp.float32
narrow = jnp.bfloat16


def device_pairs(n_line, move):
    pairs = []
    for z in range(n_line):
        for x in range(2):
            for c in range(2):
                to_z, to_x, to_c = move(z, x, c)
                pairs.append(((z * 2 + x) * 2 + c, (to_z * 2 + to_x) * 2 + to_c))
    return pairs


def turn(value, n_line, by):
    return lax.ppermute(value, plane, device_pairs(n_line, lambda z, x, c: ((z + by) % n_line, x, c)))


def swap(value, n_line, core, side):
    return lax.ppermute(value, plane, device_pairs(n_line, lambda z, x, c: (z, x ^ side, c ^ core)))


def after(value, *earlier):
    return lax.optimization_barrier((value,) + earlier)[0]


def call(body, outs, name, scratch=(), outside=0):
    vmem = pl.BlockSpec(memory_space=pltpu.VMEM)
    anywhere = pl.BlockSpec(memory_space=pl.ANY)

    def run(place, *operands):
        return pl.pallas_call(
            body,
            out_shape=outs,
            in_specs=[pl.BlockSpec(memory_space=pltpu.SMEM)]
            + [anywhere] * outside
            + [vmem] * (len(operands) - outside),
            out_specs=[vmem] * len(outs),
            scratch_shapes=list(scratch),
            compiler_params=pltpu.CompilerParams(vmem_limit_bytes=40 * 1024 * 1024),
            cost_estimate=pl.CostEstimate(flops=0, bytes_accessed=0, transcendentals=0),
            name=name,
        )(place, *operands)

    return run


def columns_body(n_line, block, place, tokens, *refs):
    own, other, across, sems = refs
    pieces = (own, across.at[0], other, across.at[1])
    copies = []
    for core in range(2):
        for side in range(2):
            owner = (place[1] ^ side) * 2 + (place[2] ^ core)
            for z in range(n_line):
                start = pl.multiple_of((z * 4 + owner) * block, block)
                piece = pieces[core * 2 + side].at[:, pl.ds(z * block, block)]
                copies.append(
                    pltpu.make_async_copy(tokens.at[:, pl.ds(start, block)], piece, sems.at[len(copies)])
                )
    for copy in copies:
        copy.start()
    for copy in copies:
        copy.wait()


def payload_body(place, routes, levels, cotangent, payload):
    tok_rows = cotangent.shape[0]
    gate_rows = payload.shape[0] - tok_rows
    payload[:tok_rows, :] = cotangent[...]
    expert = lax.broadcasted_iota(jnp.int32, (gate_rows, tok_rows), 0)
    total = jnp.zeros((gate_rows, tok_rows), jnp.int32)
    for k in range(routes.shape[0]):
        total = total + jnp.where(expert == routes[k : k + 1, :], levels[k : k + 1, :], 0)
    low = total & 31
    payload[tok_rows:, :tok_rows] = (total - low).astype(wide).astype(narrow)
    payload[tok_rows:, tok_rows : 2 * tok_rows] = low.astype(wide).astype(narrow)
    rest = payload.shape[1] - 2 * tok_rows
    payload[tok_rows:, 2 * tok_rows :] = jnp.zeros((gate_rows, rest), narrow)


def project_body(n_line, place, *refs):
    pieces, downs = refs[:4], refs[4 : 4 + n_line]
    keep, send, down = refs[4 + n_line :]
    block = downs[0].shape[0]
    for back in range(n_line):
        z = lax.rem(place[0] + n_line - back, n_line)
        down[pl.ds(pl.multiple_of(z * block, block), block), :] = downs[back][...]
    for core, out in ((1, send), (0, keep)):
        for side in range(2):
            out[side] = jnp.dot(pieces[core * 2 + side][...], down[...], preferred_element_type=wide)


def gate_tile(payload, tok_rows, expert):
    packed = payload[tok_rows:, :]
    rows = lax.broadcasted_iota(jnp.int32, (packed.shape[0], 128), 0)
    pick = jnp.where(rows == expert, 1.0, 0.0).astype(narrow)
    dot = functools.partial(lax.dot_general, dimension_numbers=contract_first, preferred_element_type=wide)
    total = dot(packed[:, :tok_rows], pick) + dot(packed[:, tok_rows : 2 * tok_rows], pick)
    return total * gate_unit


def expert_body(count, place, *refs):
    rows_in, payloads = refs[:count], refs[count : 2 * count]
    own, core, *sides = refs[2 * count : 2 * count + 6]
    weights = (own.at[0], own.at[1], sides[0], sides[1], core.at[0], core.at[1], sides[2], sides[3])
    outs = refs[2 * count + 6 :]
    combined, deltas = outs[:count], outs[count : 2 * count]
    hiddens, scaleds, back_pres = outs[2 * count :]
    tok_rows, width = rows_in[0].shape
    for first in range(0, count, 2):
        group = range(first, min(first + 2, count))
        span = slice(first * tok_rows, (first + len(group)) * tok_rows)
        stack = lambda values: jnp.concatenate(list(values), axis=0)
        rows = stack(rows_in[i][...] for i in group)
        cotangent = stack(payloads[i][:tok_rows, :] for i in group).astype(wide)
        out_sum = jnp.zeros(rows.shape, wide)
        delta_sum = jnp.zeros(rows.shape, wide)
        for e in range(4):
            weight_in, weight_out = weights[2 * e], weights[2 * e + 1]
            gate = stack(gate_tile(payloads[i], tok_rows, place[3 + e]) for i in group)
            gate = jnp.concatenate([gate] * (width // 128), axis=1)
            active = jnp.maximum(jnp.dot(rows, weight_in[...], preferred_element_type=wide), 0.0)
            hidden = (active * active).astype(narrow)
            hiddens[e, span, :] = hidden
            scaled = (gate * cotangent).astype(narrow)
            scaleds[e, span, :] = scaled
            back_hidden = lax.dot_general(scaled, weight_out[...], contract_last, preferred_element_type=wide)
            back_pre = (back_hidden * 2.0 * active).astype(narrow)
            back_pres[e, span, :] = back_pre
            result = jnp.dot(hidden, weight_out[...], preferred_element_type=wide).astype(narrow)
            out_sum = out_sum + gate * result.astype(wide)
            back_rows = lax.dot_general(back_pre, weight_in[...], contract_last, preferred_element_type=wide)
            delta_sum = delta_sum + back_rows.astype(narrow).astype(wide)
        for i in group:
            part = slice((i - first) * tok_rows, (i - first + 1) * tok_rows)
            combined[i][...] = out_sum[part].astype(combined[i].dtype)
            deltas[i][...] = delta_sum[part].astype(deltas[i].dtype)


def weight_grad_body(n_rows, n_sets, place, *refs):
    rows_in = refs[:n_rows]
    sets = [refs[n_rows + 3 * i : n_rows + 3 * i + 3] for i in range(n_sets)]
    near, far, other = refs[n_rows + 3 * n_sets :]
    dot = functools.partial(lax.dot_general, dimension_numbers=contract_first, preferred_element_type=wide)
    rows = jnp.concatenate([r[...] for r in rows_in], axis=0)
    for core in (1, 0):
        for side in (1, 0):
            hidden, scaled, back_pre = (
                jnp.concatenate([values[i][core * 2 + side] for values in sets], axis=0) for i in range(3)
            )
            grad_in, grad_out = dot(rows, back_pre), dot(hidden, scaled)
            if core:
                other[2 * side] = grad_in.astype(narrow)
                other[2 * side + 1] = grad_out.astype(narrow)
            else:
                own = far if side else near
                own[0], own[1] = grad_in, grad_out


def down_grad_body(n_line, place, *refs):
    pieces, deltas, core_deltas, blocks = refs[:4], refs[4:6], refs[6], refs[7:]
    tokens = jnp.concatenate([p[...] for p in pieces], axis=0)
    delta = jnp.concatenate([d[...] for d in deltas] + [core_deltas[0], core_deltas[1]], axis=0)
    part = lax.dot_general(tokens, delta, contract_first, preferred_element_type=wide)
    block = blocks[0].shape[0]
    for z in range(n_line):
        for back in range(n_line):

            @pl.when(lax.rem(place[0] + n_line - back, n_line) == z)
            def _(z=z, back=back):
                blocks[back][...] = part[z * block : (z + 1) * block].astype(blocks[back].dtype)


def token_grad_body(place, delta, core_deltas, down, side_down, own, other):
    for rows, out in ((core_deltas[0], other), (delta[...], own)):
        for side, weight in enumerate((down, side_down)):
            out[side] = lax.dot_general(
                rows, weight[...], contract_last, preferred_element_type=wide
            ).astype(narrow)


def arrange_body(n_line, block, place, own, other, out):
    for core, pieces in enumerate((own, other)):
        for side in range(2):
            owner = (place[1] ^ side) * 2 + (place[2] ^ core)
            for z in range(n_line):
                start = pl.multiple_of((z * 4 + owner) * block, block)
                out[:, pl.ds(start, block)] = pieces[side, :, z * block : (z + 1) * block]


def all_rows(tokens, routes, gate_levels, latent_grad, down_weight, expert_in, expert_out):
    tok_rows, width = tokens.shape
    latent_width = down_weight.shape[1]
    hidden_width = expert_in.shape[2]
    n_major = lax.axis_size("expert")
    n_line = n_major // 2
    n_experts = n_major * 2
    block = width // n_experts
    major = lax.axis_index("expert")
    my_core = lax.axis_index("dp")
    place = jnp.stack(
        [major // 2, major % 2, my_core]
        + [(major ^ side) * 2 + (my_core ^ core) for core in range(2) for side in range(2)]
    ).astype(jnp.int32)
    shape = jax.ShapeDtypeStruct
    rows_of = lambda kind: shape((tok_rows, latent_width), kind)

    downs = [down_weight] + [turn(down_weight, n_line, back) for back in range(1, n_line)]

    gate_rows = -(-n_experts // 16) * 16
    columns = call(
        functools.partial(columns_body, n_line, block),
        [shape((tok_rows, n_line * block), narrow)] * 2 + [shape((2, tok_rows, n_line * block), narrow)],
        "columns",
        scratch=[pltpu.SemaphoreType.DMA((4 * n_line,))],
        outside=1,
    )(place, tokens)
    (payload,) = call(payload_body, [shape((tok_rows + gate_rows, latent_width), narrow)], "payload")(
        place, routes.T, gate_levels.T, latent_grad
    )
    across = swap(columns[2], n_line, 0, 1)
    near_tokens = [columns[0], across[0], swap(after(columns[1], across), n_line, 1, 0), swap(across[1], n_line, 1, 0)]
    side_in = swap(after(expert_in[0], across, near_tokens[2]), n_line, 0, 1)

    project = call(
        functools.partial(project_body, n_line),
        [shape((2, tok_rows, latent_width), wide)] * 2 + [shape((n_line * block, latent_width), narrow)],
        "project",
    )
    keep, send, down = project(place, *near_tokens, *downs)
    half = keep + after(swap(send, n_line, 1, 0), side_in)
    payloads = [payload] + [turn(after(payload, half), n_line, back) for back in range(1, n_line)]
    own = jnp.concatenate([expert_in, expert_out])
    core_own = swap(after(own, half), n_line, 1, 0)
    latent = (half[0] + after(swap(half[1], n_line, 0, 1), core_own, *payloads[1:])).astype(narrow)
    ends = [1, n_line - 1]
    middle = list(range(2, n_line - 1))
    groups = [ends, middle, [0]]
    rows = [latent] + [turn(latent, n_line, back) for back in range(1, n_line)]

    side_out = swap(after(expert_out[0], latent), n_line, 0, 1)
    far_in = swap(after(side_in, latent), n_line, 1, 0)
    far_out = swap(after(side_out, *rows[1:]), n_line, 1, 0)
    weights = [own, core_own, side_in, side_out, far_in, far_out]
    side_down = swap(after(down, side_out), n_line, 0, 1)

    outs_of, deltas_of, saved = [None] * n_line, [None] * n_line, []
    for group in groups:
        count = len(group)
        kind = narrow if group[0] else wide
        if group == middle:
            rows[group[0]] = after(rows[group[0]], deltas_of[1])
        if not group[0]:
            rows[0] = after(latent, deltas_of[middle[0]])
        values = call(
            functools.partial(expert_body, count),
            [rows_of(kind)] * (2 * count) + [shape((4, count * tok_rows, hidden_width), narrow)] * 3,
            "experts",
        )(place, *(rows[i] for i in group), *(payloads[i] for i in group), *weights)
        for i, back in enumerate(group):
            outs_of[back], deltas_of[back] = values[i], values[count + i]
        saved.append(list(values[2 * count :]))

    def home(value, back):
        return turn(value, n_line, n_line - back) if back else value

    delta_lines = [home(value, back) for back, value in enumerate(deltas_of)]

    pair = (2, latent_width, hidden_width)
    near, far, other = call(
        functools.partial(weight_grad_body, n_line, len(groups)),
        [shape(pair, wide)] * 2 + [shape((4, latent_width, hidden_width), narrow)],
        "weight_grads",
    )(
        after(place, side_down),
        *(rows[i] for group in groups for i in group),
        *(value for values in saved for value in values),
    )
    delta_lines = [after(line, near) for line in delta_lines]
    delta = sum(line.astype(wide) for line in delta_lines).astype(narrow)
    side_delta = swap(delta, n_line, 0, 1)
    out_lines = [outs_of[0]] + [home(after(outs_of[back], delta), back) for back in range(1, n_line)]
    latent_out = sum(line.astype(wide) for line in out_lines).astype(narrow)
    other = swap(after(other, delta), n_line, 1, 0)
    far = swap((far + other[2:].astype(wide)).astype(narrow), n_line, 0, 1)
    core_deltas = swap(jnp.stack([delta, after(side_delta, out_lines[1], out_lines[-1])]), n_line, 1, 0)
    blocks = call(
        functools.partial(down_grad_body, n_line),
        [shape((block, latent_width), wide)] + [shape((block, latent_width), narrow)] * (n_line - 1),
        "down_grad",
    )(after(place, *out_lines[1:]), *near_tokens, delta, side_delta, core_deltas)
    weight_grad = (near + other[:2].astype(wide) + far.astype(wide)).astype(narrow)
    both = [shape((2, tok_rows, n_line * block), narrow)] * 2
    own_grads, core_grads = call(token_grad_body, both, "token_grad")(
        place, after(delta, blocks[1]), core_deltas, down, side_down
    )
    (grad_tokens,) = call(
        functools.partial(arrange_body, n_line, block), [shape((tok_rows, width), narrow)], "arrange"
    )(place, own_grads, swap(core_grads, n_line, 1, 0))
    blocks = [blocks[0]] + [home(blocks[back], back) for back in range(1, n_line)]
    grad_down = sum(value.astype(wide) for value in blocks)
    return (latent_out, grad_tokens, grad_down, weight_grad[:1], weight_grad[1:])


def slot_table(routes, capacity):
    flat = routes.reshape(-1)
    count = flat.shape[0]
    order = jnp.arange(count, dtype=jnp.int32)
    same = (flat[:, None] == flat[None, :]) & (order[None, :] < order[:, None])
    placed = jnp.sum(jnp.where(same, 1, 0), axis=1).astype(jnp.int32)
    return flat * capacity + placed


def routed_rows(tokens, routes, gate_levels, latent_grad, down_weight, expert_in, expert_out):
    tok_rows = tokens.shape[0]
    top = routes.shape[1]
    latent_width = down_weight.shape[1]
    n_major = lax.axis_size("expert")
    n_minor = lax.axis_size("dp")
    n_experts = n_major * n_minor
    capacity = 3 * tok_rows * top // (2 * n_experts)
    entries = tok_rows * top
    contract_last = (((1,), (1,)), ((), ()))
    contract_first = (((0,), (0,)), ((), ()))
    full_down = lax.all_gather(down_weight, ("expert", "dp"), axis=0, tiled=True)
    latent = jnp.dot(tokens, full_down, preferred_element_type=jnp.float32)
    latent = latent.astype(jnp.bfloat16)
    dest = slot_table(routes, capacity)
    source = (
        jnp.full((n_experts * capacity,), entries, jnp.int32)
        .at[dest]
        .set(jnp.arange(entries, dtype=jnp.int32))
    )
    token_of = jnp.where(source < entries, source // top, tok_rows)
    gates = gate_levels.astype(jnp.float32) * gate_unit
    zero_row = jnp.zeros((1, latent_width), jnp.bfloat16)
    latent_pad = jnp.concatenate([latent, zero_row], axis=0)
    send_latent = latent_pad[token_of].reshape(n_major, n_minor, capacity, latent_width)
    scaled = (gates[:, :, None] * latent_grad.astype(jnp.float32)[:, None, :]).astype(jnp.bfloat16)
    scaled_pad = jnp.concatenate([scaled.reshape(entries, latent_width), zero_row], axis=0)
    send_grad = scaled_pad[source].reshape(n_major, n_minor, capacity, latent_width)
    arrived = lax.all_to_all(
        lax.all_to_all(send_latent, "expert", split_axis=0, concat_axis=0, tiled=True),
        "dp",
        split_axis=1,
        concat_axis=1,
        tiled=True,
    )
    rows = arrived.reshape(-1, latent_width)
    weight_in = expert_in[0]
    weight_out = expert_out[0]
    before = jnp.dot(rows, weight_in, preferred_element_type=jnp.float32)
    active = jnp.maximum(before, 0.0)
    hidden = (active * active).astype(jnp.bfloat16)
    result = jnp.dot(hidden, weight_out, preferred_element_type=jnp.float32).astype(jnp.bfloat16)
    returned = lax.all_to_all(
        lax.all_to_all(
            result.reshape(n_major, n_minor, capacity, latent_width),
            "expert",
            split_axis=0,
            concat_axis=0,
            tiled=True,
        ),
        "dp",
        split_axis=1,
        concat_axis=1,
        tiled=True,
    )
    picked = returned.reshape(n_experts * capacity, latent_width)[dest].astype(jnp.float32)
    picked = picked.reshape(tok_rows, top, latent_width)
    latent_out = jnp.sum(gates[:, :, None] * picked, axis=1).astype(jnp.bfloat16)
    arrived_grad = lax.all_to_all(
        lax.all_to_all(send_grad, "expert", split_axis=0, concat_axis=0, tiled=True),
        "dp",
        split_axis=1,
        concat_axis=1,
        tiled=True,
    )
    grad_rows = arrived_grad.reshape(-1, latent_width)
    back_hidden = lax.dot_general(
        grad_rows, weight_out, contract_last, preferred_element_type=jnp.float32
    )
    back_pre = (back_hidden * 2.0 * active).astype(jnp.bfloat16)
    grad_out = lax.dot_general(
        hidden, grad_rows, contract_first, preferred_element_type=jnp.float32
    ).astype(jnp.bfloat16)
    grad_in = lax.dot_general(
        rows, back_pre, contract_first, preferred_element_type=jnp.float32
    ).astype(jnp.bfloat16)
    back_rows = lax.dot_general(
        back_pre, weight_in, contract_last, preferred_element_type=jnp.float32
    ).astype(jnp.bfloat16)
    came_back = lax.all_to_all(
        lax.all_to_all(
            back_rows.reshape(n_major, n_minor, capacity, latent_width),
            "expert",
            split_axis=0,
            concat_axis=0,
            tiled=True,
        ),
        "dp",
        split_axis=1,
        concat_axis=1,
        tiled=True,
    )
    gathered_back = came_back.reshape(n_experts * capacity, latent_width)[dest].astype(jnp.float32)
    latent_delta = jnp.sum(gathered_back.reshape(tok_rows, top, latent_width), axis=1).astype(
        jnp.bfloat16
    )
    grad_tokens = lax.dot_general(
        latent_delta, full_down, contract_last, preferred_element_type=jnp.float32
    )
    grad_tokens = grad_tokens.astype(jnp.bfloat16)
    grad_down = lax.psum_scatter(
        lax.dot_general(tokens, latent_delta, contract_first, preferred_element_type=jnp.float32),
        ("expert", "dp"),
        scatter_dimension=0,
        tiled=True,
    )
    return (latent_out, grad_tokens, grad_down, grad_in[None], grad_out[None])


def on_device(tokens, routes, *others):
    n_major = lax.axis_size("expert")
    n_experts = n_major * lax.axis_size("dp")
    few = n_experts <= 2 * routes.shape[1] and n_major % 2 == 0 and n_major >= 6 and lax.axis_size("dp") == 2
    return (all_rows if few else routed_rows)(tokens, routes, *others)


def solution(mesh):
    in_specs = (
        P(("group", "expert", "dp"), None),
        P(("group", "expert", "dp"), None),
        P(("group", "expert", "dp"), None),
        P(("group", "expert", "dp"), None),
        P(("expert", "dp"), None),
        P(("expert", "dp"), None, None),
        P(("expert", "dp"), None, None),
    )
    out_specs = (
        P(("group", "expert", "dp"), None),
        P(("group", "expert", "dp"), None),
        P(("group", "expert", "dp"), None),
        P(("group", "expert", "dp"), None, None),
        P(("group", "expert", "dp"), None, None),
    )
    return jax.shard_map(
        on_device, mesh=mesh, in_specs=in_specs, out_specs=out_specs, check_vma=False
    )
```

```python
import functools

import jax
import jax.numpy as jnp
from jax import lax
from jax.experimental import pallas as pl
from jax.experimental.pallas import tpu as pltpu
from jax.sharding import PartitionSpec as P

gate_unit = 1.0 / 1024.0
contract_last = (((1,), (1,)), ((), ()))
contract_first = (((0,), (0,)), ((), ()))
plane = ("expert", "dp")
wide = jnp.float32
narrow = jnp.bfloat16


def device_pairs(n_line, move):
    pairs = []
    for z in range(n_line):
        for x in range(2):
            for c in range(2):
                to_z, to_x, to_c = move(z, x, c)
                pairs.append(((z * 2 + x) * 2 + c, (to_z * 2 + to_x) * 2 + to_c))
    return pairs


def turn(value, n_line, by):
    return lax.ppermute(value, plane, device_pairs(n_line, lambda z, x, c: ((z + by) % n_line, x, c)))


def swap(value, n_line, core, side):
    return lax.ppermute(value, plane, device_pairs(n_line, lambda z, x, c: (z, x ^ side, c ^ core)))


def after(value, *earlier):
    return lax.optimization_barrier((value,) + earlier)[0]


def call(body, outs, name, scratch=(), outside=0):
    vmem = pl.BlockSpec(memory_space=pltpu.VMEM)
    anywhere = pl.BlockSpec(memory_space=pl.ANY)

    def run(place, *operands):
        return pl.pallas_call(
            body,
            out_shape=outs,
            in_specs=[pl.BlockSpec(memory_space=pltpu.SMEM)]
            + [anywhere] * outside
            + [vmem] * (len(operands) - outside),
            out_specs=[vmem] * len(outs),
            scratch_shapes=list(scratch),
            compiler_params=pltpu.CompilerParams(vmem_limit_bytes=40 * 1024 * 1024),
            cost_estimate=pl.CostEstimate(flops=0, bytes_accessed=0, transcendentals=0),
            name=name,
        )(place, *operands)

    return run


def columns_body(n_line, block, place, tokens, *refs):
    own, other, across, sems = refs
    pieces = (own, across.at[0], other, across.at[1])
    copies = []
    for core in range(2):
        for side in range(2):
            owner = (place[1] ^ side) * 2 + (place[2] ^ core)
            for z in range(n_line):
                start = pl.multiple_of((z * 4 + owner) * block, block)
                piece = pieces[core * 2 + side].at[:, pl.ds(z * block, block)]
                copies.append(
                    pltpu.make_async_copy(tokens.at[:, pl.ds(start, block)], piece, sems.at[len(copies)])
                )
    for copy in copies:
        copy.start()
    for copy in copies:
        copy.wait()


def payload_body(place, routes, levels, cotangent, payload):
    tok_rows = cotangent.shape[0]
    gate_rows = payload.shape[0] - tok_rows
    payload[:tok_rows, :] = cotangent[...]
    expert = lax.broadcasted_iota(jnp.int32, (gate_rows, tok_rows), 0)
    total = jnp.zeros((gate_rows, tok_rows), jnp.int32)
    for k in range(routes.shape[0]):
        total = total + jnp.where(expert == routes[k : k + 1, :], levels[k : k + 1, :], 0)
    low = total & 31
    payload[tok_rows:, :tok_rows] = (total - low).astype(wide).astype(narrow)
    payload[tok_rows:, tok_rows : 2 * tok_rows] = low.astype(wide).astype(narrow)
    rest = payload.shape[1] - 2 * tok_rows
    payload[tok_rows:, 2 * tok_rows :] = jnp.zeros((gate_rows, rest), narrow)


def project_body(n_line, place, *refs):
    pieces, downs = refs[:4], refs[4 : 4 + n_line]
    keep, send, down = refs[4 + n_line :]
    block = downs[0].shape[0]
    for back in range(n_line):
        z = lax.rem(place[0] + n_line - back, n_line)
        down[pl.ds(pl.multiple_of(z * block, block), block), :] = downs[back][...]
    for core, out in ((1, send), (0, keep)):
        for side in range(2):
            out[side] = jnp.dot(pieces[core * 2 + side][...], down[...], preferred_element_type=wide)


def gate_tile(payload, tok_rows, expert):
    packed = payload[tok_rows:, :]
    rows = lax.broadcasted_iota(jnp.int32, (packed.shape[0], 128), 0)
    pick = jnp.where(rows == expert, 1.0, 0.0).astype(narrow)
    dot = functools.partial(lax.dot_general, dimension_numbers=contract_first, preferred_element_type=wide)
    total = dot(packed[:, :tok_rows], pick) + dot(packed[:, tok_rows : 2 * tok_rows], pick)
    return total * gate_unit


def expert_body(count, place, *refs):
    rows_in, payloads = refs[:count], refs[count : 2 * count]
    own, core, side_out, core_out = refs[2 * count : 2 * count + 4]
    weights = (own.at[0], own.at[1], own.at[2], side_out, core.at[0], core.at[1], core.at[2], core_out)
    outs = refs[2 * count + 4 :]
    combined, deltas = outs[:count], outs[count : 2 * count]
    hiddens, scaleds, back_pres = outs[2 * count :]
    tok_rows, width = rows_in[0].shape
    for first in range(0, count, 2):
        group = range(first, min(first + 2, count))
        span = slice(first * tok_rows, (first + len(group)) * tok_rows)
        stack = lambda values: jnp.concatenate(list(values), axis=0)
        rows = stack(rows_in[i][...] for i in group)
        cotangent = stack(payloads[i][:tok_rows, :] for i in group).astype(wide)
        out_sum = jnp.zeros(rows.shape, wide)
        delta_sum = jnp.zeros(rows.shape, wide)
        for e in range(4):
            weight_in, weight_out = weights[2 * e], weights[2 * e + 1]
            gate = stack(gate_tile(payloads[i], tok_rows, place[3 + e]) for i in group)
            gate = jnp.concatenate([gate] * (width // 128), axis=1)
            active = jnp.maximum(jnp.dot(rows, weight_in[...], preferred_element_type=wide), 0.0)
            hidden = (active * active).astype(narrow)
            hiddens[e, span, :] = hidden
            scaled = (gate * cotangent).astype(narrow)
            scaleds[e, span, :] = scaled
            back_hidden = lax.dot_general(scaled, weight_out[...], contract_last, preferred_element_type=wide)
            back_pre = (back_hidden * 2.0 * active).astype(narrow)
            back_pres[e, span, :] = back_pre
            result = jnp.dot(hidden, weight_out[...], preferred_element_type=wide).astype(narrow)
            out_sum = out_sum + gate * result.astype(wide)
            back_rows = lax.dot_general(back_pre, weight_in[...], contract_last, preferred_element_type=wide)
            delta_sum = delta_sum + back_rows.astype(narrow).astype(wide)
        for i in group:
            part = slice((i - first) * tok_rows, (i - first + 1) * tok_rows)
            combined[i][...] = out_sum[part].astype(combined[i].dtype)
            deltas[i][...] = delta_sum[part].astype(deltas[i].dtype)


def weight_grad_body(n_rows, n_sets, place, *refs):
    rows_in = refs[:n_rows]
    sets = [refs[n_rows + 3 * i : n_rows + 3 * i + 3] for i in range(n_sets)]
    near, far, other = refs[n_rows + 3 * n_sets :]
    dot = functools.partial(lax.dot_general, dimension_numbers=contract_first, preferred_element_type=wide)
    rows = jnp.concatenate([r[...] for r in rows_in], axis=0)
    for core in (1, 0):
        for side in (1, 0):
            hidden, scaled, back_pre = (
                jnp.concatenate([values[i][core * 2 + side] for values in sets], axis=0) for i in range(3)
            )
            grad_in, grad_out = dot(rows, back_pre), dot(hidden, scaled)
            if core:
                other[2 * side] = grad_in.astype(narrow)
                other[2 * side + 1] = grad_out.astype(narrow)
            else:
                own = far if side else near
                own[0], own[1] = grad_in, grad_out


def down_grad_body(n_line, place, *refs):
    pieces, deltas, core_deltas, blocks = refs[:4], refs[4:6], refs[6], refs[7:]
    tokens = jnp.concatenate([p[...] for p in pieces], axis=0)
    delta = jnp.concatenate([d[...] for d in deltas] + [core_deltas[0], core_deltas[1]], axis=0)
    part = lax.dot_general(tokens, delta, contract_first, preferred_element_type=wide)
    block = blocks[0].shape[0]
    for z in range(n_line):
        for back in range(n_line):

            @pl.when(lax.rem(place[0] + n_line - back, n_line) == z)
            def _(z=z, back=back):
                blocks[back][...] = part[z * block : (z + 1) * block].astype(blocks[back].dtype)


def token_grad_body(place, delta, core_deltas, down, side_down, own, other):
    for rows, out in ((core_deltas[0], other), (delta[...], own)):
        for side, weight in enumerate((down, side_down)):
            out[side] = lax.dot_general(
                rows, weight[...], contract_last, preferred_element_type=wide
            ).astype(narrow)


def arrange_body(n_line, block, place, own, other, out):
    for core, pieces in enumerate((own, other)):
        for side in range(2):
            owner = (place[1] ^ side) * 2 + (place[2] ^ core)
            for z in range(n_line):
                start = pl.multiple_of((z * 4 + owner) * block, block)
                out[:, pl.ds(start, block)] = pieces[side, :, z * block : (z + 1) * block]


def all_rows(tokens, routes, gate_levels, latent_grad, down_weight, expert_in, expert_out):
    tok_rows, width = tokens.shape
    latent_width = down_weight.shape[1]
    hidden_width = expert_in.shape[2]
    n_major = lax.axis_size("expert")
    n_line = n_major // 2
    n_experts = n_major * 2
    block = width // n_experts
    major = lax.axis_index("expert")
    my_core = lax.axis_index("dp")
    place = jnp.stack(
        [major // 2, major % 2, my_core]
        + [(major ^ side) * 2 + (my_core ^ core) for core in range(2) for side in range(2)]
    ).astype(jnp.int32)
    shape = jax.ShapeDtypeStruct
    rows_of = lambda kind: shape((tok_rows, latent_width), kind)

    downs = [down_weight] + [turn(down_weight, n_line, back) for back in range(1, n_line)]

    gate_rows = -(-n_experts // 16) * 16
    columns = call(
        functools.partial(columns_body, n_line, block),
        [shape((tok_rows, n_line * block), narrow)] * 2 + [shape((2, tok_rows, n_line * block), narrow)],
        "columns",
        scratch=[pltpu.SemaphoreType.DMA((4 * n_line,))],
        outside=1,
    )(place, tokens)
    (payload,) = call(payload_body, [shape((tok_rows + gate_rows, latent_width), narrow)], "payload")(
        place, routes.T, gate_levels.T, latent_grad
    )
    side_in = swap(expert_in[0], n_line, 0, 1)
    across = swap(columns[2], n_line, 0, 1)
    near_tokens = [columns[0], across[0], swap(after(columns[1], across), n_line, 1, 0), swap(across[1], n_line, 1, 0)]

    project = call(
        functools.partial(project_body, n_line),
        [shape((2, tok_rows, latent_width), wide)] * 2 + [shape((n_line * block, latent_width), narrow)],
        "project",
    )
    keep, send, down = project(after(place, side_in), *near_tokens, *downs)
    half = keep + swap(send, n_line, 1, 0)
    payloads = [payload] + [turn(after(payload, *downs[1:]), n_line, back) for back in range(1, n_line)]
    own = jnp.concatenate([expert_in, expert_out, side_in[None]])
    core_own = swap(after(own, half), n_line, 1, 0)
    latent = (half[0] + after(swap(half[1], n_line, 0, 1), core_own, *payloads[1:])).astype(narrow)
    ends = [1, n_line - 1]
    middle = list(range(2, n_line - 1))
    groups = [ends, middle, [0]]
    rows = [latent] + [turn(latent, n_line, back) for back in range(1, n_line)]

    side_out = swap(after(expert_out[0], latent), n_line, 0, 1)
    core_out = swap(after(side_out, *rows[1:]), n_line, 1, 0)
    weights = [own, core_own, side_out, core_out]
    side_down = swap(after(down, side_out), n_line, 0, 1)

    outs_of, deltas_of, saved = [None] * n_line, [None] * n_line, []
    for group in groups:
        count = len(group)
        kind = narrow if group[0] else wide
        if group == middle:
            rows[group[0]] = after(rows[group[0]], deltas_of[1])
        if not group[0]:
            rows[0] = after(latent, deltas_of[middle[0]])
        values = call(
            functools.partial(expert_body, count),
            [rows_of(kind)] * (2 * count) + [shape((4, count * tok_rows, hidden_width), narrow)] * 3,
            "experts",
        )(place, *(rows[i] for i in group), *(payloads[i] for i in group), *weights)
        for i, back in enumerate(group):
            outs_of[back], deltas_of[back] = values[i], values[count + i]
        saved.append(list(values[2 * count :]))

    def home(value, back):
        return turn(value, n_line, n_line - back) if back else value

    delta_lines = [home(value, back) for back, value in enumerate(deltas_of)]

    pair = (2, latent_width, hidden_width)
    near, far, other = call(
        functools.partial(weight_grad_body, n_line, len(groups)),
        [shape(pair, wide)] * 2 + [shape((4, latent_width, hidden_width), narrow)],
        "weight_grads",
    )(
        after(place, side_down),
        *(rows[i] for group in groups for i in group),
        *(value for values in saved for value in values),
    )
    delta_lines = [after(line, near) for line in delta_lines]
    delta = sum(line.astype(wide) for line in delta_lines).astype(narrow)
    side_delta = swap(delta, n_line, 0, 1)
    out_lines = [outs_of[0]] + [home(outs_of[back], back) for back in range(1, n_line)]
    latent_out = sum(line.astype(wide) for line in out_lines).astype(narrow)
    other = swap(after(other, delta), n_line, 1, 0)
    far = swap((far + after(other[2:], side_delta, out_lines[1]).astype(wide)).astype(narrow), n_line, 0, 1)
    core_deltas = swap(jnp.stack([delta, side_delta]), n_line, 1, 0)
    blocks = call(
        functools.partial(down_grad_body, n_line),
        [shape((block, latent_width), wide)] + [shape((block, latent_width), narrow)] * (n_line - 1),
        "down_grad",
    )(after(place, *out_lines[1:]), *near_tokens, delta, side_delta, core_deltas)
    weight_grad = (near + other[:2].astype(wide) + far.astype(wide)).astype(narrow)
    both = [shape((2, tok_rows, n_line * block), narrow)] * 2
    own_grads, core_grads = call(token_grad_body, both, "token_grad")(
        place, after(delta, blocks[1]), core_deltas, down, side_down
    )
    (grad_tokens,) = call(
        functools.partial(arrange_body, n_line, block), [shape((tok_rows, width), narrow)], "arrange"
    )(place, own_grads, swap(core_grads, n_line, 1, 0))
    blocks = [blocks[0]] + [home(blocks[back], back) for back in range(1, n_line)]
    grad_down = sum(value.astype(wide) for value in blocks)
    return (latent_out, grad_tokens, grad_down, weight_grad[:1], weight_grad[1:])


def slot_table(routes, capacity):
    flat = routes.reshape(-1)
    count = flat.shape[0]
    order = jnp.arange(count, dtype=jnp.int32)
    same = (flat[:, None] == flat[None, :]) & (order[None, :] < order[:, None])
    placed = jnp.sum(jnp.where(same, 1, 0), axis=1).astype(jnp.int32)
    return flat * capacity + placed


def routed_rows(tokens, routes, gate_levels, latent_grad, down_weight, expert_in, expert_out):
    tok_rows = tokens.shape[0]
    top = routes.shape[1]
    latent_width = down_weight.shape[1]
    n_major = lax.axis_size("expert")
    n_minor = lax.axis_size("dp")
    n_experts = n_major * n_minor
    capacity = 3 * tok_rows * top // (2 * n_experts)
    entries = tok_rows * top
    contract_last = (((1,), (1,)), ((), ()))
    contract_first = (((0,), (0,)), ((), ()))
    full_down = lax.all_gather(down_weight, ("expert", "dp"), axis=0, tiled=True)
    latent = jnp.dot(tokens, full_down, preferred_element_type=jnp.float32)
    latent = latent.astype(jnp.bfloat16)
    dest = slot_table(routes, capacity)
    source = (
        jnp.full((n_experts * capacity,), entries, jnp.int32)
        .at[dest]
        .set(jnp.arange(entries, dtype=jnp.int32))
    )
    token_of = jnp.where(source < entries, source // top, tok_rows)
    gates = gate_levels.astype(jnp.float32) * gate_unit
    zero_row = jnp.zeros((1, latent_width), jnp.bfloat16)
    latent_pad = jnp.concatenate([latent, zero_row], axis=0)
    send_latent = latent_pad[token_of].reshape(n_major, n_minor, capacity, latent_width)
    scaled = (gates[:, :, None] * latent_grad.astype(jnp.float32)[:, None, :]).astype(jnp.bfloat16)
    scaled_pad = jnp.concatenate([scaled.reshape(entries, latent_width), zero_row], axis=0)
    send_grad = scaled_pad[source].reshape(n_major, n_minor, capacity, latent_width)
    arrived = lax.all_to_all(
        lax.all_to_all(send_latent, "expert", split_axis=0, concat_axis=0, tiled=True),
        "dp",
        split_axis=1,
        concat_axis=1,
        tiled=True,
    )
    rows = arrived.reshape(-1, latent_width)
    weight_in = expert_in[0]
    weight_out = expert_out[0]
    before = jnp.dot(rows, weight_in, preferred_element_type=jnp.float32)
    active = jnp.maximum(before, 0.0)
    hidden = (active * active).astype(jnp.bfloat16)
    result = jnp.dot(hidden, weight_out, preferred_element_type=jnp.float32).astype(jnp.bfloat16)
    returned = lax.all_to_all(
        lax.all_to_all(
            result.reshape(n_major, n_minor, capacity, latent_width),
            "expert",
            split_axis=0,
            concat_axis=0,
            tiled=True,
        ),
        "dp",
        split_axis=1,
        concat_axis=1,
        tiled=True,
    )
    picked = returned.reshape(n_experts * capacity, latent_width)[dest].astype(jnp.float32)
    picked = picked.reshape(tok_rows, top, latent_width)
    latent_out = jnp.sum(gates[:, :, None] * picked, axis=1).astype(jnp.bfloat16)
    arrived_grad = lax.all_to_all(
        lax.all_to_all(send_grad, "expert", split_axis=0, concat_axis=0, tiled=True),
        "dp",
        split_axis=1,
        concat_axis=1,
        tiled=True,
    )
    grad_rows = arrived_grad.reshape(-1, latent_width)
    back_hidden = lax.dot_general(
        grad_rows, weight_out, contract_last, preferred_element_type=jnp.float32
    )
    back_pre = (back_hidden * 2.0 * active).astype(jnp.bfloat16)
    grad_out = lax.dot_general(
        hidden, grad_rows, contract_first, preferred_element_type=jnp.float32
    ).astype(jnp.bfloat16)
    grad_in = lax.dot_general(
        rows, back_pre, contract_first, preferred_element_type=jnp.float32
    ).astype(jnp.bfloat16)
    back_rows = lax.dot_general(
        back_pre, weight_in, contract_last, preferred_element_type=jnp.float32
    ).astype(jnp.bfloat16)
    came_back = lax.all_to_all(
        lax.all_to_all(
            back_rows.reshape(n_major, n_minor, capacity, latent_width),
            "expert",
            split_axis=0,
            concat_axis=0,
            tiled=True,
        ),
        "dp",
        split_axis=1,
        concat_axis=1,
        tiled=True,
    )
    gathered_back = came_back.reshape(n_experts * capacity, latent_width)[dest].astype(jnp.float32)
    latent_delta = jnp.sum(gathered_back.reshape(tok_rows, top, latent_width), axis=1).astype(
        jnp.bfloat16
    )
    grad_tokens = lax.dot_general(
        latent_delta, full_down, contract_last, preferred_element_type=jnp.float32
    )
    grad_tokens = grad_tokens.astype(jnp.bfloat16)
    grad_down = lax.psum_scatter(
        lax.dot_general(tokens, latent_delta, contract_first, preferred_element_type=jnp.float32),
        ("expert", "dp"),
        scatter_dimension=0,
        tiled=True,
    )
    return (latent_out, grad_tokens, grad_down, grad_in[None], grad_out[None])


def on_device(tokens, routes, *others):
    n_major = lax.axis_size("expert")
    n_experts = n_major * lax.axis_size("dp")
    few = n_experts <= 2 * routes.shape[1] and n_major % 2 == 0 and n_major >= 6 and lax.axis_size("dp") == 2
    return (all_rows if few else routed_rows)(tokens, routes, *others)


def solution(mesh):
    in_specs = (
        P(("group", "expert", "dp"), None),
        P(("group", "expert", "dp"), None),
        P(("group", "expert", "dp"), None),
        P(("group", "expert", "dp"), None),
        P(("expert", "dp"), None),
        P(("expert", "dp"), None, None),
        P(("expert", "dp"), None, None),
    )
    out_specs = (
        P(("group", "expert", "dp"), None),
        P(("group", "expert", "dp"), None),
        P(("group", "expert", "dp"), None),
        P(("group", "expert", "dp"), None, None),
        P(("group", "expert", "dp"), None, None),
    )
    return jax.shard_map(
        on_device, mesh=mesh, in_specs=in_specs, out_specs=out_specs, check_vma=False
    )
```

```python
import functools

import jax
import jax.numpy as jnp
from jax import lax
from jax.experimental import pallas as pl
from jax.experimental.pallas import tpu as pltpu
from jax.sharding import PartitionSpec as P

gate_unit = 1.0 / 1024.0
contract_last = (((1,), (1,)), ((), ()))
contract_first = (((0,), (0,)), ((), ()))
plane = ("expert", "dp")
wide = jnp.float32
narrow = jnp.bfloat16


def device_pairs(n_line, move):
    pairs = []
    for z in range(n_line):
        for x in range(2):
            for c in range(2):
                to_z, to_x, to_c = move(z, x, c)
                pairs.append(((z * 2 + x) * 2 + c, (to_z * 2 + to_x) * 2 + to_c))
    return pairs


def turn(value, n_line, by):
    return lax.ppermute(value, plane, device_pairs(n_line, lambda z, x, c: ((z + by) % n_line, x, c)))


def swap(value, n_line, core, side):
    return lax.ppermute(value, plane, device_pairs(n_line, lambda z, x, c: (z, x ^ side, c ^ core)))


def after(value, *earlier):
    return lax.optimization_barrier((value,) + earlier)[0]


def call(body, outs, name, scratch=(), outside=0):
    vmem = pl.BlockSpec(memory_space=pltpu.VMEM)
    anywhere = pl.BlockSpec(memory_space=pl.ANY)

    def run(place, *operands):
        return pl.pallas_call(
            body,
            out_shape=outs,
            in_specs=[pl.BlockSpec(memory_space=pltpu.SMEM)]
            + [anywhere] * outside
            + [vmem] * (len(operands) - outside),
            out_specs=[vmem] * len(outs),
            scratch_shapes=list(scratch),
            compiler_params=pltpu.CompilerParams(vmem_limit_bytes=40 * 1024 * 1024),
            cost_estimate=pl.CostEstimate(flops=0, bytes_accessed=0, transcendentals=0),
            name=name,
        )(place, *operands)

    return run


def columns_body(n_line, block, place, tokens, *refs):
    own, other, across, sems = refs
    pieces = (own, across.at[0], other, across.at[1])
    copies = []
    for core in range(2):
        for side in range(2):
            owner = (place[1] ^ side) * 2 + (place[2] ^ core)
            for z in range(n_line):
                start = pl.multiple_of((z * 4 + owner) * block, block)
                piece = pieces[core * 2 + side].at[:, pl.ds(z * block, block)]
                copies.append(
                    pltpu.make_async_copy(tokens.at[:, pl.ds(start, block)], piece, sems.at[len(copies)])
                )
    for copy in copies:
        copy.start()
    for copy in copies:
        copy.wait()


def payload_body(place, routes, levels, cotangent, payload):
    tok_rows = cotangent.shape[0]
    gate_rows = payload.shape[0] - tok_rows
    payload[:tok_rows, :] = cotangent[...]
    expert = lax.broadcasted_iota(jnp.int32, (gate_rows, tok_rows), 0)
    total = jnp.zeros((gate_rows, tok_rows), jnp.int32)
    for k in range(routes.shape[0]):
        total = total + jnp.where(expert == routes[k : k + 1, :], levels[k : k + 1, :], 0)
    low = total & 31
    payload[tok_rows:, :tok_rows] = (total - low).astype(wide).astype(narrow)
    payload[tok_rows:, tok_rows : 2 * tok_rows] = low.astype(wide).astype(narrow)
    rest = payload.shape[1] - 2 * tok_rows
    payload[tok_rows:, 2 * tok_rows :] = jnp.zeros((gate_rows, rest), narrow)


def project_body(n_line, place, *refs):
    pieces, downs = refs[:4], refs[4 : 4 + n_line]
    keep, send, down = refs[4 + n_line :]
    block = downs[0].shape[0]
    for back in range(n_line):
        z = lax.rem(place[0] + n_line - back, n_line)
        down[pl.ds(pl.multiple_of(z * block, block), block), :] = downs[back][...]
    for core, out in ((1, send), (0, keep)):
        for side in range(2):
            out[side] = jnp.dot(pieces[core * 2 + side][...], down[...], preferred_element_type=wide)


def gate_tile(payload, tok_rows, expert):
    packed = payload[tok_rows:, :]
    rows = lax.broadcasted_iota(jnp.int32, (packed.shape[0], 128), 0)
    pick = jnp.where(rows == expert, 1.0, 0.0).astype(narrow)
    dot = functools.partial(lax.dot_general, dimension_numbers=contract_first, preferred_element_type=wide)
    total = dot(packed[:, :tok_rows], pick) + dot(packed[:, tok_rows : 2 * tok_rows], pick)
    return total * gate_unit


def expert_body(count, place, *refs):
    rows_in, payloads = refs[:count], refs[count : 2 * count]
    own, core, *sides = refs[2 * count : 2 * count + 6]
    weights = (own.at[0], own.at[1], sides[0], sides[1], core.at[0], core.at[1], sides[2], sides[3])
    outs = refs[2 * count + 6 :]
    *sums, hiddens, scaleds, back_pres = outs
    tok_rows, width = rows_in[0].shape
    for first in range(0, count, 2):
        group = range(first, min(first + 2, count))
        span = slice(first * tok_rows, (first + len(group)) * tok_rows)
        stack = lambda values: jnp.concatenate(list(values), axis=0)
        rows = stack(rows_in[i][...] for i in group)
        cotangent = stack(payloads[i][:tok_rows, :] for i in group).astype(wide)
        out_sum = jnp.zeros(rows.shape, wide)
        delta_sum = jnp.zeros(rows.shape, wide)
        for e in range(4):
            weight_in, weight_out = weights[2 * e], weights[2 * e + 1]
            gate = stack(gate_tile(payloads[i], tok_rows, place[3 + e]) for i in group)
            gate = jnp.concatenate([gate] * (width // 128), axis=1)
            active = jnp.maximum(jnp.dot(rows, weight_in[...], preferred_element_type=wide), 0.0)
            hidden = (active * active).astype(narrow)
            hiddens[e, span, :] = hidden
            scaled = (gate * cotangent).astype(narrow)
            scaleds[e, span, :] = scaled
            back_hidden = lax.dot_general(scaled, weight_out[...], contract_last, preferred_element_type=wide)
            back_pre = (back_hidden * 2.0 * active).astype(narrow)
            back_pres[e, span, :] = back_pre
            result = jnp.dot(hidden, weight_out[...], preferred_element_type=wide).astype(narrow)
            out_sum = out_sum + gate * result.astype(wide)
            back_rows = lax.dot_general(back_pre, weight_in[...], contract_last, preferred_element_type=wide)
            delta_sum = delta_sum + back_rows.astype(narrow).astype(wide)
        for i in group:
            part = slice((i - first) * tok_rows, (i - first + 1) * tok_rows)
            out = sums.pop(0)
            delta_out, sum_out = (out, sums.pop(0)) if len(out.shape) == 2 else (out.at[0], out.at[1])
            delta_out[...] = delta_sum[part].astype(out.dtype)
            sum_out[...] = out_sum[part].astype(out.dtype)


def weight_grad_body(n_rows, n_sets, place, *refs):
    rows_in = refs[:n_rows]
    sets = [refs[n_rows + 3 * i : n_rows + 3 * i + 3] for i in range(n_sets)]
    near, far, other = refs[n_rows + 3 * n_sets :]
    dot = functools.partial(lax.dot_general, dimension_numbers=contract_first, preferred_element_type=wide)
    rows = jnp.concatenate([r[...] for r in rows_in], axis=0)
    for core in (1, 0):
        for side in (1, 0):
            hidden, scaled, back_pre = (
                jnp.concatenate([values[i][core * 2 + side] for values in sets], axis=0) for i in range(3)
            )
            grad_in, grad_out = dot(rows, back_pre), dot(hidden, scaled)
            if core:
                other[2 * side] = grad_in.astype(narrow)
                other[2 * side + 1] = grad_out.astype(narrow)
            else:
                own = far if side else near
                own[0], own[1] = grad_in, grad_out


def down_grad_body(n_line, place, *refs):
    pieces, deltas, core_deltas, blocks = refs[:4], refs[4:6], refs[6], refs[7:]
    tokens = jnp.concatenate([p[...] for p in pieces], axis=0)
    delta = jnp.concatenate([d[...] for d in deltas] + [core_deltas[0], core_deltas[1]], axis=0)
    part = lax.dot_general(tokens, delta, contract_first, preferred_element_type=wide)
    block = blocks[0].shape[0]
    for z in range(n_line):
        for back in range(n_line):

            @pl.when(lax.rem(place[0] + n_line - back, n_line) == z)
            def _(z=z, back=back):
                blocks[back][...] = part[z * block : (z + 1) * block].astype(blocks[back].dtype)


def token_grad_body(n_line, block, place, delta, downs, core_downs, out):
    for i, weight in enumerate((downs.at[0], downs.at[1], core_downs.at[0], core_downs.at[1])):
        owner = (place[1] ^ (i % 2)) * 2 + (place[2] ^ (i // 2))
        part = lax.dot_general(delta[...], weight[...], contract_last, preferred_element_type=wide)
        part = part.astype(narrow)
        for z in range(n_line):
            start = pl.multiple_of((z * 4 + owner) * block, block)
            out[:, pl.ds(start, block)] = part[:, z * block : (z + 1) * block]


def all_rows(tokens, routes, gate_levels, latent_grad, down_weight, expert_in, expert_out):
    tok_rows, width = tokens.shape
    latent_width = down_weight.shape[1]
    hidden_width = expert_in.shape[2]
    n_major = lax.axis_size("expert")
    n_line = n_major // 2
    n_experts = n_major * 2
    block = width // n_experts
    major = lax.axis_index("expert")
    my_core = lax.axis_index("dp")
    place = jnp.stack(
        [major // 2, major % 2, my_core]
        + [(major ^ side) * 2 + (my_core ^ core) for core in range(2) for side in range(2)]
    ).astype(jnp.int32)
    shape = jax.ShapeDtypeStruct
    rows_of = lambda kind: shape((tok_rows, latent_width), kind)

    downs = [down_weight] + [turn(down_weight, n_line, back) for back in range(1, n_line)]

    gate_rows = -(-n_experts // 16) * 16
    columns = call(
        functools.partial(columns_body, n_line, block),
        [shape((tok_rows, n_line * block), narrow)] * 2 + [shape((2, tok_rows, n_line * block), narrow)],
        "columns",
        scratch=[pltpu.SemaphoreType.DMA((4 * n_line,))],
        outside=1,
    )(place, tokens)
    (payload,) = call(payload_body, [shape((tok_rows + gate_rows, latent_width), narrow)], "payload")(
        place, routes.T, gate_levels.T, latent_grad
    )
    own = jnp.concatenate([expert_in, expert_out])
    core_own = swap(own, n_line, 1, 0)
    across = swap(columns[2], n_line, 0, 1)
    near_tokens = [columns[0], across[0], swap(after(columns[1], across, core_own), n_line, 1, 0), swap(across[1], n_line, 1, 0)]
    side_in = swap(after(expert_in[0], near_tokens[2]), n_line, 0, 1)

    project = call(
        functools.partial(project_body, n_line),
        [shape((2, tok_rows, latent_width), wide)] * 2 + [shape((n_line * block, latent_width), narrow)],
        "project",
    )
    keep, send, down = project(place, *near_tokens, *downs)
    half = keep + swap(send, n_line, 1, 0)
    payloads = [payload] + [turn(after(payload, *downs[1:]), n_line, back) for back in range(1, n_line)]
    crossed = swap(half[1].astype(narrow), n_line, 0, 1).astype(wide)
    latent = (half[0] + after(crossed, side_in, *payloads[1:])).astype(narrow)
    middle = list(range(2, n_line - 1))
    groups = [[1] + middle, [n_line - 1, 0]]
    rows = [latent] + [turn(latent, n_line, back) for back in range(1, n_line)]

    side_out = swap(after(expert_out[0], latent), n_line, 0, 1)
    core_in = swap(after(side_in, latent), n_line, 1, 0)
    core_out = swap(after(side_out, *rows[1:]), n_line, 1, 0)
    weights = [own, core_own, side_in, side_out, core_in, core_out]
    side_down = swap(after(down, side_out), n_line, 0, 1)
    both_down = jnp.stack([down, side_down])
    core_down = swap(both_down, n_line, 1, 0)

    sums, saved = [None] * n_line, []
    done = latent
    for group in groups:
        count = len(group)
        outs = []
        for back in group:
            kind = narrow if back else wide
            outs += [rows_of(kind)] * 2 if back in middle else [shape((2, tok_rows, latent_width), kind)]
        values = call(
            functools.partial(expert_body, count),
            outs + [shape((4, count * tok_rows, hidden_width), narrow)] * 3,
            "experts",
        )(after(place, done), *(rows[i] for i in group), *(payloads[i] for i in group), *weights)
        done, saved = values[0], saved + [list(values[-3:])]
        values = list(values[:-3])
        for back in group:
            sums[back] = [values.pop(0) for _ in range(2 if back in middle else 1)]

    lines = [
        [turn(value, n_line, n_line - back) if back else value for value in values]
        for back, values in enumerate(sums)
    ]
    delta_lines = [values[0] if len(values) == 2 else values[0][0] for values in lines]
    out_lines = [values[1] if len(values) == 2 else values[0][1] for values in lines]

    pair = (2, latent_width, hidden_width)
    near, far, other = call(
        functools.partial(weight_grad_body, n_line, len(groups)),
        [shape(pair, wide)] * 2 + [shape((4, latent_width, hidden_width), narrow)],
        "weight_grads",
    )(
        after(place, delta_lines[1]),
        *(rows[i] for group in groups for i in group),
        *(value for values in saved for value in values),
    )
    delta_lines = [after(line, near, both_down) for line in delta_lines]
    delta = sum(line.astype(wide) for line in delta_lines).astype(narrow)
    side_delta = swap(delta, n_line, 0, 1)
    latent_out = sum(line.astype(wide) for line in out_lines).astype(narrow)
    other = swap(after(other, delta), n_line, 1, 0)
    far = (far + other[2:].astype(wide)).astype(narrow)
    far = swap(after(far, side_delta, *(out_lines[back] for back in middle)), n_line, 0, 1)
    core_deltas = swap(jnp.stack([delta, after(side_delta, *(out_lines[back] for back in middle))]), n_line, 1, 0)
    blocks = call(
        functools.partial(down_grad_body, n_line),
        [shape((block, latent_width), wide)] + [shape((block, latent_width), narrow)] * (n_line - 1),
        "down_grad",
    )(after(place, *(out_lines[back] for back in middle)), *near_tokens, delta, side_delta, core_deltas)
    weight_grad = (near + other[:2].astype(wide) + far.astype(wide)).astype(narrow)
    (grad_tokens,) = call(
        functools.partial(token_grad_body, n_line, block), [shape((tok_rows, width), narrow)], "token_grad"
    )(place, after(delta, blocks[1]), both_down, core_down)
    blocks = [blocks[0]] + [turn(blocks[back], n_line, n_line - back) for back in range(1, n_line)]
    grad_down = sum(value.astype(wide) for value in blocks)
    return (latent_out, grad_tokens, grad_down, weight_grad[:1], weight_grad[1:])


def slot_table(routes, capacity):
    flat = routes.reshape(-1)
    count = flat.shape[0]
    order = jnp.arange(count, dtype=jnp.int32)
    same = (flat[:, None] == flat[None, :]) & (order[None, :] < order[:, None])
    placed = jnp.sum(jnp.where(same, 1, 0), axis=1).astype(jnp.int32)
    return flat * capacity + placed


def routed_rows(tokens, routes, gate_levels, latent_grad, down_weight, expert_in, expert_out):
    tok_rows = tokens.shape[0]
    top = routes.shape[1]
    latent_width = down_weight.shape[1]
    n_major = lax.axis_size("expert")
    n_minor = lax.axis_size("dp")
    n_experts = n_major * n_minor
    capacity = 3 * tok_rows * top // (2 * n_experts)
    entries = tok_rows * top
    contract_last = (((1,), (1,)), ((), ()))
    contract_first = (((0,), (0,)), ((), ()))
    full_down = lax.all_gather(down_weight, ("expert", "dp"), axis=0, tiled=True)
    latent = jnp.dot(tokens, full_down, preferred_element_type=jnp.float32)
    latent = latent.astype(jnp.bfloat16)
    dest = slot_table(routes, capacity)
    source = (
        jnp.full((n_experts * capacity,), entries, jnp.int32)
        .at[dest]
        .set(jnp.arange(entries, dtype=jnp.int32))
    )
    token_of = jnp.where(source < entries, source // top, tok_rows)
    gates = gate_levels.astype(jnp.float32) * gate_unit
    zero_row = jnp.zeros((1, latent_width), jnp.bfloat16)
    latent_pad = jnp.concatenate([latent, zero_row], axis=0)
    send_latent = latent_pad[token_of].reshape(n_major, n_minor, capacity, latent_width)
    scaled = (gates[:, :, None] * latent_grad.astype(jnp.float32)[:, None, :]).astype(jnp.bfloat16)
    scaled_pad = jnp.concatenate([scaled.reshape(entries, latent_width), zero_row], axis=0)
    send_grad = scaled_pad[source].reshape(n_major, n_minor, capacity, latent_width)
    arrived = lax.all_to_all(
        lax.all_to_all(send_latent, "expert", split_axis=0, concat_axis=0, tiled=True),
        "dp",
        split_axis=1,
        concat_axis=1,
        tiled=True,
    )
    rows = arrived.reshape(-1, latent_width)
    weight_in = expert_in[0]
    weight_out = expert_out[0]
    before = jnp.dot(rows, weight_in, preferred_element_type=jnp.float32)
    active = jnp.maximum(before, 0.0)
    hidden = (active * active).astype(jnp.bfloat16)
    result = jnp.dot(hidden, weight_out, preferred_element_type=jnp.float32).astype(jnp.bfloat16)
    returned = lax.all_to_all(
        lax.all_to_all(
            result.reshape(n_major, n_minor, capacity, latent_width),
            "expert",
            split_axis=0,
            concat_axis=0,
            tiled=True,
        ),
        "dp",
        split_axis=1,
        concat_axis=1,
        tiled=True,
    )
    picked = returned.reshape(n_experts * capacity, latent_width)[dest].astype(jnp.float32)
    picked = picked.reshape(tok_rows, top, latent_width)
    latent_out = jnp.sum(gates[:, :, None] * picked, axis=1).astype(jnp.bfloat16)
    arrived_grad = lax.all_to_all(
        lax.all_to_all(send_grad, "expert", split_axis=0, concat_axis=0, tiled=True),
        "dp",
        split_axis=1,
        concat_axis=1,
        tiled=True,
    )
    grad_rows = arrived_grad.reshape(-1, latent_width)
    back_hidden = lax.dot_general(
        grad_rows, weight_out, contract_last, preferred_element_type=jnp.float32
    )
    back_pre = (back_hidden * 2.0 * active).astype(jnp.bfloat16)
    grad_out = lax.dot_general(
        hidden, grad_rows, contract_first, preferred_element_type=jnp.float32
    ).astype(jnp.bfloat16)
    grad_in = lax.dot_general(
        rows, back_pre, contract_first, preferred_element_type=jnp.float32
    ).astype(jnp.bfloat16)
    back_rows = lax.dot_general(
        back_pre, weight_in, contract_last, preferred_element_type=jnp.float32
    ).astype(jnp.bfloat16)
    came_back = lax.all_to_all(
        lax.all_to_all(
            back_rows.reshape(n_major, n_minor, capacity, latent_width),
            "expert",
            split_axis=0,
            concat_axis=0,
            tiled=True,
        ),
        "dp",
        split_axis=1,
        concat_axis=1,
        tiled=True,
    )
    gathered_back = came_back.reshape(n_experts * capacity, latent_width)[dest].astype(jnp.float32)
    latent_delta = jnp.sum(gathered_back.reshape(tok_rows, top, latent_width), axis=1).astype(
        jnp.bfloat16
    )
    grad_tokens = lax.dot_general(
        latent_delta, full_down, contract_last, preferred_element_type=jnp.float32
    )
    grad_tokens = grad_tokens.astype(jnp.bfloat16)
    grad_down = lax.psum_scatter(
        lax.dot_general(tokens, latent_delta, contract_first, preferred_element_type=jnp.float32),
        ("expert", "dp"),
        scatter_dimension=0,
        tiled=True,
    )
    return (latent_out, grad_tokens, grad_down, grad_in[None], grad_out[None])


def on_device(tokens, routes, *others):
    n_major = lax.axis_size("expert")
    n_experts = n_major * lax.axis_size("dp")
    few = n_experts <= 2 * routes.shape[1] and n_major % 2 == 0 and n_major >= 6 and lax.axis_size("dp") == 2
    return (all_rows if few else routed_rows)(tokens, routes, *others)


def solution(mesh):
    in_specs = (
        P(("group", "expert", "dp"), None),
        P(("group", "expert", "dp"), None),
        P(("group", "expert", "dp"), None),
        P(("group", "expert", "dp"), None),
        P(("expert", "dp"), None),
        P(("expert", "dp"), None, None),
        P(("expert", "dp"), None, None),
    )
    out_specs = (
        P(("group", "expert", "dp"), None),
        P(("group", "expert", "dp"), None),
        P(("group", "expert", "dp"), None),
        P(("group", "expert", "dp"), None, None),
        P(("group", "expert", "dp"), None, None),
    )
    return jax.shard_map(
        on_device, mesh=mesh, in_specs=in_specs, out_specs=out_specs, check_vma=False
    )
```

```python
import functools

import jax
import jax.numpy as jnp
from jax import lax
from jax.experimental import pallas as pl
from jax.experimental.pallas import tpu as pltpu
from jax.sharding import PartitionSpec as P

gate_unit = 1.0 / 1024.0
contract_last = (((1,), (1,)), ((), ()))
contract_first = (((0,), (0,)), ((), ()))
plane = ("expert", "dp")
wide = jnp.float32
narrow = jnp.bfloat16


def device_pairs(n_line, move):
    pairs = []
    for z in range(n_line):
        for x in range(2):
            for c in range(2):
                to_z, to_x, to_c = move(z, x, c)
                pairs.append(((z * 2 + x) * 2 + c, (to_z * 2 + to_x) * 2 + to_c))
    return pairs


def turn(value, n_line, by):
    return lax.ppermute(value, plane, device_pairs(n_line, lambda z, x, c: ((z + by) % n_line, x, c)))


def swap(value, n_line, core, side):
    return lax.ppermute(value, plane, device_pairs(n_line, lambda z, x, c: (z, x ^ side, c ^ core)))


def after(value, *earlier):
    return lax.optimization_barrier((value,) + earlier)[0]


def call(body, outs, name, scratch=(), outside=0):
    vmem = pl.BlockSpec(memory_space=pltpu.VMEM)
    anywhere = pl.BlockSpec(memory_space=pl.ANY)

    def run(place, *operands):
        return pl.pallas_call(
            body,
            out_shape=outs,
            in_specs=[pl.BlockSpec(memory_space=pltpu.SMEM)]
            + [anywhere] * outside
            + [vmem] * (len(operands) - outside),
            out_specs=[vmem] * len(outs),
            scratch_shapes=list(scratch),
            compiler_params=pltpu.CompilerParams(vmem_limit_bytes=40 * 1024 * 1024),
            cost_estimate=pl.CostEstimate(flops=0, bytes_accessed=0, transcendentals=0),
            name=name,
        )(place, *operands)

    return run


def columns_body(n_line, block, place, tokens, expert_in, expert_out, *refs):
    own, other, across, weights, sems = refs
    pieces = (own, across.at[0], other, across.at[1])
    copies = []
    for i, weight in enumerate((expert_in, expert_out)):
        copies.append(pltpu.make_async_copy(weight, weights.at[pl.ds(i, 1)], sems.at[i]))
    for core in range(2):
        for side in range(2):
            owner = (place[1] ^ side) * 2 + (place[2] ^ core)
            for z in range(n_line):
                start = pl.multiple_of((z * 4 + owner) * block, block)
                piece = pieces[core * 2 + side].at[:, pl.ds(z * block, block)]
                copies.append(
                    pltpu.make_async_copy(tokens.at[:, pl.ds(start, block)], piece, sems.at[len(copies)])
                )
    for copy in copies:
        copy.start()
    for copy in copies:
        copy.wait()


def payload_body(place, routes, levels, cotangent, payload):
    tok_rows = cotangent.shape[0]
    gate_rows = payload.shape[0] - tok_rows
    payload[:tok_rows, :] = cotangent[...]
    expert = lax.broadcasted_iota(jnp.int32, (gate_rows, tok_rows), 0)
    total = jnp.zeros((gate_rows, tok_rows), jnp.int32)
    for k in range(routes.shape[0]):
        total = total + jnp.where(expert == routes[k : k + 1, :], levels[k : k + 1, :], 0)
    low = total & 31
    payload[tok_rows:, :tok_rows] = (total - low).astype(wide).astype(narrow)
    payload[tok_rows:, tok_rows : 2 * tok_rows] = low.astype(wide).astype(narrow)
    rest = payload.shape[1] - 2 * tok_rows
    payload[tok_rows:, 2 * tok_rows :] = jnp.zeros((gate_rows, rest), narrow)


def project_body(n_line, place, *refs):
    own, across, core, core_across, *downs = refs[: 4 + n_line]
    pieces = (own, across.at[0], core, core_across)
    keep, send, down = refs[4 + n_line :]
    block = downs[0].shape[0]
    for back in range(n_line):
        z = lax.rem(place[0] + n_line - back, n_line)
        down[pl.ds(pl.multiple_of(z * block, block), block), :] = downs[back][...]
    for core, out in ((1, send), (0, keep)):
        for side in range(2):
            out[side] = jnp.dot(pieces[core * 2 + side][...], down[...], preferred_element_type=wide)


def gate_tile(payload, tok_rows, expert):
    packed = payload[tok_rows:, :]
    rows = lax.broadcasted_iota(jnp.int32, (packed.shape[0], 128), 0)
    pick = jnp.where(rows == expert, 1.0, 0.0).astype(narrow)
    dot = functools.partial(lax.dot_general, dimension_numbers=contract_first, preferred_element_type=wide)
    total = dot(packed[:, :tok_rows], pick) + dot(packed[:, tok_rows : 2 * tok_rows], pick)
    return total * gate_unit


def expert_body(count, place, *refs):
    rows_in, payloads = refs[:count], refs[count : 2 * count]
    own, core, *sides = refs[2 * count : 2 * count + 6]
    weights = (own.at[0], own.at[1], sides[0], sides[1], core.at[0], core.at[1], sides[2], sides[3])
    outs = refs[2 * count + 6 :]
    *sums, hiddens, scaleds, back_pres = outs
    tok_rows, width = rows_in[0].shape
    for first in range(0, count, 2):
        group = range(first, min(first + 2, count))
        span = slice(first * tok_rows, (first + len(group)) * tok_rows)
        stack = lambda values: jnp.concatenate(list(values), axis=0)
        rows = stack(rows_in[i][...] for i in group)
        cotangent = stack(payloads[i][:tok_rows, :] for i in group).astype(wide)
        out_sum = jnp.zeros(rows.shape, wide)
        delta_sum = jnp.zeros(rows.shape, wide)
        for e in range(4):
            weight_in, weight_out = weights[2 * e], weights[2 * e + 1]
            gate = stack(gate_tile(payloads[i], tok_rows, place[3 + e]) for i in group)
            gate = jnp.concatenate([gate] * (width // 128), axis=1)
            active = jnp.maximum(jnp.dot(rows, weight_in[...], preferred_element_type=wide), 0.0)
            hidden = (active * active).astype(narrow)
            hiddens[e, span, :] = hidden
            scaled = (gate * cotangent).astype(narrow)
            scaleds[e, span, :] = scaled
            back_hidden = lax.dot_general(scaled, weight_out[...], contract_last, preferred_element_type=wide)
            back_pre = (back_hidden * 2.0 * active).astype(narrow)
            back_pres[e, span, :] = back_pre
            result = jnp.dot(hidden, weight_out[...], preferred_element_type=wide).astype(narrow)
            out_sum = out_sum + gate * result.astype(wide)
            back_rows = lax.dot_general(back_pre, weight_in[...], contract_last, preferred_element_type=wide)
            delta_sum = delta_sum + back_rows.astype(narrow).astype(wide)
        for i in group:
            part = slice((i - first) * tok_rows, (i - first + 1) * tok_rows)
            out = sums.pop(0)
            out[...] = delta_sum[part].astype(out.dtype)
            out = sums.pop(0)
            out[...] = out_sum[part].astype(out.dtype)


def weight_grad_body(n_rows, n_sets, place, *refs):
    rows_in = refs[:n_rows]
    sets = [refs[n_rows + 3 * i : n_rows + 3 * i + 3] for i in range(n_sets)]
    near, far, other = refs[n_rows + 3 * n_sets :]
    dot = functools.partial(lax.dot_general, dimension_numbers=contract_first, preferred_element_type=wide)
    rows = jnp.concatenate([r[...] for r in rows_in], axis=0)
    for core in (1, 0):
        for side in (1, 0):
            hidden, scaled, back_pre = (
                jnp.concatenate([values[i][core * 2 + side] for values in sets], axis=0) for i in range(3)
            )
            grad_in, grad_out = dot(rows, back_pre), dot(hidden, scaled)
            if core:
                other[2 * side] = grad_in.astype(narrow)
                other[2 * side + 1] = grad_out.astype(narrow)
            else:
                own = far if side else near
                own[0], own[1] = grad_in, grad_out


def down_grad_body(n_line, place, *refs):
    own, across, core, core_across, *deltas, core_deltas = refs[:7]
    blocks = refs[7:]
    tokens = jnp.concatenate([own[...], across[0], core[...], core_across[...]], axis=0)
    delta = jnp.concatenate([d[...] for d in deltas] + [core_deltas[0], core_deltas[1]], axis=0)
    part = lax.dot_general(tokens, delta, contract_first, preferred_element_type=wide)
    block = blocks[0].shape[0]
    for z in range(n_line):
        for back in range(n_line):

            @pl.when(lax.rem(place[0] + n_line - back, n_line) == z)
            def _(z=z, back=back):
                blocks[back][...] = part[z * block : (z + 1) * block].astype(blocks[back].dtype)


def token_grad_body(n_line, block, place, delta, downs, core_downs, out):
    for i, weight in enumerate((downs.at[0], downs.at[1], core_downs.at[0], core_downs.at[1])):
        owner = (place[1] ^ (i % 2)) * 2 + (place[2] ^ (i // 2))
        part = lax.dot_general(delta[...], weight[...], contract_last, preferred_element_type=wide)
        part = part.astype(narrow)
        for z in range(n_line):
            start = pl.multiple_of((z * 4 + owner) * block, block)
            out[:, pl.ds(start, block)] = part[:, z * block : (z + 1) * block]


def all_rows(tokens, routes, gate_levels, latent_grad, down_weight, expert_in, expert_out):
    tok_rows, width = tokens.shape
    latent_width = down_weight.shape[1]
    hidden_width = expert_in.shape[2]
    n_major = lax.axis_size("expert")
    n_line = n_major // 2
    n_experts = n_major * 2
    block = width // n_experts
    major = lax.axis_index("expert")
    my_core = lax.axis_index("dp")
    place = jnp.stack(
        [major // 2, major % 2, my_core]
        + [(major ^ side) * 2 + (my_core ^ core) for core in range(2) for side in range(2)]
    ).astype(jnp.int32)
    shape = jax.ShapeDtypeStruct
    rows_of = lambda kind: shape((tok_rows, latent_width), kind)

    downs = [down_weight] + [turn(down_weight, n_line, back) for back in range(1, n_line)]

    gate_rows = -(-n_experts // 16) * 16
    columns = call(
        functools.partial(columns_body, n_line, block),
        [shape((tok_rows, n_line * block), narrow)] * 2
        + [shape((2, tok_rows, n_line * block), narrow), shape((2, latent_width, hidden_width), narrow)],
        "columns",
        scratch=[pltpu.SemaphoreType.DMA((4 * n_line + 2,))],
        outside=3,
    )(place, tokens, expert_in, expert_out)
    (payload,) = call(payload_body, [shape((tok_rows + gate_rows, latent_width), narrow)], "payload")(
        place, routes.T, gate_levels.T, latent_grad
    )
    own = columns[3]
    core_own = swap(own, n_line, 1, 0)
    across = swap(columns[2], n_line, 0, 1)
    core_tokens = [swap(after(columns[1], across, core_own), n_line, 1, 0), swap(across[1], n_line, 1, 0)]
    side_in = swap(after(expert_in[0], across), n_line, 0, 1)

    project = call(
        functools.partial(project_body, n_line),
        [shape((2, tok_rows, latent_width), wide)] * 2 + [shape((n_line * block, latent_width), narrow)],
        "project",
    )
    keep, send, down = project(after(place, payload), columns[0], across, *core_tokens, *downs)
    half = keep + swap(send, n_line, 1, 0)
    payloads = [payload] + [turn(after(payload, *downs[1:]), n_line, back) for back in range(1, n_line)]
    crossed = swap(half[1].astype(narrow), n_line, 0, 1).astype(wide)
    latent = (half[0] + after(crossed, side_in, *payloads[1:])).astype(narrow)
    middle = list(range(2, n_line - 1))
    groups = [[1] + middle, [n_line - 1, 0]]
    rows = [latent] + [turn(latent, n_line, back) for back in range(1, n_line)]

    side_out = swap(after(expert_out[0], latent), n_line, 0, 1)
    core_in = swap(after(side_in, latent), n_line, 1, 0)
    core_out = swap(after(side_out, *rows[1:]), n_line, 1, 0)
    weights = [own, core_own, side_in, side_out, core_in, core_out]
    side_down = swap(after(down, *rows[1:]), n_line, 0, 1)

    both_down = jnp.stack([down, side_down])
    deltas_of, outs_of, saved = [None] * n_line, [None] * n_line, []
    done = latent
    for group in groups:
        count = len(group)
        outs = [rows_of(narrow if back else wide) for back in group for _ in range(2)]
        values = call(
            functools.partial(expert_body, count),
            outs + [shape((4, count * tok_rows, hidden_width), narrow)] * 3,
            "experts",
        )(after(place, done), *(rows[i] for i in group), *(payloads[i] for i in group), *weights)
        done, saved = values[0], saved + [list(values[-3:])]
        for i, back in enumerate(group):
            deltas_of[back], outs_of[back] = values[2 * i], values[2 * i + 1]

    def home(value, back):
        return turn(value, n_line, n_line - back) if back else value

    delta_lines = [home(value, back) for back, value in enumerate(deltas_of)]

    pair = (2, latent_width, hidden_width)
    near, far, other = call(
        functools.partial(weight_grad_body, n_line, len(groups)),
        [shape(pair, wide)] * 2 + [shape((4, latent_width, hidden_width), narrow)],
        "weight_grads",
    )(
        after(place, delta_lines[1]),
        *(rows[i] for group in groups for i in group),
        *(value for values in saved for value in values),
    )
    delta_lines = [after(line, near, both_down) for line in delta_lines]
    delta = sum(line.astype(wide) for line in delta_lines).astype(narrow)
    side_delta = swap(delta, n_line, 0, 1)
    first_out = home(outs_of[1], 1)
    other = swap(after(other, delta), n_line, 1, 0)
    far = (far + other[2:].astype(wide)).astype(narrow)
    sent = far
    far = swap(after(far, side_delta), n_line, 0, 1)
    core_deltas = swap(jnp.stack([delta, after(side_delta, first_out, sent)]), n_line, 1, 0)
    blocks = call(
        functools.partial(down_grad_body, n_line),
        [shape((block, latent_width), wide)] + [shape((block, latent_width), narrow)] * (n_line - 1),
        "down_grad",
    )(place, columns[0], across, *core_tokens, delta, side_delta, core_deltas)
    core_down = swap(after(both_down, blocks[1]), n_line, 1, 0)
    (grad_tokens,) = call(
        functools.partial(token_grad_body, n_line, block), [shape((tok_rows, width), narrow)], "token_grad"
    )(place, after(delta, blocks[1]), both_down, core_down)
    blocks = [blocks[0]] + [turn(blocks[back], n_line, n_line - back) for back in range(1, n_line)]
    first_block = blocks[1]
    out_lines = [outs_of[0], first_out] + [home(after(outs_of[back], first_block), back) for back in range(2, n_line)]
    latent_out = sum(line.astype(wide) for line in out_lines).astype(narrow)
    grad_down = sum(value.astype(wide) for value in blocks)
    weight_grad = (near + other[:2].astype(wide) + after(far, grad_tokens).astype(wide)).astype(narrow)
    return (latent_out, grad_tokens, grad_down, weight_grad[:1], weight_grad[1:])


def slot_table(routes, capacity):
    flat = routes.reshape(-1)
    count = flat.shape[0]
    order = jnp.arange(count, dtype=jnp.int32)
    same = (flat[:, None] == flat[None, :]) & (order[None, :] < order[:, None])
    placed = jnp.sum(jnp.where(same, 1, 0), axis=1).astype(jnp.int32)
    return flat * capacity + placed


def routed_rows(tokens, routes, gate_levels, latent_grad, down_weight, expert_in, expert_out):
    tok_rows = tokens.shape[0]
    top = routes.shape[1]
    latent_width = down_weight.shape[1]
    n_major = lax.axis_size("expert")
    n_minor = lax.axis_size("dp")
    n_experts = n_major * n_minor
    capacity = 3 * tok_rows * top // (2 * n_experts)
    entries = tok_rows * top
    contract_last = (((1,), (1,)), ((), ()))
    contract_first = (((0,), (0,)), ((), ()))
    full_down = lax.all_gather(down_weight, ("expert", "dp"), axis=0, tiled=True)
    latent = jnp.dot(tokens, full_down, preferred_element_type=jnp.float32)
    latent = latent.astype(jnp.bfloat16)
    dest = slot_table(routes, capacity)
    source = (
        jnp.full((n_experts * capacity,), entries, jnp.int32)
        .at[dest]
        .set(jnp.arange(entries, dtype=jnp.int32))
    )
    token_of = jnp.where(source < entries, source // top, tok_rows)
    gates = gate_levels.astype(jnp.float32) * gate_unit
    zero_row = jnp.zeros((1, latent_width), jnp.bfloat16)
    latent_pad = jnp.concatenate([latent, zero_row], axis=0)
    send_latent = latent_pad[token_of].reshape(n_major, n_minor, capacity, latent_width)
    scaled = (gates[:, :, None] * latent_grad.astype(jnp.float32)[:, None, :]).astype(jnp.bfloat16)
    scaled_pad = jnp.concatenate([scaled.reshape(entries, latent_width), zero_row], axis=0)
    send_grad = scaled_pad[source].reshape(n_major, n_minor, capacity, latent_width)
    arrived = lax.all_to_all(
        lax.all_to_all(send_latent, "expert", split_axis=0, concat_axis=0, tiled=True),
        "dp",
        split_axis=1,
        concat_axis=1,
        tiled=True,
    )
    rows = arrived.reshape(-1, latent_width)
    weight_in = expert_in[0]
    weight_out = expert_out[0]
    before = jnp.dot(rows, weight_in, preferred_element_type=jnp.float32)
    active = jnp.maximum(before, 0.0)
    hidden = (active * active).astype(jnp.bfloat16)
    result = jnp.dot(hidden, weight_out, preferred_element_type=jnp.float32).astype(jnp.bfloat16)
    returned = lax.all_to_all(
        lax.all_to_all(
            result.reshape(n_major, n_minor, capacity, latent_width),
            "expert",
            split_axis=0,
            concat_axis=0,
            tiled=True,
        ),
        "dp",
        split_axis=1,
        concat_axis=1,
        tiled=True,
    )
    picked = returned.reshape(n_experts * capacity, latent_width)[dest].astype(jnp.float32)
    picked = picked.reshape(tok_rows, top, latent_width)
    latent_out = jnp.sum(gates[:, :, None] * picked, axis=1).astype(jnp.bfloat16)
    arrived_grad = lax.all_to_all(
        lax.all_to_all(send_grad, "expert", split_axis=0, concat_axis=0, tiled=True),
        "dp",
        split_axis=1,
        concat_axis=1,
        tiled=True,
    )
    grad_rows = arrived_grad.reshape(-1, latent_width)
    back_hidden = lax.dot_general(
        grad_rows, weight_out, contract_last, preferred_element_type=jnp.float32
    )
    back_pre = (back_hidden * 2.0 * active).astype(jnp.bfloat16)
    grad_out = lax.dot_general(
        hidden, grad_rows, contract_first, preferred_element_type=jnp.float32
    ).astype(jnp.bfloat16)
    grad_in = lax.dot_general(
        rows, back_pre, contract_first, preferred_element_type=jnp.float32
    ).astype(jnp.bfloat16)
    back_rows = lax.dot_general(
        back_pre, weight_in, contract_last, preferred_element_type=jnp.float32
    ).astype(jnp.bfloat16)
    came_back = lax.all_to_all(
        lax.all_to_all(
            back_rows.reshape(n_major, n_minor, capacity, latent_width),
            "expert",
            split_axis=0,
            concat_axis=0,
            tiled=True,
        ),
        "dp",
        split_axis=1,
        concat_axis=1,
        tiled=True,
    )
    gathered_back = came_back.reshape(n_experts * capacity, latent_width)[dest].astype(jnp.float32)
    latent_delta = jnp.sum(gathered_back.reshape(tok_rows, top, latent_width), axis=1).astype(
        jnp.bfloat16
    )
    grad_tokens = lax.dot_general(
        latent_delta, full_down, contract_last, preferred_element_type=jnp.float32
    )
    grad_tokens = grad_tokens.astype(jnp.bfloat16)
    grad_down = lax.psum_scatter(
        lax.dot_general(tokens, latent_delta, contract_first, preferred_element_type=jnp.float32),
        ("expert", "dp"),
        scatter_dimension=0,
        tiled=True,
    )
    return (latent_out, grad_tokens, grad_down, grad_in[None], grad_out[None])


def on_device(tokens, routes, *others):
    n_major = lax.axis_size("expert")
    n_experts = n_major * lax.axis_size("dp")
    few = n_experts <= 2 * routes.shape[1] and n_major % 2 == 0 and n_major >= 6 and lax.axis_size("dp") == 2
    return (all_rows if few else routed_rows)(tokens, routes, *others)


def solution(mesh):
    in_specs = (
        P(("group", "expert", "dp"), None),
        P(("group", "expert", "dp"), None),
        P(("group", "expert", "dp"), None),
        P(("group", "expert", "dp"), None),
        P(("expert", "dp"), None),
        P(("expert", "dp"), None, None),
        P(("expert", "dp"), None, None),
    )
    out_specs = (
        P(("group", "expert", "dp"), None),
        P(("group", "expert", "dp"), None),
        P(("group", "expert", "dp"), None),
        P(("group", "expert", "dp"), None, None),
        P(("group", "expert", "dp"), None, None),
    )
    return jax.shard_map(
        on_device, mesh=mesh, in_specs=in_specs, out_specs=out_specs, check_vma=False
    )
```

```python
import functools

import jax
import jax.numpy as jnp
from jax import lax
from jax.experimental import pallas as pl
from jax.experimental.pallas import tpu as pltpu
from jax.sharding import PartitionSpec as P

gate_unit = 1.0 / 1024.0
contract_last = (((1,), (1,)), ((), ()))
contract_first = (((0,), (0,)), ((), ()))
plane = ("expert", "dp")
wide = jnp.float32
narrow = jnp.bfloat16


def device_pairs(n_line, move):
    pairs = []
    for z in range(n_line):
        for x in range(2):
            for c in range(2):
                to_z, to_x, to_c = move(z, x, c)
                pairs.append(((z * 2 + x) * 2 + c, (to_z * 2 + to_x) * 2 + to_c))
    return pairs


def turn(value, n_line, by):
    return lax.ppermute(value, plane, device_pairs(n_line, lambda z, x, c: ((z + by) % n_line, x, c)))


def swap(value, n_line, core, side):
    return lax.ppermute(value, plane, device_pairs(n_line, lambda z, x, c: (z, x ^ side, c ^ core)))


def after(value, *earlier):
    return lax.optimization_barrier((value,) + earlier)[0]


def call(body, outs, name, scratch=(), outside=0):
    vmem = pl.BlockSpec(memory_space=pltpu.VMEM)
    outer = pl.BlockSpec(memory_space=pltpu.HBM)

    def run(place, *operands):
        return pl.pallas_call(
            body,
            out_shape=outs,
            in_specs=[pl.BlockSpec(memory_space=pltpu.SMEM)]
            + [outer] * outside
            + [vmem] * (len(operands) - outside),
            out_specs=[vmem] * len(outs),
            scratch_shapes=list(scratch),
            compiler_params=pltpu.CompilerParams(vmem_limit_bytes=40 * 1024 * 1024),
            cost_estimate=pl.CostEstimate(flops=0, bytes_accessed=0, transcendentals=0),
            name=name,
        )(place, *operands)

    return run


def columns_body(n_line, block, place, tokens, expert_in, expert_out, *refs):
    own, other, across, weights, sems = refs
    pieces = (own, across.at[0], other, across.at[1])
    copies = []
    for i, weight in enumerate((expert_in, expert_out)):
        copies.append(pltpu.make_async_copy(weight, weights.at[pl.ds(i, 1)], sems.at[i]))
    for core in range(2):
        for side in range(2):
            owner = (place[1] ^ side) * 2 + (place[2] ^ core)
            for z in range(n_line):
                start = pl.multiple_of((z * 4 + owner) * block, block)
                piece = pieces[core * 2 + side].at[:, pl.ds(z * block, block)]
                copies.append(
                    pltpu.make_async_copy(tokens.at[:, pl.ds(start, block)], piece, sems.at[len(copies)])
                )
    for copy in copies:
        copy.start()
    for copy in copies:
        copy.wait()


def payload_body(place, routes, levels, cotangent, payload):
    tok_rows = cotangent.shape[0]
    gate_rows = payload.shape[0] - tok_rows
    payload[:tok_rows, :] = cotangent[...]
    expert = lax.broadcasted_iota(jnp.int32, (gate_rows, tok_rows), 0)
    total = jnp.zeros((gate_rows, tok_rows), jnp.int32)
    for k in range(routes.shape[0]):
        total = total + jnp.where(expert == routes[k : k + 1, :], levels[k : k + 1, :], 0)
    low = total & 31
    payload[tok_rows:, :tok_rows] = (total - low).astype(wide).astype(narrow)
    payload[tok_rows:, tok_rows : 2 * tok_rows] = low.astype(wide).astype(narrow)
    rest = payload.shape[1] - 2 * tok_rows
    payload[tok_rows:, 2 * tok_rows :] = jnp.zeros((gate_rows, rest), narrow)


def project_body(n_line, place, *refs):
    own, across, core, core_across, *downs = refs[: 4 + n_line]
    pieces = (own, across.at[0], core, core_across)
    keep, send, down = refs[4 + n_line :]
    block = downs[0].shape[0]
    for back in range(n_line):
        z = lax.rem(place[0] + n_line - back, n_line)
        down[pl.ds(pl.multiple_of(z * block, block), block), :] = downs[back][...]
    for core, out in ((1, send), (0, keep)):
        for side in range(2):
            out[side] = jnp.dot(pieces[core * 2 + side][...], down[...], preferred_element_type=wide)


def gate_tile(payload, tok_rows, expert):
    packed = payload[tok_rows:, :]
    rows = lax.broadcasted_iota(jnp.int32, (packed.shape[0], 128), 0)
    pick = jnp.where(rows == expert, 1.0, 0.0).astype(narrow)
    dot = functools.partial(lax.dot_general, dimension_numbers=contract_first, preferred_element_type=wide)
    total = dot(packed[:, :tok_rows], pick) + dot(packed[:, tok_rows : 2 * tok_rows], pick)
    return total * gate_unit


def expert_body(count, place, *refs):
    rows_in, payloads = refs[:count], refs[count : 2 * count]
    own, core, *sides = refs[2 * count : 2 * count + 6]
    weights = (own.at[0], own.at[1], sides[0], sides[1], core.at[0], core.at[1], sides[2], sides[3])
    outs = refs[2 * count + 6 :]
    *sums, hiddens, scaleds, back_pres = outs
    tok_rows, width = rows_in[0].shape
    for first in range(0, count, 2):
        group = range(first, min(first + 2, count))
        span = slice(first * tok_rows, (first + len(group)) * tok_rows)
        stack = lambda values: jnp.concatenate(list(values), axis=0)
        rows = stack(rows_in[i][...] for i in group)
        cotangent = stack(payloads[i][:tok_rows, :] for i in group).astype(wide)
        out_sum = jnp.zeros(rows.shape, wide)
        delta_sum = jnp.zeros(rows.shape, wide)
        for e in range(4):
            weight_in, weight_out = weights[2 * e], weights[2 * e + 1]
            gate = stack(gate_tile(payloads[i], tok_rows, place[3 + e]) for i in group)
            gate = jnp.concatenate([gate] * (width // 128), axis=1)
            active = jnp.maximum(jnp.dot(rows, weight_in[...], preferred_element_type=wide), 0.0)
            hidden = (active * active).astype(narrow)
            hiddens[e, span, :] = hidden
            scaled = (gate * cotangent).astype(narrow)
            scaleds[e, span, :] = scaled
            back_hidden = lax.dot_general(scaled, weight_out[...], contract_last, preferred_element_type=wide)
            back_pre = (back_hidden * 2.0 * active).astype(narrow)
            back_pres[e, span, :] = back_pre
            result = jnp.dot(hidden, weight_out[...], preferred_element_type=wide).astype(narrow)
            out_sum = out_sum + gate * result.astype(wide)
            back_rows = lax.dot_general(back_pre, weight_in[...], contract_last, preferred_element_type=wide)
            delta_sum = delta_sum + back_rows.astype(narrow).astype(wide)
        for i in group:
            part = slice((i - first) * tok_rows, (i - first + 1) * tok_rows)
            out = sums.pop(0)
            out[...] = delta_sum[part].astype(out.dtype)
            out = sums.pop(0)
            out[...] = out_sum[part].astype(out.dtype)


def weight_grad_body(n_rows, n_sets, place, *refs):
    rows_in = refs[:n_rows]
    sets = [refs[n_rows + 3 * i : n_rows + 3 * i + 3] for i in range(n_sets)]
    near, far, other = refs[n_rows + 3 * n_sets :]
    dot = functools.partial(lax.dot_general, dimension_numbers=contract_first, preferred_element_type=wide)
    rows = jnp.concatenate([r[...] for r in rows_in], axis=0)
    for core in (1, 0):
        for side in (1, 0):
            hidden, scaled, back_pre = (
                jnp.concatenate([values[i][core * 2 + side] for values in sets], axis=0) for i in range(3)
            )
            grad_in, grad_out = dot(rows, back_pre), dot(hidden, scaled)
            if core:
                other[2 * side] = grad_in.astype(narrow)
                other[2 * side + 1] = grad_out.astype(narrow)
            else:
                own = far if side else near
                own[0], own[1] = grad_in, grad_out


def down_grad_body(n_line, place, *refs):
    own, across, core, core_across, *deltas, core_deltas = refs[:7]
    riders, blocks = refs[7:-n_line], refs[-n_line:]
    tokens = jnp.concatenate([own[...], across[0], core[...], core_across[...]], axis=0)
    delta = jnp.concatenate([d[...] for d in deltas] + [core_deltas[0], core_deltas[1]], axis=0)
    part = lax.dot_general(tokens, delta, contract_first, preferred_element_type=wide)
    block = blocks[0].shape[0]
    targets = [out if len(out.shape) == 2 else out.at[0] for out in blocks]
    for rider, out in zip(riders, [out for out in blocks if len(out.shape) == 3]):
        out[1] = rider[...]
    for z in range(n_line):
        for back in range(n_line):

            @pl.when(lax.rem(place[0] + n_line - back, n_line) == z)
            def _(z=z, back=back):
                targets[back][...] = part[z * block : (z + 1) * block].astype(targets[back].dtype)


def token_grad_body(n_line, block, place, delta, downs, core_downs, out):
    for i, weight in enumerate((downs.at[0], downs.at[1], core_downs.at[0], core_downs.at[1])):
        owner = (place[1] ^ (i % 2)) * 2 + (place[2] ^ (i // 2))
        part = lax.dot_general(delta[...], weight[...], contract_last, preferred_element_type=wide)
        part = part.astype(narrow)
        for z in range(n_line):
            start = pl.multiple_of((z * 4 + owner) * block, block)
            out[:, pl.ds(start, block)] = part[:, z * block : (z + 1) * block]


def all_rows(tokens, routes, gate_levels, latent_grad, down_weight, expert_in, expert_out):
    tok_rows, width = tokens.shape
    latent_width = down_weight.shape[1]
    hidden_width = expert_in.shape[2]
    n_major = lax.axis_size("expert")
    n_line = n_major // 2
    n_experts = n_major * 2
    block = width // n_experts
    major = lax.axis_index("expert")
    my_core = lax.axis_index("dp")
    place = jnp.stack(
        [major // 2, major % 2, my_core]
        + [(major ^ side) * 2 + (my_core ^ core) for core in range(2) for side in range(2)]
    ).astype(jnp.int32)
    shape = jax.ShapeDtypeStruct
    rows_of = lambda kind: shape((tok_rows, latent_width), kind)

    downs = [down_weight] + [turn(down_weight, n_line, back) for back in range(1, n_line)]

    gate_rows = -(-n_experts // 16) * 16
    columns = call(
        functools.partial(columns_body, n_line, block),
        [shape((tok_rows, n_line * block), narrow)] * 2
        + [shape((2, tok_rows, n_line * block), narrow), shape((2, latent_width, hidden_width), narrow)],
        "columns",
        scratch=[pltpu.SemaphoreType.DMA((4 * n_line + 2,))],
        outside=3,
    )(place, tokens, expert_in, expert_out)
    (payload,) = call(payload_body, [shape((tok_rows + gate_rows, latent_width), narrow)], "payload")(
        place, routes.T, gate_levels.T, latent_grad
    )
    own = columns[3]
    core_own = swap(own, n_line, 1, 0)
    across = swap(columns[2], n_line, 0, 1)
    core_tokens = [swap(after(columns[1], across, core_own), n_line, 1, 0), swap(across[1], n_line, 1, 0)]
    side_in = swap(after(expert_in[0], across), n_line, 0, 1)

    project = call(
        functools.partial(project_body, n_line),
        [shape((2, tok_rows, latent_width), wide)] * 2 + [shape((n_line * block, latent_width), narrow)],
        "project",
    )
    keep, send, down = project(after(place, payload), columns[0], across, *core_tokens, *downs)
    half = keep + swap(send, n_line, 1, 0)
    payloads = [payload] + [turn(after(payload, *downs[1:]), n_line, back) for back in range(1, n_line)]
    crossed = swap(half[1].astype(narrow), n_line, 0, 1).astype(wide)
    latent = (half[0] + after(crossed, side_in, *payloads[1:])).astype(narrow)
    groups = [[*range(1, n_line), 0]]
    riding = range(2, n_line)
    rows = [latent] + [turn(latent, n_line, back) for back in range(1, n_line)]

    side_out = swap(after(expert_out[0], latent), n_line, 0, 1)
    core_in = swap(after(side_in, latent), n_line, 1, 0)
    core_out = swap(after(side_out, *rows[1:]), n_line, 1, 0)
    weights = [own, core_own, side_in, side_out, core_in, core_out]
    side_down = swap(after(down, *rows[1:]), n_line, 0, 1)

    both_down = jnp.stack([down, side_down])
    deltas_of, outs_of, saved = [None] * n_line, [None] * n_line, []
    done = latent
    for group in groups:
        count = len(group)
        outs = [rows_of(narrow if back else wide) for back in group for _ in range(2)]
        values = call(
            functools.partial(expert_body, count),
            outs + [shape((4, count * tok_rows, hidden_width), narrow)] * 3,
            "experts",
        )(after(place, done), *(rows[i] for i in group), *(payloads[i] for i in group), *weights)
        done, saved = values[0], saved + [list(values[-3:])]
        for i, back in enumerate(group):
            deltas_of[back], outs_of[back] = values[2 * i], values[2 * i + 1]

    def home(value, back):
        return turn(value, n_line, n_line - back) if back else value

    delta_lines = [home(value, back) for back, value in enumerate(deltas_of)]

    pair = (2, latent_width, hidden_width)
    near, far, other = call(
        functools.partial(weight_grad_body, n_line, len(groups)),
        [shape(pair, wide)] * 2 + [shape((4, latent_width, hidden_width), narrow)],
        "weight_grads",
    )(
        after(place, delta_lines[1]),
        *(rows[i] for group in groups for i in group),
        *(value for values in saved for value in values),
    )
    delta_lines = [after(line, near, both_down) for line in delta_lines]
    delta = sum(line.astype(wide) for line in delta_lines).astype(narrow)
    side_delta = swap(delta, n_line, 0, 1)
    out_lines = [outs_of[0]] + [home(outs_of[back], back) if back not in riding else None for back in range(1, n_line)]
    other = swap(after(other, delta), n_line, 1, 0)
    far = (far + after(other, out_lines[1])[2:].astype(wide)).astype(narrow)
    sent = far
    far = swap(after(far, side_delta), n_line, 0, 1)
    core_deltas = swap(jnp.stack([delta, after(side_delta, sent)]), n_line, 1, 0)
    blocks = call(
        functools.partial(down_grad_body, n_line),
        [
            shape((2, block, latent_width) if back in riding else (block, latent_width), narrow if back else wide)
            for back in range(n_line)
        ],
        "down_grad",
    )(place, columns[0], across, *core_tokens, delta, side_delta, core_deltas, *(outs_of[back] for back in riding))
    core_down = swap(after(both_down, blocks[1]), n_line, 1, 0)
    (grad_tokens,) = call(
        functools.partial(token_grad_body, n_line, block), [shape((tok_rows, width), narrow)], "token_grad"
    )(place, after(delta, blocks[1]), both_down, core_down)
    blocks = [blocks[0]] + [turn(blocks[back], n_line, n_line - back) for back in range(1, n_line)]
    grad_down = sum((value[0] if back in riding else value).astype(wide) for back, value in enumerate(blocks))
    out_lines = [blocks[back][1] if back in riding else line for back, line in enumerate(out_lines)]
    out_lines[0] = after(out_lines[0], grad_tokens)
    latent_out = sum(line.astype(wide) for line in out_lines).astype(narrow)
    weight_grad = (near + other[:2].astype(wide) + far.astype(wide)).astype(narrow)
    return (latent_out, grad_tokens, grad_down, weight_grad[:1], weight_grad[1:])


def slot_table(routes, capacity):
    flat = routes.reshape(-1)
    count = flat.shape[0]
    order = jnp.arange(count, dtype=jnp.int32)
    same = (flat[:, None] == flat[None, :]) & (order[None, :] < order[:, None])
    placed = jnp.sum(jnp.where(same, 1, 0), axis=1).astype(jnp.int32)
    return flat * capacity + placed


def routed_rows(tokens, routes, gate_levels, latent_grad, down_weight, expert_in, expert_out):
    tok_rows = tokens.shape[0]
    top = routes.shape[1]
    latent_width = down_weight.shape[1]
    n_major = lax.axis_size("expert")
    n_minor = lax.axis_size("dp")
    n_experts = n_major * n_minor
    capacity = 3 * tok_rows * top // (2 * n_experts)
    entries = tok_rows * top
    contract_last = (((1,), (1,)), ((), ()))
    contract_first = (((0,), (0,)), ((), ()))
    full_down = lax.all_gather(down_weight, ("expert", "dp"), axis=0, tiled=True)
    latent = jnp.dot(tokens, full_down, preferred_element_type=jnp.float32)
    latent = latent.astype(jnp.bfloat16)
    dest = slot_table(routes, capacity)
    source = (
        jnp.full((n_experts * capacity,), entries, jnp.int32)
        .at[dest]
        .set(jnp.arange(entries, dtype=jnp.int32))
    )
    token_of = jnp.where(source < entries, source // top, tok_rows)
    gates = gate_levels.astype(jnp.float32) * gate_unit
    zero_row = jnp.zeros((1, latent_width), jnp.bfloat16)
    latent_pad = jnp.concatenate([latent, zero_row], axis=0)
    send_latent = latent_pad[token_of].reshape(n_major, n_minor, capacity, latent_width)
    scaled = (gates[:, :, None] * latent_grad.astype(jnp.float32)[:, None, :]).astype(jnp.bfloat16)
    scaled_pad = jnp.concatenate([scaled.reshape(entries, latent_width), zero_row], axis=0)
    send_grad = scaled_pad[source].reshape(n_major, n_minor, capacity, latent_width)
    arrived = lax.all_to_all(
        lax.all_to_all(send_latent, "expert", split_axis=0, concat_axis=0, tiled=True),
        "dp",
        split_axis=1,
        concat_axis=1,
        tiled=True,
    )
    rows = arrived.reshape(-1, latent_width)
    weight_in = expert_in[0]
    weight_out = expert_out[0]
    before = jnp.dot(rows, weight_in, preferred_element_type=jnp.float32)
    active = jnp.maximum(before, 0.0)
    hidden = (active * active).astype(jnp.bfloat16)
    result = jnp.dot(hidden, weight_out, preferred_element_type=jnp.float32).astype(jnp.bfloat16)
    returned = lax.all_to_all(
        lax.all_to_all(
            result.reshape(n_major, n_minor, capacity, latent_width),
            "expert",
            split_axis=0,
            concat_axis=0,
            tiled=True,
        ),
        "dp",
        split_axis=1,
        concat_axis=1,
        tiled=True,
    )
    picked = returned.reshape(n_experts * capacity, latent_width)[dest].astype(jnp.float32)
    picked = picked.reshape(tok_rows, top, latent_width)
    latent_out = jnp.sum(gates[:, :, None] * picked, axis=1).astype(jnp.bfloat16)
    arrived_grad = lax.all_to_all(
        lax.all_to_all(send_grad, "expert", split_axis=0, concat_axis=0, tiled=True),
        "dp",
        split_axis=1,
        concat_axis=1,
        tiled=True,
    )
    grad_rows = arrived_grad.reshape(-1, latent_width)
    back_hidden = lax.dot_general(
        grad_rows, weight_out, contract_last, preferred_element_type=jnp.float32
    )
    back_pre = (back_hidden * 2.0 * active).astype(jnp.bfloat16)
    grad_out = lax.dot_general(
        hidden, grad_rows, contract_first, preferred_element_type=jnp.float32
    ).astype(jnp.bfloat16)
    grad_in = lax.dot_general(
        rows, back_pre, contract_first, preferred_element_type=jnp.float32
    ).astype(jnp.bfloat16)
    back_rows = lax.dot_general(
        back_pre, weight_in, contract_last, preferred_element_type=jnp.float32
    ).astype(jnp.bfloat16)
    came_back = lax.all_to_all(
        lax.all_to_all(
            back_rows.reshape(n_major, n_minor, capacity, latent_width),
            "expert",
            split_axis=0,
            concat_axis=0,
            tiled=True,
        ),
        "dp",
        split_axis=1,
        concat_axis=1,
        tiled=True,
    )
    gathered_back = came_back.reshape(n_experts * capacity, latent_width)[dest].astype(jnp.float32)
    latent_delta = jnp.sum(gathered_back.reshape(tok_rows, top, latent_width), axis=1).astype(
        jnp.bfloat16
    )
    grad_tokens = lax.dot_general(
        latent_delta, full_down, contract_last, preferred_element_type=jnp.float32
    )
    grad_tokens = grad_tokens.astype(jnp.bfloat16)
    grad_down = lax.psum_scatter(
        lax.dot_general(tokens, latent_delta, contract_first, preferred_element_type=jnp.float32),
        ("expert", "dp"),
        scatter_dimension=0,
        tiled=True,
    )
    return (latent_out, grad_tokens, grad_down, grad_in[None], grad_out[None])


def on_device(tokens, routes, *others):
    n_major = lax.axis_size("expert")
    n_experts = n_major * lax.axis_size("dp")
    few = n_experts <= 2 * routes.shape[1] and n_major % 2 == 0 and n_major >= 6 and lax.axis_size("dp") == 2
    return (all_rows if few else routed_rows)(tokens, routes, *others)


def solution(mesh):
    in_specs = (
        P(("group", "expert", "dp"), None),
        P(("group", "expert", "dp"), None),
        P(("group", "expert", "dp"), None),
        P(("group", "expert", "dp"), None),
        P(("expert", "dp"), None),
        P(("expert", "dp"), None, None),
        P(("expert", "dp"), None, None),
    )
    out_specs = (
        P(("group", "expert", "dp"), None),
        P(("group", "expert", "dp"), None),
        P(("group", "expert", "dp"), None),
        P(("group", "expert", "dp"), None, None),
        P(("group", "expert", "dp"), None, None),
    )
    return jax.shard_map(
        on_device, mesh=mesh, in_specs=in_specs, out_specs=out_specs, check_vma=False
    )
```

```python
import functools

import jax
import jax.numpy as jnp
from jax import lax
from jax.experimental import pallas as pl
from jax.experimental.pallas import tpu as pltpu
from jax.sharding import PartitionSpec as P

gate_unit = 1.0 / 1024.0
contract_last = (((1,), (1,)), ((), ()))
contract_first = (((0,), (0,)), ((), ()))
plane = ("expert", "dp")
wide = jnp.float32
narrow = jnp.bfloat16


def device_pairs(n_line, move):
    pairs = []
    for z in range(n_line):
        for x in range(2):
            for c in range(2):
                to_z, to_x, to_c = move(z, x, c)
                pairs.append(((z * 2 + x) * 2 + c, (to_z * 2 + to_x) * 2 + to_c))
    return pairs


def turn(value, n_line, by):
    return lax.ppermute(value, plane, device_pairs(n_line, lambda z, x, c: ((z + by) % n_line, x, c)))


def swap(value, n_line, core, side):
    return lax.ppermute(value, plane, device_pairs(n_line, lambda z, x, c: (z, x ^ side, c ^ core)))


def after(value, *earlier):
    return lax.optimization_barrier((value,) + earlier)[0]


def call(body, outs, name, scratch=(), outside=0):
    vmem = pl.BlockSpec(memory_space=pltpu.VMEM)
    outer = pl.BlockSpec(memory_space=pltpu.HBM)

    def run(place, *operands):
        return pl.pallas_call(
            body,
            out_shape=outs,
            in_specs=[pl.BlockSpec(memory_space=pltpu.SMEM)]
            + [outer] * outside
            + [vmem] * (len(operands) - outside),
            out_specs=[vmem] * len(outs),
            scratch_shapes=list(scratch),
            compiler_params=pltpu.CompilerParams(vmem_limit_bytes=40 * 1024 * 1024),
            cost_estimate=pl.CostEstimate(flops=0, bytes_accessed=0, transcendentals=0),
            name=name,
        )(place, *operands)

    return run


def columns_body(n_line, block, place, tokens, *refs):
    own, other, across, sems = refs
    pieces = (own, across.at[0], other, across.at[1])
    copies = []
    for core in range(2):
        for side in range(2):
            owner = (place[1] ^ side) * 2 + (place[2] ^ core)
            for z in range(n_line):
                start = pl.multiple_of((z * 4 + owner) * block, block)
                piece = pieces[core * 2 + side].at[:, pl.ds(z * block, block)]
                copies.append(
                    pltpu.make_async_copy(tokens.at[:, pl.ds(start, block)], piece, sems.at[len(copies)])
                )
    for copy in copies:
        copy.start()
    for copy in copies:
        copy.wait()


def stack_body(place, first, second, out):
    out[0], out[1] = first[...], second[...]


def add_body(place, *refs):
    total = refs[0][...].astype(wide)
    for value in refs[1:-1]:
        total = total + value[...].astype(wide)
    refs[-1][...] = total.astype(refs[-1].dtype)


def half_body(place, keep, arrived, mine, other):
    mine[...] = keep[0] + arrived[0]
    other[...] = (keep[1] + arrived[1]).astype(narrow)


def far_body(place, far, arrived, out):
    out[...] = (far[...] + arrived[2:].astype(wide)).astype(narrow)


def near_body(place, near, arrived, far, grad_in, grad_out):
    for i, out in enumerate((grad_in, grad_out)):
        out[0] = (near[i] + arrived[i].astype(wide) + far[i].astype(wide)).astype(narrow)


def last_body(riding, place, *refs):
    n_line = (len(refs) - 2 + len(riding)) // 2
    blocks, pieces, grad_down, combined = refs[:n_line], list(refs[n_line:-2]), refs[-2], refs[-1]
    total = blocks[0][...]
    out_total = pieces.pop(0)[...]
    for back in range(1, n_line):
        block = blocks[back].at[0] if back in riding else blocks[back]
        piece = blocks[back].at[1] if back in riding else pieces.pop(0)
        total = total + block[...].astype(wide)
        out_total = out_total + piece[...].astype(wide)
    grad_down[...] = total
    combined[...] = out_total.astype(narrow)


def payload_body(place, routes, levels, cotangent, payload):
    tok_rows = cotangent.shape[0]
    gate_rows = payload.shape[0] - tok_rows
    payload[:tok_rows, :] = cotangent[...]
    expert = lax.broadcasted_iota(jnp.int32, (gate_rows, tok_rows), 0)
    total = jnp.zeros((gate_rows, tok_rows), jnp.int32)
    for k in range(routes.shape[0]):
        total = total + jnp.where(expert == routes[k : k + 1, :], levels[k : k + 1, :], 0)
    low = total & 31
    payload[tok_rows:, :tok_rows] = (total - low).astype(wide).astype(narrow)
    payload[tok_rows:, tok_rows : 2 * tok_rows] = low.astype(wide).astype(narrow)
    rest = payload.shape[1] - 2 * tok_rows
    payload[tok_rows:, 2 * tok_rows :] = jnp.zeros((gate_rows, rest), narrow)


def project_body(n_line, place, *refs):
    own, across, core, core_across, *downs = refs[: 4 + n_line]
    pieces = (own, across.at[0], core, core_across)
    keep, send, down = refs[4 + n_line :]
    block = downs[0].shape[0]
    for back in range(n_line):
        z = lax.rem(place[0] + n_line - back, n_line)
        down[pl.ds(pl.multiple_of(z * block, block), block), :] = downs[back][...]
    for core, out in ((1, send), (0, keep)):
        for side in range(2):
            out[side] = jnp.dot(pieces[core * 2 + side][...], down[...], preferred_element_type=wide)


def gate_tile(payload, tok_rows, expert):
    packed = payload[tok_rows:, :]
    rows = lax.broadcasted_iota(jnp.int32, (packed.shape[0], 128), 0)
    pick = jnp.where(rows == expert, 1.0, 0.0).astype(narrow)
    dot = functools.partial(lax.dot_general, dimension_numbers=contract_first, preferred_element_type=wide)
    total = dot(packed[:, :tok_rows], pick) + dot(packed[:, tok_rows : 2 * tok_rows], pick)
    return total * gate_unit


def expert_body(count, place, *refs):
    rows_in, payloads = refs[:count], refs[count : 2 * count]
    own, core, *sides = refs[2 * count : 2 * count + 6]
    weights = (own.at[0], own.at[1], sides[0], sides[1], core.at[0], core.at[1], sides[2], sides[3])
    outs = refs[2 * count + 6 :]
    *sums, hiddens, scaleds, back_pres = outs
    tok_rows, width = rows_in[0].shape
    for first in range(0, count, 2):
        group = range(first, min(first + 2, count))
        span = slice(first * tok_rows, (first + len(group)) * tok_rows)
        stack = lambda values: jnp.concatenate(list(values), axis=0)
        rows = stack(rows_in[i][...] for i in group)
        cotangent = stack(payloads[i][:tok_rows, :] for i in group).astype(wide)
        out_sum = jnp.zeros(rows.shape, wide)
        delta_sum = jnp.zeros(rows.shape, wide)
        for e in range(4):
            weight_in, weight_out = weights[2 * e], weights[2 * e + 1]
            gate = stack(gate_tile(payloads[i], tok_rows, place[3 + e]) for i in group)
            gate = jnp.concatenate([gate] * (width // 128), axis=1)
            active = jnp.maximum(jnp.dot(rows, weight_in[...], preferred_element_type=wide), 0.0)
            hidden = (active * active).astype(narrow)
            hiddens[e, span, :] = hidden
            scaled = (gate * cotangent).astype(narrow)
            scaleds[e, span, :] = scaled
            back_hidden = lax.dot_general(scaled, weight_out[...], contract_last, preferred_element_type=wide)
            back_pre = (back_hidden * 2.0 * active).astype(narrow)
            back_pres[e, span, :] = back_pre
            result = jnp.dot(hidden, weight_out[...], preferred_element_type=wide).astype(narrow)
            out_sum = out_sum + gate * result.astype(wide)
            back_rows = lax.dot_general(back_pre, weight_in[...], contract_last, preferred_element_type=wide)
            delta_sum = delta_sum + back_rows.astype(narrow).astype(wide)
        for i in group:
            part = slice((i - first) * tok_rows, (i - first + 1) * tok_rows)
            out = sums.pop(0)
            out[...] = delta_sum[part].astype(out.dtype)
            out = sums.pop(0)
            out[...] = out_sum[part].astype(out.dtype)


def weight_grad_body(n_rows, n_sets, place, *refs):
    rows_in = refs[:n_rows]
    sets = [refs[n_rows + 3 * i : n_rows + 3 * i + 3] for i in range(n_sets)]
    near, far, other = refs[n_rows + 3 * n_sets :]
    dot = functools.partial(lax.dot_general, dimension_numbers=contract_first, preferred_element_type=wide)
    rows = jnp.concatenate([r[...] for r in rows_in], axis=0)
    for core in (1, 0):
        for side in (1, 0):
            hidden, scaled, back_pre = (
                jnp.concatenate([values[i][core * 2 + side] for values in sets], axis=0) for i in range(3)
            )
            grad_in, grad_out = dot(rows, back_pre), dot(hidden, scaled)
            if core:
                other[2 * side] = grad_in.astype(narrow)
                other[2 * side + 1] = grad_out.astype(narrow)
            else:
                own = far if side else near
                own[0], own[1] = grad_in, grad_out


def down_grad_body(n_line, place, *refs):
    own, across, core, core_across, *deltas, core_deltas = refs[:7]
    riders, blocks = refs[7:-n_line], refs[-n_line:]
    tokens = jnp.concatenate([own[...], across[0], core[...], core_across[...]], axis=0)
    delta = jnp.concatenate([d[...] for d in deltas] + [core_deltas[0], core_deltas[1]], axis=0)
    part = lax.dot_general(tokens, delta, contract_first, preferred_element_type=wide)
    block = blocks[0].shape[0]
    targets = [out if len(out.shape) == 2 else out.at[0] for out in blocks]
    for rider, out in zip(riders, [out for out in blocks if len(out.shape) == 3]):
        out[1] = rider[...]
    for z in range(n_line):
        for back in range(n_line):

            @pl.when(lax.rem(place[0] + n_line - back, n_line) == z)
            def _(z=z, back=back):
                targets[back][...] = part[z * block : (z + 1) * block].astype(targets[back].dtype)


def token_grad_body(n_line, block, place, delta, downs, core_downs, out):
    for i, weight in enumerate((downs.at[0], downs.at[1], core_downs.at[0], core_downs.at[1])):
        owner = (place[1] ^ (i % 2)) * 2 + (place[2] ^ (i // 2))
        part = lax.dot_general(delta[...], weight[...], contract_last, preferred_element_type=wide)
        part = part.astype(narrow)
        for z in range(n_line):
            start = pl.multiple_of((z * 4 + owner) * block, block)
            out[:, pl.ds(start, block)] = part[:, z * block : (z + 1) * block]


def all_rows(tokens, routes, gate_levels, latent_grad, down_weight, expert_in, expert_out):
    tok_rows, width = tokens.shape
    latent_width = down_weight.shape[1]
    hidden_width = expert_in.shape[2]
    n_major = lax.axis_size("expert")
    n_line = n_major // 2
    n_experts = n_major * 2
    block = width // n_experts
    major = lax.axis_index("expert")
    my_core = lax.axis_index("dp")
    place = jnp.stack(
        [major // 2, major % 2, my_core]
        + [(major ^ side) * 2 + (my_core ^ core) for core in range(2) for side in range(2)]
    ).astype(jnp.int32)
    shape = jax.ShapeDtypeStruct
    rows_of = lambda kind: shape((tok_rows, latent_width), kind)

    downs = [down_weight] + [turn(down_weight, n_line, back) for back in range(1, n_line)]

    gate_rows = -(-n_experts // 16) * 16
    columns = call(
        functools.partial(columns_body, n_line, block),
        [shape((tok_rows, n_line * block), narrow)] * 2
        + [shape((2, tok_rows, n_line * block), narrow)],
        "columns",
        scratch=[pltpu.SemaphoreType.DMA((4 * n_line,))],
        outside=1,
    )(place, tokens)
    stack = lambda first, second, *earlier: call(
        stack_body, [shape((2,) + first.shape, narrow)], "stack"
    )(after(place, *earlier) if earlier else place, first, second)[0]
    (payload,) = call(payload_body, [shape((tok_rows + gate_rows, latent_width), narrow)], "payload")(
        place, routes.T, gate_levels.T, latent_grad
    )
    own = stack(expert_in[0], expert_out[0], downs[1])
    core_own = swap(own, n_line, 1, 0)
    across = swap(columns[2], n_line, 0, 1)
    core_tokens = [swap(after(columns[1], across, core_own), n_line, 1, 0), swap(across[1], n_line, 1, 0)]
    side_in = swap(after(expert_in[0], across), n_line, 0, 1)

    project = call(
        functools.partial(project_body, n_line),
        [shape((2, tok_rows, latent_width), wide)] * 2 + [shape((n_line * block, latent_width), narrow)],
        "project",
    )
    keep, send, down = project(after(place, payload), columns[0], across, *core_tokens, *downs)
    half, cross = call(half_body, [rows_of(wide), rows_of(narrow)], "half")(
        place, keep, swap(send, n_line, 1, 0)
    )
    payloads = [payload] + [turn(after(payload, *downs[1:]), n_line, back) for back in range(1, n_line)]
    crossed = swap(cross, n_line, 0, 1)
    (latent,) = call(add_body, [rows_of(narrow)], "latent")(
        place, half, after(crossed, side_in, *payloads[1:])
    )
    groups = [[*range(1, n_line), 0]]
    riding = range(2, n_line)
    rows = [latent] + [turn(latent, n_line, back) for back in range(1, n_line)]

    side_out = swap(after(expert_out[0], latent), n_line, 0, 1)
    core_in = swap(after(side_in, latent), n_line, 1, 0)
    core_out = swap(after(side_out, *rows[1:]), n_line, 1, 0)
    weights = [own, core_own, side_in, side_out, core_in, core_out]
    side_down = swap(after(down, *rows[1:]), n_line, 0, 1)

    both_down = stack(down, side_down)
    deltas_of, outs_of, saved = [None] * n_line, [None] * n_line, []
    done = latent
    for group in groups:
        count = len(group)
        outs = [rows_of(narrow if back else wide) for back in group for _ in range(2)]
        values = call(
            functools.partial(expert_body, count),
            outs + [shape((4, count * tok_rows, hidden_width), narrow)] * 3,
            "experts",
        )(after(place, done), *(rows[i] for i in group), *(payloads[i] for i in group), *weights)
        done, saved = values[0], saved + [list(values[-3:])]
        for i, back in enumerate(group):
            deltas_of[back], outs_of[back] = values[2 * i], values[2 * i + 1]

    def home(value, back):
        return turn(value, n_line, n_line - back) if back else value

    delta_lines = [home(value, back) for back, value in enumerate(deltas_of)]

    pair = (2, latent_width, hidden_width)
    near, far, other = call(
        functools.partial(weight_grad_body, n_line, len(groups)),
        [shape(pair, wide)] * 2 + [shape((4, latent_width, hidden_width), narrow)],
        "weight_grads",
    )(
        after(place, delta_lines[1]),
        *(rows[i] for group in groups for i in group),
        *(value for values in saved for value in values),
    )
    delta_lines = [after(line, near, both_down) for line in delta_lines]
    (delta,) = call(add_body, [rows_of(narrow)], "latent_delta")(place, *delta_lines)
    side_delta = swap(delta, n_line, 0, 1)
    out_lines = [outs_of[0]] + [home(outs_of[back], back) if back not in riding else None for back in range(1, n_line)]
    other = swap(after(other, delta), n_line, 1, 0)
    (far,) = call(far_body, [shape(pair, narrow)], "far_grads")(place, far, after(other, out_lines[1]))
    sent = far
    far = swap(after(far, side_delta), n_line, 0, 1)
    core_deltas = swap(stack(delta, side_delta, sent), n_line, 1, 0)
    blocks = call(
        functools.partial(down_grad_body, n_line),
        [
            shape((2, block, latent_width) if back in riding else (block, latent_width), narrow if back else wide)
            for back in range(n_line)
        ],
        "down_grad",
    )(place, columns[0], across, *core_tokens, delta, side_delta, core_deltas, *(outs_of[back] for back in riding))
    core_down = swap(after(both_down, blocks[1]), n_line, 1, 0)
    (grad_tokens,) = call(
        functools.partial(token_grad_body, n_line, block), [shape((tok_rows, width), narrow)], "token_grad"
    )(place, after(delta, blocks[1]), both_down, core_down)
    blocks = [blocks[0]] + [turn(blocks[back], n_line, n_line - back) for back in range(1, n_line)]
    grad_down, latent_out = call(
        functools.partial(last_body, riding), [shape((block, latent_width), wide), rows_of(narrow)], "last_sums"
    )(after(place, grad_tokens), *blocks, *(line for line in out_lines if line is not None))
    grad_in, grad_out = call(
        near_body, [shape(expert_in.shape, narrow), shape(expert_out.shape, narrow)], "near_grads"
    )(after(place, grad_down), near, other, far)
    return (latent_out, grad_tokens, grad_down, grad_in, grad_out)


def slot_table(routes, capacity):
    flat = routes.reshape(-1)
    count = flat.shape[0]
    order = jnp.arange(count, dtype=jnp.int32)
    same = (flat[:, None] == flat[None, :]) & (order[None, :] < order[:, None])
    placed = jnp.sum(jnp.where(same, 1, 0), axis=1).astype(jnp.int32)
    return flat * capacity + placed


def routed_rows(tokens, routes, gate_levels, latent_grad, down_weight, expert_in, expert_out):
    tok_rows = tokens.shape[0]
    top = routes.shape[1]
    latent_width = down_weight.shape[1]
    n_major = lax.axis_size("expert")
    n_minor = lax.axis_size("dp")
    n_experts = n_major * n_minor
    capacity = 3 * tok_rows * top // (2 * n_experts)
    entries = tok_rows * top
    contract_last = (((1,), (1,)), ((), ()))
    contract_first = (((0,), (0,)), ((), ()))
    full_down = lax.all_gather(down_weight, ("expert", "dp"), axis=0, tiled=True)
    latent = jnp.dot(tokens, full_down, preferred_element_type=jnp.float32)
    latent = latent.astype(jnp.bfloat16)
    dest = slot_table(routes, capacity)
    source = (
        jnp.full((n_experts * capacity,), entries, jnp.int32)
        .at[dest]
        .set(jnp.arange(entries, dtype=jnp.int32))
    )
    token_of = jnp.where(source < entries, source // top, tok_rows)
    gates = gate_levels.astype(jnp.float32) * gate_unit
    zero_row = jnp.zeros((1, latent_width), jnp.bfloat16)
    latent_pad = jnp.concatenate([latent, zero_row], axis=0)
    send_latent = latent_pad[token_of].reshape(n_major, n_minor, capacity, latent_width)
    scaled = (gates[:, :, None] * latent_grad.astype(jnp.float32)[:, None, :]).astype(jnp.bfloat16)
    scaled_pad = jnp.concatenate([scaled.reshape(entries, latent_width), zero_row], axis=0)
    send_grad = scaled_pad[source].reshape(n_major, n_minor, capacity, latent_width)
    arrived = lax.all_to_all(
        lax.all_to_all(send_latent, "expert", split_axis=0, concat_axis=0, tiled=True),
        "dp",
        split_axis=1,
        concat_axis=1,
        tiled=True,
    )
    rows = arrived.reshape(-1, latent_width)
    weight_in = expert_in[0]
    weight_out = expert_out[0]
    before = jnp.dot(rows, weight_in, preferred_element_type=jnp.float32)
    active = jnp.maximum(before, 0.0)
    hidden = (active * active).astype(jnp.bfloat16)
    result = jnp.dot(hidden, weight_out, preferred_element_type=jnp.float32).astype(jnp.bfloat16)
    returned = lax.all_to_all(
        lax.all_to_all(
            result.reshape(n_major, n_minor, capacity, latent_width),
            "expert",
            split_axis=0,
            concat_axis=0,
            tiled=True,
        ),
        "dp",
        split_axis=1,
        concat_axis=1,
        tiled=True,
    )
    picked = returned.reshape(n_experts * capacity, latent_width)[dest].astype(jnp.float32)
    picked = picked.reshape(tok_rows, top, latent_width)
    latent_out = jnp.sum(gates[:, :, None] * picked, axis=1).astype(jnp.bfloat16)
    arrived_grad = lax.all_to_all(
        lax.all_to_all(send_grad, "expert", split_axis=0, concat_axis=0, tiled=True),
        "dp",
        split_axis=1,
        concat_axis=1,
        tiled=True,
    )
    grad_rows = arrived_grad.reshape(-1, latent_width)
    back_hidden = lax.dot_general(
        grad_rows, weight_out, contract_last, preferred_element_type=jnp.float32
    )
    back_pre = (back_hidden * 2.0 * active).astype(jnp.bfloat16)
    grad_out = lax.dot_general(
        hidden, grad_rows, contract_first, preferred_element_type=jnp.float32
    ).astype(jnp.bfloat16)
    grad_in = lax.dot_general(
        rows, back_pre, contract_first, preferred_element_type=jnp.float32
    ).astype(jnp.bfloat16)
    back_rows = lax.dot_general(
        back_pre, weight_in, contract_last, preferred_element_type=jnp.float32
    ).astype(jnp.bfloat16)
    came_back = lax.all_to_all(
        lax.all_to_all(
            back_rows.reshape(n_major, n_minor, capacity, latent_width),
            "expert",
            split_axis=0,
            concat_axis=0,
            tiled=True,
        ),
        "dp",
        split_axis=1,
        concat_axis=1,
        tiled=True,
    )
    gathered_back = came_back.reshape(n_experts * capacity, latent_width)[dest].astype(jnp.float32)
    latent_delta = jnp.sum(gathered_back.reshape(tok_rows, top, latent_width), axis=1).astype(
        jnp.bfloat16
    )
    grad_tokens = lax.dot_general(
        latent_delta, full_down, contract_last, preferred_element_type=jnp.float32
    )
    grad_tokens = grad_tokens.astype(jnp.bfloat16)
    grad_down = lax.psum_scatter(
        lax.dot_general(tokens, latent_delta, contract_first, preferred_element_type=jnp.float32),
        ("expert", "dp"),
        scatter_dimension=0,
        tiled=True,
    )
    return (latent_out, grad_tokens, grad_down, grad_in[None], grad_out[None])


def on_device(tokens, routes, *others):
    n_major = lax.axis_size("expert")
    n_experts = n_major * lax.axis_size("dp")
    few = n_experts <= 2 * routes.shape[1] and n_major % 2 == 0 and n_major >= 6 and lax.axis_size("dp") == 2
    return (all_rows if few else routed_rows)(tokens, routes, *others)


def solution(mesh):
    in_specs = (
        P(("group", "expert", "dp"), None),
        P(("group", "expert", "dp"), None),
        P(("group", "expert", "dp"), None),
        P(("group", "expert", "dp"), None),
        P(("expert", "dp"), None),
        P(("expert", "dp"), None, None),
        P(("expert", "dp"), None, None),
    )
    out_specs = (
        P(("group", "expert", "dp"), None),
        P(("group", "expert", "dp"), None),
        P(("group", "expert", "dp"), None),
        P(("group", "expert", "dp"), None, None),
        P(("group", "expert", "dp"), None, None),
    )
    return jax.shard_map(
        on_device, mesh=mesh, in_specs=in_specs, out_specs=out_specs, check_vma=False
    )
```

```python
import functools

import jax
import jax.numpy as jnp
from jax import lax
from jax.experimental import pallas as pl
from jax.experimental.pallas import tpu as pltpu
from jax.sharding import PartitionSpec as P

gate_unit = 1.0 / 1024.0
contract_last = (((1,), (1,)), ((), ()))
contract_first = (((0,), (0,)), ((), ()))
plane = ("expert", "dp")
wide = jnp.float32
narrow = jnp.bfloat16


def device_pairs(n_line, move):
    pairs = []
    for z in range(n_line):
        for x in range(2):
            for c in range(2):
                to_z, to_x, to_c = move(z, x, c)
                pairs.append(((z * 2 + x) * 2 + c, (to_z * 2 + to_x) * 2 + to_c))
    return pairs


def turn(value, n_line, by):
    return lax.ppermute(value, plane, device_pairs(n_line, lambda z, x, c: ((z + by) % n_line, x, c)))


def swap(value, n_line, core, side):
    return lax.ppermute(value, plane, device_pairs(n_line, lambda z, x, c: (z, x ^ side, c ^ core)))


def after(value, *earlier):
    return lax.optimization_barrier((value,) + earlier)[0]


def call(body, outs, name, scratch=(), outside=0):
    vmem = pl.BlockSpec(memory_space=pltpu.VMEM)
    outer = pl.BlockSpec(memory_space=pltpu.HBM)

    def run(place, *operands):
        return pl.pallas_call(
            body,
            out_shape=outs,
            in_specs=[pl.BlockSpec(memory_space=pltpu.SMEM)]
            + [outer] * outside
            + [vmem] * (len(operands) - outside),
            out_specs=[vmem] * len(outs),
            scratch_shapes=list(scratch),
            compiler_params=pltpu.CompilerParams(vmem_limit_bytes=40 * 1024 * 1024),
            cost_estimate=pl.CostEstimate(flops=0, bytes_accessed=0, transcendentals=0),
            name=name,
        )(place, *operands)

    return run


def columns_body(n_line, block, place, tokens, expert_in, expert_out, *refs):
    own, other, across, weights, sems = refs
    pieces = (own, across.at[0], other, across.at[1])
    copies = []
    for i, weight in enumerate((expert_in, expert_out)):
        copies.append(pltpu.make_async_copy(weight, weights.at[pl.ds(i, 1)], sems.at[i]))
    for core in range(2):
        for side in range(2):
            owner = (place[1] ^ side) * 2 + (place[2] ^ core)
            for z in range(n_line):
                start = pl.multiple_of((z * 4 + owner) * block, block)
                piece = pieces[core * 2 + side].at[:, pl.ds(z * block, block)]
                copies.append(
                    pltpu.make_async_copy(tokens.at[:, pl.ds(start, block)], piece, sems.at[len(copies)])
                )
    for copy in copies:
        copy.start()
    for copy in copies:
        copy.wait()


def stack_body(place, first, second, out):
    out[0], out[1] = first[...], second[...]


def add_body(place, *refs):
    total = refs[0][...].astype(wide)
    for value in refs[1:-1]:
        total = total + value[...].astype(wide)
    refs[-1][...] = total.astype(refs[-1].dtype)


def half_body(place, keep, arrived, mine, other):
    mine[...] = keep[0] + arrived[0]
    other[...] = (keep[1] + arrived[1]).astype(narrow)


def core_sum_body(place, near, far, arrived, near_out, far_out):
    far_out[...] = (far[...] + arrived[2:].astype(wide)).astype(narrow)
    near_out[...] = near[...] + arrived[:2].astype(wide)


def near_body(place, near, far, grad_in, grad_out):
    for i, out in enumerate((grad_in, grad_out)):
        out[0] = (near[i] + far[i].astype(wide)).astype(narrow)


def last_body(riding, place, *refs):
    n_line = (len(refs) - 2 + len(riding)) // 2
    blocks, pieces, grad_down, combined = refs[:n_line], list(refs[n_line:-2]), refs[-2], refs[-1]
    total = blocks[0][...]
    out_total = pieces.pop(0)[...]
    for back in range(1, n_line):
        block = blocks[back].at[0] if back in riding else blocks[back]
        piece = blocks[back].at[1] if back in riding else pieces.pop(0)
        total = total + block[...].astype(wide)
        out_total = out_total + piece[...].astype(wide)
    grad_down[...] = total
    combined[...] = out_total.astype(narrow)


def payload_body(place, routes, levels, cotangent, payload):
    tok_rows = cotangent.shape[0]
    gate_rows = payload.shape[0] - tok_rows
    payload[:tok_rows, :] = cotangent[...]
    expert = lax.broadcasted_iota(jnp.int32, (gate_rows, tok_rows), 0)
    total = jnp.zeros((gate_rows, tok_rows), jnp.int32)
    for k in range(routes.shape[0]):
        total = total + jnp.where(expert == routes[k : k + 1, :], levels[k : k + 1, :], 0)
    low = total & 31
    payload[tok_rows:, :tok_rows] = (total - low).astype(wide).astype(narrow)
    payload[tok_rows:, tok_rows : 2 * tok_rows] = low.astype(wide).astype(narrow)
    rest = payload.shape[1] - 2 * tok_rows
    payload[tok_rows:, 2 * tok_rows :] = jnp.zeros((gate_rows, rest), narrow)


def project_body(n_line, place, *refs):
    own, across, core, core_across, *downs = refs[: 4 + n_line]
    pieces = (own, across.at[0], core, core_across)
    keep, send, down = refs[4 + n_line :]
    block = downs[0].shape[0]
    for back in range(n_line):
        z = lax.rem(place[0] + n_line - back, n_line)
        down[pl.ds(pl.multiple_of(z * block, block), block), :] = downs[back][...]
    for core, out in ((1, send), (0, keep)):
        for side in range(2):
            out[side] = jnp.dot(pieces[core * 2 + side][...], down[...], preferred_element_type=wide)


def gate_tile(payload, tok_rows, expert):
    packed = payload[tok_rows:, :]
    rows = lax.broadcasted_iota(jnp.int32, (packed.shape[0], 128), 0)
    pick = jnp.where(rows == expert, 1.0, 0.0).astype(narrow)
    dot = functools.partial(lax.dot_general, dimension_numbers=contract_first, preferred_element_type=wide)
    total = dot(packed[:, :tok_rows], pick) + dot(packed[:, tok_rows : 2 * tok_rows], pick)
    return total * gate_unit


def expert_body(count, place, *refs):
    rows_in, payloads = refs[:count], refs[count : 2 * count]
    own, core, *sides = refs[2 * count : 2 * count + 6]
    weights = (own.at[0], own.at[1], sides[0], sides[1], core.at[0], core.at[1], sides[2], sides[3])
    outs = refs[2 * count + 6 :]
    *sums, hiddens, scaleds, back_pres = outs
    tok_rows, width = rows_in[0].shape
    for first in range(0, count, 2):
        group = range(first, min(first + 2, count))
        span = slice(first * tok_rows, (first + len(group)) * tok_rows)
        stack = lambda values: jnp.concatenate(list(values), axis=0)
        rows = stack(rows_in[i][...] for i in group)
        cotangent = stack(payloads[i][:tok_rows, :] for i in group).astype(wide)
        out_sum = jnp.zeros(rows.shape, wide)
        delta_sum = jnp.zeros(rows.shape, wide)
        for e in range(4):
            weight_in, weight_out = weights[2 * e], weights[2 * e + 1]
            gate = stack(gate_tile(payloads[i], tok_rows, place[3 + e]) for i in group)
            gate = jnp.concatenate([gate] * (width // 128), axis=1)
            active = jnp.maximum(jnp.dot(rows, weight_in[...], preferred_element_type=wide), 0.0)
            hidden = (active * active).astype(narrow)
            hiddens[e, span, :] = hidden
            scaled = (gate * cotangent).astype(narrow)
            scaleds[e, span, :] = scaled
            back_hidden = lax.dot_general(scaled, weight_out[...], contract_last, preferred_element_type=wide)
            back_pre = (back_hidden * 2.0 * active).astype(narrow)
            back_pres[e, span, :] = back_pre
            result = jnp.dot(hidden, weight_out[...], preferred_element_type=wide).astype(narrow)
            out_sum = out_sum + gate * result.astype(wide)
            back_rows = lax.dot_general(back_pre, weight_in[...], contract_last, preferred_element_type=wide)
            delta_sum = delta_sum + back_rows.astype(narrow).astype(wide)
        for i in group:
            part = slice((i - first) * tok_rows, (i - first + 1) * tok_rows)
            out = sums.pop(0)
            out[...] = delta_sum[part].astype(out.dtype)
            out = sums.pop(0)
            out[...] = out_sum[part].astype(out.dtype)


def weight_grad_body(n_rows, n_sets, place, *refs):
    rows_in = refs[:n_rows]
    sets = [refs[n_rows + 3 * i : n_rows + 3 * i + 3] for i in range(n_sets)]
    near, far, other = refs[n_rows + 3 * n_sets :]
    dot = functools.partial(lax.dot_general, dimension_numbers=contract_first, preferred_element_type=wide)
    rows = jnp.concatenate([r[...] for r in rows_in], axis=0)
    for core in (1, 0):
        for side in (1, 0):
            hidden, scaled, back_pre = (
                jnp.concatenate([values[i][core * 2 + side] for values in sets], axis=0) for i in range(3)
            )
            grad_in, grad_out = dot(rows, back_pre), dot(hidden, scaled)
            if core:
                other[2 * side] = grad_in.astype(narrow)
                other[2 * side + 1] = grad_out.astype(narrow)
            else:
                own = far if side else near
                own[0], own[1] = grad_in, grad_out


def down_grad_body(n_line, place, *refs):
    own, across, core, core_across, *deltas, core_deltas = refs[:7]
    riders, blocks = refs[7:-n_line], refs[-n_line:]
    tokens = jnp.concatenate([own[...], across[0], core[...], core_across[...]], axis=0)
    delta = jnp.concatenate([d[...] for d in deltas] + [core_deltas[0], core_deltas[1]], axis=0)
    part = lax.dot_general(tokens, delta, contract_first, preferred_element_type=wide)
    block = blocks[0].shape[0]
    targets = [out if len(out.shape) == 2 else out.at[0] for out in blocks]
    for rider, out in zip(riders, [out for out in blocks if len(out.shape) == 3]):
        out[1] = rider[...]
    for z in range(n_line):
        for back in range(n_line):

            @pl.when(lax.rem(place[0] + n_line - back, n_line) == z)
            def _(z=z, back=back):
                targets[back][...] = part[z * block : (z + 1) * block].astype(targets[back].dtype)


def token_grad_body(n_line, block, place, delta, downs, core_downs, out):
    for i, weight in enumerate((downs.at[0], downs.at[1], core_downs.at[0], core_downs.at[1])):
        owner = (place[1] ^ (i % 2)) * 2 + (place[2] ^ (i // 2))
        part = lax.dot_general(delta[...], weight[...], contract_last, preferred_element_type=wide)
        part = part.astype(narrow)
        for z in range(n_line):
            start = pl.multiple_of((z * 4 + owner) * block, block)
            out[:, pl.ds(start, block)] = part[:, z * block : (z + 1) * block]


def all_rows(tokens, routes, gate_levels, latent_grad, down_weight, expert_in, expert_out):
    tok_rows, width = tokens.shape
    latent_width = down_weight.shape[1]
    hidden_width = expert_in.shape[2]
    n_major = lax.axis_size("expert")
    n_line = n_major // 2
    n_experts = n_major * 2
    block = width // n_experts
    major = lax.axis_index("expert")
    my_core = lax.axis_index("dp")
    place = jnp.stack(
        [major // 2, major % 2, my_core]
        + [(major ^ side) * 2 + (my_core ^ core) for core in range(2) for side in range(2)]
    ).astype(jnp.int32)
    shape = jax.ShapeDtypeStruct
    rows_of = lambda kind: shape((tok_rows, latent_width), kind)

    downs = [down_weight] + [turn(down_weight, n_line, back) for back in range(1, n_line)]

    gate_rows = -(-n_experts // 16) * 16
    columns = call(
        functools.partial(columns_body, n_line, block),
        [shape((tok_rows, n_line * block), narrow)] * 2
        + [shape((2, tok_rows, n_line * block), narrow), shape((2, latent_width, hidden_width), narrow)],
        "columns",
        scratch=[pltpu.SemaphoreType.DMA((4 * n_line + 2,))],
        outside=3,
    )(place, *(pltpu.with_memory_space_constraint(value, pltpu.HBM) for value in (tokens, expert_in, expert_out)))
    stack = lambda first, second, *earlier: call(
        stack_body, [shape((2,) + first.shape, narrow)], "stack"
    )(after(place, *earlier) if earlier else place, first, second)[0]
    (payload,) = call(payload_body, [shape((tok_rows + gate_rows, latent_width), narrow)], "payload")(
        place, routes.T, gate_levels.T, latent_grad
    )
    own = columns[3]
    core_own = swap(own, n_line, 1, 0)
    across = swap(columns[2], n_line, 0, 1)
    core_tokens = [swap(after(columns[1], across, core_own), n_line, 1, 0), swap(across[1], n_line, 1, 0)]
    side_in = swap(after(expert_in[0], across), n_line, 0, 1)

    project = call(
        functools.partial(project_body, n_line),
        [shape((2, tok_rows, latent_width), wide)] * 2 + [shape((n_line * block, latent_width), narrow)],
        "project",
    )
    keep, send, down = project(after(place, payload), columns[0], across, *core_tokens, *downs)
    half, cross = call(half_body, [rows_of(wide), rows_of(narrow)], "half")(
        place, keep, swap(send, n_line, 1, 0)
    )
    payloads = [payload] + [turn(after(payload, *downs[1:]), n_line, back) for back in range(1, n_line)]
    crossed = swap(cross, n_line, 0, 1)
    (latent,) = call(add_body, [rows_of(narrow)], "latent")(
        place, half, after(crossed, side_in, *payloads[1:])
    )
    groups = [[*range(1, n_line), 0]]
    riding = range(2, n_line)
    rows = [latent] + [turn(latent, n_line, back) for back in range(1, n_line)]

    side_out = swap(after(expert_out[0], latent), n_line, 0, 1)
    core_in = swap(after(side_in, latent), n_line, 1, 0)
    core_out = swap(after(side_out, *rows[1:]), n_line, 1, 0)
    weights = [own, core_own, side_in, side_out, core_in, core_out]
    side_down = swap(after(down, *rows[1:]), n_line, 0, 1)

    both_down = stack(down, side_down)
    deltas_of, outs_of, saved = [None] * n_line, [None] * n_line, []
    done = latent
    for group in groups:
        count = len(group)
        outs = [rows_of(narrow if back else wide) for back in group for _ in range(2)]
        values = call(
            functools.partial(expert_body, count),
            outs + [shape((4, count * tok_rows, hidden_width), narrow)] * 3,
            "experts",
        )(after(place, done), *(rows[i] for i in group), *(payloads[i] for i in group), *weights)
        done, saved = values[0], saved + [list(values[-3:])]
        for i, back in enumerate(group):
            deltas_of[back], outs_of[back] = values[2 * i], values[2 * i + 1]

    def home(value, back):
        return turn(value, n_line, n_line - back) if back else value

    delta_lines = [home(value, back) for back, value in enumerate(deltas_of)]

    pair = (2, latent_width, hidden_width)
    near, far, other = call(
        functools.partial(weight_grad_body, n_line, len(groups)),
        [shape(pair, wide)] * 2 + [shape((4, latent_width, hidden_width), narrow)],
        "weight_grads",
    )(
        after(place, delta_lines[1]),
        *(rows[i] for group in groups for i in group),
        *(value for values in saved for value in values),
    )
    core_down = swap(after(both_down, near), n_line, 1, 0)
    delta_lines = [after(line, near, both_down) for line in delta_lines]
    (delta,) = call(add_body, [rows_of(narrow)], "latent_delta")(place, *delta_lines)
    side_delta = swap(delta, n_line, 0, 1)
    (grad_tokens,) = call(
        functools.partial(token_grad_body, n_line, block), [shape((tok_rows, width), narrow)], "token_grad"
    )(place, delta, both_down, core_down)
    out_lines = [outs_of[0]] + [home(outs_of[back], back) if back not in riding else None for back in range(1, n_line)]
    other = swap(after(other, delta), n_line, 1, 0)
    near, far = call(core_sum_body, [shape(pair, wide), shape(pair, narrow)], "core_sums")(
        after(place, grad_tokens), near, far, after(other, out_lines[1])
    )
    sent = far
    far = swap(after(far, side_delta), n_line, 0, 1)
    core_deltas = swap(stack(delta, side_delta, sent), n_line, 1, 0)
    blocks = call(
        functools.partial(down_grad_body, n_line),
        [
            shape((2, block, latent_width) if back in riding else (block, latent_width), narrow if back else wide)
            for back in range(n_line)
        ],
        "down_grad",
    )(place, columns[0], across, *core_tokens, delta, side_delta, core_deltas, *(outs_of[back] for back in riding))
    blocks = [blocks[0]] + [turn(blocks[back], n_line, n_line - back) for back in range(1, n_line)]
    grad_down, latent_out = call(
        functools.partial(last_body, riding), [shape((block, latent_width), wide), rows_of(narrow)], "last_sums"
    )(place, *blocks, *(line for line in out_lines if line is not None))
    grad_in, grad_out = call(
        near_body, [shape(expert_in.shape, narrow), shape(expert_out.shape, narrow)], "near_grads"
    )(place, near, far)
    return (latent_out, grad_tokens, grad_down, grad_in, grad_out)


def slot_table(routes, capacity):
    flat = routes.reshape(-1)
    count = flat.shape[0]
    order = jnp.arange(count, dtype=jnp.int32)
    same = (flat[:, None] == flat[None, :]) & (order[None, :] < order[:, None])
    placed = jnp.sum(jnp.where(same, 1, 0), axis=1).astype(jnp.int32)
    return flat * capacity + placed


def routed_rows(tokens, routes, gate_levels, latent_grad, down_weight, expert_in, expert_out):
    tok_rows = tokens.shape[0]
    top = routes.shape[1]
    latent_width = down_weight.shape[1]
    n_major = lax.axis_size("expert")
    n_minor = lax.axis_size("dp")
    n_experts = n_major * n_minor
    capacity = 3 * tok_rows * top // (2 * n_experts)
    entries = tok_rows * top
    contract_last = (((1,), (1,)), ((), ()))
    contract_first = (((0,), (0,)), ((), ()))
    full_down = lax.all_gather(down_weight, ("expert", "dp"), axis=0, tiled=True)
    latent = jnp.dot(tokens, full_down, preferred_element_type=jnp.float32)
    latent = latent.astype(jnp.bfloat16)
    dest = slot_table(routes, capacity)
    source = (
        jnp.full((n_experts * capacity,), entries, jnp.int32)
        .at[dest]
        .set(jnp.arange(entries, dtype=jnp.int32))
    )
    token_of = jnp.where(source < entries, source // top, tok_rows)
    gates = gate_levels.astype(jnp.float32) * gate_unit
    zero_row = jnp.zeros((1, latent_width), jnp.bfloat16)
    latent_pad = jnp.concatenate([latent, zero_row], axis=0)
    send_latent = latent_pad[token_of].reshape(n_major, n_minor, capacity, latent_width)
    scaled = (gates[:, :, None] * latent_grad.astype(jnp.float32)[:, None, :]).astype(jnp.bfloat16)
    scaled_pad = jnp.concatenate([scaled.reshape(entries, latent_width), zero_row], axis=0)
    send_grad = scaled_pad[source].reshape(n_major, n_minor, capacity, latent_width)
    arrived = lax.all_to_all(
        lax.all_to_all(send_latent, "expert", split_axis=0, concat_axis=0, tiled=True),
        "dp",
        split_axis=1,
        concat_axis=1,
        tiled=True,
    )
    rows = arrived.reshape(-1, latent_width)
    weight_in = expert_in[0]
    weight_out = expert_out[0]
    before = jnp.dot(rows, weight_in, preferred_element_type=jnp.float32)
    active = jnp.maximum(before, 0.0)
    hidden = (active * active).astype(jnp.bfloat16)
    result = jnp.dot(hidden, weight_out, preferred_element_type=jnp.float32).astype(jnp.bfloat16)
    returned = lax.all_to_all(
        lax.all_to_all(
            result.reshape(n_major, n_minor, capacity, latent_width),
            "expert",
            split_axis=0,
            concat_axis=0,
            tiled=True,
        ),
        "dp",
        split_axis=1,
        concat_axis=1,
        tiled=True,
    )
    picked = returned.reshape(n_experts * capacity, latent_width)[dest].astype(jnp.float32)
    picked = picked.reshape(tok_rows, top, latent_width)
    latent_out = jnp.sum(gates[:, :, None] * picked, axis=1).astype(jnp.bfloat16)
    arrived_grad = lax.all_to_all(
        lax.all_to_all(send_grad, "expert", split_axis=0, concat_axis=0, tiled=True),
        "dp",
        split_axis=1,
        concat_axis=1,
        tiled=True,
    )
    grad_rows = arrived_grad.reshape(-1, latent_width)
    back_hidden = lax.dot_general(
        grad_rows, weight_out, contract_last, preferred_element_type=jnp.float32
    )
    back_pre = (back_hidden * 2.0 * active).astype(jnp.bfloat16)
    grad_out = lax.dot_general(
        hidden, grad_rows, contract_first, preferred_element_type=jnp.float32
    ).astype(jnp.bfloat16)
    grad_in = lax.dot_general(
        rows, back_pre, contract_first, preferred_element_type=jnp.float32
    ).astype(jnp.bfloat16)
    back_rows = lax.dot_general(
        back_pre, weight_in, contract_last, preferred_element_type=jnp.float32
    ).astype(jnp.bfloat16)
    came_back = lax.all_to_all(
        lax.all_to_all(
            back_rows.reshape(n_major, n_minor, capacity, latent_width),
            "expert",
            split_axis=0,
            concat_axis=0,
            tiled=True,
        ),
        "dp",
        split_axis=1,
        concat_axis=1,
        tiled=True,
    )
    gathered_back = came_back.reshape(n_experts * capacity, latent_width)[dest].astype(jnp.float32)
    latent_delta = jnp.sum(gathered_back.reshape(tok_rows, top, latent_width), axis=1).astype(
        jnp.bfloat16
    )
    grad_tokens = lax.dot_general(
        latent_delta, full_down, contract_last, preferred_element_type=jnp.float32
    )
    grad_tokens = grad_tokens.astype(jnp.bfloat16)
    grad_down = lax.psum_scatter(
        lax.dot_general(tokens, latent_delta, contract_first, preferred_element_type=jnp.float32),
        ("expert", "dp"),
        scatter_dimension=0,
        tiled=True,
    )
    return (latent_out, grad_tokens, grad_down, grad_in[None], grad_out[None])


def on_device(tokens, routes, *others):
    n_major = lax.axis_size("expert")
    n_experts = n_major * lax.axis_size("dp")
    few = n_experts <= 2 * routes.shape[1] and n_major % 2 == 0 and n_major >= 6 and lax.axis_size("dp") == 2
    return (all_rows if few else routed_rows)(tokens, routes, *others)


def solution(mesh):
    in_specs = (
        P(("group", "expert", "dp"), None),
        P(("group", "expert", "dp"), None),
        P(("group", "expert", "dp"), None),
        P(("group", "expert", "dp"), None),
        P(("expert", "dp"), None),
        P(("expert", "dp"), None, None),
        P(("expert", "dp"), None, None),
    )
    out_specs = (
        P(("group", "expert", "dp"), None),
        P(("group", "expert", "dp"), None),
        P(("group", "expert", "dp"), None),
        P(("group", "expert", "dp"), None, None),
        P(("group", "expert", "dp"), None, None),
    )
    return jax.shard_map(
        on_device, mesh=mesh, in_specs=in_specs, out_specs=out_specs, check_vma=False
    )
```

```python
import functools

import jax
import jax.numpy as jnp
from jax import lax
from jax.experimental import pallas as pl
from jax.experimental.pallas import tpu as pltpu
from jax.sharding import PartitionSpec as P

gate_unit = 1.0 / 1024.0
contract_last = (((1,), (1,)), ((), ()))
contract_first = (((0,), (0,)), ((), ()))
plane = ("expert", "dp")
wide = jnp.float32
narrow = jnp.bfloat16


def device_pairs(n_line, move):
    pairs = []
    for z in range(n_line):
        for x in range(2):
            for c in range(2):
                to_z, to_x, to_c = move(z, x, c)
                pairs.append(((z * 2 + x) * 2 + c, (to_z * 2 + to_x) * 2 + to_c))
    return pairs


def turn(value, n_line, by):
    return lax.ppermute(value, plane, device_pairs(n_line, lambda z, x, c: ((z + by) % n_line, x, c)))


def swap(value, n_line, core, side):
    return lax.ppermute(value, plane, device_pairs(n_line, lambda z, x, c: (z, x ^ side, c ^ core)))


def after(value, *earlier):
    return lax.optimization_barrier((value,) + earlier)[0]


def call(body, outs, name, scratch=(), outside=0):
    vmem = pl.BlockSpec(memory_space=pltpu.VMEM)
    outer = pl.BlockSpec(memory_space=pltpu.HBM)

    def run(place, *operands):
        return pl.pallas_call(
            body,
            out_shape=outs,
            in_specs=[pl.BlockSpec(memory_space=pltpu.SMEM)]
            + [outer] * outside
            + [vmem] * (len(operands) - outside),
            out_specs=[vmem] * len(outs),
            scratch_shapes=list(scratch),
            compiler_params=pltpu.CompilerParams(vmem_limit_bytes=40 * 1024 * 1024),
            cost_estimate=pl.CostEstimate(flops=0, bytes_accessed=0, transcendentals=0),
            name=name,
        )(place, *operands)

    return run


def columns_body(n_line, block, place, tokens, expert_in, expert_out, *refs):
    own, other, across, weights, sems = refs
    pieces = (own, across.at[0], other, across.at[1])
    copies = []
    for i, weight in enumerate((expert_in, expert_out)):
        copies.append(pltpu.make_async_copy(weight, weights.at[pl.ds(i, 1)], sems.at[i]))
    for core in range(2):
        for side in range(2):
            owner = (place[1] ^ side) * 2 + (place[2] ^ core)
            for z in range(n_line):
                start = pl.multiple_of((z * 4 + owner) * block, block)
                piece = pieces[core * 2 + side].at[:, pl.ds(z * block, block)]
                copies.append(
                    pltpu.make_async_copy(tokens.at[:, pl.ds(start, block)], piece, sems.at[len(copies)])
                )
    for copy in copies:
        copy.start()
    for copy in copies:
        copy.wait()


def stack_body(place, first, second, out):
    out[0], out[1] = first[...], second[...]


def add_body(place, *refs):
    total = refs[0][...].astype(wide)
    for value in refs[1:-1]:
        total = total + value[...].astype(wide)
    refs[-1][...] = total.astype(refs[-1].dtype)


def half_body(place, keep, arrived, mine, other):
    mine[...] = keep[0] + arrived[0]
    other[...] = (keep[1] + arrived[1]).astype(narrow)


def core_sum_body(place, near, far, arrived, near_out, far_out):
    far_out[...] = (far[...] + arrived[2:].astype(wide)).astype(narrow)
    near_out[...] = near[...] + arrived[:2].astype(wide)


def near_body(place, near, far, grad_in, grad_out):
    for i, out in enumerate((grad_in, grad_out)):
        out[0] = (near[i] + far[i].astype(wide)).astype(narrow)


def last_body(riding, place, *refs):
    n_line = (len(refs) - 2 + len(riding)) // 2
    blocks, pieces, grad_down, combined = refs[:n_line], list(refs[n_line:-2]), refs[-2], refs[-1]
    total = blocks[0][...]
    out_total = pieces.pop(0)[...]
    for back in range(1, n_line):
        block = blocks[back].at[0] if back in riding else blocks[back]
        piece = blocks[back].at[1] if back in riding else pieces.pop(0)
        total = total + block[...].astype(wide)
        out_total = out_total + piece[...].astype(wide)
    grad_down[...] = total
    combined[...] = out_total.astype(narrow)


def payload_body(place, routes, levels, cotangent, payload):
    tok_rows = cotangent.shape[0]
    gate_rows = payload.shape[0] - tok_rows
    payload[:tok_rows, :] = cotangent[...]
    expert = lax.broadcasted_iota(jnp.int32, (gate_rows, tok_rows), 0)
    total = jnp.zeros((gate_rows, tok_rows), jnp.int32)
    for k in range(routes.shape[0]):
        total = total + jnp.where(expert == routes[k : k + 1, :], levels[k : k + 1, :], 0)
    low = total & 31
    payload[tok_rows:, :tok_rows] = (total - low).astype(wide).astype(narrow)
    payload[tok_rows:, tok_rows : 2 * tok_rows] = low.astype(wide).astype(narrow)
    rest = payload.shape[1] - 2 * tok_rows
    payload[tok_rows:, 2 * tok_rows :] = jnp.zeros((gate_rows, rest), narrow)


def project_body(n_line, place, *refs):
    own, across, core, core_across, *downs = refs[: 4 + n_line]
    pieces = (own, across.at[0], core, core_across)
    keep, send, down = refs[4 + n_line :]
    block = downs[0].shape[0]
    for back in range(n_line):
        z = lax.rem(place[0] + n_line - back, n_line)
        down[pl.ds(pl.multiple_of(z * block, block), block), :] = downs[back][...]
    for core, out in ((1, send), (0, keep)):
        for side in range(2):
            out[side] = jnp.dot(pieces[core * 2 + side][...], down[...], preferred_element_type=wide)


def gate_tile(payload, tok_rows, expert):
    packed = payload[tok_rows:, :]
    rows = lax.broadcasted_iota(jnp.int32, (packed.shape[0], 128), 0)
    pick = jnp.where(rows == expert, 1.0, 0.0).astype(narrow)
    dot = functools.partial(lax.dot_general, dimension_numbers=contract_first, preferred_element_type=wide)
    total = dot(packed[:, :tok_rows], pick) + dot(packed[:, tok_rows : 2 * tok_rows], pick)
    return total * gate_unit


def expert_body(count, place, *refs):
    rows_in, payloads = refs[:count], refs[count : 2 * count]
    own, core, *sides = refs[2 * count : 2 * count + 6]
    weights = (own.at[0], own.at[1], sides[0], sides[1], core.at[0], core.at[1], sides[2], sides[3])
    outs = refs[2 * count + 6 :]
    *sums, hiddens, scaleds, back_pres = outs
    tok_rows, width = rows_in[0].shape
    for first in range(0, count, 2):
        group = range(first, min(first + 2, count))
        span = slice(first * tok_rows, (first + len(group)) * tok_rows)
        stack = lambda values: jnp.concatenate(list(values), axis=0)
        rows = stack(rows_in[i][...] for i in group)
        cotangent = stack(payloads[i][:tok_rows, :] for i in group).astype(wide)
        out_sum = jnp.zeros(rows.shape, wide)
        delta_sum = jnp.zeros(rows.shape, wide)
        for e in range(4):
            weight_in, weight_out = weights[2 * e], weights[2 * e + 1]
            gate = stack(gate_tile(payloads[i], tok_rows, place[3 + e]) for i in group)
            gate = jnp.concatenate([gate] * (width // 128), axis=1)
            active = jnp.maximum(jnp.dot(rows, weight_in[...], preferred_element_type=wide), 0.0)
            hidden = (active * active).astype(narrow)
            hiddens[e, span, :] = hidden
            scaled = (gate * cotangent).astype(narrow)
            scaleds[e, span, :] = scaled
            back_hidden = lax.dot_general(scaled, weight_out[...], contract_last, preferred_element_type=wide)
            back_pre = (back_hidden * 2.0 * active).astype(narrow)
            back_pres[e, span, :] = back_pre
            result = jnp.dot(hidden, weight_out[...], preferred_element_type=wide).astype(narrow)
            out_sum = out_sum + gate * result.astype(wide)
            back_rows = lax.dot_general(back_pre, weight_in[...], contract_last, preferred_element_type=wide)
            delta_sum = delta_sum + back_rows.astype(narrow).astype(wide)
        for i in group:
            part = slice((i - first) * tok_rows, (i - first + 1) * tok_rows)
            out = sums.pop(0)
            out[...] = delta_sum[part].astype(out.dtype)
            out = sums.pop(0)
            out[...] = out_sum[part].astype(out.dtype)


def weight_grad_body(n_rows, n_sets, place, *refs):
    rows_in = refs[:n_rows]
    sets = [refs[n_rows + 3 * i : n_rows + 3 * i + 3] for i in range(n_sets)]
    near, far, other = refs[n_rows + 3 * n_sets :]
    dot = functools.partial(lax.dot_general, dimension_numbers=contract_first, preferred_element_type=wide)
    rows = jnp.concatenate([r[...] for r in rows_in], axis=0)
    for core in (1, 0):
        for side in (1, 0):
            hidden, scaled, back_pre = (
                jnp.concatenate([values[i][core * 2 + side] for values in sets], axis=0) for i in range(3)
            )
            grad_in, grad_out = dot(rows, back_pre), dot(hidden, scaled)
            if core:
                other[2 * side] = grad_in.astype(narrow)
                other[2 * side + 1] = grad_out.astype(narrow)
            else:
                own = far if side else near
                own[0], own[1] = grad_in, grad_out


def down_grad_body(n_line, place, *refs):
    own, across, core, core_across, *deltas, core_deltas = refs[:7]
    riders, blocks = refs[7:-n_line], refs[-n_line:]
    tokens = jnp.concatenate([own[...], across[0], core[...], core_across[...]], axis=0)
    delta = jnp.concatenate([d[...] for d in deltas] + [core_deltas[0], core_deltas[1]], axis=0)
    part = lax.dot_general(tokens, delta, contract_first, preferred_element_type=wide)
    block = blocks[0].shape[0]
    targets = [out if len(out.shape) == 2 else out.at[0] for out in blocks]
    for rider, out in zip(riders, [out for out in blocks if len(out.shape) == 3]):
        out[1] = rider[...]
    for z in range(n_line):
        for back in range(n_line):

            @pl.when(lax.rem(place[0] + n_line - back, n_line) == z)
            def _(z=z, back=back):
                targets[back][...] = part[z * block : (z + 1) * block].astype(targets[back].dtype)


def token_grad_body(n_line, block, place, delta, downs, core_downs, out):
    for i, weight in enumerate((downs.at[0], downs.at[1], core_downs.at[0], core_downs.at[1])):
        owner = (place[1] ^ (i % 2)) * 2 + (place[2] ^ (i // 2))
        part = lax.dot_general(delta[...], weight[...], contract_last, preferred_element_type=wide)
        part = part.astype(narrow)
        for z in range(n_line):
            start = pl.multiple_of((z * 4 + owner) * block, block)
            out[:, pl.ds(start, block)] = part[:, z * block : (z + 1) * block]


def all_rows(tokens, routes, gate_levels, latent_grad, down_weight, expert_in, expert_out):
    tok_rows, width = tokens.shape
    latent_width = down_weight.shape[1]
    hidden_width = expert_in.shape[2]
    n_major = lax.axis_size("expert")
    n_line = n_major // 2
    n_experts = n_major * 2
    block = width // n_experts
    major = lax.axis_index("expert")
    my_core = lax.axis_index("dp")
    place = jnp.stack(
        [major // 2, major % 2, my_core]
        + [(major ^ side) * 2 + (my_core ^ core) for core in range(2) for side in range(2)]
    ).astype(jnp.int32)
    shape = jax.ShapeDtypeStruct
    rows_of = lambda kind: shape((tok_rows, latent_width), kind)

    downs = [down_weight] + [turn(down_weight, n_line, back) for back in range(1, n_line)]

    gate_rows = -(-n_experts // 16) * 16
    columns = call(
        functools.partial(columns_body, n_line, block),
        [shape((tok_rows, n_line * block), narrow)] * 2
        + [shape((2, tok_rows, n_line * block), narrow), shape((2, latent_width, hidden_width), narrow)],
        "columns",
        scratch=[pltpu.SemaphoreType.DMA((4 * n_line + 2,))],
        outside=3,
    )(place, *(pltpu.with_memory_space_constraint(value, pltpu.HBM) for value in (tokens, expert_in, expert_out)))
    stack = lambda first, second, *earlier: call(
        stack_body, [shape((2,) + first.shape, narrow)], "stack"
    )(after(place, *earlier) if earlier else place, first, second)[0]
    (payload,) = call(payload_body, [shape((tok_rows + gate_rows, latent_width), narrow)], "payload")(
        place, routes.T, gate_levels.T, latent_grad
    )
    own = columns[3]
    core_own = swap(own, n_line, 1, 0)
    across = swap(columns[2], n_line, 0, 1)
    core_tokens = [swap(after(columns[1], across, core_own), n_line, 1, 0), swap(across[1], n_line, 1, 0)]
    side_in = swap(after(expert_in[0], across), n_line, 0, 1)

    project = call(
        functools.partial(project_body, n_line),
        [shape((2, tok_rows, latent_width), wide)] * 2 + [shape((n_line * block, latent_width), narrow)],
        "project",
    )
    keep, send, down = project(after(place, payload), columns[0], across, *core_tokens, *downs)
    half, cross = call(half_body, [rows_of(wide), rows_of(narrow)], "half")(
        place, keep, swap(send, n_line, 1, 0)
    )
    payloads = [payload] + [turn(after(payload, *downs[1:]), n_line, back) for back in range(1, n_line)]
    crossed = swap(cross, n_line, 0, 1)
    (latent,) = call(add_body, [rows_of(narrow)], "latent")(
        place, half, after(crossed, side_in, *payloads[1:])
    )
    groups = [[*range(1, n_line), 0]]
    riding = range(2, n_line)
    rows = [latent] + [turn(latent, n_line, back) for back in range(1, n_line)]

    side_out = swap(after(expert_out[0], latent), n_line, 0, 1)
    core_in = swap(after(side_in, latent), n_line, 1, 0)
    core_out = swap(after(side_out, rows[1]), n_line, 1, 0)
    weights = [own, core_own, side_in, side_out, core_in, core_out]
    side_down = swap(after(down, *rows[1:]), n_line, 0, 1)

    both_down = stack(down, side_down)
    deltas_of, outs_of, saved = [None] * n_line, [None] * n_line, []
    done = latent
    for group in groups:
        count = len(group)
        outs = [rows_of(narrow if back else wide) for back in group for _ in range(2)]
        values = call(
            functools.partial(expert_body, count),
            outs + [shape((4, count * tok_rows, hidden_width), narrow)] * 3,
            "experts",
        )(after(place, done), *(rows[i] for i in group), *(payloads[i] for i in group), *weights)
        done, saved = values[0], saved + [list(values[-3:])]
        for i, back in enumerate(group):
            deltas_of[back], outs_of[back] = values[2 * i], values[2 * i + 1]

    def home(value, back):
        return turn(value, n_line, n_line - back) if back else value

    delta_lines = [home(value, back) for back, value in enumerate(deltas_of)]

    pair = (2, latent_width, hidden_width)
    near, far, other = call(
        functools.partial(weight_grad_body, n_line, len(groups)),
        [shape(pair, wide)] * 2 + [shape((4, latent_width, hidden_width), narrow)],
        "weight_grads",
    )(
        after(place, delta_lines[1]),
        *(rows[i] for group in groups for i in group),
        *(value for values in saved for value in values),
    )
    delta_lines = [after(line, near, both_down) for line in delta_lines]
    (delta,) = call(add_body, [rows_of(narrow)], "latent_delta")(place, *delta_lines)
    side_delta = swap(delta, n_line, 0, 1)
    out_lines = [outs_of[0]] + [home(outs_of[back], back) if back not in riding else None for back in range(1, n_line)]
    other = swap(after(other, delta), n_line, 1, 0)
    near, far = call(core_sum_body, [shape(pair, wide), shape(pair, narrow)], "core_sums")(
        place, near, far, after(other, out_lines[1])
    )
    sent = far
    far = swap(after(far, side_delta), n_line, 0, 1)
    core_deltas = swap(stack(delta, side_delta, sent), n_line, 1, 0)
    blocks = call(
        functools.partial(down_grad_body, n_line),
        [
            shape((2, block, latent_width) if back in riding else (block, latent_width), narrow if back else wide)
            for back in range(n_line)
        ],
        "down_grad",
    )(place, columns[0], across, *core_tokens, delta, side_delta, core_deltas, *(outs_of[back] for back in riding))
    core_down = swap(after(both_down, blocks[1]), n_line, 1, 0)
    (grad_tokens,) = call(
        functools.partial(token_grad_body, n_line, block), [shape((tok_rows, width), narrow)], "token_grad"
    )(place, after(delta, blocks[1]), both_down, core_down)
    blocks = [blocks[0]] + [turn(blocks[back], n_line, n_line - back) for back in range(1, n_line)]
    grad_down, latent_out = call(
        functools.partial(last_body, riding), [shape((block, latent_width), wide), rows_of(narrow)], "last_sums"
    )(after(place, grad_tokens), *blocks, *(line for line in out_lines if line is not None))
    grad_in, grad_out = call(
        near_body, [shape(expert_in.shape, narrow), shape(expert_out.shape, narrow)], "near_grads"
    )(place, near, far)
    return (latent_out, grad_tokens, grad_down, grad_in, grad_out)


def slot_table(routes, capacity):
    flat = routes.reshape(-1)
    count = flat.shape[0]
    order = jnp.arange(count, dtype=jnp.int32)
    same = (flat[:, None] == flat[None, :]) & (order[None, :] < order[:, None])
    placed = jnp.sum(jnp.where(same, 1, 0), axis=1).astype(jnp.int32)
    return flat * capacity + placed


def routed_rows(tokens, routes, gate_levels, latent_grad, down_weight, expert_in, expert_out):
    tok_rows = tokens.shape[0]
    top = routes.shape[1]
    latent_width = down_weight.shape[1]
    n_major = lax.axis_size("expert")
    n_minor = lax.axis_size("dp")
    n_experts = n_major * n_minor
    capacity = 3 * tok_rows * top // (2 * n_experts)
    entries = tok_rows * top
    contract_last = (((1,), (1,)), ((), ()))
    contract_first = (((0,), (0,)), ((), ()))
    full_down = lax.all_gather(down_weight, ("expert", "dp"), axis=0, tiled=True)
    latent = jnp.dot(tokens, full_down, preferred_element_type=jnp.float32)
    latent = latent.astype(jnp.bfloat16)
    dest = slot_table(routes, capacity)
    source = (
        jnp.full((n_experts * capacity,), entries, jnp.int32)
        .at[dest]
        .set(jnp.arange(entries, dtype=jnp.int32))
    )
    token_of = jnp.where(source < entries, source // top, tok_rows)
    gates = gate_levels.astype(jnp.float32) * gate_unit
    zero_row = jnp.zeros((1, latent_width), jnp.bfloat16)
    latent_pad = jnp.concatenate([latent, zero_row], axis=0)
    send_latent = latent_pad[token_of].reshape(n_major, n_minor, capacity, latent_width)
    scaled = (gates[:, :, None] * latent_grad.astype(jnp.float32)[:, None, :]).astype(jnp.bfloat16)
    scaled_pad = jnp.concatenate([scaled.reshape(entries, latent_width), zero_row], axis=0)
    send_grad = scaled_pad[source].reshape(n_major, n_minor, capacity, latent_width)
    arrived = lax.all_to_all(
        lax.all_to_all(send_latent, "expert", split_axis=0, concat_axis=0, tiled=True),
        "dp",
        split_axis=1,
        concat_axis=1,
        tiled=True,
    )
    rows = arrived.reshape(-1, latent_width)
    weight_in = expert_in[0]
    weight_out = expert_out[0]
    before = jnp.dot(rows, weight_in, preferred_element_type=jnp.float32)
    active = jnp.maximum(before, 0.0)
    hidden = (active * active).astype(jnp.bfloat16)
    result = jnp.dot(hidden, weight_out, preferred_element_type=jnp.float32).astype(jnp.bfloat16)
    returned = lax.all_to_all(
        lax.all_to_all(
            result.reshape(n_major, n_minor, capacity, latent_width),
            "expert",
            split_axis=0,
            concat_axis=0,
            tiled=True,
        ),
        "dp",
        split_axis=1,
        concat_axis=1,
        tiled=True,
    )
    picked = returned.reshape(n_experts * capacity, latent_width)[dest].astype(jnp.float32)
    picked = picked.reshape(tok_rows, top, latent_width)
    latent_out = jnp.sum(gates[:, :, None] * picked, axis=1).astype(jnp.bfloat16)
    arrived_grad = lax.all_to_all(
        lax.all_to_all(send_grad, "expert", split_axis=0, concat_axis=0, tiled=True),
        "dp",
        split_axis=1,
        concat_axis=1,
        tiled=True,
    )
    grad_rows = arrived_grad.reshape(-1, latent_width)
    back_hidden = lax.dot_general(
        grad_rows, weight_out, contract_last, preferred_element_type=jnp.float32
    )
    back_pre = (back_hidden * 2.0 * active).astype(jnp.bfloat16)
    grad_out = lax.dot_general(
        hidden, grad_rows, contract_first, preferred_element_type=jnp.float32
    ).astype(jnp.bfloat16)
    grad_in = lax.dot_general(
        rows, back_pre, contract_first, preferred_element_type=jnp.float32
    ).astype(jnp.bfloat16)
    back_rows = lax.dot_general(
        back_pre, weight_in, contract_last, preferred_element_type=jnp.float32
    ).astype(jnp.bfloat16)
    came_back = lax.all_to_all(
        lax.all_to_all(
            back_rows.reshape(n_major, n_minor, capacity, latent_width),
            "expert",
            split_axis=0,
            concat_axis=0,
            tiled=True,
        ),
        "dp",
        split_axis=1,
        concat_axis=1,
        tiled=True,
    )
    gathered_back = came_back.reshape(n_experts * capacity, latent_width)[dest].astype(jnp.float32)
    latent_delta = jnp.sum(gathered_back.reshape(tok_rows, top, latent_width), axis=1).astype(
        jnp.bfloat16
    )
    grad_tokens = lax.dot_general(
        latent_delta, full_down, contract_last, preferred_element_type=jnp.float32
    )
    grad_tokens = grad_tokens.astype(jnp.bfloat16)
    grad_down = lax.psum_scatter(
        lax.dot_general(tokens, latent_delta, contract_first, preferred_element_type=jnp.float32),
        ("expert", "dp"),
        scatter_dimension=0,
        tiled=True,
    )
    return (latent_out, grad_tokens, grad_down, grad_in[None], grad_out[None])


def on_device(tokens, routes, *others):
    n_major = lax.axis_size("expert")
    n_experts = n_major * lax.axis_size("dp")
    few = n_experts <= 2 * routes.shape[1] and n_major % 2 == 0 and n_major >= 6 and lax.axis_size("dp") == 2
    return (all_rows if few else routed_rows)(tokens, routes, *others)


def solution(mesh):
    in_specs = (
        P(("group", "expert", "dp"), None),
        P(("group", "expert", "dp"), None),
        P(("group", "expert", "dp"), None),
        P(("group", "expert", "dp"), None),
        P(("expert", "dp"), None),
        P(("expert", "dp"), None, None),
        P(("expert", "dp"), None, None),
    )
    out_specs = (
        P(("group", "expert", "dp"), None),
        P(("group", "expert", "dp"), None),
        P(("group", "expert", "dp"), None),
        P(("group", "expert", "dp"), None, None),
        P(("group", "expert", "dp"), None, None),
    )
    return jax.shard_map(
        on_device, mesh=mesh, in_specs=in_specs, out_specs=out_specs, check_vma=False
    )
```

```python
import functools

import jax
import jax.numpy as jnp
from jax import lax
from jax.experimental import pallas as pl
from jax.experimental.pallas import tpu as pltpu
from jax.sharding import PartitionSpec as P

gate_unit = 1.0 / 1024.0
contract_last = (((1,), (1,)), ((), ()))
contract_first = (((0,), (0,)), ((), ()))
plane = ("expert", "dp")
wide = jnp.float32
narrow = jnp.bfloat16


def device_pairs(n_line, move):
    pairs = []
    for z in range(n_line):
        for x in range(2):
            for c in range(2):
                to_z, to_x, to_c = move(z, x, c)
                pairs.append(((z * 2 + x) * 2 + c, (to_z * 2 + to_x) * 2 + to_c))
    return pairs


def turn(value, n_line, by):
    return lax.ppermute(value, plane, device_pairs(n_line, lambda z, x, c: ((z + by) % n_line, x, c)))


def swap(value, n_line, core, side):
    return lax.ppermute(value, plane, device_pairs(n_line, lambda z, x, c: (z, x ^ side, c ^ core)))


def after(value, *earlier):
    return lax.optimization_barrier((value,) + earlier)[0]


def call(body, outs, name, scratch=(), outside=0, flops=0):
    vmem = pl.BlockSpec(memory_space=pltpu.VMEM)
    outer = pl.BlockSpec(memory_space=pltpu.HBM)

    def run(place, *operands):
        return pl.pallas_call(
            body,
            out_shape=outs,
            in_specs=[pl.BlockSpec(memory_space=pltpu.SMEM)]
            + [outer] * outside
            + [vmem] * (len(operands) - outside),
            out_specs=[vmem] * len(outs),
            scratch_shapes=list(scratch),
            compiler_params=pltpu.CompilerParams(vmem_limit_bytes=40 * 1024 * 1024),
            cost_estimate=pl.CostEstimate(flops=flops, bytes_accessed=0, transcendentals=0),
            name=name,
        )(place, *operands)

    return run


def columns_body(n_line, block, place, tokens, expert_in, expert_out, *refs):
    own, other, across, weights, sems = refs
    pieces = (own, across.at[0], other, across.at[1])
    copies = []
    for i, weight in enumerate((expert_in, expert_out)):
        copies.append(pltpu.make_async_copy(weight, weights.at[pl.ds(i, 1)], sems.at[i]))
    for core in range(2):
        for side in range(2):
            owner = (place[1] ^ side) * 2 + (place[2] ^ core)
            for z in range(n_line):
                start = pl.multiple_of((z * 4 + owner) * block, block)
                piece = pieces[core * 2 + side].at[:, pl.ds(z * block, block)]
                copies.append(
                    pltpu.make_async_copy(tokens.at[:, pl.ds(start, block)], piece, sems.at[len(copies)])
                )
    for copy in copies:
        copy.start()
    for copy in copies:
        copy.wait()


def stack_body(place, first, second, out):
    out[0], out[1] = first[...], second[...]


def add_body(place, *refs):
    total = refs[0][...].astype(wide)
    for value in refs[1:-1]:
        total = total + value[...].astype(wide)
    refs[-1][...] = total.astype(refs[-1].dtype)


def half_body(place, keep, arrived, mine, other):
    mine[...] = keep[0] + arrived[0]
    other[...] = (keep[1] + arrived[1]).astype(narrow)


def far_body(place, far, arrived, first, rest):
    split, width = first.shape[0], far.shape[1]
    total = [far[i] + arrived[i].astype(wide) for i in range(2)]
    first[...] = total[0][:split].astype(narrow)
    rest[: width - split] = total[0][split:].astype(narrow)
    rest[width - split :] = total[1].astype(narrow)


def pack_body(place, grads, down, side_down, out):
    out[:2] = grads[...]
    out[2], out[3] = down[...], side_down[...]


def last_body(riding, n_line, place, near, others, first, rest, *refs):
    blocks, pieces = refs[:n_line], list(refs[n_line:-4])
    grad_down, combined, *grads = refs[-4:]
    split = grads[0].shape[1] - first.shape[0]
    far = (jnp.concatenate([first[...], rest[:split]], axis=0), rest[split:])
    for i, out in enumerate(grads):
        out[0] = (near[i] + others[i].astype(wide) + far[i].astype(wide)).astype(narrow)
    total = blocks[0][...]
    out_total = pieces.pop(0)[...]
    for back in range(1, n_line):
        block = blocks[back].at[0] if back in riding else blocks[back]
        piece = blocks[back].at[1] if back in riding else pieces.pop(0)
        total = total + block[...].astype(wide)
        out_total = out_total + piece[...].astype(wide)
    grad_down[...] = total
    combined[...] = out_total.astype(narrow)


def payload_body(place, routes, levels, cotangent, payload):
    tok_rows = cotangent.shape[0]
    gate_rows = payload.shape[0] - tok_rows
    payload[:tok_rows, :] = cotangent[...]
    expert = lax.broadcasted_iota(jnp.int32, (gate_rows, tok_rows), 0)
    total = jnp.zeros((gate_rows, tok_rows), jnp.int32)
    for k in range(routes.shape[0]):
        total = total + jnp.where(expert == routes[k : k + 1, :], levels[k : k + 1, :], 0)
    low = total & 31
    payload[tok_rows:, :tok_rows] = (total - low).astype(wide).astype(narrow)
    payload[tok_rows:, tok_rows : 2 * tok_rows] = low.astype(wide).astype(narrow)
    rest = payload.shape[1] - 2 * tok_rows
    payload[tok_rows:, 2 * tok_rows :] = jnp.zeros((gate_rows, rest), narrow)


def project_body(n_line, place, *refs):
    own, across, core, core_across, *downs = refs[: 4 + n_line]
    pieces = (own, across.at[0], core, core_across)
    keep, send, down = refs[4 + n_line :]
    block = downs[0].shape[0]
    for back in range(n_line):
        z = lax.rem(place[0] + n_line - back, n_line)
        down[pl.ds(pl.multiple_of(z * block, block), block), :] = downs[back][...]
    for core, out in ((1, send), (0, keep)):
        for side in range(2):
            out[side] = jnp.dot(pieces[core * 2 + side][...], down[...], preferred_element_type=wide)


def gate_tile(payload, tok_rows, expert):
    packed = payload[tok_rows:, :]
    rows = lax.broadcasted_iota(jnp.int32, (packed.shape[0], 128), 0)
    pick = jnp.where(rows == expert, 1.0, 0.0).astype(narrow)
    dot = functools.partial(lax.dot_general, dimension_numbers=contract_first, preferred_element_type=wide)
    total = dot(packed[:, :tok_rows], pick) + dot(packed[:, tok_rows : 2 * tok_rows], pick)
    return total * gate_unit


def expert_body(count, place, *refs):
    rows_in, payloads = refs[:count], refs[count : 2 * count]
    own, core, *sides = refs[2 * count : 2 * count + 6]
    weights = (own.at[0], own.at[1], sides[0], sides[1], core.at[0], core.at[1], sides[2], sides[3])
    outs = refs[2 * count + 6 :]
    *sums, hiddens, scaleds, back_pres = outs
    tok_rows, width = rows_in[0].shape
    for first in range(0, count, 2):
        group = range(first, min(first + 2, count))
        span = slice(first * tok_rows, (first + len(group)) * tok_rows)
        stack = lambda values: jnp.concatenate(list(values), axis=0)
        rows = stack(rows_in[i][...] for i in group)
        cotangent = stack(payloads[i][:tok_rows, :] for i in group).astype(wide)
        out_sum = jnp.zeros(rows.shape, wide)
        delta_sum = jnp.zeros(rows.shape, wide)
        for e in range(4):
            weight_in, weight_out = weights[2 * e], weights[2 * e + 1]
            gate = stack(gate_tile(payloads[i], tok_rows, place[3 + e]) for i in group)
            gate = jnp.concatenate([gate] * (width // 128), axis=1)
            active = jnp.maximum(jnp.dot(rows, weight_in[...], preferred_element_type=wide), 0.0)
            hidden = (active * active).astype(narrow)
            hiddens[e, span, :] = hidden
            scaled = (gate * cotangent).astype(narrow)
            scaleds[e, span, :] = scaled
            back_hidden = lax.dot_general(scaled, weight_out[...], contract_last, preferred_element_type=wide)
            back_pre = (back_hidden * 2.0 * active).astype(narrow)
            back_pres[e, span, :] = back_pre
            result = jnp.dot(hidden, weight_out[...], preferred_element_type=wide).astype(narrow)
            out_sum = out_sum + gate * result.astype(wide)
            back_rows = lax.dot_general(back_pre, weight_in[...], contract_last, preferred_element_type=wide)
            delta_sum = delta_sum + back_rows.astype(narrow).astype(wide)
        for i in group:
            part = slice((i - first) * tok_rows, (i - first + 1) * tok_rows)
            out = sums.pop(0)
            out[...] = delta_sum[part].astype(out.dtype)
            out = sums.pop(0)
            out[...] = out_sum[part].astype(out.dtype)


def weight_grad_body(n_rows, n_sets, place, *refs):
    rows_in = refs[:n_rows]
    sets = [refs[n_rows + 3 * i : n_rows + 3 * i + 3] for i in range(n_sets)]
    near, far, near_other, far_other = refs[n_rows + 3 * n_sets :]
    dot = functools.partial(lax.dot_general, dimension_numbers=contract_first, preferred_element_type=wide)
    rows = jnp.concatenate([r[...] for r in rows_in], axis=0)
    for core in (1, 0):
        for side in (1, 0):
            hidden, scaled, back_pre = (
                jnp.concatenate([values[i][core * 2 + side] for values in sets], axis=0) for i in range(3)
            )
            grad_in, grad_out = dot(rows, back_pre), dot(hidden, scaled)
            out = ((near, far), (near_other, far_other))[core][side]
            out[0], out[1] = grad_in.astype(out.dtype), grad_out.astype(out.dtype)


def down_grad_body(n_line, place, *refs):
    own, across, core, core_across, *deltas, core_deltas = refs[:7]
    riders, blocks = refs[7:-n_line], refs[-n_line:]
    tokens = jnp.concatenate([own[...], across[0], core[...], core_across[...]], axis=0)
    delta = jnp.concatenate([d[...] for d in deltas] + [core_deltas[0], core_deltas[1]], axis=0)
    part = lax.dot_general(tokens, delta, contract_first, preferred_element_type=wide)
    block = blocks[0].shape[0]
    targets = [out if len(out.shape) == 2 else out.at[0] for out in blocks]
    for rider, out in zip(riders, [out for out in blocks if len(out.shape) == 3]):
        out[1] = rider[...]
    for z in range(n_line):
        for back in range(n_line):

            @pl.when(lax.rem(place[0] + n_line - back, n_line) == z)
            def _(z=z, back=back):
                targets[back][...] = part[z * block : (z + 1) * block].astype(targets[back].dtype)


def token_grad_body(n_line, block, place, delta, held, arrived, out):
    for i, weight in enumerate((held.at[2], held.at[3], arrived.at[2], arrived.at[3])):
        owner = (place[1] ^ (i % 2)) * 2 + (place[2] ^ (i // 2))
        part = lax.dot_general(delta[...], weight[...], contract_last, preferred_element_type=wide)
        part = part.astype(narrow)
        for z in range(n_line):
            start = pl.multiple_of((z * 4 + owner) * block, block)
            out[:, pl.ds(start, block)] = part[:, z * block : (z + 1) * block]


def all_rows(tokens, routes, gate_levels, latent_grad, down_weight, expert_in, expert_out):
    tok_rows, width = tokens.shape
    latent_width = down_weight.shape[1]
    hidden_width = expert_in.shape[2]
    n_major = lax.axis_size("expert")
    n_line = n_major // 2
    n_experts = n_major * 2
    block = width // n_experts
    major = lax.axis_index("expert")
    my_core = lax.axis_index("dp")
    place = jnp.stack(
        [major // 2, major % 2, my_core]
        + [(major ^ side) * 2 + (my_core ^ core) for core in range(2) for side in range(2)]
    ).astype(jnp.int32)
    shape = jax.ShapeDtypeStruct
    rows_of = lambda kind: shape((tok_rows, latent_width), kind)

    downs = [down_weight] + [turn(down_weight, n_line, back) for back in range(1, n_line)]

    gate_rows = -(-n_experts // 16) * 16
    columns = call(
        functools.partial(columns_body, n_line, block),
        [shape((tok_rows, n_line * block), narrow)] * 2
        + [shape((2, tok_rows, n_line * block), narrow), shape((2, latent_width, hidden_width), narrow)],
        "columns",
        scratch=[pltpu.SemaphoreType.DMA((4 * n_line + 2,))],
        outside=3,
    )(place, *(pltpu.with_memory_space_constraint(value, pltpu.HBM) for value in (tokens, expert_in, expert_out)))
    stack = lambda first, second, *earlier: call(
        stack_body, [shape((2,) + first.shape, narrow)], "stack"
    )(after(place, *earlier) if earlier else place, first, second)[0]
    (payload,) = call(payload_body, [shape((tok_rows + gate_rows, latent_width), narrow)], "payload")(
        place, routes.T, gate_levels.T, latent_grad
    )
    own = columns[3]
    core_own = swap(own, n_line, 1, 0)
    across = swap(columns[2], n_line, 0, 1)
    core_tokens = [swap(after(columns[1], across, core_own), n_line, 1, 0), swap(across[1], n_line, 1, 0)]
    side_in = swap(after(expert_in[0], across), n_line, 0, 1)

    project = call(
        functools.partial(project_body, n_line),
        [shape((2, tok_rows, latent_width), wide)] * 2 + [shape((n_line * block, latent_width), narrow)],
        "project",
    )
    keep, send, down = project(after(place, payload), columns[0], across, *core_tokens, *downs)
    half, cross = call(half_body, [rows_of(wide), rows_of(narrow)], "half")(
        place, keep, swap(send, n_line, 1, 0)
    )
    payloads = [payload] + [turn(after(payload, *downs[1:]), n_line, back) for back in range(1, n_line)]
    crossed = swap(cross, n_line, 0, 1)
    (latent,) = call(add_body, [rows_of(narrow)], "latent")(
        place, half, after(crossed, side_in, *payloads[1:])
    )
    groups = [[*range(1, n_line), 0]]
    riding = (1, n_line - 1)
    rows = [latent] + [turn(latent, n_line, back) for back in range(1, n_line)]

    side_out = swap(after(expert_out[0], latent), n_line, 0, 1)
    core_in = swap(after(side_in, latent), n_line, 1, 0)
    core_out = swap(after(side_out, *rows[1:]), n_line, 1, 0)
    weights = [own, core_own, side_in, side_out, core_in, core_out]
    side_down = swap(after(down, *rows[1:]), n_line, 0, 1)

    deltas_of, outs_of, saved = [None] * n_line, [None] * n_line, []
    done = latent
    for group in groups:
        count = len(group)
        outs = [rows_of(narrow if back else wide) for back in group for _ in range(2)]
        values = call(
            functools.partial(expert_body, count),
            outs + [shape((4, count * tok_rows, hidden_width), narrow)] * 3,
            "experts",
        )(after(place, done), *(rows[i] for i in group), *(payloads[i] for i in group), *weights)
        done, saved = values[0], saved + [list(values[-3:])]
        for i, back in enumerate(group):
            deltas_of[back], outs_of[back] = values[2 * i], values[2 * i + 1]

    def home(value, back):
        return turn(value, n_line, n_line - back) if back else value

    delta_lines = [home(value, back) for back, value in enumerate(deltas_of)]

    pair = (2, latent_width, hidden_width)
    near, far, near_other, far_other = call(
        functools.partial(weight_grad_body, n_line, len(groups)),
        [shape(pair, wide)] * 2 + [shape(pair, narrow)] * 2,
        "weight_grads",
        flops=2 * 8 * n_line * tok_rows * latent_width * hidden_width,
    )(
        place,
        *(rows[i] for group in groups for i in group),
        *(value for values in saved for value in values),
    )
    far_other = swap(after(far_other, side_down), n_line, 1, 0)
    quarter = latent_width // 2
    far_first, far_rest = call(
        far_body, [shape((rows, hidden_width), narrow) for rows in (quarter, 2 * latent_width - quarter)], "far_grads"
    )(place, far, far_other)
    far_first = swap(far_first, n_line, 0, 1)
    delta_lines = [after(line, near) for line in delta_lines]
    (delta,) = call(add_body, [rows_of(narrow)], "latent_delta")(place, *delta_lines)
    side_delta = swap(delta, n_line, 0, 1)
    out_lines = [outs_of[0]] + [home(outs_of[back], back) if back not in riding else None for back in range(1, n_line)]
    far_rest = swap(after(far_rest, side_delta), n_line, 0, 1)
    (others,) = call(pack_body, [shape((4, latent_width, hidden_width), narrow)], "pack")(
        after(place, delta), near_other, down, side_down
    )
    core_deltas = swap(stack(delta, side_delta, others, far_first, *(out_lines[back] for back in range(1, n_line) if back not in riding)), n_line, 1, 0)
    blocks = call(
        functools.partial(down_grad_body, n_line),
        [
            shape((2, block, latent_width) if back in riding else (block, latent_width), narrow if back else wide)
            for back in range(n_line)
        ],
        "down_grad",
    )(place, columns[0], across, *core_tokens, delta, side_delta, core_deltas, *(outs_of[back] for back in riding))
    others = [others, swap(after(others, blocks[1]), n_line, 1, 0)]
    (grad_tokens,) = call(
        functools.partial(token_grad_body, n_line, block), [shape((tok_rows, width), narrow)], "token_grad"
    )(place, after(delta, blocks[1]), *others)
    blocks = [blocks[0]] + [turn(blocks[back], n_line, n_line - back) for back in range(1, n_line)]
    grad_down, latent_out, grad_in, grad_out = call(
        functools.partial(last_body, riding, n_line),
        [shape((block, latent_width), wide), rows_of(narrow)]
        + [shape(value.shape, narrow) for value in (expert_in, expert_out)],
        "last_sums",
    )(after(place, grad_tokens), near, others[1], far_first, far_rest, *blocks, *(line for line in out_lines if line is not None))
    return (latent_out, grad_tokens, grad_down, grad_in, grad_out)


def slot_table(routes, capacity):
    flat = routes.reshape(-1)
    count = flat.shape[0]
    order = jnp.arange(count, dtype=jnp.int32)
    same = (flat[:, None] == flat[None, :]) & (order[None, :] < order[:, None])
    placed = jnp.sum(jnp.where(same, 1, 0), axis=1).astype(jnp.int32)
    return flat * capacity + placed


def routed_rows(tokens, routes, gate_levels, latent_grad, down_weight, expert_in, expert_out):
    tok_rows = tokens.shape[0]
    top = routes.shape[1]
    latent_width = down_weight.shape[1]
    n_major = lax.axis_size("expert")
    n_minor = lax.axis_size("dp")
    n_experts = n_major * n_minor
    capacity = 3 * tok_rows * top // (2 * n_experts)
    entries = tok_rows * top
    contract_last = (((1,), (1,)), ((), ()))
    contract_first = (((0,), (0,)), ((), ()))
    full_down = lax.all_gather(down_weight, ("expert", "dp"), axis=0, tiled=True)
    latent = jnp.dot(tokens, full_down, preferred_element_type=jnp.float32)
    latent = latent.astype(jnp.bfloat16)
    dest = slot_table(routes, capacity)
    source = (
        jnp.full((n_experts * capacity,), entries, jnp.int32)
        .at[dest]
        .set(jnp.arange(entries, dtype=jnp.int32))
    )
    token_of = jnp.where(source < entries, source // top, tok_rows)
    gates = gate_levels.astype(jnp.float32) * gate_unit
    zero_row = jnp.zeros((1, latent_width), jnp.bfloat16)
    latent_pad = jnp.concatenate([latent, zero_row], axis=0)
    send_latent = latent_pad[token_of].reshape(n_major, n_minor, capacity, latent_width)
    scaled = (gates[:, :, None] * latent_grad.astype(jnp.float32)[:, None, :]).astype(jnp.bfloat16)
    scaled_pad = jnp.concatenate([scaled.reshape(entries, latent_width), zero_row], axis=0)
    send_grad = scaled_pad[source].reshape(n_major, n_minor, capacity, latent_width)
    arrived = lax.all_to_all(
        lax.all_to_all(send_latent, "expert", split_axis=0, concat_axis=0, tiled=True),
        "dp",
        split_axis=1,
        concat_axis=1,
        tiled=True,
    )
    rows = arrived.reshape(-1, latent_width)
    weight_in = expert_in[0]
    weight_out = expert_out[0]
    before = jnp.dot(rows, weight_in, preferred_element_type=jnp.float32)
    active = jnp.maximum(before, 0.0)
    hidden = (active * active).astype(jnp.bfloat16)
    result = jnp.dot(hidden, weight_out, preferred_element_type=jnp.float32).astype(jnp.bfloat16)
    returned = lax.all_to_all(
        lax.all_to_all(
            result.reshape(n_major, n_minor, capacity, latent_width),
            "expert",
            split_axis=0,
            concat_axis=0,
            tiled=True,
        ),
        "dp",
        split_axis=1,
        concat_axis=1,
        tiled=True,
    )
    picked = returned.reshape(n_experts * capacity, latent_width)[dest].astype(jnp.float32)
    picked = picked.reshape(tok_rows, top, latent_width)
    latent_out = jnp.sum(gates[:, :, None] * picked, axis=1).astype(jnp.bfloat16)
    arrived_grad = lax.all_to_all(
        lax.all_to_all(send_grad, "expert", split_axis=0, concat_axis=0, tiled=True),
        "dp",
        split_axis=1,
        concat_axis=1,
        tiled=True,
    )
    grad_rows = arrived_grad.reshape(-1, latent_width)
    back_hidden = lax.dot_general(
        grad_rows, weight_out, contract_last, preferred_element_type=jnp.float32
    )
    back_pre = (back_hidden * 2.0 * active).astype(jnp.bfloat16)
    grad_out = lax.dot_general(
        hidden, grad_rows, contract_first, preferred_element_type=jnp.float32
    ).astype(jnp.bfloat16)
    grad_in = lax.dot_general(
        rows, back_pre, contract_first, preferred_element_type=jnp.float32
    ).astype(jnp.bfloat16)
    back_rows = lax.dot_general(
        back_pre, weight_in, contract_last, preferred_element_type=jnp.float32
    ).astype(jnp.bfloat16)
    came_back = lax.all_to_all(
        lax.all_to_all(
            back_rows.reshape(n_major, n_minor, capacity, latent_width),
            "expert",
            split_axis=0,
            concat_axis=0,
            tiled=True,
        ),
        "dp",
        split_axis=1,
        concat_axis=1,
        tiled=True,
    )
    gathered_back = came_back.reshape(n_experts * capacity, latent_width)[dest].astype(jnp.float32)
    latent_delta = jnp.sum(gathered_back.reshape(tok_rows, top, latent_width), axis=1).astype(
        jnp.bfloat16
    )
    grad_tokens = lax.dot_general(
        latent_delta, full_down, contract_last, preferred_element_type=jnp.float32
    )
    grad_tokens = grad_tokens.astype(jnp.bfloat16)
    grad_down = lax.psum_scatter(
        lax.dot_general(tokens, latent_delta, contract_first, preferred_element_type=jnp.float32),
        ("expert", "dp"),
        scatter_dimension=0,
        tiled=True,
    )
    return (latent_out, grad_tokens, grad_down, grad_in[None], grad_out[None])


def on_device(tokens, routes, *others):
    n_major = lax.axis_size("expert")
    n_experts = n_major * lax.axis_size("dp")
    few = n_experts <= 2 * routes.shape[1] and n_major % 2 == 0 and n_major >= 6 and lax.axis_size("dp") == 2
    return (all_rows if few else routed_rows)(tokens, routes, *others)


def solution(mesh):
    in_specs = (
        P(("group", "expert", "dp"), None),
        P(("group", "expert", "dp"), None),
        P(("group", "expert", "dp"), None),
        P(("group", "expert", "dp"), None),
        P(("expert", "dp"), None),
        P(("expert", "dp"), None, None),
        P(("expert", "dp"), None, None),
    )
    out_specs = (
        P(("group", "expert", "dp"), None),
        P(("group", "expert", "dp"), None),
        P(("group", "expert", "dp"), None),
        P(("group", "expert", "dp"), None, None),
        P(("group", "expert", "dp"), None, None),
    )
    return jax.shard_map(
        on_device, mesh=mesh, in_specs=in_specs, out_specs=out_specs, check_vma=False
    )
```

```python
import functools

import jax
import jax.numpy as jnp
from jax import lax
from jax.experimental import pallas as pl
from jax.experimental.pallas import tpu as pltpu
from jax.sharding import PartitionSpec as P

gate_unit = 1.0 / 1024.0
contract_last = (((1,), (1,)), ((), ()))
contract_first = (((0,), (0,)), ((), ()))
plane = ("expert", "dp")
wide = jnp.float32
narrow = jnp.bfloat16


def device_pairs(n_line, move):
    pairs = []
    for z in range(n_line):
        for x in range(2):
            for c in range(2):
                to_z, to_x, to_c = move(z, x, c)
                pairs.append(((z * 2 + x) * 2 + c, (to_z * 2 + to_x) * 2 + to_c))
    return pairs


def turn(value, n_line, by):
    return lax.ppermute(value, plane, device_pairs(n_line, lambda z, x, c: ((z + by) % n_line, x, c)))


def swap(value, n_line, core, side):
    return lax.ppermute(value, plane, device_pairs(n_line, lambda z, x, c: (z, x ^ side, c ^ core)))


def after(value, *earlier):
    return lax.optimization_barrier((value,) + earlier)[0]


def call(body, outs, name, scratch=(), outside=0, flops=0):
    vmem = pl.BlockSpec(memory_space=pltpu.VMEM)
    outer = pl.BlockSpec(memory_space=pltpu.HBM)

    def run(place, *operands):
        return pl.pallas_call(
            body,
            out_shape=outs,
            in_specs=[pl.BlockSpec(memory_space=pltpu.SMEM)]
            + [outer] * outside
            + [vmem] * (len(operands) - outside),
            out_specs=[vmem] * len(outs),
            scratch_shapes=list(scratch),
            compiler_params=pltpu.CompilerParams(vmem_limit_bytes=40 * 1024 * 1024),
            cost_estimate=pl.CostEstimate(flops=flops, bytes_accessed=0, transcendentals=0),
            name=name,
        )(place, *operands)

    return run


def columns_body(n_line, block, place, tokens, expert_in, expert_out, *refs):
    own, other, across, weights, sems = refs
    pieces = (own, across.at[0], other, across.at[1])
    copies = []
    for i, weight in enumerate((expert_in, expert_out)):
        copies.append(pltpu.make_async_copy(weight, weights.at[pl.ds(i, 1)], sems.at[i]))
    for core in range(2):
        for side in range(2):
            owner = (place[1] ^ side) * 2 + (place[2] ^ core)
            for z in range(n_line):
                start = pl.multiple_of((z * 4 + owner) * block, block)
                piece = pieces[core * 2 + side].at[:, pl.ds(z * block, block)]
                copies.append(
                    pltpu.make_async_copy(tokens.at[:, pl.ds(start, block)], piece, sems.at[len(copies)])
                )
    for copy in copies:
        copy.start()
    for copy in copies:
        copy.wait()


def stack_body(place, first, second, out):
    out[0], out[1] = first[...], second[...]


def add_body(place, *refs):
    total = refs[0][...].astype(wide)
    for value in refs[1:-1]:
        total = total + value[...].astype(wide)
    refs[-1][...] = total.astype(refs[-1].dtype)


def half_body(place, keep, arrived, mine, other):
    mine[...] = keep[0] + arrived[0]
    other[...] = (keep[1] + arrived[1]).astype(narrow)


def far_body(place, far, arrived, first, rest):
    split, width = first.shape[0], far.shape[1]
    total = [far[i] + arrived[i].astype(wide) for i in range(2)]
    first[...] = total[0][:split].astype(narrow)
    rest[: width - split] = total[0][split:].astype(narrow)
    rest[width - split :] = total[1].astype(narrow)


def pack_body(place, grads, down, side_down, out):
    out[:2] = grads[...]
    out[2], out[3] = down[...], side_down[...]


def last_body(riding, n_line, place, near, others, first, rest, *refs):
    blocks, pieces = refs[:n_line], list(refs[n_line:-4])
    grad_down, combined, *grads = refs[-4:]
    split = grads[0].shape[1] - first.shape[0]
    far = (jnp.concatenate([first[...], rest[:split]], axis=0), rest[split:])
    for i, out in enumerate(grads):
        out[0] = (near[i] + others[i].astype(wide) + far[i].astype(wide)).astype(narrow)
    total = blocks[0][...]
    out_total = pieces.pop(0)[...]
    for back in range(1, n_line):
        block = blocks[back].at[0] if back in riding else blocks[back]
        piece = blocks[back].at[1] if back in riding else pieces.pop(0)
        total = total + block[...].astype(wide)
        out_total = out_total + piece[...].astype(wide)
    grad_down[...] = total
    combined[...] = out_total.astype(narrow)


def payload_body(place, routes, levels, cotangent, payload):
    tok_rows = cotangent.shape[0]
    gate_rows = payload.shape[0] - tok_rows
    payload[:tok_rows, :] = cotangent[...]
    expert = lax.broadcasted_iota(jnp.int32, (gate_rows, tok_rows), 0)
    total = jnp.zeros((gate_rows, tok_rows), jnp.int32)
    for k in range(routes.shape[0]):
        total = total + jnp.where(expert == routes[k : k + 1, :], levels[k : k + 1, :], 0)
    low = total & 31
    payload[tok_rows:, :tok_rows] = (total - low).astype(wide).astype(narrow)
    payload[tok_rows:, tok_rows : 2 * tok_rows] = low.astype(wide).astype(narrow)
    rest = payload.shape[1] - 2 * tok_rows
    payload[tok_rows:, 2 * tok_rows :] = jnp.zeros((gate_rows, rest), narrow)


def project_body(n_line, place, *refs):
    own, across, core, core_across, *downs = refs[: 4 + n_line]
    pieces = (own, across.at[0], core, core_across)
    keep, send, down = refs[4 + n_line :]
    block = downs[0].shape[0]
    for back in range(n_line):
        z = lax.rem(place[0] + n_line - back, n_line)
        down[pl.ds(pl.multiple_of(z * block, block), block), :] = downs[back][...]
    for core, out in ((1, send), (0, keep)):
        for side in range(2):
            out[side] = jnp.dot(pieces[core * 2 + side][...], down[...], preferred_element_type=wide)


def gate_tile(payload, tok_rows, expert):
    packed = payload[tok_rows:, :]
    rows = lax.broadcasted_iota(jnp.int32, (packed.shape[0], 128), 0)
    pick = jnp.where(rows == expert, 1.0, 0.0).astype(narrow)
    dot = functools.partial(lax.dot_general, dimension_numbers=contract_first, preferred_element_type=wide)
    total = dot(packed[:, :tok_rows], pick) + dot(packed[:, tok_rows : 2 * tok_rows], pick)
    return total * gate_unit


def expert_body(count, place, *refs):
    rows_in, payloads = refs[:count], refs[count : 2 * count]
    own, core, *sides = refs[2 * count : 2 * count + 6]
    weights = (own.at[0], own.at[1], sides[0], sides[1], core.at[0], core.at[1], sides[2], sides[3])
    outs = refs[2 * count + 6 :]
    *sums, hiddens, scaleds, back_pres = outs
    tok_rows, width = rows_in[0].shape
    for first in range(0, count, 2):
        group = range(first, min(first + 2, count))
        span = slice(first * tok_rows, (first + len(group)) * tok_rows)
        stack = lambda values: jnp.concatenate(list(values), axis=0)
        rows = stack(rows_in[i][...] for i in group)
        cotangent = stack(payloads[i][:tok_rows, :] for i in group).astype(wide)
        out_sum = jnp.zeros(rows.shape, wide)
        delta_sum = jnp.zeros(rows.shape, wide)
        for e in range(4):
            weight_in, weight_out = weights[2 * e], weights[2 * e + 1]
            gate = stack(gate_tile(payloads[i], tok_rows, place[3 + e]) for i in group)
            gate = jnp.concatenate([gate] * (width // 128), axis=1)
            active = jnp.maximum(jnp.dot(rows, weight_in[...], preferred_element_type=wide), 0.0)
            hidden = (active * active).astype(narrow)
            hiddens[e, span, :] = hidden
            scaled = (gate * cotangent).astype(narrow)
            scaleds[e, span, :] = scaled
            back_hidden = lax.dot_general(scaled, weight_out[...], contract_last, preferred_element_type=wide)
            back_pre = (back_hidden * 2.0 * active).astype(narrow)
            back_pres[e, span, :] = back_pre
            result = jnp.dot(hidden, weight_out[...], preferred_element_type=wide).astype(narrow)
            out_sum = out_sum + gate * result.astype(wide)
            back_rows = lax.dot_general(back_pre, weight_in[...], contract_last, preferred_element_type=wide)
            delta_sum = delta_sum + back_rows.astype(narrow).astype(wide)
        for i in group:
            part = slice((i - first) * tok_rows, (i - first + 1) * tok_rows)
            out = sums.pop(0)
            out[...] = delta_sum[part].astype(out.dtype)
            out = sums.pop(0)
            out[...] = out_sum[part].astype(out.dtype)


def weight_grad_body(n_rows, n_sets, place, *refs):
    rows_in = refs[:n_rows]
    sets = [refs[n_rows + 3 * i : n_rows + 3 * i + 3] for i in range(n_sets)]
    near, far, near_other, far_other = refs[n_rows + 3 * n_sets :]
    dot = functools.partial(lax.dot_general, dimension_numbers=contract_first, preferred_element_type=wide)
    rows = jnp.concatenate([r[...] for r in rows_in], axis=0)
    for core in (1, 0):
        for side in (1, 0):
            hidden, scaled, back_pre = (
                jnp.concatenate([values[i][core * 2 + side] for values in sets], axis=0) for i in range(3)
            )
            grad_in, grad_out = dot(rows, back_pre), dot(hidden, scaled)
            out = ((near, far), (near_other, far_other))[core][side]
            out[0], out[1] = grad_in.astype(out.dtype), grad_out.astype(out.dtype)


def down_grad_body(n_line, place, *refs):
    own, across, core, core_across, *deltas, core_deltas = refs[:7]
    riders, blocks = refs[7:-n_line], refs[-n_line:]
    tokens = jnp.concatenate([own[...], across[0], core[...], core_across[...]], axis=0)
    delta = jnp.concatenate([d[...] for d in deltas] + [core_deltas[0], core_deltas[1]], axis=0)
    part = lax.dot_general(tokens, delta, contract_first, preferred_element_type=wide)
    block = blocks[0].shape[0]
    targets = [out if len(out.shape) == 2 else out.at[0] for out in blocks]
    for rider, out in zip(riders, [out for out in blocks if len(out.shape) == 3]):
        out[1] = rider[...]
    for z in range(n_line):
        for back in range(n_line):

            @pl.when(lax.rem(place[0] + n_line - back, n_line) == z)
            def _(z=z, back=back):
                targets[back][...] = part[z * block : (z + 1) * block].astype(targets[back].dtype)


def token_grad_body(n_line, block, place, delta, held, arrived, out):
    for i, weight in enumerate((held.at[2], held.at[3], arrived.at[2], arrived.at[3])):
        owner = (place[1] ^ (i % 2)) * 2 + (place[2] ^ (i // 2))
        part = lax.dot_general(delta[...], weight[...], contract_last, preferred_element_type=wide)
        part = part.astype(narrow)
        for z in range(n_line):
            start = pl.multiple_of((z * 4 + owner) * block, block)
            out[:, pl.ds(start, block)] = part[:, z * block : (z + 1) * block]


def all_rows(tokens, routes, gate_levels, latent_grad, down_weight, expert_in, expert_out):
    tok_rows, width = tokens.shape
    latent_width = down_weight.shape[1]
    hidden_width = expert_in.shape[2]
    n_major = lax.axis_size("expert")
    n_line = n_major // 2
    n_experts = n_major * 2
    block = width // n_experts
    major = lax.axis_index("expert")
    my_core = lax.axis_index("dp")
    place = jnp.stack(
        [major // 2, major % 2, my_core]
        + [(major ^ side) * 2 + (my_core ^ core) for core in range(2) for side in range(2)]
    ).astype(jnp.int32)
    shape = jax.ShapeDtypeStruct
    rows_of = lambda kind: shape((tok_rows, latent_width), kind)

    downs = [down_weight] + [turn(down_weight, n_line, back) for back in range(1, n_line)]

    gate_rows = -(-n_experts // 16) * 16
    columns = call(
        functools.partial(columns_body, n_line, block),
        [shape((tok_rows, n_line * block), narrow)] * 2
        + [shape((2, tok_rows, n_line * block), narrow), shape((2, latent_width, hidden_width), narrow)],
        "columns",
        scratch=[pltpu.SemaphoreType.DMA((4 * n_line + 2,))],
        outside=3,
    )(place, *(pltpu.with_memory_space_constraint(value, pltpu.HBM) for value in (tokens, expert_in, expert_out)))
    stack = lambda first, second, *earlier: call(
        stack_body, [shape((2,) + first.shape, narrow)], "stack"
    )(after(place, *earlier) if earlier else place, first, second)[0]
    (payload,) = call(payload_body, [shape((tok_rows + gate_rows, latent_width), narrow)], "payload")(
        place, routes.T, gate_levels.T, latent_grad
    )
    own = columns[3]
    core_own = swap(own, n_line, 1, 0)
    across = swap(columns[2], n_line, 0, 1)
    core_tokens = [swap(after(columns[1], across, core_own), n_line, 1, 0), swap(across[1], n_line, 1, 0)]
    side_in = swap(after(expert_in[0], across), n_line, 0, 1)

    project = call(
        functools.partial(project_body, n_line),
        [shape((2, tok_rows, latent_width), wide)] * 2 + [shape((n_line * block, latent_width), narrow)],
        "project",
    )
    keep, send, down = project(after(place, payload), columns[0], across, *core_tokens, *downs)
    half, cross = call(half_body, [rows_of(wide), rows_of(narrow)], "half")(
        place, keep, swap(send, n_line, 1, 0)
    )
    payloads = [payload] + [turn(after(payload, *downs[1:]), n_line, back) for back in range(1, n_line)]
    crossed = swap(cross, n_line, 0, 1)
    (latent,) = call(add_body, [rows_of(narrow)], "latent")(
        place, half, after(crossed, side_in, *payloads[1:])
    )
    groups = [[*range(1, n_line), 0]]
    riding = (1, n_line - 1)
    rows = [latent] + [turn(latent, n_line, back) for back in range(1, n_line)]

    side_out = swap(after(expert_out[0], latent), n_line, 0, 1)
    core_in = swap(after(side_in, latent), n_line, 1, 0)
    core_out = swap(after(side_out, *rows[1:]), n_line, 1, 0)
    weights = [own, core_own, side_in, side_out, core_in, core_out]
    side_down = swap(after(down, rows[1]), n_line, 0, 1)

    deltas_of, outs_of, saved = [None] * n_line, [None] * n_line, []
    done = latent
    for group in groups:
        count = len(group)
        outs = [rows_of(narrow if back else wide) for back in group for _ in range(2)]
        values = call(
            functools.partial(expert_body, count),
            outs + [shape((4, count * tok_rows, hidden_width), narrow)] * 3,
            "experts",
        )(after(place, done), *(rows[i] for i in group), *(payloads[i] for i in group), *weights)
        done, saved = values[0], saved + [list(values[-3:])]
        for i, back in enumerate(group):
            deltas_of[back], outs_of[back] = values[2 * i], values[2 * i + 1]

    def home(value, back):
        return turn(value, n_line, n_line - back) if back else value

    delta_lines = [home(value, back) for back, value in enumerate(deltas_of)]

    pair = (2, latent_width, hidden_width)
    near, far, near_other, far_other = call(
        functools.partial(weight_grad_body, n_line, len(groups)),
        [shape(pair, wide)] * 2 + [shape(pair, narrow)] * 2,
        "weight_grads",
        flops=2 * 8 * n_line * tok_rows * latent_width * hidden_width,
    )(
        place,
        *(rows[i] for group in groups for i in group),
        *(value for values in saved for value in values),
    )
    far_other = swap(far_other, n_line, 1, 0)
    ahead = latent_width // 2
    far_first, far_rest = call(
        far_body, [shape((rows, hidden_width), narrow) for rows in (ahead, 2 * latent_width - ahead)], "far_grads"
    )(place, far, far_other)
    far_first = swap(far_first, n_line, 0, 1)
    delta_lines = [after(line, near, far_rest) for line in delta_lines]
    (delta,) = call(add_body, [rows_of(narrow)], "latent_delta")(place, *delta_lines)
    side_delta = swap(delta, n_line, 0, 1)
    out_lines = [outs_of[0]] + [home(after(outs_of[back], delta), back) if back not in riding else None for back in range(1, n_line)]
    far_rest = swap(after(far_rest, side_delta), n_line, 0, 1)
    (others,) = call(pack_body, [shape((4, latent_width, hidden_width), narrow)], "pack")(
        after(place, delta), near_other, down, side_down
    )
    core_deltas = swap(stack(delta, side_delta, others, far_first, *(out_lines[back] for back in range(1, n_line) if back not in riding)), n_line, 1, 0)
    blocks = call(
        functools.partial(down_grad_body, n_line),
        [
            shape((2, block, latent_width) if back in riding else (block, latent_width), narrow if back else wide)
            for back in range(n_line)
        ],
        "down_grad",
    )(place, columns[0], across, *core_tokens, delta, side_delta, core_deltas, *(outs_of[back] for back in riding))
    others = [others, swap(after(others, blocks[1]), n_line, 1, 0)]
    (grad_tokens,) = call(
        functools.partial(token_grad_body, n_line, block), [shape((tok_rows, width), narrow)], "token_grad"
    )(place, after(delta, blocks[1]), *others)
    blocks = [blocks[0]] + [turn(blocks[back], n_line, n_line - back) for back in range(1, n_line)]
    grad_down, latent_out, grad_in, grad_out = call(
        functools.partial(last_body, riding, n_line),
        [shape((block, latent_width), wide), rows_of(narrow)]
        + [shape(value.shape, narrow) for value in (expert_in, expert_out)],
        "last_sums",
    )(after(place, grad_tokens), near, others[1], far_first, far_rest, *blocks, *(line for line in out_lines if line is not None))
    return (latent_out, grad_tokens, grad_down, grad_in, grad_out)


def slot_table(routes, capacity):
    flat = routes.reshape(-1)
    count = flat.shape[0]
    order = jnp.arange(count, dtype=jnp.int32)
    same = (flat[:, None] == flat[None, :]) & (order[None, :] < order[:, None])
    placed = jnp.sum(jnp.where(same, 1, 0), axis=1).astype(jnp.int32)
    return flat * capacity + placed


def routed_rows(tokens, routes, gate_levels, latent_grad, down_weight, expert_in, expert_out):
    tok_rows = tokens.shape[0]
    top = routes.shape[1]
    latent_width = down_weight.shape[1]
    n_major = lax.axis_size("expert")
    n_minor = lax.axis_size("dp")
    n_experts = n_major * n_minor
    capacity = 3 * tok_rows * top // (2 * n_experts)
    entries = tok_rows * top
    contract_last = (((1,), (1,)), ((), ()))
    contract_first = (((0,), (0,)), ((), ()))
    full_down = lax.all_gather(down_weight, ("expert", "dp"), axis=0, tiled=True)
    latent = jnp.dot(tokens, full_down, preferred_element_type=jnp.float32)
    latent = latent.astype(jnp.bfloat16)
    dest = slot_table(routes, capacity)
    source = (
        jnp.full((n_experts * capacity,), entries, jnp.int32)
        .at[dest]
        .set(jnp.arange(entries, dtype=jnp.int32))
    )
    token_of = jnp.where(source < entries, source // top, tok_rows)
    gates = gate_levels.astype(jnp.float32) * gate_unit
    zero_row = jnp.zeros((1, latent_width), jnp.bfloat16)
    latent_pad = jnp.concatenate([latent, zero_row], axis=0)
    send_latent = latent_pad[token_of].reshape(n_major, n_minor, capacity, latent_width)
    scaled = (gates[:, :, None] * latent_grad.astype(jnp.float32)[:, None, :]).astype(jnp.bfloat16)
    scaled_pad = jnp.concatenate([scaled.reshape(entries, latent_width), zero_row], axis=0)
    send_grad = scaled_pad[source].reshape(n_major, n_minor, capacity, latent_width)
    arrived = lax.all_to_all(
        lax.all_to_all(send_latent, "expert", split_axis=0, concat_axis=0, tiled=True),
        "dp",
        split_axis=1,
        concat_axis=1,
        tiled=True,
    )
    rows = arrived.reshape(-1, latent_width)
    weight_in = expert_in[0]
    weight_out = expert_out[0]
    before = jnp.dot(rows, weight_in, preferred_element_type=jnp.float32)
    active = jnp.maximum(before, 0.0)
    hidden = (active * active).astype(jnp.bfloat16)
    result = jnp.dot(hidden, weight_out, preferred_element_type=jnp.float32).astype(jnp.bfloat16)
    returned = lax.all_to_all(
        lax.all_to_all(
            result.reshape(n_major, n_minor, capacity, latent_width),
            "expert",
            split_axis=0,
            concat_axis=0,
            tiled=True,
        ),
        "dp",
        split_axis=1,
        concat_axis=1,
        tiled=True,
    )
    picked = returned.reshape(n_experts * capacity, latent_width)[dest].astype(jnp.float32)
    picked = picked.reshape(tok_rows, top, latent_width)
    latent_out = jnp.sum(gates[:, :, None] * picked, axis=1).astype(jnp.bfloat16)
    arrived_grad = lax.all_to_all(
        lax.all_to_all(send_grad, "expert", split_axis=0, concat_axis=0, tiled=True),
        "dp",
        split_axis=1,
        concat_axis=1,
        tiled=True,
    )
    grad_rows = arrived_grad.reshape(-1, latent_width)
    back_hidden = lax.dot_general(
        grad_rows, weight_out, contract_last, preferred_element_type=jnp.float32
    )
    back_pre = (back_hidden * 2.0 * active).astype(jnp.bfloat16)
    grad_out = lax.dot_general(
        hidden, grad_rows, contract_first, preferred_element_type=jnp.float32
    ).astype(jnp.bfloat16)
    grad_in = lax.dot_general(
        rows, back_pre, contract_first, preferred_element_type=jnp.float32
    ).astype(jnp.bfloat16)
    back_rows = lax.dot_general(
        back_pre, weight_in, contract_last, preferred_element_type=jnp.float32
    ).astype(jnp.bfloat16)
    came_back = lax.all_to_all(
        lax.all_to_all(
            back_rows.reshape(n_major, n_minor, capacity, latent_width),
            "expert",
            split_axis=0,
            concat_axis=0,
            tiled=True,
        ),
        "dp",
        split_axis=1,
        concat_axis=1,
        tiled=True,
    )
    gathered_back = came_back.reshape(n_experts * capacity, latent_width)[dest].astype(jnp.float32)
    latent_delta = jnp.sum(gathered_back.reshape(tok_rows, top, latent_width), axis=1).astype(
        jnp.bfloat16
    )
    grad_tokens = lax.dot_general(
        latent_delta, full_down, contract_last, preferred_element_type=jnp.float32
    )
    grad_tokens = grad_tokens.astype(jnp.bfloat16)
    grad_down = lax.psum_scatter(
        lax.dot_general(tokens, latent_delta, contract_first, preferred_element_type=jnp.float32),
        ("expert", "dp"),
        scatter_dimension=0,
        tiled=True,
    )
    return (latent_out, grad_tokens, grad_down, grad_in[None], grad_out[None])


def on_device(tokens, routes, *others):
    n_major = lax.axis_size("expert")
    n_experts = n_major * lax.axis_size("dp")
    few = n_experts <= 2 * routes.shape[1] and n_major % 2 == 0 and n_major >= 6 and lax.axis_size("dp") == 2
    return (all_rows if few else routed_rows)(tokens, routes, *others)


def solution(mesh):
    in_specs = (
        P(("group", "expert", "dp"), None),
        P(("group", "expert", "dp"), None),
        P(("group", "expert", "dp"), None),
        P(("group", "expert", "dp"), None),
        P(("expert", "dp"), None),
        P(("expert", "dp"), None, None),
        P(("expert", "dp"), None, None),
    )
    out_specs = (
        P(("group", "expert", "dp"), None),
        P(("group", "expert", "dp"), None),
        P(("group", "expert", "dp"), None),
        P(("group", "expert", "dp"), None, None),
        P(("group", "expert", "dp"), None, None),
    )
    return jax.shard_map(
        on_device, mesh=mesh, in_specs=in_specs, out_specs=out_specs, check_vma=False
    )
```

```python
import functools

import jax
import jax.numpy as jnp
from jax import lax
from jax.experimental import pallas as pl
from jax.experimental.pallas import tpu as pltpu
from jax.sharding import PartitionSpec as P

gate_unit = 1.0 / 1024.0
contract_last = (((1,), (1,)), ((), ()))
contract_first = (((0,), (0,)), ((), ()))
plane = ("expert", "dp")
wide = jnp.float32
narrow = jnp.bfloat16


def device_pairs(n_line, move):
    pairs = []
    for z in range(n_line):
        for x in range(2):
            for c in range(2):
                to_z, to_x, to_c = move(z, x, c)
                pairs.append(((z * 2 + x) * 2 + c, (to_z * 2 + to_x) * 2 + to_c))
    return pairs


def turn(value, n_line, by):
    return lax.ppermute(value, plane, device_pairs(n_line, lambda z, x, c: (z ^ by, x, c)))


def swap(value, n_line, core, side):
    return lax.ppermute(value, plane, device_pairs(n_line, lambda z, x, c: (z, x ^ side, c ^ core)))


def after(value, *earlier):
    return lax.optimization_barrier((value,) + earlier)[0]


def call(body, outs, name, scratch=(), outside=0, flops=0):
    vmem = pl.BlockSpec(memory_space=pltpu.VMEM)
    outer = pl.BlockSpec(memory_space=pltpu.HBM)

    def run(place, *operands):
        return pl.pallas_call(
            body,
            out_shape=outs,
            in_specs=[pl.BlockSpec(memory_space=pltpu.SMEM)]
            + [outer] * outside
            + [vmem] * (len(operands) - outside),
            out_specs=[vmem] * len(outs),
            scratch_shapes=list(scratch),
            compiler_params=pltpu.CompilerParams(vmem_limit_bytes=40 * 1024 * 1024),
            cost_estimate=pl.CostEstimate(flops=flops, bytes_accessed=0, transcendentals=0),
            name=name,
        )(place, *operands)

    return run


def columns_body(n_line, block, place, tokens, expert_in, expert_out, *refs):
    own, other, across, weights, sems = refs
    pieces = (own, across.at[0], other, across.at[1])
    copies = []
    for i, weight in enumerate((expert_in, expert_out)):
        copies.append(pltpu.make_async_copy(weight, weights.at[pl.ds(i, 1)], sems.at[i]))
    for core in range(2):
        for side in range(2):
            owner = (place[1] ^ side) * 2 + (place[2] ^ core)
            for z in range(n_line):
                start = pl.multiple_of((z * 4 + owner) * block, block)
                piece = pieces[core * 2 + side].at[:, pl.ds(z * block, block)]
                copies.append(
                    pltpu.make_async_copy(tokens.at[:, pl.ds(start, block)], piece, sems.at[len(copies)])
                )
    for copy in copies:
        copy.start()
    for copy in copies:
        copy.wait()


def stack_body(place, first, second, out):
    out[0], out[1] = first[...], second[...]


def add_body(place, *refs):
    total = refs[0][...].astype(wide)
    for value in refs[1:-1]:
        total = total + value[...].astype(wide)
    refs[-1][...] = total.astype(refs[-1].dtype)


def half_body(place, keep, arrived, mine, other):
    mine[...] = keep[0] + arrived[0]
    other[...] = (keep[1] + arrived[1]).astype(narrow)


def far_body(place, far, arrived, first, rest):
    split, width = first.shape[0], far.shape[1]
    total = [far[i] + arrived[i].astype(wide) for i in range(2)]
    first[...] = total[0][:split].astype(narrow)
    rest[: width - split] = total[0][split:].astype(narrow)
    rest[width - split :] = total[1].astype(narrow)


def pack_body(place, grads, down, side_down, out):
    out[:2] = grads[...]
    out[2], out[3] = down[...], side_down[...]


def last_body(riding, n_line, place, near, others, first, rest, *refs):
    blocks, pieces = refs[:n_line], list(refs[n_line:-4])
    grad_down, combined, *grads = refs[-4:]
    split = grads[0].shape[1] - first.shape[0]
    far = (jnp.concatenate([first[...], rest[:split]], axis=0), rest[split:])
    for i, out in enumerate(grads):
        out[0] = (near[i] + others[i].astype(wide) + far[i].astype(wide)).astype(narrow)
    total = blocks[0][...]
    out_total = pieces.pop(0)[...]
    for back in range(1, n_line):
        block = blocks[back].at[0] if back in riding else blocks[back]
        piece = blocks[back].at[1] if back in riding else pieces.pop(0)
        total = total + block[...].astype(wide)
        out_total = out_total + piece[...].astype(wide)
    grad_down[...] = total
    combined[...] = out_total.astype(narrow)


def payload_body(place, routes, levels, cotangent, payload):
    tok_rows = cotangent.shape[0]
    gate_rows = payload.shape[0] - tok_rows
    payload[:tok_rows, :] = cotangent[...]
    expert = lax.broadcasted_iota(jnp.int32, (gate_rows, tok_rows), 0)
    total = jnp.zeros((gate_rows, tok_rows), jnp.int32)
    for k in range(routes.shape[0]):
        total = total + jnp.where(expert == routes[k : k + 1, :], levels[k : k + 1, :], 0)
    low = total & 31
    payload[tok_rows:, :tok_rows] = (total - low).astype(wide).astype(narrow)
    payload[tok_rows:, tok_rows : 2 * tok_rows] = low.astype(wide).astype(narrow)
    rest = payload.shape[1] - 2 * tok_rows
    payload[tok_rows:, 2 * tok_rows :] = jnp.zeros((gate_rows, rest), narrow)


def project_body(n_line, place, *refs):
    own, across, core, core_across, *downs = refs[: 4 + n_line]
    pieces = (own, across.at[0], core, core_across)
    keep, send, down = refs[4 + n_line :]
    block = downs[0].shape[0]
    for back in range(n_line):
        z = place[0] ^ back
        down[pl.ds(pl.multiple_of(z * block, block), block), :] = downs[back][...]
    for core, out in ((1, send), (0, keep)):
        for side in range(2):
            out[side] = jnp.dot(pieces[core * 2 + side][...], down[...], preferred_element_type=wide)


def gate_tile(payload, tok_rows, expert):
    packed = payload[tok_rows:, :]
    rows = lax.broadcasted_iota(jnp.int32, (packed.shape[0], 128), 0)
    pick = jnp.where(rows == expert, 1.0, 0.0).astype(narrow)
    dot = functools.partial(lax.dot_general, dimension_numbers=contract_first, preferred_element_type=wide)
    total = dot(packed[:, :tok_rows], pick) + dot(packed[:, tok_rows : 2 * tok_rows], pick)
    return total * gate_unit


def expert_body(count, place, *refs):
    rows_in, payloads = refs[:count], refs[count : 2 * count]
    own, core, *sides = refs[2 * count : 2 * count + 6]
    weights = (own.at[0], own.at[1], sides[0], sides[1], core.at[0], core.at[1], sides[2], sides[3])
    outs = refs[2 * count + 6 :]
    *sums, hiddens, scaleds, back_pres = outs
    tok_rows, width = rows_in[0].shape
    for first in range(0, count, 2):
        group = range(first, min(first + 2, count))
        span = slice(first * tok_rows, (first + len(group)) * tok_rows)
        stack = lambda values: jnp.concatenate(list(values), axis=0)
        rows = stack(rows_in[i][...] for i in group)
        cotangent = stack(payloads[i][:tok_rows, :] for i in group).astype(wide)
        out_sum = jnp.zeros(rows.shape, wide)
        delta_sum = jnp.zeros(rows.shape, wide)
        for e in range(4):
            weight_in, weight_out = weights[2 * e], weights[2 * e + 1]
            gate = stack(gate_tile(payloads[i], tok_rows, place[3 + e]) for i in group)
            gate = jnp.concatenate([gate] * (width // 128), axis=1)
            active = jnp.maximum(jnp.dot(rows, weight_in[...], preferred_element_type=wide), 0.0)
            hidden = (active * active).astype(narrow)
            hiddens[e, span, :] = hidden
            scaled = (gate * cotangent).astype(narrow)
            scaleds[e, span, :] = scaled
            back_hidden = lax.dot_general(scaled, weight_out[...], contract_last, preferred_element_type=wide)
            back_pre = (back_hidden * 2.0 * active).astype(narrow)
            back_pres[e, span, :] = back_pre
            result = jnp.dot(hidden, weight_out[...], preferred_element_type=wide).astype(narrow)
            out_sum = out_sum + gate * result.astype(wide)
            back_rows = lax.dot_general(back_pre, weight_in[...], contract_last, preferred_element_type=wide)
            delta_sum = delta_sum + back_rows.astype(narrow).astype(wide)
        for i in group:
            part = slice((i - first) * tok_rows, (i - first + 1) * tok_rows)
            out = sums.pop(0)
            out[...] = delta_sum[part].astype(out.dtype)
            out = sums.pop(0)
            out[...] = out_sum[part].astype(out.dtype)


def weight_grad_body(n_rows, n_sets, place, *refs):
    rows_in = refs[:n_rows]
    sets = [refs[n_rows + 3 * i : n_rows + 3 * i + 3] for i in range(n_sets)]
    near, far, near_other, far_other = refs[n_rows + 3 * n_sets :]
    dot = functools.partial(lax.dot_general, dimension_numbers=contract_first, preferred_element_type=wide)
    rows = jnp.concatenate([r[...] for r in rows_in], axis=0)
    for core in (1, 0):
        for side in (1, 0):
            hidden, scaled, back_pre = (
                jnp.concatenate([values[i][core * 2 + side] for values in sets], axis=0) for i in range(3)
            )
            grad_in, grad_out = dot(rows, back_pre), dot(hidden, scaled)
            out = ((near, far), (near_other, far_other))[core][side]
            out[0], out[1] = grad_in.astype(out.dtype), grad_out.astype(out.dtype)


def down_grad_body(n_line, place, *refs):
    own, across, core, core_across, *deltas, core_deltas = refs[:7]
    riders, blocks = refs[7:-n_line], refs[-n_line:]
    tokens = jnp.concatenate([own[...], across[0], core[...], core_across[...]], axis=0)
    delta = jnp.concatenate([d[...] for d in deltas] + [core_deltas[0], core_deltas[1]], axis=0)
    part = lax.dot_general(tokens, delta, contract_first, preferred_element_type=wide)
    block = blocks[0].shape[0]
    targets = [out if len(out.shape) == 2 else out.at[0] for out in blocks]
    for rider, out in zip(riders, [out for out in blocks if len(out.shape) == 3]):
        out[1] = rider[...]
    for z in range(n_line):
        for back in range(n_line):

            @pl.when((place[0] ^ back) == z)
            def _(z=z, back=back):
                targets[back][...] = part[z * block : (z + 1) * block].astype(targets[back].dtype)


def token_grad_body(n_line, block, place, delta, held, arrived, out):
    for i, weight in enumerate((held.at[2], held.at[3], arrived.at[2], arrived.at[3])):
        owner = (place[1] ^ (i % 2)) * 2 + (place[2] ^ (i // 2))
        part = lax.dot_general(delta[...], weight[...], contract_last, preferred_element_type=wide)
        part = part.astype(narrow)
        for z in range(n_line):
            start = pl.multiple_of((z * 4 + owner) * block, block)
            out[:, pl.ds(start, block)] = part[:, z * block : (z + 1) * block]


def all_rows(tokens, routes, gate_levels, latent_grad, down_weight, expert_in, expert_out):
    tok_rows, width = tokens.shape
    latent_width = down_weight.shape[1]
    hidden_width = expert_in.shape[2]
    n_major = lax.axis_size("expert")
    n_line = n_major // 2
    n_experts = n_major * 2
    block = width // n_experts
    major = lax.axis_index("expert")
    my_core = lax.axis_index("dp")
    place = jnp.stack(
        [major // 2, major % 2, my_core]
        + [(major ^ side) * 2 + (my_core ^ core) for core in range(2) for side in range(2)]
    ).astype(jnp.int32)
    shape = jax.ShapeDtypeStruct
    rows_of = lambda kind: shape((tok_rows, latent_width), kind)

    downs = [down_weight] + [turn(down_weight, n_line, back) for back in range(1, n_line)]

    gate_rows = -(-n_experts // 16) * 16
    columns = call(
        functools.partial(columns_body, n_line, block),
        [shape((tok_rows, n_line * block), narrow)] * 2
        + [shape((2, tok_rows, n_line * block), narrow), shape((2, latent_width, hidden_width), narrow)],
        "columns",
        scratch=[pltpu.SemaphoreType.DMA((4 * n_line + 2,))],
        outside=3,
    )(place, *(pltpu.with_memory_space_constraint(value, pltpu.HBM) for value in (tokens, expert_in, expert_out)))
    stack = lambda first, second, *earlier: call(
        stack_body, [shape((2,) + first.shape, narrow)], "stack"
    )(after(place, *earlier) if earlier else place, first, second)[0]
    (payload,) = call(payload_body, [shape((tok_rows + gate_rows, latent_width), narrow)], "payload")(
        place, routes.T, gate_levels.T, latent_grad
    )
    own = columns[3]
    core_own = swap(own, n_line, 1, 0)
    across = swap(columns[2], n_line, 0, 1)
    core_tokens = [swap(after(columns[1], across, core_own), n_line, 1, 0), swap(across[1], n_line, 1, 0)]
    side_in = swap(after(expert_in[0], across), n_line, 0, 1)

    project = call(
        functools.partial(project_body, n_line),
        [shape((2, tok_rows, latent_width), wide)] * 2 + [shape((n_line * block, latent_width), narrow)],
        "project",
    )
    keep, send, down = project(after(place, payload), columns[0], across, *core_tokens, *downs)
    half, cross = call(half_body, [rows_of(wide), rows_of(narrow)], "half")(
        place, keep, swap(send, n_line, 1, 0)
    )
    payloads = [payload] + [turn(after(payload, *downs[1:]), n_line, back) for back in range(1, n_line)]
    crossed = swap(cross, n_line, 0, 1)
    (latent,) = call(add_body, [rows_of(narrow)], "latent")(
        place, half, after(crossed, side_in, *payloads[1:])
    )
    groups = [[*range(1, n_line), 0]]
    riding = (1, n_line - 1)
    rows = [latent] + [turn(latent, n_line, back) for back in range(1, n_line)]

    side_out = swap(after(expert_out[0], latent), n_line, 0, 1)
    core_in = swap(after(side_in, latent), n_line, 1, 0)
    core_out = swap(after(side_out, *rows[1:]), n_line, 1, 0)
    weights = [own, core_own, side_in, side_out, core_in, core_out]
    side_down = swap(after(down, rows[1]), n_line, 0, 1)

    deltas_of, outs_of, saved = [None] * n_line, [None] * n_line, []
    done = latent
    for group in groups:
        count = len(group)
        outs = [rows_of(narrow if back else wide) for back in group for _ in range(2)]
        values = call(
            functools.partial(expert_body, count),
            outs + [shape((4, count * tok_rows, hidden_width), narrow)] * 3,
            "experts",
        )(after(place, done), *(rows[i] for i in group), *(payloads[i] for i in group), *weights)
        done, saved = values[0], saved + [list(values[-3:])]
        for i, back in enumerate(group):
            deltas_of[back], outs_of[back] = values[2 * i], values[2 * i + 1]

    def home(value, back):
        return turn(value, n_line, back) if back else value

    delta_lines = [home(value, back) for back, value in enumerate(deltas_of)]

    pair = (2, latent_width, hidden_width)
    near, far, near_other, far_other = call(
        functools.partial(weight_grad_body, n_line, len(groups)),
        [shape(pair, wide)] * 2 + [shape(pair, narrow)] * 2,
        "weight_grads",
        flops=2 * 8 * n_line * tok_rows * latent_width * hidden_width,
    )(
        place,
        *(rows[i] for group in groups for i in group),
        *(value for values in saved for value in values),
    )
    far_other = swap(far_other, n_line, 1, 0)
    ahead = latent_width // 2
    far_first, far_rest = call(
        far_body, [shape((rows, hidden_width), narrow) for rows in (ahead, 2 * latent_width - ahead)], "far_grads"
    )(place, far, far_other)
    far_first = swap(far_first, n_line, 0, 1)
    delta_lines = [after(line, near, far_rest) for line in delta_lines]
    (delta,) = call(add_body, [rows_of(narrow)], "latent_delta")(place, *delta_lines)
    side_delta = swap(delta, n_line, 0, 1)
    out_lines = [outs_of[0]] + [home(after(outs_of[back], delta), back) if back not in riding else None for back in range(1, n_line)]
    far_rest = swap(after(far_rest, side_delta), n_line, 0, 1)
    (others,) = call(pack_body, [shape((4, latent_width, hidden_width), narrow)], "pack")(
        after(place, delta), near_other, down, side_down
    )
    core_deltas = swap(stack(delta, side_delta, others, far_first, *(out_lines[back] for back in range(1, n_line) if back not in riding)), n_line, 1, 0)
    blocks = call(
        functools.partial(down_grad_body, n_line),
        [
            shape((2, block, latent_width) if back in riding else (block, latent_width), narrow if back else wide)
            for back in range(n_line)
        ],
        "down_grad",
    )(place, columns[0], across, *core_tokens, delta, side_delta, core_deltas, *(outs_of[back] for back in riding))
    others = [others, swap(after(others, blocks[1]), n_line, 1, 0)]
    (grad_tokens,) = call(
        functools.partial(token_grad_body, n_line, block), [shape((tok_rows, width), narrow)], "token_grad"
    )(place, after(delta, blocks[1]), *others)
    blocks = [blocks[0]] + [turn(blocks[back], n_line, back) for back in range(1, n_line)]
    grad_down, latent_out, grad_in, grad_out = call(
        functools.partial(last_body, riding, n_line),
        [shape((block, latent_width), wide), rows_of(narrow)]
        + [shape(value.shape, narrow) for value in (expert_in, expert_out)],
        "last_sums",
    )(after(place, grad_tokens), near, others[1], far_first, far_rest, *blocks, *(line for line in out_lines if line is not None))
    return (latent_out, grad_tokens, grad_down, grad_in, grad_out)


def slot_table(routes, capacity):
    flat = routes.reshape(-1)
    count = flat.shape[0]
    order = jnp.arange(count, dtype=jnp.int32)
    same = (flat[:, None] == flat[None, :]) & (order[None, :] < order[:, None])
    placed = jnp.sum(jnp.where(same, 1, 0), axis=1).astype(jnp.int32)
    return flat * capacity + placed


def routed_rows(tokens, routes, gate_levels, latent_grad, down_weight, expert_in, expert_out):
    tok_rows = tokens.shape[0]
    top = routes.shape[1]
    latent_width = down_weight.shape[1]
    n_major = lax.axis_size("expert")
    n_minor = lax.axis_size("dp")
    n_experts = n_major * n_minor
    capacity = 3 * tok_rows * top // (2 * n_experts)
    entries = tok_rows * top
    contract_last = (((1,), (1,)), ((), ()))
    contract_first = (((0,), (0,)), ((), ()))
    full_down = lax.all_gather(down_weight, ("expert", "dp"), axis=0, tiled=True)
    latent = jnp.dot(tokens, full_down, preferred_element_type=jnp.float32)
    latent = latent.astype(jnp.bfloat16)
    dest = slot_table(routes, capacity)
    source = (
        jnp.full((n_experts * capacity,), entries, jnp.int32)
        .at[dest]
        .set(jnp.arange(entries, dtype=jnp.int32))
    )
    token_of = jnp.where(source < entries, source // top, tok_rows)
    gates = gate_levels.astype(jnp.float32) * gate_unit
    zero_row = jnp.zeros((1, latent_width), jnp.bfloat16)
    latent_pad = jnp.concatenate([latent, zero_row], axis=0)
    send_latent = latent_pad[token_of].reshape(n_major, n_minor, capacity, latent_width)
    scaled = (gates[:, :, None] * latent_grad.astype(jnp.float32)[:, None, :]).astype(jnp.bfloat16)
    scaled_pad = jnp.concatenate([scaled.reshape(entries, latent_width), zero_row], axis=0)
    send_grad = scaled_pad[source].reshape(n_major, n_minor, capacity, latent_width)
    arrived = lax.all_to_all(
        lax.all_to_all(send_latent, "expert", split_axis=0, concat_axis=0, tiled=True),
        "dp",
        split_axis=1,
        concat_axis=1,
        tiled=True,
    )
    rows = arrived.reshape(-1, latent_width)
    weight_in = expert_in[0]
    weight_out = expert_out[0]
    before = jnp.dot(rows, weight_in, preferred_element_type=jnp.float32)
    active = jnp.maximum(before, 0.0)
    hidden = (active * active).astype(jnp.bfloat16)
    result = jnp.dot(hidden, weight_out, preferred_element_type=jnp.float32).astype(jnp.bfloat16)
    returned = lax.all_to_all(
        lax.all_to_all(
            result.reshape(n_major, n_minor, capacity, latent_width),
            "expert",
            split_axis=0,
            concat_axis=0,
            tiled=True,
        ),
        "dp",
        split_axis=1,
        concat_axis=1,
        tiled=True,
    )
    picked = returned.reshape(n_experts * capacity, latent_width)[dest].astype(jnp.float32)
    picked = picked.reshape(tok_rows, top, latent_width)
    latent_out = jnp.sum(gates[:, :, None] * picked, axis=1).astype(jnp.bfloat16)
    arrived_grad = lax.all_to_all(
        lax.all_to_all(send_grad, "expert", split_axis=0, concat_axis=0, tiled=True),
        "dp",
        split_axis=1,
        concat_axis=1,
        tiled=True,
    )
    grad_rows = arrived_grad.reshape(-1, latent_width)
    back_hidden = lax.dot_general(
        grad_rows, weight_out, contract_last, preferred_element_type=jnp.float32
    )
    back_pre = (back_hidden * 2.0 * active).astype(jnp.bfloat16)
    grad_out = lax.dot_general(
        hidden, grad_rows, contract_first, preferred_element_type=jnp.float32
    ).astype(jnp.bfloat16)
    grad_in = lax.dot_general(
        rows, back_pre, contract_first, preferred_element_type=jnp.float32
    ).astype(jnp.bfloat16)
    back_rows = lax.dot_general(
        back_pre, weight_in, contract_last, preferred_element_type=jnp.float32
    ).astype(jnp.bfloat16)
    came_back = lax.all_to_all(
        lax.all_to_all(
            back_rows.reshape(n_major, n_minor, capacity, latent_width),
            "expert",
            split_axis=0,
            concat_axis=0,
            tiled=True,
        ),
        "dp",
        split_axis=1,
        concat_axis=1,
        tiled=True,
    )
    gathered_back = came_back.reshape(n_experts * capacity, latent_width)[dest].astype(jnp.float32)
    latent_delta = jnp.sum(gathered_back.reshape(tok_rows, top, latent_width), axis=1).astype(
        jnp.bfloat16
    )
    grad_tokens = lax.dot_general(
        latent_delta, full_down, contract_last, preferred_element_type=jnp.float32
    )
    grad_tokens = grad_tokens.astype(jnp.bfloat16)
    grad_down = lax.psum_scatter(
        lax.dot_general(tokens, latent_delta, contract_first, preferred_element_type=jnp.float32),
        ("expert", "dp"),
        scatter_dimension=0,
        tiled=True,
    )
    return (latent_out, grad_tokens, grad_down, grad_in[None], grad_out[None])


def on_device(tokens, routes, *others):
    n_major = lax.axis_size("expert")
    n_experts = n_major * lax.axis_size("dp")
    few = n_experts <= 2 * routes.shape[1] and n_major >= 8 and n_major & (n_major - 1) == 0 and lax.axis_size("dp") == 2
    return (all_rows if few else routed_rows)(tokens, routes, *others)


def solution(mesh):
    in_specs = (
        P(("group", "expert", "dp"), None),
        P(("group", "expert", "dp"), None),
        P(("group", "expert", "dp"), None),
        P(("group", "expert", "dp"), None),
        P(("expert", "dp"), None),
        P(("expert", "dp"), None, None),
        P(("expert", "dp"), None, None),
    )
    out_specs = (
        P(("group", "expert", "dp"), None),
        P(("group", "expert", "dp"), None),
        P(("group", "expert", "dp"), None),
        P(("group", "expert", "dp"), None, None),
        P(("group", "expert", "dp"), None, None),
    )
    return jax.shard_map(
        on_device, mesh=mesh, in_specs=in_specs, out_specs=out_specs, check_vma=False
    )
```

```python
import functools

import jax
import jax.numpy as jnp
from jax import lax
from jax.experimental import pallas as pl
from jax.experimental.pallas import tpu as pltpu
from jax.sharding import PartitionSpec as P

gate_unit = 1.0 / 1024.0
contract_last = (((1,), (1,)), ((), ()))
contract_first = (((0,), (0,)), ((), ()))
plane = ("expert", "dp")
wide = jnp.float32
narrow = jnp.bfloat16


def device_pairs(n_line, move):
    pairs = []
    for z in range(n_line):
        for x in range(2):
            for c in range(2):
                to_z, to_x, to_c = move(z, x, c)
                pairs.append(((z * 2 + x) * 2 + c, (to_z * 2 + to_x) * 2 + to_c))
    return pairs


def turn(value, n_line, by):
    return lax.ppermute(value, plane, device_pairs(n_line, lambda z, x, c: ((z + by) % n_line, x, c)))


def swap(value, n_line, core, side):
    return lax.ppermute(value, plane, device_pairs(n_line, lambda z, x, c: (z, x ^ side, c ^ core)))


def after(value, *earlier):
    return lax.optimization_barrier((value,) + earlier)[0]


def call(body, outs, name, scratch=(), outside=0, flops=0):
    vmem = pl.BlockSpec(memory_space=pltpu.VMEM)
    outer = pl.BlockSpec(memory_space=pltpu.HBM)

    def run(place, *operands):
        return pl.pallas_call(
            body,
            out_shape=outs,
            in_specs=[pl.BlockSpec(memory_space=pltpu.SMEM)]
            + [outer] * outside
            + [vmem] * (len(operands) - outside),
            out_specs=[vmem] * len(outs),
            scratch_shapes=list(scratch),
            compiler_params=pltpu.CompilerParams(vmem_limit_bytes=40 * 1024 * 1024),
            cost_estimate=pl.CostEstimate(flops=flops, bytes_accessed=0, transcendentals=0),
            name=name,
        )(place, *operands)

    return run


def columns_body(n_line, block, place, tokens, expert_in, expert_out, *refs):
    own, other, across, weights, sems = refs
    pieces = (own, across.at[0], other, across.at[1])
    copies = []
    for i, weight in enumerate((expert_in, expert_out)):
        copies.append(pltpu.make_async_copy(weight, weights.at[pl.ds(i, 1)], sems.at[i]))
    for core in range(2):
        for side in range(2):
            owner = (place[1] ^ side) * 2 + (place[2] ^ core)
            for z in range(n_line):
                start = pl.multiple_of((z * 4 + owner) * block, block)
                piece = pieces[core * 2 + side].at[:, pl.ds(z * block, block)]
                copies.append(
                    pltpu.make_async_copy(tokens.at[:, pl.ds(start, block)], piece, sems.at[len(copies)])
                )
    for copy in copies:
        copy.start()
    for copy in copies:
        copy.wait()


def stack_body(place, first, second, out):
    out[0], out[1] = first[...], second[...]


def add_body(place, *refs):
    total = refs[0][...].astype(wide)
    for value in refs[1:-1]:
        total = total + value[...].astype(wide)
    refs[-1][...] = total.astype(refs[-1].dtype)


def half_body(place, keep, arrived, mine, other):
    mine[...] = keep[0] + arrived[0]
    other[...] = (keep[1] + arrived[1]).astype(narrow)


def far_body(place, far, arrived, first, rest):
    split, width = first.shape[0], far.shape[1]
    total = [far[i] + arrived[i].astype(wide) for i in range(2)]
    first[...] = total[0][:split].astype(narrow)
    rest[: width - split] = total[0][split:].astype(narrow)
    rest[width - split :] = total[1].astype(narrow)


def pack_body(place, grads, down, side_down, out):
    out[:2] = grads[...]
    out[2], out[3] = down[...], side_down[...]


def last_body(riding, n_line, place, near, others, first, rest, *refs):
    blocks, pieces = refs[:n_line], list(refs[n_line:-4])
    grad_down, combined, *grads = refs[-4:]
    split = grads[0].shape[1] - first.shape[0]
    far = (jnp.concatenate([first[...], rest[:split]], axis=0), rest[split:])
    for i, out in enumerate(grads):
        out[0] = (near[i] + others[i].astype(wide) + far[i].astype(wide)).astype(narrow)
    total = blocks[0][...]
    out_total = pieces.pop(0)[...]
    for back in range(1, n_line):
        block = blocks[back].at[0] if back in riding else blocks[back]
        piece = blocks[back].at[1] if back in riding else pieces.pop(0)
        total = total + block[...].astype(wide)
        out_total = out_total + piece[...].astype(wide)
    grad_down[...] = total
    combined[...] = out_total.astype(narrow)


def payload_body(place, routes, levels, cotangent, payload):
    tok_rows = cotangent.shape[0]
    gate_rows = payload.shape[0] - tok_rows
    payload[:tok_rows, :] = cotangent[...]
    expert = lax.broadcasted_iota(jnp.int32, (gate_rows, tok_rows), 0)
    total = jnp.zeros((gate_rows, tok_rows), jnp.int32)
    for k in range(routes.shape[0]):
        total = total + jnp.where(expert == routes[k : k + 1, :], levels[k : k + 1, :], 0)
    low = total & 31
    payload[tok_rows:, :tok_rows] = (total - low).astype(wide).astype(narrow)
    payload[tok_rows:, tok_rows : 2 * tok_rows] = low.astype(wide).astype(narrow)
    rest = payload.shape[1] - 2 * tok_rows
    payload[tok_rows:, 2 * tok_rows :] = jnp.zeros((gate_rows, rest), narrow)


def project_body(n_line, place, *refs):
    own, across, core, core_across, *downs = refs[: 4 + n_line]
    pieces = (own, across.at[0], core, core_across)
    keep, send, down = refs[4 + n_line :]
    block = downs[0].shape[0]
    for back in range(n_line):
        z = lax.rem(place[0] + n_line - back, n_line)
        down[pl.ds(pl.multiple_of(z * block, block), block), :] = downs[back][...]
    for core, out in ((1, send), (0, keep)):
        for side in range(2):
            out[side] = jnp.dot(pieces[core * 2 + side][...], down[...], preferred_element_type=wide)


def gate_tile(payload, tok_rows, expert):
    packed = payload[tok_rows:, :]
    rows = lax.broadcasted_iota(jnp.int32, (packed.shape[0], 128), 0)
    pick = jnp.where(rows == expert, 1.0, 0.0).astype(narrow)
    dot = functools.partial(lax.dot_general, dimension_numbers=contract_first, preferred_element_type=wide)
    total = dot(packed[:, :tok_rows], pick) + dot(packed[:, tok_rows : 2 * tok_rows], pick)
    return total * gate_unit


def expert_body(count, place, *refs):
    rows_in, payloads = refs[:count], refs[count : 2 * count]
    own, core, *sides = refs[2 * count : 2 * count + 6]
    weights = (own.at[0], own.at[1], sides[0], sides[1], core.at[0], core.at[1], sides[2], sides[3])
    outs = refs[2 * count + 6 :]
    *sums, hiddens, scaleds, back_pres = outs
    tok_rows, width = rows_in[0].shape
    for first in range(0, count, 4):
        group = range(first, min(first + 4, count))
        span = slice(first * tok_rows, (first + len(group)) * tok_rows)
        stack = lambda values: jnp.concatenate(list(values), axis=0)
        rows = stack(rows_in[i][...] for i in group)
        cotangent = stack(payloads[i][:tok_rows, :] for i in group).astype(wide)
        out_sum = jnp.zeros(rows.shape, wide)
        delta_sum = jnp.zeros(rows.shape, wide)
        for e in range(4):
            weight_in, weight_out = weights[2 * e], weights[2 * e + 1]
            gate = stack(gate_tile(payloads[i], tok_rows, place[3 + e]) for i in group)
            gate = jnp.concatenate([gate] * (width // 128), axis=1)
            active = jnp.maximum(jnp.dot(rows, weight_in[...], preferred_element_type=wide), 0.0)
            hidden = (active * active).astype(narrow)
            hiddens[e, span, :] = hidden
            scaled = (gate * cotangent).astype(narrow)
            scaleds[e, span, :] = scaled
            back_hidden = lax.dot_general(scaled, weight_out[...], contract_last, preferred_element_type=wide)
            back_pre = (back_hidden * 2.0 * active).astype(narrow)
            back_pres[e, span, :] = back_pre
            result = jnp.dot(hidden, weight_out[...], preferred_element_type=wide).astype(narrow)
            out_sum = out_sum + gate * result.astype(wide)
            back_rows = lax.dot_general(back_pre, weight_in[...], contract_last, preferred_element_type=wide)
            delta_sum = delta_sum + back_rows.astype(narrow).astype(wide)
        for i in group:
            part = slice((i - first) * tok_rows, (i - first + 1) * tok_rows)
            out = sums.pop(0)
            out[...] = delta_sum[part].astype(out.dtype)
            out = sums.pop(0)
            out[...] = out_sum[part].astype(out.dtype)


def weight_grad_body(n_rows, n_sets, place, *refs):
    rows_in = refs[:n_rows]
    sets = [refs[n_rows + 3 * i : n_rows + 3 * i + 3] for i in range(n_sets)]
    near, far, near_other, far_other = refs[n_rows + 3 * n_sets :]
    dot = functools.partial(lax.dot_general, dimension_numbers=contract_first, preferred_element_type=wide)
    rows = jnp.concatenate([r[...] for r in rows_in], axis=0)
    for core in (1, 0):
        for side in (1, 0):
            hidden, scaled, back_pre = (
                jnp.concatenate([values[i][core * 2 + side] for values in sets], axis=0) for i in range(3)
            )
            grad_in, grad_out = dot(rows, back_pre), dot(hidden, scaled)
            out = ((near, far), (near_other, far_other))[core][side]
            out[0], out[1] = grad_in.astype(out.dtype), grad_out.astype(out.dtype)


def down_grad_body(n_line, place, *refs):
    own, across, core, core_across, *deltas, core_deltas = refs[:7]
    riders, blocks = refs[7:-n_line], refs[-n_line:]
    tokens = jnp.concatenate([own[...], across[0], core[...], core_across[...]], axis=0)
    delta = jnp.concatenate([d[...] for d in deltas] + [core_deltas[0], core_deltas[1]], axis=0)
    part = lax.dot_general(tokens, delta, contract_first, preferred_element_type=wide)
    block = blocks[0].shape[0]
    targets = [out if len(out.shape) == 2 else out.at[0] for out in blocks]
    for rider, out in zip(riders, [out for out in blocks if len(out.shape) == 3]):
        out[1] = rider[...]
    for z in range(n_line):
        for back in range(n_line):

            @pl.when(lax.rem(place[0] + n_line - back, n_line) == z)
            def _(z=z, back=back):
                targets[back][...] = part[z * block : (z + 1) * block].astype(targets[back].dtype)


def token_grad_body(n_line, block, place, delta, held, arrived, out):
    for i, weight in enumerate((held.at[2], held.at[3], arrived.at[2], arrived.at[3])):
        owner = (place[1] ^ (i % 2)) * 2 + (place[2] ^ (i // 2))
        part = lax.dot_general(delta[...], weight[...], contract_last, preferred_element_type=wide)
        part = part.astype(narrow)
        for z in range(n_line):
            start = pl.multiple_of((z * 4 + owner) * block, block)
            out[:, pl.ds(start, block)] = part[:, z * block : (z + 1) * block]


def all_rows(tokens, routes, gate_levels, latent_grad, down_weight, expert_in, expert_out):
    tok_rows, width = tokens.shape
    latent_width = down_weight.shape[1]
    hidden_width = expert_in.shape[2]
    n_major = lax.axis_size("expert")
    n_line = n_major // 2
    n_experts = n_major * 2
    block = width // n_experts
    major = lax.axis_index("expert")
    my_core = lax.axis_index("dp")
    place = jnp.stack(
        [major // 2, major % 2, my_core]
        + [(major ^ side) * 2 + (my_core ^ core) for core in range(2) for side in range(2)]
    ).astype(jnp.int32)
    shape = jax.ShapeDtypeStruct
    rows_of = lambda kind: shape((tok_rows, latent_width), kind)

    downs = [down_weight] + [turn(down_weight, n_line, back) for back in range(1, n_line)]

    gate_rows = -(-n_experts // 16) * 16
    columns = call(
        functools.partial(columns_body, n_line, block),
        [shape((tok_rows, n_line * block), narrow)] * 2
        + [shape((2, tok_rows, n_line * block), narrow), shape((2, latent_width, hidden_width), narrow)],
        "columns",
        scratch=[pltpu.SemaphoreType.DMA((4 * n_line + 2,))],
        outside=3,
    )(place, *(pltpu.with_memory_space_constraint(value, pltpu.HBM) for value in (tokens, expert_in, expert_out)))
    stack = lambda first, second, *earlier: call(
        stack_body, [shape((2,) + first.shape, narrow)], "stack"
    )(after(place, *earlier) if earlier else place, first, second)[0]
    (payload,) = call(payload_body, [shape((tok_rows + gate_rows, latent_width), narrow)], "payload")(
        place, routes.T, gate_levels.T, latent_grad
    )
    own = columns[3]
    core_own = swap(own, n_line, 1, 0)
    across = swap(columns[2], n_line, 0, 1)
    core_tokens = [swap(after(columns[1], across, core_own), n_line, 1, 0), swap(across[1], n_line, 1, 0)]
    side_in = swap(after(expert_in[0], across), n_line, 0, 1)

    project = call(
        functools.partial(project_body, n_line),
        [shape((2, tok_rows, latent_width), wide)] * 2 + [shape((n_line * block, latent_width), narrow)],
        "project",
    )
    keep, send, down = project(after(place, payload), columns[0], across, *core_tokens, *downs)
    half, cross = call(half_body, [rows_of(wide), rows_of(narrow)], "half")(
        place, keep, swap(send, n_line, 1, 0)
    )
    payloads = [payload] + [turn(after(payload, *downs[1:]), n_line, back) for back in range(1, n_line)]
    crossed = swap(cross, n_line, 0, 1)
    (latent,) = call(add_body, [rows_of(narrow)], "latent")(
        place, half, after(crossed, side_in, *payloads[1:])
    )
    groups = [[*range(1, n_line), 0]]
    riding = (1, n_line - 1)
    rows = [latent] + [turn(latent, n_line, back) for back in range(1, n_line)]

    side_out = swap(after(expert_out[0], latent), n_line, 0, 1)
    core_in = swap(after(side_in, latent), n_line, 1, 0)
    core_out = swap(after(side_out, *rows[1:]), n_line, 1, 0)
    weights = [own, core_own, side_in, side_out, core_in, core_out]
    side_down = swap(after(down, rows[1]), n_line, 0, 1)

    deltas_of, outs_of, saved = [None] * n_line, [None] * n_line, []
    done = latent
    for group in groups:
        count = len(group)
        outs = [rows_of(narrow if back else wide) for back in group for _ in range(2)]
        values = call(
            functools.partial(expert_body, count),
            outs + [shape((4, count * tok_rows, hidden_width), narrow)] * 3,
            "experts",
        )(after(place, done), *(rows[i] for i in group), *(payloads[i] for i in group), *weights)
        done, saved = values[0], saved + [list(values[-3:])]
        for i, back in enumerate(group):
            deltas_of[back], outs_of[back] = values[2 * i], values[2 * i + 1]

    def home(value, back):
        return turn(value, n_line, n_line - back) if back else value

    delta_lines = [home(value, back) for back, value in enumerate(deltas_of)]

    pair = (2, latent_width, hidden_width)
    near, far, near_other, far_other = call(
        functools.partial(weight_grad_body, n_line, len(groups)),
        [shape(pair, wide)] * 2 + [shape(pair, narrow)] * 2,
        "weight_grads",
        flops=2 * 8 * n_line * tok_rows * latent_width * hidden_width,
    )(
        place,
        *(rows[i] for group in groups for i in group),
        *(value for values in saved for value in values),
    )
    far_other = swap(far_other, n_line, 1, 0)
    ahead = latent_width // 2
    far_first, far_rest = call(
        far_body, [shape((rows, hidden_width), narrow) for rows in (ahead, 2 * latent_width - ahead)], "far_grads"
    )(place, far, far_other)
    far_first = swap(far_first, n_line, 0, 1)
    delta_lines = [after(line, near, far_rest) for line in delta_lines]
    (delta,) = call(add_body, [rows_of(narrow)], "latent_delta")(place, *delta_lines)
    side_delta = swap(delta, n_line, 0, 1)
    out_lines = [outs_of[0]] + [home(after(outs_of[back], delta), back) if back not in riding else None for back in range(1, n_line)]
    far_rest = swap(after(far_rest, side_delta), n_line, 0, 1)
    (others,) = call(pack_body, [shape((4, latent_width, hidden_width), narrow)], "pack")(
        after(place, delta), near_other, down, side_down
    )
    core_deltas = swap(stack(delta, side_delta, others, far_first, *(out_lines[back] for back in range(1, n_line) if back not in riding)), n_line, 1, 0)
    blocks = call(
        functools.partial(down_grad_body, n_line),
        [
            shape((2, block, latent_width) if back in riding else (block, latent_width), narrow if back else wide)
            for back in range(n_line)
        ],
        "down_grad",
    )(place, columns[0], across, *core_tokens, delta, side_delta, core_deltas, *(outs_of[back] for back in riding))
    others = [others, swap(after(others, blocks[1]), n_line, 1, 0)]
    (grad_tokens,) = call(
        functools.partial(token_grad_body, n_line, block), [shape((tok_rows, width), narrow)], "token_grad"
    )(place, after(delta, blocks[1]), *others)
    blocks = [blocks[0]] + [turn(blocks[back], n_line, n_line - back) for back in range(1, n_line)]
    grad_down, latent_out, grad_in, grad_out = call(
        functools.partial(last_body, riding, n_line),
        [shape((block, latent_width), wide), rows_of(narrow)]
        + [shape(value.shape, narrow) for value in (expert_in, expert_out)],
        "last_sums",
    )(after(place, grad_tokens), near, others[1], far_first, far_rest, *blocks, *(line for line in out_lines if line is not None))
    return (latent_out, grad_tokens, grad_down, grad_in, grad_out)


def slot_table(routes, capacity):
    flat = routes.reshape(-1)
    count = flat.shape[0]
    order = jnp.arange(count, dtype=jnp.int32)
    same = (flat[:, None] == flat[None, :]) & (order[None, :] < order[:, None])
    placed = jnp.sum(jnp.where(same, 1, 0), axis=1).astype(jnp.int32)
    return flat * capacity + placed


def routed_rows(tokens, routes, gate_levels, latent_grad, down_weight, expert_in, expert_out):
    tok_rows = tokens.shape[0]
    top = routes.shape[1]
    latent_width = down_weight.shape[1]
    n_major = lax.axis_size("expert")
    n_minor = lax.axis_size("dp")
    n_experts = n_major * n_minor
    capacity = 3 * tok_rows * top // (2 * n_experts)
    entries = tok_rows * top
    contract_last = (((1,), (1,)), ((), ()))
    contract_first = (((0,), (0,)), ((), ()))
    full_down = lax.all_gather(down_weight, ("expert", "dp"), axis=0, tiled=True)
    latent = jnp.dot(tokens, full_down, preferred_element_type=jnp.float32)
    latent = latent.astype(jnp.bfloat16)
    dest = slot_table(routes, capacity)
    source = (
        jnp.full((n_experts * capacity,), entries, jnp.int32)
        .at[dest]
        .set(jnp.arange(entries, dtype=jnp.int32))
    )
    token_of = jnp.where(source < entries, source // top, tok_rows)
    gates = gate_levels.astype(jnp.float32) * gate_unit
    zero_row = jnp.zeros((1, latent_width), jnp.bfloat16)
    latent_pad = jnp.concatenate([latent, zero_row], axis=0)
    send_latent = latent_pad[token_of].reshape(n_major, n_minor, capacity, latent_width)
    scaled = (gates[:, :, None] * latent_grad.astype(jnp.float32)[:, None, :]).astype(jnp.bfloat16)
    scaled_pad = jnp.concatenate([scaled.reshape(entries, latent_width), zero_row], axis=0)
    send_grad = scaled_pad[source].reshape(n_major, n_minor, capacity, latent_width)
    arrived = lax.all_to_all(
        lax.all_to_all(send_latent, "expert", split_axis=0, concat_axis=0, tiled=True),
        "dp",
        split_axis=1,
        concat_axis=1,
        tiled=True,
    )
    rows = arrived.reshape(-1, latent_width)
    weight_in = expert_in[0]
    weight_out = expert_out[0]
    before = jnp.dot(rows, weight_in, preferred_element_type=jnp.float32)
    active = jnp.maximum(before, 0.0)
    hidden = (active * active).astype(jnp.bfloat16)
    result = jnp.dot(hidden, weight_out, preferred_element_type=jnp.float32).astype(jnp.bfloat16)
    returned = lax.all_to_all(
        lax.all_to_all(
            result.reshape(n_major, n_minor, capacity, latent_width),
            "expert",
            split_axis=0,
            concat_axis=0,
            tiled=True,
        ),
        "dp",
        split_axis=1,
        concat_axis=1,
        tiled=True,
    )
    picked = returned.reshape(n_experts * capacity, latent_width)[dest].astype(jnp.float32)
    picked = picked.reshape(tok_rows, top, latent_width)
    latent_out = jnp.sum(gates[:, :, None] * picked, axis=1).astype(jnp.bfloat16)
    arrived_grad = lax.all_to_all(
        lax.all_to_all(send_grad, "expert", split_axis=0, concat_axis=0, tiled=True),
        "dp",
        split_axis=1,
        concat_axis=1,
        tiled=True,
    )
    grad_rows = arrived_grad.reshape(-1, latent_width)
    back_hidden = lax.dot_general(
        grad_rows, weight_out, contract_last, preferred_element_type=jnp.float32
    )
    back_pre = (back_hidden * 2.0 * active).astype(jnp.bfloat16)
    grad_out = lax.dot_general(
        hidden, grad_rows, contract_first, preferred_element_type=jnp.float32
    ).astype(jnp.bfloat16)
    grad_in = lax.dot_general(
        rows, back_pre, contract_first, preferred_element_type=jnp.float32
    ).astype(jnp.bfloat16)
    back_rows = lax.dot_general(
        back_pre, weight_in, contract_last, preferred_element_type=jnp.float32
    ).astype(jnp.bfloat16)
    came_back = lax.all_to_all(
        lax.all_to_all(
            back_rows.reshape(n_major, n_minor, capacity, latent_width),
            "expert",
            split_axis=0,
            concat_axis=0,
            tiled=True,
        ),
        "dp",
        split_axis=1,
        concat_axis=1,
        tiled=True,
    )
    gathered_back = came_back.reshape(n_experts * capacity, latent_width)[dest].astype(jnp.float32)
    latent_delta = jnp.sum(gathered_back.reshape(tok_rows, top, latent_width), axis=1).astype(
        jnp.bfloat16
    )
    grad_tokens = lax.dot_general(
        latent_delta, full_down, contract_last, preferred_element_type=jnp.float32
    )
    grad_tokens = grad_tokens.astype(jnp.bfloat16)
    grad_down = lax.psum_scatter(
        lax.dot_general(tokens, latent_delta, contract_first, preferred_element_type=jnp.float32),
        ("expert", "dp"),
        scatter_dimension=0,
        tiled=True,
    )
    return (latent_out, grad_tokens, grad_down, grad_in[None], grad_out[None])


def on_device(tokens, routes, *others):
    n_major = lax.axis_size("expert")
    n_experts = n_major * lax.axis_size("dp")
    few = n_experts <= 2 * routes.shape[1] and n_major % 2 == 0 and n_major >= 6 and lax.axis_size("dp") == 2
    return (all_rows if few else routed_rows)(tokens, routes, *others)


def solution(mesh):
    in_specs = (
        P(("group", "expert", "dp"), None),
        P(("group", "expert", "dp"), None),
        P(("group", "expert", "dp"), None),
        P(("group", "expert", "dp"), None),
        P(("expert", "dp"), None),
        P(("expert", "dp"), None, None),
        P(("expert", "dp"), None, None),
    )
    out_specs = (
        P(("group", "expert", "dp"), None),
        P(("group", "expert", "dp"), None),
        P(("group", "expert", "dp"), None),
        P(("group", "expert", "dp"), None, None),
        P(("group", "expert", "dp"), None, None),
    )
    return jax.shard_map(
        on_device, mesh=mesh, in_specs=in_specs, out_specs=out_specs, check_vma=False
    )
```

```python
import functools

import jax
import jax.numpy as jnp
from jax import lax
from jax.experimental import pallas as pl
from jax.experimental.pallas import tpu as pltpu
from jax.sharding import PartitionSpec as P

gate_unit = 1.0 / 1024.0
contract_last = (((1,), (1,)), ((), ()))
contract_first = (((0,), (0,)), ((), ()))
plane = ("expert", "dp")
wide = jnp.float32
narrow = jnp.bfloat16


def device_pairs(n_line, move):
    pairs = []
    for z in range(n_line):
        for x in range(2):
            for c in range(2):
                to_z, to_x, to_c = move(z, x, c)
                pairs.append(((z * 2 + x) * 2 + c, (to_z * 2 + to_x) * 2 + to_c))
    return pairs


def turn(value, n_line, by):
    return lax.ppermute(value, plane, device_pairs(n_line, lambda z, x, c: ((z + by) % n_line, x, c)))


def swap(value, n_line, core, side):
    return lax.ppermute(value, plane, device_pairs(n_line, lambda z, x, c: (z, x ^ side, c ^ core)))


def after(value, *earlier):
    return lax.optimization_barrier((value,) + earlier)[0]


def call(body, outs, name, scratch=(), outside=0, flops=0):
    vmem = pl.BlockSpec(memory_space=pltpu.VMEM)
    outer = pl.BlockSpec(memory_space=pltpu.HBM)

    def run(place, *operands):
        return pl.pallas_call(
            body,
            out_shape=outs,
            in_specs=[pl.BlockSpec(memory_space=pltpu.SMEM)]
            + [outer] * outside
            + [vmem] * (len(operands) - outside),
            out_specs=[vmem] * len(outs),
            scratch_shapes=list(scratch),
            compiler_params=pltpu.CompilerParams(vmem_limit_bytes=40 * 1024 * 1024),
            cost_estimate=pl.CostEstimate(flops=flops, bytes_accessed=0, transcendentals=0),
            name=name,
        )(place, *operands)

    return run


def columns_body(n_line, block, place, tokens, expert_in, expert_out, *refs):
    own, other, across, weights, sems = refs
    pieces = (own, across.at[0], other, across.at[1])
    copies = []
    for i, weight in enumerate((expert_in, expert_out)):
        copies.append(pltpu.make_async_copy(weight, weights.at[pl.ds(i, 1)], sems.at[i]))
    for core in range(2):
        for side in range(2):
            owner = (place[1] ^ side) * 2 + (place[2] ^ core)
            for z in range(n_line):
                start = pl.multiple_of((z * 4 + owner) * block, block)
                piece = pieces[core * 2 + side].at[:, pl.ds(z * block, block)]
                copies.append(
                    pltpu.make_async_copy(tokens.at[:, pl.ds(start, block)], piece, sems.at[len(copies)])
                )
    for copy in copies:
        copy.start()
    for copy in copies:
        copy.wait()


def stack_body(place, first, second, out):
    out[0], out[1] = first[...], second[...]


def add_body(place, *refs):
    total = refs[0][...].astype(wide)
    for value in refs[1:-1]:
        total = total + value[...].astype(wide)
    refs[-1][...] = total.astype(refs[-1].dtype)


def half_body(place, keep, arrived, mine, other):
    mine[...] = keep[0] + arrived[0]
    other[...] = (keep[1] + arrived[1]).astype(narrow)


def far_body(place, far, arrived, first, rest):
    split, width = first.shape[0], far.shape[1]
    total = [far[i] + arrived[i].astype(wide) for i in range(2)]
    first[...] = total[0][:split].astype(narrow)
    rest[: width - split] = total[0][split:].astype(narrow)
    rest[width - split :] = total[1].astype(narrow)


def pack_body(place, grads, down, side_down, out):
    out[:2] = grads[...]
    out[2], out[3] = down[...], side_down[...]


def last_body(riding, n_line, place, near, others, first, rest, *refs):
    blocks, pieces = refs[:n_line], list(refs[n_line:-4])
    grad_down, combined, *grads = refs[-4:]
    split = grads[0].shape[1] - first.shape[0]
    far = (jnp.concatenate([first[...], rest[:split]], axis=0), rest[split:])
    for i, out in enumerate(grads):
        out[0] = (near[i] + others[i].astype(wide) + far[i].astype(wide)).astype(narrow)
    total = blocks[0][...]
    out_total = pieces.pop(0)[...]
    for back in range(1, n_line):
        block = blocks[back].at[0] if back in riding else blocks[back]
        piece = blocks[back].at[1] if back in riding else pieces.pop(0)
        total = total + block[...].astype(wide)
        out_total = out_total + piece[...].astype(wide)
    grad_down[...] = total
    combined[...] = out_total.astype(narrow)


def payload_body(place, routes, levels, cotangent, payload):
    tok_rows = cotangent.shape[0]
    gate_rows = payload.shape[0] - tok_rows
    payload[:tok_rows, :] = cotangent[...]
    expert = lax.broadcasted_iota(jnp.int32, (gate_rows, tok_rows), 0)
    total = jnp.zeros((gate_rows, tok_rows), jnp.int32)
    for k in range(routes.shape[0]):
        total = total + jnp.where(expert == routes[k : k + 1, :], levels[k : k + 1, :], 0)
    low = total & 31
    payload[tok_rows:, :tok_rows] = (total - low).astype(wide).astype(narrow)
    payload[tok_rows:, tok_rows : 2 * tok_rows] = low.astype(wide).astype(narrow)
    rest = payload.shape[1] - 2 * tok_rows
    payload[tok_rows:, 2 * tok_rows :] = jnp.zeros((gate_rows, rest), narrow)


def project_body(n_line, place, *refs):
    own, across, core, core_across, *downs = refs[: 4 + n_line]
    pieces = (own, across.at[0], core, core_across)
    keep, send, down = refs[4 + n_line :]
    block = downs[0].shape[0]
    for back in range(n_line):
        z = lax.rem(place[0] + n_line - back, n_line)
        down[pl.ds(pl.multiple_of(z * block, block), block), :] = downs[back][...]
    for core, out in ((1, send), (0, keep)):
        for side in range(2):
            out[side] = jnp.dot(pieces[core * 2 + side][...], down[...], preferred_element_type=wide)


def gate_tile(payload, tok_rows, expert):
    packed = payload[tok_rows:, :]
    rows = lax.broadcasted_iota(jnp.int32, (packed.shape[0], 128), 0)
    pick = jnp.where(rows == expert, 1.0, 0.0).astype(narrow)
    dot = functools.partial(lax.dot_general, dimension_numbers=contract_first, preferred_element_type=wide)
    total = dot(packed[:, :tok_rows], pick) + dot(packed[:, tok_rows : 2 * tok_rows], pick)
    return total * gate_unit


def expert_body(count, place, *refs):
    rows_in, payloads = refs[:count], refs[count : 2 * count]
    own, core, *sides = refs[2 * count : 2 * count + 6]
    weights = (own.at[0], own.at[1], sides[0], sides[1], core.at[0], core.at[1], sides[2], sides[3])
    outs = refs[2 * count + 6 :]
    *sums, hiddens, scaleds, back_pres = outs
    tok_rows, width = rows_in[0].shape
    for first in range(0, count, 4):
        group = range(first, min(first + 4, count))
        span = slice(first * tok_rows, (first + len(group)) * tok_rows)
        stack = lambda values: jnp.concatenate(list(values), axis=0)
        rows = stack(rows_in[i][...] for i in group)
        cotangent = stack(payloads[i][:tok_rows, :] for i in group).astype(wide)
        out_sum = jnp.zeros(rows.shape, wide)
        delta_sum = jnp.zeros(rows.shape, wide)
        for e in range(4):
            weight_in, weight_out = weights[2 * e], weights[2 * e + 1]
            gate = stack(gate_tile(payloads[i], tok_rows, place[3 + e]) for i in group)
            gate = jnp.concatenate([gate] * (width // 128), axis=1)
            active = jnp.maximum(jnp.dot(rows, weight_in[...], preferred_element_type=wide), 0.0)
            hidden = (active * active).astype(narrow)
            hiddens[e, span, :] = hidden
            scaled = (gate * cotangent).astype(narrow)
            scaleds[e, span, :] = scaled
            back_hidden = lax.dot_general(scaled, weight_out[...], contract_last, preferred_element_type=wide)
            back_pre = (back_hidden * 2.0 * active).astype(narrow)
            back_pres[e, span, :] = back_pre
            result = jnp.dot(hidden, weight_out[...], preferred_element_type=wide).astype(narrow)
            out_sum = out_sum + gate * result.astype(wide)
            back_rows = lax.dot_general(back_pre, weight_in[...], contract_last, preferred_element_type=wide)
            delta_sum = delta_sum + back_rows.astype(narrow).astype(wide)
        for i in group:
            part = slice((i - first) * tok_rows, (i - first + 1) * tok_rows)
            out = sums.pop(0)
            out[...] = delta_sum[part].astype(out.dtype)
            out = sums.pop(0)
            out[...] = out_sum[part].astype(out.dtype)


def weight_grad_body(side, n_rows, n_sets, place, *refs):
    rows_in = refs[:n_rows]
    sets = [refs[n_rows + 3 * i : n_rows + 3 * i + 3] for i in range(n_sets)]
    outs = refs[n_rows + 3 * n_sets :]
    dot = functools.partial(lax.dot_general, dimension_numbers=contract_first, preferred_element_type=wide)
    rows = jnp.concatenate([r[...] for r in rows_in], axis=0)
    for core, out in enumerate(outs):
        hidden, scaled, back_pre = (
            jnp.concatenate([values[i][core * 2 + side] for values in sets], axis=0) for i in range(3)
        )
        out[0] = dot(rows, back_pre).astype(out.dtype)
        out[1] = dot(hidden, scaled).astype(out.dtype)


def down_grad_body(n_line, place, *refs):
    own, across, core, core_across, *deltas, core_deltas = refs[:7]
    riders, blocks = refs[7:-n_line], refs[-n_line:]
    tokens = jnp.concatenate([own[...], across[0], core[...], core_across[...]], axis=0)
    delta = jnp.concatenate([d[...] for d in deltas] + [core_deltas[0], core_deltas[1]], axis=0)
    part = lax.dot_general(tokens, delta, contract_first, preferred_element_type=wide)
    block = blocks[0].shape[0]
    targets = [out if len(out.shape) == 2 else out.at[0] for out in blocks]
    for rider, out in zip(riders, [out for out in blocks if len(out.shape) == 3]):
        out[1] = rider[...]
    for z in range(n_line):
        for back in range(n_line):

            @pl.when(lax.rem(place[0] + n_line - back, n_line) == z)
            def _(z=z, back=back):
                targets[back][...] = part[z * block : (z + 1) * block].astype(targets[back].dtype)


def token_grad_body(n_line, block, place, delta, held, arrived, out):
    for i, weight in enumerate((held.at[2], held.at[3], arrived.at[2], arrived.at[3])):
        owner = (place[1] ^ (i % 2)) * 2 + (place[2] ^ (i // 2))
        part = lax.dot_general(delta[...], weight[...], contract_last, preferred_element_type=wide)
        part = part.astype(narrow)
        for z in range(n_line):
            start = pl.multiple_of((z * 4 + owner) * block, block)
            out[:, pl.ds(start, block)] = part[:, z * block : (z + 1) * block]


def all_rows(tokens, routes, gate_levels, latent_grad, down_weight, expert_in, expert_out):
    tok_rows, width = tokens.shape
    latent_width = down_weight.shape[1]
    hidden_width = expert_in.shape[2]
    n_major = lax.axis_size("expert")
    n_line = n_major // 2
    n_experts = n_major * 2
    block = width // n_experts
    major = lax.axis_index("expert")
    my_core = lax.axis_index("dp")
    place = jnp.stack(
        [major // 2, major % 2, my_core]
        + [(major ^ side) * 2 + (my_core ^ core) for core in range(2) for side in range(2)]
    ).astype(jnp.int32)
    shape = jax.ShapeDtypeStruct
    rows_of = lambda kind: shape((tok_rows, latent_width), kind)

    downs = [down_weight] + [turn(down_weight, n_line, back) for back in range(1, n_line)]

    gate_rows = -(-n_experts // 16) * 16
    columns = call(
        functools.partial(columns_body, n_line, block),
        [shape((tok_rows, n_line * block), narrow)] * 2
        + [shape((2, tok_rows, n_line * block), narrow), shape((2, latent_width, hidden_width), narrow)],
        "columns",
        scratch=[pltpu.SemaphoreType.DMA((4 * n_line + 2,))],
        outside=3,
    )(place, *(pltpu.with_memory_space_constraint(value, pltpu.HBM) for value in (tokens, expert_in, expert_out)))
    stack = lambda first, second, *earlier: call(
        stack_body, [shape((2,) + first.shape, narrow)], "stack"
    )(after(place, *earlier) if earlier else place, first, second)[0]
    (payload,) = call(payload_body, [shape((tok_rows + gate_rows, latent_width), narrow)], "payload")(
        place, routes.T, gate_levels.T, latent_grad
    )
    own = columns[3]
    core_own = swap(own, n_line, 1, 0)
    across = swap(columns[2], n_line, 0, 1)
    core_tokens = [swap(after(columns[1], across, core_own), n_line, 1, 0), swap(across[1], n_line, 1, 0)]
    side_in = swap(after(expert_in[0], across), n_line, 0, 1)

    project = call(
        functools.partial(project_body, n_line),
        [shape((2, tok_rows, latent_width), wide)] * 2 + [shape((n_line * block, latent_width), narrow)],
        "project",
    )
    keep, send, down = project(after(place, payload), columns[0], across, *core_tokens, *downs)
    half, cross = call(half_body, [rows_of(wide), rows_of(narrow)], "half")(
        place, keep, swap(send, n_line, 1, 0)
    )
    payloads = [payload] + [turn(after(payload, *downs[1:]), n_line, back) for back in range(1, n_line)]
    crossed = swap(cross, n_line, 0, 1)
    (latent,) = call(add_body, [rows_of(narrow)], "latent")(
        place, half, after(crossed, side_in, *payloads[1:])
    )
    groups = [[*range(1, n_line), 0]]
    riding = (1, n_line - 1)
    rows = [latent] + [turn(latent, n_line, back) for back in range(1, n_line)]

    side_out = swap(after(expert_out[0], latent), n_line, 0, 1)
    core_in = swap(after(side_in, latent), n_line, 1, 0)
    core_out = swap(after(side_out, *rows[1:]), n_line, 1, 0)
    weights = [own, core_own, side_in, side_out, core_in, core_out]
    side_down = swap(after(down, rows[1]), n_line, 0, 1)

    deltas_of, outs_of, saved = [None] * n_line, [None] * n_line, []
    done = latent
    for group in groups:
        count = len(group)
        outs = [rows_of(narrow if back else wide) for back in group for _ in range(2)]
        values = call(
            functools.partial(expert_body, count),
            outs + [shape((4, count * tok_rows, hidden_width), narrow)] * 3,
            "experts",
        )(after(place, done), *(rows[i] for i in group), *(payloads[i] for i in group), *weights)
        done, saved = values[0], saved + [list(values[-3:])]
        for i, back in enumerate(group):
            deltas_of[back], outs_of[back] = values[2 * i], values[2 * i + 1]

    def home(value, back):
        return turn(value, n_line, n_line - back) if back else value

    delta_lines = [home(value, back) for back, value in enumerate(deltas_of)]

    pair = (2, latent_width, hidden_width)

    def weight_grads(side, *earlier):
        return call(
            functools.partial(weight_grad_body, side, n_line, len(groups)),
            [shape(pair, wide), shape(pair, narrow)],
            "weight_grads",
            flops=2 * 4 * n_line * tok_rows * latent_width * hidden_width,
        )(
            after(place, *earlier),
            *(rows[i] for group in groups for i in group),
            *(value for values in saved for value in values),
        )

    far, far_other = weight_grads(1)
    far_other = swap(far_other, n_line, 1, 0)
    ahead = latent_width // 2
    far_first, far_rest = call(
        far_body, [shape((rows, hidden_width), narrow) for rows in (ahead, 2 * latent_width - ahead)], "far_grads"
    )(place, far, far_other)
    far_first = swap(far_first, n_line, 0, 1)
    delta_lines = [after(line, far_rest) for line in delta_lines]
    (delta,) = call(add_body, [rows_of(narrow)], "latent_delta")(place, *delta_lines)
    side_delta = swap(delta, n_line, 0, 1)
    out_lines = [outs_of[0]] + [home(after(outs_of[back], delta), back) if back not in riding else None for back in range(1, n_line)]
    far_rest = swap(after(far_rest, side_delta), n_line, 0, 1)
    near, near_other = weight_grads(0, delta)
    (others,) = call(pack_body, [shape((4, latent_width, hidden_width), narrow)], "pack")(
        after(place, delta), near_other, down, side_down
    )
    core_deltas = swap(stack(delta, side_delta, others, far_first, *(out_lines[back] for back in range(1, n_line) if back not in riding)), n_line, 1, 0)
    blocks = call(
        functools.partial(down_grad_body, n_line),
        [
            shape((2, block, latent_width) if back in riding else (block, latent_width), narrow if back else wide)
            for back in range(n_line)
        ],
        "down_grad",
    )(place, columns[0], across, *core_tokens, delta, side_delta, core_deltas, *(outs_of[back] for back in riding))
    others = [others, swap(after(others, blocks[1]), n_line, 1, 0)]
    (grad_tokens,) = call(
        functools.partial(token_grad_body, n_line, block), [shape((tok_rows, width), narrow)], "token_grad"
    )(place, after(delta, blocks[1]), *others)
    blocks = [blocks[0]] + [turn(blocks[back], n_line, n_line - back) for back in range(1, n_line)]
    grad_down, latent_out, grad_in, grad_out = call(
        functools.partial(last_body, riding, n_line),
        [shape((block, latent_width), wide), rows_of(narrow)]
        + [shape(value.shape, narrow) for value in (expert_in, expert_out)],
        "last_sums",
    )(after(place, grad_tokens), near, others[1], far_first, far_rest, *blocks, *(line for line in out_lines if line is not None))
    return (latent_out, grad_tokens, grad_down, grad_in, grad_out)


def slot_table(routes, capacity):
    flat = routes.reshape(-1)
    count = flat.shape[0]
    order = jnp.arange(count, dtype=jnp.int32)
    same = (flat[:, None] == flat[None, :]) & (order[None, :] < order[:, None])
    placed = jnp.sum(jnp.where(same, 1, 0), axis=1).astype(jnp.int32)
    return flat * capacity + placed


def routed_rows(tokens, routes, gate_levels, latent_grad, down_weight, expert_in, expert_out):
    tok_rows = tokens.shape[0]
    top = routes.shape[1]
    latent_width = down_weight.shape[1]
    n_major = lax.axis_size("expert")
    n_minor = lax.axis_size("dp")
    n_experts = n_major * n_minor
    capacity = 3 * tok_rows * top // (2 * n_experts)
    entries = tok_rows * top
    contract_last = (((1,), (1,)), ((), ()))
    contract_first = (((0,), (0,)), ((), ()))
    full_down = lax.all_gather(down_weight, ("expert", "dp"), axis=0, tiled=True)
    latent = jnp.dot(tokens, full_down, preferred_element_type=jnp.float32)
    latent = latent.astype(jnp.bfloat16)
    dest = slot_table(routes, capacity)
    source = (
        jnp.full((n_experts * capacity,), entries, jnp.int32)
        .at[dest]
        .set(jnp.arange(entries, dtype=jnp.int32))
    )
    token_of = jnp.where(source < entries, source // top, tok_rows)
    gates = gate_levels.astype(jnp.float32) * gate_unit
    zero_row = jnp.zeros((1, latent_width), jnp.bfloat16)
    latent_pad = jnp.concatenate([latent, zero_row], axis=0)
    send_latent = latent_pad[token_of].reshape(n_major, n_minor, capacity, latent_width)
    scaled = (gates[:, :, None] * latent_grad.astype(jnp.float32)[:, None, :]).astype(jnp.bfloat16)
    scaled_pad = jnp.concatenate([scaled.reshape(entries, latent_width), zero_row], axis=0)
    send_grad = scaled_pad[source].reshape(n_major, n_minor, capacity, latent_width)
    arrived = lax.all_to_all(
        lax.all_to_all(send_latent, "expert", split_axis=0, concat_axis=0, tiled=True),
        "dp",
        split_axis=1,
        concat_axis=1,
        tiled=True,
    )
    rows = arrived.reshape(-1, latent_width)
    weight_in = expert_in[0]
    weight_out = expert_out[0]
    before = jnp.dot(rows, weight_in, preferred_element_type=jnp.float32)
    active = jnp.maximum(before, 0.0)
    hidden = (active * active).astype(jnp.bfloat16)
    result = jnp.dot(hidden, weight_out, preferred_element_type=jnp.float32).astype(jnp.bfloat16)
    returned = lax.all_to_all(
        lax.all_to_all(
            result.reshape(n_major, n_minor, capacity, latent_width),
            "expert",
            split_axis=0,
            concat_axis=0,
            tiled=True,
        ),
        "dp",
        split_axis=1,
        concat_axis=1,
        tiled=True,
    )
    picked = returned.reshape(n_experts * capacity, latent_width)[dest].astype(jnp.float32)
    picked = picked.reshape(tok_rows, top, latent_width)
    latent_out = jnp.sum(gates[:, :, None] * picked, axis=1).astype(jnp.bfloat16)
    arrived_grad = lax.all_to_all(
        lax.all_to_all(send_grad, "expert", split_axis=0, concat_axis=0, tiled=True),
        "dp",
        split_axis=1,
        concat_axis=1,
        tiled=True,
    )
    grad_rows = arrived_grad.reshape(-1, latent_width)
    back_hidden = lax.dot_general(
        grad_rows, weight_out, contract_last, preferred_element_type=jnp.float32
    )
    back_pre = (back_hidden * 2.0 * active).astype(jnp.bfloat16)
    grad_out = lax.dot_general(
        hidden, grad_rows, contract_first, preferred_element_type=jnp.float32
    ).astype(jnp.bfloat16)
    grad_in = lax.dot_general(
        rows, back_pre, contract_first, preferred_element_type=jnp.float32
    ).astype(jnp.bfloat16)
    back_rows = lax.dot_general(
        back_pre, weight_in, contract_last, preferred_element_type=jnp.float32
    ).astype(jnp.bfloat16)
    came_back = lax.all_to_all(
        lax.all_to_all(
            back_rows.reshape(n_major, n_minor, capacity, latent_width),
            "expert",
            split_axis=0,
            concat_axis=0,
            tiled=True,
        ),
        "dp",
        split_axis=1,
        concat_axis=1,
        tiled=True,
    )
    gathered_back = came_back.reshape(n_experts * capacity, latent_width)[dest].astype(jnp.float32)
    latent_delta = jnp.sum(gathered_back.reshape(tok_rows, top, latent_width), axis=1).astype(
        jnp.bfloat16
    )
    grad_tokens = lax.dot_general(
        latent_delta, full_down, contract_last, preferred_element_type=jnp.float32
    )
    grad_tokens = grad_tokens.astype(jnp.bfloat16)
    grad_down = lax.psum_scatter(
        lax.dot_general(tokens, latent_delta, contract_first, preferred_element_type=jnp.float32),
        ("expert", "dp"),
        scatter_dimension=0,
        tiled=True,
    )
    return (latent_out, grad_tokens, grad_down, grad_in[None], grad_out[None])


def on_device(tokens, routes, *others):
    n_major = lax.axis_size("expert")
    n_experts = n_major * lax.axis_size("dp")
    few = n_experts <= 2 * routes.shape[1] and n_major % 2 == 0 and n_major >= 6 and lax.axis_size("dp") == 2
    return (all_rows if few else routed_rows)(tokens, routes, *others)


def solution(mesh):
    in_specs = (
        P(("group", "expert", "dp"), None),
        P(("group", "expert", "dp"), None),
        P(("group", "expert", "dp"), None),
        P(("group", "expert", "dp"), None),
        P(("expert", "dp"), None),
        P(("expert", "dp"), None, None),
        P(("expert", "dp"), None, None),
    )
    out_specs = (
        P(("group", "expert", "dp"), None),
        P(("group", "expert", "dp"), None),
        P(("group", "expert", "dp"), None),
        P(("group", "expert", "dp"), None, None),
        P(("group", "expert", "dp"), None, None),
    )
    return jax.shard_map(
        on_device, mesh=mesh, in_specs=in_specs, out_specs=out_specs, check_vma=False
    )
```

```python
import functools

import jax
import jax.numpy as jnp
from jax import lax
from jax.experimental import pallas as pl
from jax.experimental.pallas import tpu as pltpu
from jax.sharding import PartitionSpec as P

gate_unit = 1.0 / 1024.0
contract_last = (((1,), (1,)), ((), ()))
contract_first = (((0,), (0,)), ((), ()))
plane = ("expert", "dp")
wide = jnp.float32
narrow = jnp.bfloat16


def device_pairs(n_line, move):
    pairs = []
    for z in range(n_line):
        for x in range(2):
            for c in range(2):
                to_z, to_x, to_c = move(z, x, c)
                pairs.append(((z * 2 + x) * 2 + c, (to_z * 2 + to_x) * 2 + to_c))
    return pairs


def turn(value, n_line, by):
    return lax.ppermute(value, plane, device_pairs(n_line, lambda z, x, c: ((z + by) % n_line, x, c)))


def swap(value, n_line, core, side):
    return lax.ppermute(value, plane, device_pairs(n_line, lambda z, x, c: (z, x ^ side, c ^ core)))


def after(value, *earlier):
    return lax.optimization_barrier((value,) + earlier)[0]


def call(body, outs, name, scratch=(), outside=0, flops=0):
    vmem = pl.BlockSpec(memory_space=pltpu.VMEM)
    outer = pl.BlockSpec(memory_space=pltpu.HBM)

    def run(place, *operands):
        return pl.pallas_call(
            body,
            out_shape=outs,
            in_specs=[pl.BlockSpec(memory_space=pltpu.SMEM)]
            + [outer] * outside
            + [vmem] * (len(operands) - outside),
            out_specs=[vmem] * len(outs),
            scratch_shapes=list(scratch),
            compiler_params=pltpu.CompilerParams(vmem_limit_bytes=40 * 1024 * 1024),
            cost_estimate=pl.CostEstimate(flops=flops, bytes_accessed=0, transcendentals=0),
            name=name,
        )(place, *operands)

    return run


def columns_body(n_line, block, place, tokens, expert_in, expert_out, *refs):
    own, other, across, weights, sems = refs
    pieces = (own, across.at[0], other, across.at[1])
    copies = []
    for i, weight in enumerate((expert_in, expert_out)):
        copies.append(pltpu.make_async_copy(weight, weights.at[pl.ds(i, 1)], sems.at[i]))
    for core in range(2):
        for side in range(2):
            owner = (place[1] ^ side) * 2 + (place[2] ^ core)
            for z in range(n_line):
                start = pl.multiple_of((z * 4 + owner) * block, block)
                piece = pieces[core * 2 + side].at[:, pl.ds(z * block, block)]
                copies.append(
                    pltpu.make_async_copy(tokens.at[:, pl.ds(start, block)], piece, sems.at[len(copies)])
                )
    for copy in copies:
        copy.start()
    for copy in copies:
        copy.wait()


def add_body(place, *refs):
    total = refs[0][...].astype(wide)
    for value in refs[1:-1]:
        total = total + value[...].astype(wide)
    refs[-1][...] = total.astype(refs[-1].dtype)


def half_body(place, keep, arrived, mine, other):
    mine[...] = keep[0] + arrived[0]
    other[...] = (keep[1] + arrived[1]).astype(narrow)


def far_body(place, far, arrived, first, rest):
    split, width = first.shape[0], far.shape[1]
    total = [far[i] + arrived[i].astype(wide) for i in range(2)]
    first[...] = total[0][:split].astype(narrow)
    rest[: width - split] = total[0][split:].astype(narrow)
    rest[width - split :] = total[1].astype(narrow)


def pack_body(place, grads, down, side_down, out):
    out[:2] = grads[...]
    out[2], out[3] = down[...], side_down[...]


def last_body(riding, n_line, place, near, others, first, rest, *refs):
    blocks, pieces = refs[:n_line], list(refs[n_line:-4])
    grad_down, combined, *grads = refs[-4:]
    split = grads[0].shape[1] - first.shape[0]
    far = (jnp.concatenate([first[...], rest[:split]], axis=0), rest[split:])
    for i, out in enumerate(grads):
        out[0] = (near[i] + others[i].astype(wide) + far[i].astype(wide)).astype(narrow)
    total = blocks[0][...]
    out_total = pieces.pop(0)[...]
    for back in range(1, n_line):
        block = blocks[back].at[0] if back in riding else blocks[back]
        piece = blocks[back].at[1] if back in riding else pieces.pop(0)
        total = total + block[...].astype(wide)
        out_total = out_total + piece[...].astype(wide)
    grad_down[...] = total
    combined[...] = out_total.astype(narrow)


def payload_body(place, routes, levels, cotangent, payload):
    tok_rows = cotangent.shape[0]
    gate_rows = payload.shape[0] - tok_rows
    payload[:tok_rows, :] = cotangent[...]
    expert = lax.broadcasted_iota(jnp.int32, (gate_rows, tok_rows), 0)
    total = jnp.zeros((gate_rows, tok_rows), jnp.int32)
    for k in range(routes.shape[0]):
        total = total + jnp.where(expert == routes[k : k + 1, :], levels[k : k + 1, :], 0)
    low = total & 31
    payload[tok_rows:, :tok_rows] = (total - low).astype(wide).astype(narrow)
    payload[tok_rows:, tok_rows : 2 * tok_rows] = low.astype(wide).astype(narrow)
    rest = payload.shape[1] - 2 * tok_rows
    payload[tok_rows:, 2 * tok_rows :] = jnp.zeros((gate_rows, rest), narrow)


def project_body(n_line, place, *refs):
    own, across, core, core_across, *downs = refs[: 4 + n_line]
    pieces = (own, across.at[0], core, core_across)
    keep, send, down = refs[4 + n_line :]
    block = downs[0].shape[0]
    for back in range(n_line):
        z = lax.rem(place[0] + n_line - back, n_line)
        down[pl.ds(pl.multiple_of(z * block, block), block), :] = downs[back][...]
    for core, out in ((1, send), (0, keep)):
        for side in range(2):
            out[side] = jnp.dot(pieces[core * 2 + side][...], down[...], preferred_element_type=wide)


def gate_tile(payload, tok_rows, expert):
    packed = payload[tok_rows:, :]
    rows = lax.broadcasted_iota(jnp.int32, (packed.shape[0], 128), 0)
    pick = jnp.where(rows == expert, 1.0, 0.0).astype(narrow)
    dot = functools.partial(lax.dot_general, dimension_numbers=contract_first, preferred_element_type=wide)
    total = dot(packed[:, :tok_rows], pick) + dot(packed[:, tok_rows : 2 * tok_rows], pick)
    return total * gate_unit


def expert_body(count, place, *refs):
    rows_in, payloads = refs[:count], refs[count : 2 * count]
    own, core, *sides = refs[2 * count : 2 * count + 6]
    weights = (own.at[0], own.at[1], sides[0], sides[1], core.at[0], core.at[1], sides[2], sides[3])
    outs = refs[2 * count + 6 :]
    *sums, hiddens, scaleds, back_pres = outs
    tok_rows, width = rows_in[0].shape
    for first in range(0, count, 4):
        group = range(first, min(first + 4, count))
        span = slice(first * tok_rows, (first + len(group)) * tok_rows)
        stack = lambda values: jnp.concatenate(list(values), axis=0)
        rows = stack(rows_in[i][...] for i in group)
        cotangent = stack(payloads[i][:tok_rows, :] for i in group).astype(wide)
        out_sum = jnp.zeros(rows.shape, wide)
        delta_sum = jnp.zeros(rows.shape, wide)
        for e in range(4):
            weight_in, weight_out = weights[2 * e], weights[2 * e + 1]
            gate = stack(gate_tile(payloads[i], tok_rows, place[3 + e]) for i in group)
            gate = jnp.concatenate([gate] * (width // 128), axis=1)
            active = jnp.maximum(jnp.dot(rows, weight_in[...], preferred_element_type=wide), 0.0)
            hidden = (active * active).astype(narrow)
            hiddens[e, span, :] = hidden
            scaled = (gate * cotangent).astype(narrow)
            scaleds[e, span, :] = scaled
            back_hidden = lax.dot_general(scaled, weight_out[...], contract_last, preferred_element_type=wide)
            back_pre = (back_hidden * 2.0 * active).astype(narrow)
            back_pres[e, span, :] = back_pre
            result = jnp.dot(hidden, weight_out[...], preferred_element_type=wide).astype(narrow)
            out_sum = out_sum + gate * result.astype(wide)
            back_rows = lax.dot_general(back_pre, weight_in[...], contract_last, preferred_element_type=wide)
            delta_sum = delta_sum + back_rows.astype(narrow).astype(wide)
        for i in group:
            part = slice((i - first) * tok_rows, (i - first + 1) * tok_rows)
            out = sums.pop(0)
            out[...] = delta_sum[part].astype(out.dtype)
            out = sums.pop(0)
            out[...] = out_sum[part].astype(out.dtype)


def weight_grad_body(side, n_rows, n_sets, place, *refs):
    rows_in = refs[:n_rows]
    sets = [refs[n_rows + 3 * i : n_rows + 3 * i + 3] for i in range(n_sets)]
    outs = refs[n_rows + 3 * n_sets :]
    dot = functools.partial(lax.dot_general, dimension_numbers=contract_first, preferred_element_type=wide)
    rows = jnp.concatenate([r[...] for r in rows_in], axis=0)
    for core, out in enumerate(outs):
        hidden, scaled, back_pre = (
            jnp.concatenate([values[i][core * 2 + side] for values in sets], axis=0) for i in range(3)
        )
        out[0] = dot(rows, back_pre).astype(out.dtype)
        out[1] = dot(hidden, scaled).astype(out.dtype)


def down_grad_body(n_line, place, *refs):
    own, across, core, core_across, *deltas = refs[:8]
    riders, blocks = refs[8:-n_line], refs[-n_line:]
    tokens = jnp.concatenate([own[...], across[0], core[...], core_across[...]], axis=0)
    delta = jnp.concatenate([d[...] for d in deltas], axis=0)
    part = lax.dot_general(tokens, delta, contract_first, preferred_element_type=wide)
    block = blocks[0].shape[0]
    targets = [out if len(out.shape) == 2 else out.at[0] for out in blocks]
    for rider, out in zip(riders, [out for out in blocks if len(out.shape) == 3]):
        out[1] = rider[...]
    for z in range(n_line):
        for back in range(n_line):

            @pl.when(lax.rem(place[0] + n_line - back, n_line) == z)
            def _(z=z, back=back):
                targets[back][...] = part[z * block : (z + 1) * block].astype(targets[back].dtype)


def token_grad_body(n_line, block, place, delta, held, arrived, out):
    for i, weight in enumerate((held.at[2], held.at[3], arrived.at[2], arrived.at[3])):
        owner = (place[1] ^ (i % 2)) * 2 + (place[2] ^ (i // 2))
        part = lax.dot_general(delta[...], weight[...], contract_last, preferred_element_type=wide)
        part = part.astype(narrow)
        for z in range(n_line):
            start = pl.multiple_of((z * 4 + owner) * block, block)
            out[:, pl.ds(start, block)] = part[:, z * block : (z + 1) * block]


def all_rows(tokens, routes, gate_levels, latent_grad, down_weight, expert_in, expert_out):
    tok_rows, width = tokens.shape
    latent_width = down_weight.shape[1]
    hidden_width = expert_in.shape[2]
    n_major = lax.axis_size("expert")
    n_line = n_major // 2
    n_experts = n_major * 2
    block = width // n_experts
    major = lax.axis_index("expert")
    my_core = lax.axis_index("dp")
    place = jnp.stack(
        [major // 2, major % 2, my_core]
        + [(major ^ side) * 2 + (my_core ^ core) for core in range(2) for side in range(2)]
    ).astype(jnp.int32)
    shape = jax.ShapeDtypeStruct
    rows_of = lambda kind: shape((tok_rows, latent_width), kind)

    downs = [down_weight] + [turn(down_weight, n_line, back) for back in range(1, n_line)]

    gate_rows = -(-n_experts // 16) * 16
    columns = call(
        functools.partial(columns_body, n_line, block),
        [shape((tok_rows, n_line * block), narrow)] * 2
        + [shape((2, tok_rows, n_line * block), narrow), shape((2, latent_width, hidden_width), narrow)],
        "columns",
        scratch=[pltpu.SemaphoreType.DMA((4 * n_line + 2,))],
        outside=3,
    )(place, *(pltpu.with_memory_space_constraint(value, pltpu.HBM) for value in (tokens, expert_in, expert_out)))
    (payload,) = call(payload_body, [shape((tok_rows + gate_rows, latent_width), narrow)], "payload")(
        place, routes.T, gate_levels.T, latent_grad
    )
    own = columns[3]
    core_own = swap(own, n_line, 1, 0)
    across = swap(columns[2], n_line, 0, 1)
    core_tokens = [swap(after(columns[1], across, core_own), n_line, 1, 0), swap(across[1], n_line, 1, 0)]
    side_in = swap(after(expert_in[0], across), n_line, 0, 1)

    project = call(
        functools.partial(project_body, n_line),
        [shape((2, tok_rows, latent_width), wide)] * 2 + [shape((n_line * block, latent_width), narrow)],
        "project",
    )
    keep, send, down = project(after(place, payload), columns[0], across, *core_tokens, *downs)
    half, cross = call(half_body, [rows_of(wide), rows_of(narrow)], "half")(
        place, keep, swap(send, n_line, 1, 0)
    )
    payloads = [payload] + [turn(after(payload, *downs[1:]), n_line, back) for back in range(1, n_line)]
    crossed = swap(cross, n_line, 0, 1)
    (latent,) = call(add_body, [rows_of(narrow)], "latent")(
        place, half, after(crossed, side_in, *payloads[1:])
    )
    groups = [[*range(1, n_line), 0]]
    riding = (1, n_line - 1)
    rows = [latent] + [turn(latent, n_line, back) for back in range(1, n_line)]

    side_out = swap(after(expert_out[0], latent), n_line, 0, 1)
    core_in = swap(after(side_in, latent), n_line, 1, 0)
    core_out = swap(after(side_out, *rows[1:]), n_line, 1, 0)
    weights = [own, core_own, side_in, side_out, core_in, core_out]
    side_down = swap(after(down, rows[1]), n_line, 0, 1)

    deltas_of, outs_of, saved = [None] * n_line, [None] * n_line, []
    done = latent
    for group in groups:
        count = len(group)
        outs = [rows_of(narrow if back else wide) for back in group for _ in range(2)]
        values = call(
            functools.partial(expert_body, count),
            outs + [shape((4, count * tok_rows, hidden_width), narrow)] * 3,
            "experts",
        )(after(place, done), *(rows[i] for i in group), *(payloads[i] for i in group), *weights)
        done, saved = values[0], saved + [list(values[-3:])]
        for i, back in enumerate(group):
            deltas_of[back], outs_of[back] = values[2 * i], values[2 * i + 1]

    def home(value, back):
        return turn(value, n_line, n_line - back) if back else value

    delta_lines = [home(value, back) for back, value in enumerate(deltas_of)]

    pair = (2, latent_width, hidden_width)

    def weight_grads(side, *earlier):
        return call(
            functools.partial(weight_grad_body, side, n_line, len(groups)),
            [shape(pair, wide), shape(pair, narrow)],
            "weight_grads",
            flops=2 * 4 * n_line * tok_rows * latent_width * hidden_width,
        )(
            after(place, *earlier),
            *(rows[i] for group in groups for i in group),
            *(value for values in saved for value in values),
        )

    far, far_other = weight_grads(1)
    far_other = swap(far_other, n_line, 1, 0)
    ahead = latent_width // 2
    far_first, far_rest = call(
        far_body, [shape((rows, hidden_width), narrow) for rows in (ahead, 2 * latent_width - ahead)], "far_grads"
    )(place, far, far_other)
    far_first = swap(far_first, n_line, 0, 1)
    delta_lines = [after(line, far_rest) for line in delta_lines]
    (delta,) = call(add_body, [rows_of(narrow)], "latent_delta")(place, *delta_lines)
    side_delta = swap(delta, n_line, 0, 1)
    out_lines = [outs_of[0]] + [home(after(outs_of[back], delta), back) if back not in riding else None for back in range(1, n_line)]
    far_rest = swap(after(far_rest, side_delta), n_line, 0, 1)
    near, near_other = weight_grads(0, delta)
    (others,) = call(pack_body, [shape((4, latent_width, hidden_width), narrow)], "pack")(
        after(place, delta), near_other, down, side_down
    )
    beside = [out_lines[back] for back in range(1, n_line) if back not in riding]
    core_deltas = [swap(delta, n_line, 1, 0), swap(after(side_delta, others, far_first, *beside), n_line, 1, 0)]
    blocks = call(
        functools.partial(down_grad_body, n_line),
        [
            shape((2, block, latent_width) if back in riding else (block, latent_width), narrow if back else wide)
            for back in range(n_line)
        ],
        "down_grad",
    )(place, columns[0], across, *core_tokens, delta, side_delta, *core_deltas, *(outs_of[back] for back in riding))
    others = [others, swap(after(others, blocks[1]), n_line, 1, 0)]
    (grad_tokens,) = call(
        functools.partial(token_grad_body, n_line, block), [shape((tok_rows, width), narrow)], "token_grad"
    )(place, after(delta, blocks[1]), *others)
    blocks = [blocks[0]] + [turn(blocks[back], n_line, n_line - back) for back in range(1, n_line)]
    grad_down, latent_out, grad_in, grad_out = call(
        functools.partial(last_body, riding, n_line),
        [shape((block, latent_width), wide), rows_of(narrow)]
        + [shape(value.shape, narrow) for value in (expert_in, expert_out)],
        "last_sums",
    )(after(place, grad_tokens), near, others[1], far_first, far_rest, *blocks, *(line for line in out_lines if line is not None))
    return (latent_out, grad_tokens, grad_down, grad_in, grad_out)


def slot_table(routes, capacity):
    flat = routes.reshape(-1)
    count = flat.shape[0]
    order = jnp.arange(count, dtype=jnp.int32)
    same = (flat[:, None] == flat[None, :]) & (order[None, :] < order[:, None])
    placed = jnp.sum(jnp.where(same, 1, 0), axis=1).astype(jnp.int32)
    return flat * capacity + placed


def routed_rows(tokens, routes, gate_levels, latent_grad, down_weight, expert_in, expert_out):
    tok_rows = tokens.shape[0]
    top = routes.shape[1]
    latent_width = down_weight.shape[1]
    n_major = lax.axis_size("expert")
    n_minor = lax.axis_size("dp")
    n_experts = n_major * n_minor
    capacity = 3 * tok_rows * top // (2 * n_experts)
    entries = tok_rows * top
    contract_last = (((1,), (1,)), ((), ()))
    contract_first = (((0,), (0,)), ((), ()))
    full_down = lax.all_gather(down_weight, ("expert", "dp"), axis=0, tiled=True)
    latent = jnp.dot(tokens, full_down, preferred_element_type=jnp.float32)
    latent = latent.astype(jnp.bfloat16)
    dest = slot_table(routes, capacity)
    source = (
        jnp.full((n_experts * capacity,), entries, jnp.int32)
        .at[dest]
        .set(jnp.arange(entries, dtype=jnp.int32))
    )
    token_of = jnp.where(source < entries, source // top, tok_rows)
    gates = gate_levels.astype(jnp.float32) * gate_unit
    zero_row = jnp.zeros((1, latent_width), jnp.bfloat16)
    latent_pad = jnp.concatenate([latent, zero_row], axis=0)
    send_latent = latent_pad[token_of].reshape(n_major, n_minor, capacity, latent_width)
    scaled = (gates[:, :, None] * latent_grad.astype(jnp.float32)[:, None, :]).astype(jnp.bfloat16)
    scaled_pad = jnp.concatenate([scaled.reshape(entries, latent_width), zero_row], axis=0)
    send_grad = scaled_pad[source].reshape(n_major, n_minor, capacity, latent_width)
    arrived = lax.all_to_all(
        lax.all_to_all(send_latent, "expert", split_axis=0, concat_axis=0, tiled=True),
        "dp",
        split_axis=1,
        concat_axis=1,
        tiled=True,
    )
    rows = arrived.reshape(-1, latent_width)
    weight_in = expert_in[0]
    weight_out = expert_out[0]
    before = jnp.dot(rows, weight_in, preferred_element_type=jnp.float32)
    active = jnp.maximum(before, 0.0)
    hidden = (active * active).astype(jnp.bfloat16)
    result = jnp.dot(hidden, weight_out, preferred_element_type=jnp.float32).astype(jnp.bfloat16)
    returned = lax.all_to_all(
        lax.all_to_all(
            result.reshape(n_major, n_minor, capacity, latent_width),
            "expert",
            split_axis=0,
            concat_axis=0,
            tiled=True,
        ),
        "dp",
        split_axis=1,
        concat_axis=1,
        tiled=True,
    )
    picked = returned.reshape(n_experts * capacity, latent_width)[dest].astype(jnp.float32)
    picked = picked.reshape(tok_rows, top, latent_width)
    latent_out = jnp.sum(gates[:, :, None] * picked, axis=1).astype(jnp.bfloat16)
    arrived_grad = lax.all_to_all(
        lax.all_to_all(send_grad, "expert", split_axis=0, concat_axis=0, tiled=True),
        "dp",
        split_axis=1,
        concat_axis=1,
        tiled=True,
    )
    grad_rows = arrived_grad.reshape(-1, latent_width)
    back_hidden = lax.dot_general(
        grad_rows, weight_out, contract_last, preferred_element_type=jnp.float32
    )
    back_pre = (back_hidden * 2.0 * active).astype(jnp.bfloat16)
    grad_out = lax.dot_general(
        hidden, grad_rows, contract_first, preferred_element_type=jnp.float32
    ).astype(jnp.bfloat16)
    grad_in = lax.dot_general(
        rows, back_pre, contract_first, preferred_element_type=jnp.float32
    ).astype(jnp.bfloat16)
    back_rows = lax.dot_general(
        back_pre, weight_in, contract_last, preferred_element_type=jnp.float32
    ).astype(jnp.bfloat16)
    came_back = lax.all_to_all(
        lax.all_to_all(
            back_rows.reshape(n_major, n_minor, capacity, latent_width),
            "expert",
            split_axis=0,
            concat_axis=0,
            tiled=True,
        ),
        "dp",
        split_axis=1,
        concat_axis=1,
        tiled=True,
    )
    gathered_back = came_back.reshape(n_experts * capacity, latent_width)[dest].astype(jnp.float32)
    latent_delta = jnp.sum(gathered_back.reshape(tok_rows, top, latent_width), axis=1).astype(
        jnp.bfloat16
    )
    grad_tokens = lax.dot_general(
        latent_delta, full_down, contract_last, preferred_element_type=jnp.float32
    )
    grad_tokens = grad_tokens.astype(jnp.bfloat16)
    grad_down = lax.psum_scatter(
        lax.dot_general(tokens, latent_delta, contract_first, preferred_element_type=jnp.float32),
        ("expert", "dp"),
        scatter_dimension=0,
        tiled=True,
    )
    return (latent_out, grad_tokens, grad_down, grad_in[None], grad_out[None])


def on_device(tokens, routes, *others):
    n_major = lax.axis_size("expert")
    n_experts = n_major * lax.axis_size("dp")
    few = n_experts <= 2 * routes.shape[1] and n_major % 2 == 0 and n_major >= 6 and lax.axis_size("dp") == 2
    return (all_rows if few else routed_rows)(tokens, routes, *others)


def solution(mesh):
    in_specs = (
        P(("group", "expert", "dp"), None),
        P(("group", "expert", "dp"), None),
        P(("group", "expert", "dp"), None),
        P(("group", "expert", "dp"), None),
        P(("expert", "dp"), None),
        P(("expert", "dp"), None, None),
        P(("expert", "dp"), None, None),
    )
    out_specs = (
        P(("group", "expert", "dp"), None),
        P(("group", "expert", "dp"), None),
        P(("group", "expert", "dp"), None),
        P(("group", "expert", "dp"), None, None),
        P(("group", "expert", "dp"), None, None),
    )
    return jax.shard_map(
        on_device, mesh=mesh, in_specs=in_specs, out_specs=out_specs, check_vma=False
    )
```

```python
import functools

import jax
import jax.numpy as jnp
from jax import lax
from jax.experimental import pallas as pl
from jax.experimental.pallas import tpu as pltpu
from jax.sharding import PartitionSpec as P

gate_unit = 1.0 / 1024.0
contract_last = (((1,), (1,)), ((), ()))
contract_first = (((0,), (0,)), ((), ()))
plane = ("expert", "dp")
wide = jnp.float32
narrow = jnp.bfloat16


def device_pairs(n_line, move):
    pairs = []
    for z in range(n_line):
        for x in range(2):
            for c in range(2):
                to_z, to_x, to_c = move(z, x, c)
                pairs.append(((z * 2 + x) * 2 + c, (to_z * 2 + to_x) * 2 + to_c))
    return pairs


def turn(value, n_line, by):
    return lax.ppermute(value, plane, device_pairs(n_line, lambda z, x, c: ((z + by) % n_line, x, c)))


def swap(value, n_line, core, side):
    return lax.ppermute(value, plane, device_pairs(n_line, lambda z, x, c: (z, x ^ side, c ^ core)))


def after(value, *earlier):
    return lax.optimization_barrier((value,) + earlier)[0]


def call(body, outs, name, scratch=(), outside=0, flops=0):
    vmem = pl.BlockSpec(memory_space=pltpu.VMEM)
    outer = pl.BlockSpec(memory_space=pltpu.HBM)

    def run(place, *operands):
        return pl.pallas_call(
            body,
            out_shape=outs,
            in_specs=[pl.BlockSpec(memory_space=pltpu.SMEM)]
            + [outer] * outside
            + [vmem] * (len(operands) - outside),
            out_specs=[vmem] * len(outs),
            scratch_shapes=list(scratch),
            compiler_params=pltpu.CompilerParams(vmem_limit_bytes=40 * 1024 * 1024),
            cost_estimate=pl.CostEstimate(flops=flops, bytes_accessed=0, transcendentals=0),
            name=name,
        )(place, *operands)

    return run


def columns_body(n_line, block, place, tokens, expert_in, expert_out, *refs):
    own, other, across, weights, sems = refs
    pieces = (own, across.at[0], other, across.at[1])
    copies = []
    for i, weight in enumerate((expert_in, expert_out)):
        copies.append(pltpu.make_async_copy(weight, weights.at[pl.ds(i, 1)], sems.at[i]))
    for core in range(2):
        for side in range(2):
            owner = (place[1] ^ side) * 2 + (place[2] ^ core)
            for z in range(n_line):
                start = pl.multiple_of((z * 4 + owner) * block, block)
                piece = pieces[core * 2 + side].at[:, pl.ds(z * block, block)]
                copies.append(
                    pltpu.make_async_copy(tokens.at[:, pl.ds(start, block)], piece, sems.at[len(copies)])
                )
    for copy in copies:
        copy.start()
    for copy in copies:
        copy.wait()


def add_body(place, *refs):
    total = refs[0][...].astype(wide)
    for value in refs[1:-1]:
        total = total + value[...].astype(wide)
    refs[-1][...] = total.astype(refs[-1].dtype)


def half_body(place, keep, arrived, mine, other):
    mine[...] = keep[0] + arrived[0]
    other[...] = (keep[1] + arrived[1]).astype(narrow)


def far_body(place, far, arrived, first, rest):
    split, width = first.shape[0], far.shape[1]
    total = [far[i] + arrived[i].astype(wide) for i in range(2)]
    first[...] = total[0][:split].astype(narrow)
    rest[: width - split] = total[0][split:].astype(narrow)
    rest[width - split :] = total[1].astype(narrow)


def pack_body(place, grads, down, side_down, out):
    out[:2] = grads[...]
    out[2], out[3] = down[...], side_down[...]


def last_body(riding, n_line, place, near, others, first, rest, *refs):
    blocks, pieces = refs[:n_line], list(refs[n_line:-4])
    grad_down, combined, *grads = refs[-4:]
    split = grads[0].shape[1] - first.shape[0]
    far = (jnp.concatenate([first[...], rest[:split]], axis=0), rest[split:])
    for i, out in enumerate(grads):
        out[0] = (near[i] + others[i].astype(wide) + far[i].astype(wide)).astype(narrow)
    total = blocks[0][...]
    out_total = pieces.pop(0)[...]
    for back in range(1, n_line):
        block = blocks[back].at[0] if back in riding else blocks[back]
        piece = blocks[back].at[1] if back in riding else pieces.pop(0)
        total = total + block[...].astype(wide)
        out_total = out_total + piece[...].astype(wide)
    grad_down[...] = total
    combined[...] = out_total.astype(narrow)


def payload_body(place, routes, levels, cotangent, payload):
    tok_rows = cotangent.shape[0]
    gate_rows = payload.shape[0] - tok_rows
    payload[:tok_rows, :] = cotangent[...]
    expert = lax.broadcasted_iota(jnp.int32, (gate_rows, tok_rows), 0)
    total = jnp.zeros((gate_rows, tok_rows), jnp.int32)
    for k in range(routes.shape[0]):
        total = total + jnp.where(expert == routes[k : k + 1, :], levels[k : k + 1, :], 0)
    low = total & 31
    payload[tok_rows:, :tok_rows] = (total - low).astype(wide).astype(narrow)
    payload[tok_rows:, tok_rows : 2 * tok_rows] = low.astype(wide).astype(narrow)
    rest = payload.shape[1] - 2 * tok_rows
    payload[tok_rows:, 2 * tok_rows :] = jnp.zeros((gate_rows, rest), narrow)


def project_body(n_line, place, *refs):
    own, across, core, core_across, *downs = refs[: 4 + n_line]
    pieces = (own, across.at[0], core, core_across)
    keep, send, down = refs[4 + n_line :]
    block = downs[0].shape[0]
    for back in range(n_line):
        z = lax.rem(place[0] + n_line - back, n_line)
        down[pl.ds(pl.multiple_of(z * block, block), block), :] = downs[back][...]
    for core, out in ((1, send), (0, keep)):
        for side in range(2):
            out[side] = jnp.dot(pieces[core * 2 + side][...], down[...], preferred_element_type=wide)


def gate_tile(payload, tok_rows, expert):
    packed = payload[tok_rows:, :]
    rows = lax.broadcasted_iota(jnp.int32, (packed.shape[0], 128), 0)
    pick = jnp.where(rows == expert, 1.0, 0.0).astype(narrow)
    dot = functools.partial(lax.dot_general, dimension_numbers=contract_first, preferred_element_type=wide)
    total = dot(packed[:, :tok_rows], pick) + dot(packed[:, tok_rows : 2 * tok_rows], pick)
    return total * gate_unit


def expert_body(count, place, *refs):
    rows_in, payloads = refs[:count], refs[count : 2 * count]
    own, core, *sides = refs[2 * count : 2 * count + 6]
    weights = (own.at[0], own.at[1], sides[0], sides[1], core.at[0], core.at[1], sides[2], sides[3])
    outs = refs[2 * count + 6 :]
    *sums, hiddens, scaleds, back_pres = outs
    tok_rows, width = rows_in[0].shape
    for first in range(0, count, 4):
        group = range(first, min(first + 4, count))
        span = slice(first * tok_rows, (first + len(group)) * tok_rows)
        stack = lambda values: jnp.concatenate(list(values), axis=0)
        rows = stack(rows_in[i][...] for i in group)
        cotangent = stack(payloads[i][:tok_rows, :] for i in group).astype(wide)
        out_sum = jnp.zeros(rows.shape, wide)
        delta_sum = jnp.zeros(rows.shape, wide)
        for e in range(4):
            weight_in, weight_out = weights[2 * e], weights[2 * e + 1]
            gate = stack(gate_tile(payloads[i], tok_rows, place[3 + e]) for i in group)
            gate = jnp.concatenate([gate] * (width // 128), axis=1)
            active = jnp.maximum(jnp.dot(rows, weight_in[...], preferred_element_type=wide), 0.0)
            hidden = (active * active).astype(narrow)
            hiddens[e, span, :] = hidden
            scaled = (gate * cotangent).astype(narrow)
            scaleds[e, span, :] = scaled
            back_hidden = lax.dot_general(scaled, weight_out[...], contract_last, preferred_element_type=wide)
            back_pre = (back_hidden * 2.0 * active).astype(narrow)
            back_pres[e, span, :] = back_pre
            result = jnp.dot(hidden, weight_out[...], preferred_element_type=wide).astype(narrow)
            out_sum = out_sum + gate * result.astype(wide)
            back_rows = lax.dot_general(back_pre, weight_in[...], contract_last, preferred_element_type=wide)
            delta_sum = delta_sum + back_rows.astype(narrow).astype(wide)
        for i in group:
            part = slice((i - first) * tok_rows, (i - first + 1) * tok_rows)
            out = sums.pop(0)
            out[...] = delta_sum[part].astype(out.dtype)
            out = sums.pop(0)
            out[...] = out_sum[part].astype(out.dtype)


def weight_grad_body(side, n_rows, n_sets, place, *refs):
    rows_in = refs[:n_rows]
    sets = [refs[n_rows + 3 * i : n_rows + 3 * i + 3] for i in range(n_sets)]
    outs = refs[n_rows + 3 * n_sets :]
    dot = functools.partial(lax.dot_general, dimension_numbers=contract_first, preferred_element_type=wide)
    rows = jnp.concatenate([r[...] for r in rows_in], axis=0)
    for core, out in enumerate(outs):
        hidden, scaled, back_pre = (
            jnp.concatenate([values[i][core * 2 + side] for values in sets], axis=0) for i in range(3)
        )
        out[0] = dot(rows, back_pre).astype(out.dtype)
        out[1] = dot(hidden, scaled).astype(out.dtype)


def down_grad_body(n_line, place, *refs):
    own, across, core, core_across, *deltas = refs[:8]
    riders, blocks = refs[8:-n_line], refs[-n_line:]
    tokens = jnp.concatenate([own[...], across[0], core[...], core_across[...]], axis=0)
    delta = jnp.concatenate([d[...] for d in deltas], axis=0)
    part = lax.dot_general(tokens, delta, contract_first, preferred_element_type=wide)
    block = blocks[0].shape[0]
    targets = [out if len(out.shape) == 2 else out.at[0] for out in blocks]
    for rider, out in zip(riders, [out for out in blocks if len(out.shape) == 3]):
        out[1] = rider[...]
    for z in range(n_line):
        for back in range(n_line):

            @pl.when(lax.rem(place[0] + n_line - back, n_line) == z)
            def _(z=z, back=back):
                targets[back][...] = part[z * block : (z + 1) * block].astype(targets[back].dtype)


def token_grad_body(n_line, block, place, delta, held, arrived, out):
    for i, weight in enumerate((held.at[2], held.at[3], arrived.at[2], arrived.at[3])):
        owner = (place[1] ^ (i % 2)) * 2 + (place[2] ^ (i // 2))
        part = lax.dot_general(delta[...], weight[...], contract_last, preferred_element_type=wide)
        part = part.astype(narrow)
        for z in range(n_line):
            start = pl.multiple_of((z * 4 + owner) * block, block)
            out[:, pl.ds(start, block)] = part[:, z * block : (z + 1) * block]


def all_rows(tokens, routes, gate_levels, latent_grad, down_weight, expert_in, expert_out):
    tok_rows, width = tokens.shape
    latent_width = down_weight.shape[1]
    hidden_width = expert_in.shape[2]
    n_major = lax.axis_size("expert")
    n_line = n_major // 2
    n_experts = n_major * 2
    block = width // n_experts
    major = lax.axis_index("expert")
    my_core = lax.axis_index("dp")
    place = jnp.stack(
        [major // 2, major % 2, my_core]
        + [(major ^ side) * 2 + (my_core ^ core) for core in range(2) for side in range(2)]
    ).astype(jnp.int32)
    shape = jax.ShapeDtypeStruct
    rows_of = lambda kind: shape((tok_rows, latent_width), kind)

    downs = [down_weight] + [turn(down_weight, n_line, back) for back in range(1, n_line)]

    gate_rows = -(-n_experts // 16) * 16
    columns = call(
        functools.partial(columns_body, n_line, block),
        [shape((tok_rows, n_line * block), narrow)] * 2
        + [shape((2, tok_rows, n_line * block), narrow), shape((2, latent_width, hidden_width), narrow)],
        "columns",
        scratch=[pltpu.SemaphoreType.DMA((4 * n_line + 2,))],
        outside=3,
    )(place, *(pltpu.with_memory_space_constraint(value, pltpu.HBM) for value in (tokens, expert_in, expert_out)))
    (payload,) = call(payload_body, [shape((tok_rows + gate_rows, latent_width), narrow)], "payload")(
        place, routes.T, gate_levels.T, latent_grad
    )
    own = columns[3]
    core_own = swap(own, n_line, 1, 0)
    across = swap(columns[2], n_line, 0, 1)
    core_tokens = [swap(after(columns[1], across, core_own), n_line, 1, 0), swap(across[1], n_line, 1, 0)]
    side_in = swap(after(expert_in[0], core_tokens[0]), n_line, 0, 1)

    project = call(
        functools.partial(project_body, n_line),
        [shape((2, tok_rows, latent_width), wide)] * 2 + [shape((n_line * block, latent_width), narrow)],
        "project",
    )
    keep, send, down = project(after(place, payload), columns[0], across, *core_tokens, *downs)
    half, cross = call(half_body, [rows_of(wide), rows_of(narrow)], "half")(
        after(place, side_in), keep, swap(send, n_line, 1, 0)
    )
    payloads = [payload] + [turn(after(payload, *downs[1:]), n_line, back) for back in range(1, n_line)]
    crossed = swap(cross, n_line, 0, 1)
    (latent,) = call(add_body, [rows_of(narrow)], "latent")(
        place, half, after(crossed, side_in, *payloads[1:])
    )
    groups = [[*range(1, n_line), 0]]
    riding = (1, n_line - 1)
    rows = [latent] + [turn(latent, n_line, back) for back in range(1, n_line)]

    side_out = swap(after(expert_out[0], latent), n_line, 0, 1)
    core_in = swap(after(side_in, latent), n_line, 1, 0)
    core_out = swap(after(side_out, *rows[1:]), n_line, 1, 0)
    weights = [own, core_own, side_in, side_out, core_in, core_out]
    side_down = swap(after(down, rows[1]), n_line, 0, 1)

    deltas_of, outs_of, saved = [None] * n_line, [None] * n_line, []
    done = latent
    for group in groups:
        count = len(group)
        outs = [rows_of(narrow if back else wide) for back in group for _ in range(2)]
        values = call(
            functools.partial(expert_body, count),
            outs + [shape((4, count * tok_rows, hidden_width), narrow)] * 3,
            "experts",
        )(after(place, done), *(rows[i] for i in group), *(payloads[i] for i in group), *weights)
        done, saved = values[0], saved + [list(values[-3:])]
        for i, back in enumerate(group):
            deltas_of[back], outs_of[back] = values[2 * i], values[2 * i + 1]

    def home(value, back):
        return turn(value, n_line, n_line - back) if back else value

    delta_lines = [home(value, back) for back, value in enumerate(deltas_of)]

    pair = (2, latent_width, hidden_width)

    def weight_grads(side, *earlier):
        return call(
            functools.partial(weight_grad_body, side, n_line, len(groups)),
            [shape(pair, wide), shape(pair, narrow)],
            "weight_grads",
            flops=2 * 4 * n_line * tok_rows * latent_width * hidden_width,
        )(
            after(place, *earlier),
            *(rows[i] for group in groups for i in group),
            *(value for values in saved for value in values),
        )

    far, far_other = weight_grads(1)
    far_other = swap(far_other, n_line, 1, 0)
    ahead = latent_width // 2
    far_first, far_rest = call(
        far_body, [shape((rows, hidden_width), narrow) for rows in (ahead, 2 * latent_width - ahead)], "far_grads"
    )(place, far, far_other)
    far_first = swap(far_first, n_line, 0, 1)
    delta_lines = [after(line, far_rest) for line in delta_lines]
    (delta,) = call(add_body, [rows_of(narrow)], "latent_delta")(place, *delta_lines)
    side_delta = swap(delta, n_line, 0, 1)
    out_lines = [outs_of[0]] + [home(after(outs_of[back], delta), back) if back not in riding else None for back in range(1, n_line)]
    far_rest = swap(after(far_rest, side_delta), n_line, 0, 1)
    near, near_other = weight_grads(0, delta)
    (others,) = call(pack_body, [shape((4, latent_width, hidden_width), narrow)], "pack")(
        after(place, delta), near_other, down, side_down
    )
    beside = [out_lines[back] for back in range(1, n_line) if back not in riding]
    core_deltas = [swap(delta, n_line, 1, 0), swap(after(side_delta, others, far_first, *beside), n_line, 1, 0)]
    blocks = call(
        functools.partial(down_grad_body, n_line),
        [
            shape((2, block, latent_width) if back in riding else (block, latent_width), narrow if back else wide)
            for back in range(n_line)
        ],
        "down_grad",
    )(place, columns[0], across, *core_tokens, delta, side_delta, *core_deltas, *(outs_of[back] for back in riding))
    others = [others, swap(after(others, blocks[1]), n_line, 1, 0)]
    (grad_tokens,) = call(
        functools.partial(token_grad_body, n_line, block), [shape((tok_rows, width), narrow)], "token_grad"
    )(place, after(delta, blocks[1]), *others)
    blocks = [blocks[0]] + [turn(blocks[back], n_line, n_line - back) for back in range(1, n_line)]
    grad_down, latent_out, grad_in, grad_out = call(
        functools.partial(last_body, riding, n_line),
        [shape((block, latent_width), wide), rows_of(narrow)]
        + [shape(value.shape, narrow) for value in (expert_in, expert_out)],
        "last_sums",
    )(after(place, grad_tokens), near, others[1], far_first, far_rest, *blocks, *(line for line in out_lines if line is not None))
    return (latent_out, grad_tokens, grad_down, grad_in, grad_out)


def slot_table(routes, capacity):
    flat = routes.reshape(-1)
    count = flat.shape[0]
    order = jnp.arange(count, dtype=jnp.int32)
    same = (flat[:, None] == flat[None, :]) & (order[None, :] < order[:, None])
    placed = jnp.sum(jnp.where(same, 1, 0), axis=1).astype(jnp.int32)
    return flat * capacity + placed


def routed_rows(tokens, routes, gate_levels, latent_grad, down_weight, expert_in, expert_out):
    tok_rows = tokens.shape[0]
    top = routes.shape[1]
    latent_width = down_weight.shape[1]
    n_major = lax.axis_size("expert")
    n_minor = lax.axis_size("dp")
    n_experts = n_major * n_minor
    capacity = 3 * tok_rows * top // (2 * n_experts)
    entries = tok_rows * top
    contract_last = (((1,), (1,)), ((), ()))
    contract_first = (((0,), (0,)), ((), ()))
    full_down = lax.all_gather(down_weight, ("expert", "dp"), axis=0, tiled=True)
    latent = jnp.dot(tokens, full_down, preferred_element_type=jnp.float32)
    latent = latent.astype(jnp.bfloat16)
    dest = slot_table(routes, capacity)
    source = (
        jnp.full((n_experts * capacity,), entries, jnp.int32)
        .at[dest]
        .set(jnp.arange(entries, dtype=jnp.int32))
    )
    token_of = jnp.where(source < entries, source // top, tok_rows)
    gates = gate_levels.astype(jnp.float32) * gate_unit
    zero_row = jnp.zeros((1, latent_width), jnp.bfloat16)
    latent_pad = jnp.concatenate([latent, zero_row], axis=0)
    send_latent = latent_pad[token_of].reshape(n_major, n_minor, capacity, latent_width)
    scaled = (gates[:, :, None] * latent_grad.astype(jnp.float32)[:, None, :]).astype(jnp.bfloat16)
    scaled_pad = jnp.concatenate([scaled.reshape(entries, latent_width), zero_row], axis=0)
    send_grad = scaled_pad[source].reshape(n_major, n_minor, capacity, latent_width)
    arrived = lax.all_to_all(
        lax.all_to_all(send_latent, "expert", split_axis=0, concat_axis=0, tiled=True),
        "dp",
        split_axis=1,
        concat_axis=1,
        tiled=True,
    )
    rows = arrived.reshape(-1, latent_width)
    weight_in = expert_in[0]
    weight_out = expert_out[0]
    before = jnp.dot(rows, weight_in, preferred_element_type=jnp.float32)
    active = jnp.maximum(before, 0.0)
    hidden = (active * active).astype(jnp.bfloat16)
    result = jnp.dot(hidden, weight_out, preferred_element_type=jnp.float32).astype(jnp.bfloat16)
    returned = lax.all_to_all(
        lax.all_to_all(
            result.reshape(n_major, n_minor, capacity, latent_width),
            "expert",
            split_axis=0,
            concat_axis=0,
            tiled=True,
        ),
        "dp",
        split_axis=1,
        concat_axis=1,
        tiled=True,
    )
    picked = returned.reshape(n_experts * capacity, latent_width)[dest].astype(jnp.float32)
    picked = picked.reshape(tok_rows, top, latent_width)
    latent_out = jnp.sum(gates[:, :, None] * picked, axis=1).astype(jnp.bfloat16)
    arrived_grad = lax.all_to_all(
        lax.all_to_all(send_grad, "expert", split_axis=0, concat_axis=0, tiled=True),
        "dp",
        split_axis=1,
        concat_axis=1,
        tiled=True,
    )
    grad_rows = arrived_grad.reshape(-1, latent_width)
    back_hidden = lax.dot_general(
        grad_rows, weight_out, contract_last, preferred_element_type=jnp.float32
    )
    back_pre = (back_hidden * 2.0 * active).astype(jnp.bfloat16)
    grad_out = lax.dot_general(
        hidden, grad_rows, contract_first, preferred_element_type=jnp.float32
    ).astype(jnp.bfloat16)
    grad_in = lax.dot_general(
        rows, back_pre, contract_first, preferred_element_type=jnp.float32
    ).astype(jnp.bfloat16)
    back_rows = lax.dot_general(
        back_pre, weight_in, contract_last, preferred_element_type=jnp.float32
    ).astype(jnp.bfloat16)
    came_back = lax.all_to_all(
        lax.all_to_all(
            back_rows.reshape(n_major, n_minor, capacity, latent_width),
            "expert",
            split_axis=0,
            concat_axis=0,
            tiled=True,
        ),
        "dp",
        split_axis=1,
        concat_axis=1,
        tiled=True,
    )
    gathered_back = came_back.reshape(n_experts * capacity, latent_width)[dest].astype(jnp.float32)
    latent_delta = jnp.sum(gathered_back.reshape(tok_rows, top, latent_width), axis=1).astype(
        jnp.bfloat16
    )
    grad_tokens = lax.dot_general(
        latent_delta, full_down, contract_last, preferred_element_type=jnp.float32
    )
    grad_tokens = grad_tokens.astype(jnp.bfloat16)
    grad_down = lax.psum_scatter(
        lax.dot_general(tokens, latent_delta, contract_first, preferred_element_type=jnp.float32),
        ("expert", "dp"),
        scatter_dimension=0,
        tiled=True,
    )
    return (latent_out, grad_tokens, grad_down, grad_in[None], grad_out[None])


def on_device(tokens, routes, *others):
    n_major = lax.axis_size("expert")
    n_experts = n_major * lax.axis_size("dp")
    few = n_experts <= 2 * routes.shape[1] and n_major % 2 == 0 and n_major >= 6 and lax.axis_size("dp") == 2
    return (all_rows if few else routed_rows)(tokens, routes, *others)


def solution(mesh):
    in_specs = (
        P(("group", "expert", "dp"), None),
        P(("group", "expert", "dp"), None),
        P(("group", "expert", "dp"), None),
        P(("group", "expert", "dp"), None),
        P(("expert", "dp"), None),
        P(("expert", "dp"), None, None),
        P(("expert", "dp"), None, None),
    )
    out_specs = (
        P(("group", "expert", "dp"), None),
        P(("group", "expert", "dp"), None),
        P(("group", "expert", "dp"), None),
        P(("group", "expert", "dp"), None, None),
        P(("group", "expert", "dp"), None, None),
    )
    return jax.shard_map(
        on_device, mesh=mesh, in_specs=in_specs, out_specs=out_specs, check_vma=False
    )
```
